32 devices in a mesh: dp: 4 (over z), ctx: 4 (over x, core), exp: 2 (over y).
Axes of the slice: x: 2, y: 2, z: 4, core: 2. Of those that a mesh axis runs over, the one named last changes fastest.
Arguments:
- tokens: bfloat16 [8, 1536, 768], P(('dp', 'exp'), 'ctx'), may hold values from -6 to 6
- cotangent: bfloat16 [8, 1536, 768], P(('dp', 'exp'), 'ctx'), may hold values from -6 to 6
- previous: float32 [8, 1536, 12], P(('dp', 'exp'), 'ctx'), may hold values from -6 to 6
- routes: int32 [8, 1536, 2], P(('dp', 'exp'), 'ctx'), may hold values from 0 to 11, all different within a row; in each aligned block of 384 rows (0 to 383, 384 to 767, ..., all dimensions but the last counted through in order) at most 96 rows name the same one
- boundaries: int32 [8, 8], P(('dp', 'exp')), may hold values from 0 to 1535, as said below
- norm_first: bfloat16 [768], replicated, may hold values from 0.5 to 1.5
- query_weight: bfloat16 [768, 768], replicated, may hold values from -0.21875 to 0.21875
- key_weight: bfloat16 [768, 768], replicated, may hold values from -0.21875 to 0.21875
- value_weight: bfloat16 [768, 768], replicated, may hold values from -0.21875 to 0.21875
- output_weight: bfloat16 [768, 768], replicated, may hold values from -1.25 to 1.25
- norm_second: bfloat16 [768], replicated, may hold values from 0.5 to 1.5
- router: bfloat16 [768, 12], replicated, may hold values from -0.125 to 0.125
- gate_carry: bfloat16 [12, 12], replicated, may hold values from -1 to 1
- constant_map: bfloat16 [2, 768, 2], replicated, may hold values from -0.21875 to 0.21875
- constant_vector: bfloat16 [2, 768], replicated, may hold values from -6 to 6
- expert_gate: bfloat16 [8, 768, 2048], P('exp'), may hold values from -0.21875 to 0.21875
- expert_linear: bfloat16 [8, 768, 2048], P('exp'), may hold values from -0.21875 to 0.21875
- expert_down: bfloat16 [8, 2048, 768], P('exp'), may hold values from -0.5 to 0.5
Outputs:
- result: bfloat16 [8, 1536, 768], P(('dp', 'exp'), 'ctx')
- token_grads: float32 [8, 1536, 768], P(('dp', 'exp'), 'ctx')
- first_grads: float32 [768], replicated
- query_grads: float32 [768, 768], replicated
- key_grads: float32 [768, 768], replicated
- value_grads: float32 [768, 768], replicated
- output_grads: float32 [768, 768], replicated
- second_grads: float32 [768], replicated
- router_grads: float32 [768, 12], replicated
- carry_grads: float32 [12, 12], replicated
- map_grads: float32 [2, 768, 2], replicated
- vector_grads: float32 [2, 768], replicated
- gate_grads: float32 [8, 768, 2048], P('exp', None, 'dp')
- linear_grads: float32 [8, 768, 2048], P('exp', None, 'dp')
- down_grads: float32 [8, 2048, 768], P('exp', 'dp')
The draws below stay inside these ranges and needn't reach their ends.
Inputs may be any that keep to these rules, and one draw needn't show every extreme that they name: `routes`: each position names two different experts; among the 384 positions of one device no expert is named more than 96 times. `boundaries`: each row rises strictly and starts with 0; one document of each stream begins within its first 384 positions and ends within its last 384.
All inputs are finite; a program needn't handle non-finite values.
Results may differ from the reference program's by a relative error of at most 0.025.
Values may be sent and summed in bfloat16 or wider, within the bound.
A program may use at most 320 MiB of HBM per device.

```python
import math
import jax
import jax.numpy as jnp
import numpy as np
from jax import lax

D = 768
HEADS = 12
HEAD_DIM = 64
FF = 2048
TOK_DEV = 384
NDOCS = 8
N_FFN = 8
E_ALL = 12
CAP = 96
SEQ = 1536
STREAMS = 8


def draw_boundaries(key, part):
    key = jax.random.fold_in(key, 11)

    def one_row(row_key):
        order = jax.random.permutation(row_key, 2 * TOK_DEV - 2) + 1
        picked = jnp.sort(order[:NDOCS - 1])
        placed = jnp.where(picked < TOK_DEV, picked, picked + SEQ - 2 * TOK_DEV + 1)
        return jnp.concatenate([jnp.zeros((1,), jnp.int32), placed.astype(jnp.int32)])
    return jax.vmap(one_row)(jax.random.split(key, STREAMS))


def shard_levels(key, extent, pieces, low, largest):
    factor_of = 1.0
    for position, shards_of in pieces:
        draws = jax.random.uniform(jax.random.fold_in(jax.random.fold_in(key, 6), position), (shards_of,), jnp.float32, low / len(pieces), largest / len(pieces))
        factor_of = factor_of * jnp.repeat(jnp.exp(draws), extent[position] // shards_of).reshape((-1,) + (1,) * (len(extent) - 1 - position))
    return factor_of


def shared_out(own_key, own, number, rows, count, top, limit, skew):
    sequence = jax.random.permutation(own_key, count)
    heavy_load, ordinary = load_shares(count, rows * top, limit, skew, True), load_shares(count, rows * top, limit, skew, False)
    places = jnp.arange(count)

    def named(lengths, offset_by):
        used = int((lengths > 0).sum())
        fixed = max(1, used // 4)
        moved = fixed + (places - fixed + offset_by * (used - fixed)) % max(1, count - fixed)
        return jnp.zeros((count,), jnp.int32).at[sequence[jnp.where(places < fixed, places, moved)]].set(jnp.asarray(lengths, jnp.int32))

    lengths = jnp.where(number % 4 == 0, named(heavy_load, number // 4), named(ordinary, number - number // 4 - 1))
    mixed = jax.random.permutation(jax.random.fold_in(own, 3), count)
    donor, receiver = mixed[0:count // 2 * 2:2], mixed[1:count // 2 * 2:2]
    slack = jnp.minimum(lengths[donor] - 1, limit - lengths[receiver]) // 2
    slack = jnp.where((donor == sequence[0]) | (receiver == sequence[0]) | (lengths[receiver] == 0), 0, jnp.maximum(slack, 0))
    moved = jax.random.randint(jax.random.fold_in(own, 4), (count // 2,), 0, 1 << 20) % (slack + 1)
    lengths = lengths.at[donor].add(-moved).at[receiver].add(moved)
    labels = jnp.searchsorted(jnp.cumsum(lengths), jnp.arange(rows * top), side="right").astype(jnp.int32)
    grid = labels.reshape(top, rows).T
    grid = grid[jax.random.permutation(jax.random.fold_in(own, 1), rows)]
    offset_by = jax.random.randint(jax.random.fold_in(own, 2), (rows, 1), 0, top)
    return jnp.take_along_axis(grid, (jnp.arange(top)[None, :] + offset_by) % top, axis=1)


def load_shares(number_of, total, limit, slope, full):
    loads = [(1 << 20) // math.isqrt(rank ** slope) + 1 for rank in range(1, number_of + 1)]
    largest = limit if full else min(limit, max(-(-total // number_of), total * loads[0] // sum(loads)))
    least = 1 if total - largest >= number_of - 1 else 0
    counts, surplus = [largest] + [least] * (number_of - 1), total - largest - least * (number_of - 1)
    while surplus > 0:
        candidates = [i for i in range(1, number_of) if counts[i] < largest] or [i for i in range(1, number_of) if counts[i] < limit]
        pool, remaining = sum([loads[i] for i in candidates]), surplus
        for i in candidates:
            addition = min(limit - counts[i], max(1, remaining * loads[i] // pool), surplus)
            counts[i] = counts[i] + addition
            surplus = surplus - addition
    return np.array(counts)


def gaussian(stream_key, shape, deviation, bound, pieces=(), kind=jnp.bfloat16):
    values = jax.random.normal(stream_key, shape, jnp.float32) * deviation
    if len(pieces) > 0:
        values = shard_levels(stream_key, shape, pieces, -0.22, 0.18) * values
    return jnp.clip(values, min=-bound, max=bound).astype(kind)


def setup_inputs(seed: int = 0) -> dict:
    splits = jax.random.split(jax.random.key(seed), 19)
    tokens = gaussian(splits[0], (STREAMS, SEQ, D), 1.0, 6.0, ((0, 8), (1, 4)))
    cotangent = gaussian(splits[1], (STREAMS, SEQ, D), 1.0, 6.0, ((0, 8), (1, 4)))
    previous = gaussian(splits[2], (STREAMS, SEQ, E_ALL), 1.0, 6.0, ((0, 8), (1, 4)), jnp.float32)
    routes_keys = jax.random.split(jax.random.fold_in(splits[3], 1), STREAMS * SEQ // TOK_DEV)
    routes_turns = jax.random.permutation(jax.random.fold_in(splits[3], 3), STREAMS * SEQ // TOK_DEV)
    routes = jax.vmap(lambda own, number: shared_out(jax.random.fold_in(splits[3], 2), own, number, TOK_DEV, E_ALL, 2, CAP, 1))(routes_keys, routes_turns).reshape((STREAMS, SEQ, 2))
    boundaries = draw_boundaries(jax.random.fold_in(splits[18], 71), 0)
    norm_first = jnp.clip(1.0 + 0.1 * jax.random.normal(splits[5], (D,), jnp.float32), 0.5, 1.5).astype(jnp.bfloat16)
    query_weight = gaussian(splits[6], (D, D), D ** -0.5, 0.21875)
    key_weight = gaussian(splits[7], (D, D), D ** -0.5, 0.21875)
    value_weight = gaussian(splits[8], (D, D), D ** -0.5, 0.21875)
    output_weight = gaussian(splits[9], (D, D), (D // 32) ** -0.5, 1.25)
    norm_second = jnp.clip(1.0 + 0.1 * jax.random.normal(splits[10], (D,), jnp.float32), 0.5, 1.5).astype(jnp.bfloat16)
    router = gaussian(splits[11], (D, E_ALL), (3 * D) ** -0.5, 0.125)
    gate_carry = gaussian(splits[12], (E_ALL, E_ALL), (3 * E_ALL) ** -0.5, 1.0)
    constant_map = gaussian(splits[13], (2, D, 2), D ** -0.5, 0.21875)
    constant_vector = gaussian(splits[14], (2, D), 1.0, 6.0)
    expert_gate = gaussian(splits[15], (N_FFN, D, FF), D ** -0.5, 0.21875, ((0, 2),))
    expert_linear = gaussian(splits[16], (N_FFN, D, FF), D ** -0.5, 0.21875, ((0, 2),))
    expert_down = gaussian(splits[17], (N_FFN, FF, D), (FF // 16) ** -0.5, 0.5, ((0, 2),))
    return {"tokens": tokens, "cotangent": cotangent, "previous": previous, "routes": routes, "boundaries": boundaries, "norm_first": norm_first, "query_weight": query_weight, "key_weight": key_weight, "value_weight": value_weight, "output_weight": output_weight, "norm_second": norm_second, "router": router, "gate_carry": gate_carry, "constant_map": constant_map, "constant_vector": constant_vector, "expert_gate": expert_gate, "expert_linear": expert_linear, "expert_down": expert_down}


EPSILON = 1e-06
NEGATIVE = -1e+30
HIGH = lax.Precision.HIGHEST

@jax.custom_vjp
def low(v):
    return lax.optimization_barrier(v.astype(jnp.bfloat16)).astype(jnp.float32)

@jax.custom_vjp
def low_back(v):
    return v

def low_keep(v):
    return (low(v), None)

def low_pass(kept, grad):
    return (grad,)

def back_keep(v):
    return (v, None)

def back_low(kept, grad):
    return (low(grad),)
low.defvjp(low_keep, low_pass)
low_back.defvjp(back_keep, back_low)

def matmul(left, right):
    return jnp.dot(left, right, precision=HIGH)

def normalize(values, gain):
    return values * lax.rsqrt(lax.optimization_barrier(jnp.mean(values * values, axis=-1, keepdims=True)) + EPSILON) * gain

def rotary(values, positions):
    half_dim = values.shape[-1] // 2
    frequency = jnp.exp(jnp.arange(half_dim, dtype=jnp.float32) * (-2.0 * math.log(10000.0) / values.shape[-1]))
    angles = positions.astype(jnp.float32)[:, None] * frequency[None, :]
    cosine = jnp.cos(angles)[:, None, :]
    sine_part = jnp.sin(angles)[:, None, :]
    leading = values[..., :half_dim]
    trailing = values[..., half_dim:]
    return jnp.concatenate([leading * cosine - trailing * sine_part, trailing * cosine + leading * sine_part], axis=-1)

def document_ids(positions, starts):
    return lax.optimization_barrier(jnp.sum((starts[None, :] <= positions[:, None]).astype(jnp.int32), axis=1)) - 1

def attention(queries, key_heads, values, positions, documents):
    length = queries.shape[0]
    block_size = 512 if length % 512 == 0 else length
    scale = HEAD_DIM ** (-0.5)

    def one_block(block_index):
        begin = block_index * block_size
        block_queries = lax.dynamic_slice_in_dim(queries, begin, block_size, 0)
        query_pos = lax.dynamic_slice_in_dim(positions, begin, block_size, 0)
        query_doc = lax.dynamic_slice_in_dim(documents, begin, block_size, 0)
        scores = low_back(jnp.einsum('qhd,khd->qhk', block_queries, key_heads, precision=HIGH)) * scale
        allowed = ((query_doc[:, None] == documents[None, :]) & (positions[None, :] <= query_pos[:, None]))[:, None, :]
        scores = jnp.where(allowed, scores, NEGATIVE)
        weights = jax.nn.softmax(scores, axis=-1)
        return jnp.einsum('qhk,khd->qhd', low(weights), values, precision=HIGH)
    blocks = lax.map(jax.checkpoint(one_block), jnp.arange(length // block_size, dtype=jnp.int32))
    return blocks.reshape(queries.shape)

def one_stream(arrays, weights):
    tokens, previous, routes, boundaries = arrays
    norm_first, query_weight, key_weight, value_weight, output_weight, norm_second, router, gate_carry, constant_map, constant_vector, expert_gate, expert_linear, expert_down = weights
    length = tokens.shape[0]
    heads_shape = (length, HEADS, HEAD_DIM)
    positions = jnp.arange(length, dtype=jnp.int32)
    documents = document_ids(positions, boundaries)
    normed = low(normalize(tokens, norm_first))
    queries = low(rotary(low_back(matmul(normed, query_weight)).reshape(heads_shape), positions))
    key_heads = low(rotary(low_back(matmul(normed, key_weight)).reshape(heads_shape), positions))
    values = low(low_back(matmul(normed, value_weight))).reshape(heads_shape)
    attended = low_back(low(attention(queries, key_heads, values, positions, documents))).reshape(length, HEADS * HEAD_DIM)
    middle = tokens + low_back(matmul(attended, output_weight))
    second = normalize(middle, norm_second)
    second_low = low(second)
    logits = low_back(matmul(second_low, router)) + matmul(previous, gate_carry)
    gate_probs = jax.nn.softmax(logits, axis=-1)
    chosen = lax.optimization_barrier(jnp.sum((routes[:, :, None] == jnp.arange(E_ALL, dtype=jnp.int32)[None, None, :]).astype(jnp.float32), axis=1))
    gate_weights = gate_probs * chosen
    combined = jnp.zeros_like(second)
    for expert in range(N_FFN):
        inputs = low_back(second_low)
        gate_part = low_back(matmul(inputs, expert_gate[expert]))
        linear_part = low_back(matmul(inputs, expert_linear[expert]))
        hidden = low(jax.nn.silu(gate_part) * linear_part)
        expert_out = low_back(low(matmul(hidden, expert_down[expert])))
        combined = combined + gate_weights[:, expert:expert + 1] * expert_out
    combined = combined + gate_weights[:, N_FFN + 1:N_FFN + 2] * second
    for constant_index in range(2):
        mixing = jax.nn.softmax(low_back(matmul(second_low, constant_map[constant_index])), axis=-1)
        constant_term = mixing[:, 0:1] * second + mixing[:, 1:2] * constant_vector[constant_index][None, :]
        column = N_FFN + 2 + constant_index
        combined = combined + gate_weights[:, column:column + 1] * constant_term
    return middle + combined

def forward_all(tokens, weights, previous, routes, boundaries):

    def per_stream(arrays):
        return one_stream(arrays, weights)
    return lax.map(jax.checkpoint(per_stream), (tokens, previous, routes, boundaries))

def reference(tokens, cotangent, previous, routes, boundaries, norm_first, query_weight, key_weight, value_weight, output_weight, norm_second, router, gate_carry, constant_map, constant_vector, expert_gate, expert_linear, expert_down):
    floats = tuple((argument.astype(jnp.float32) for argument in (tokens, norm_first, query_weight, key_weight, value_weight, output_weight, norm_second, router, gate_carry, constant_map, constant_vector, expert_gate, expert_linear, expert_down)))

    def wrapped(stream_tokens, gain_one, query_w, key_w, value_w, output_w, gain_two, router_w, carry_w, map_w, vector_w, gate_w, linear_w, down_w):
        weights = (gain_one, query_w, key_w, value_w, output_w, gain_two, router_w, carry_w, map_w, vector_w, gate_w, linear_w, down_w)
        return forward_all(stream_tokens, weights, previous, routes, boundaries)
    result, pullback = jax.vjp(wrapped, floats[0], floats[1], floats[2], floats[3], floats[4], floats[5], floats[6], floats[7], floats[8], floats[9], floats[10], floats[11], floats[12], floats[13])
    grads = pullback(cotangent.astype(jnp.float32))
    return (result.astype(jnp.bfloat16), grads[0], grads[1], grads[2], grads[3], grads[4], grads[5], grads[6], grads[7], grads[8], grads[9], grads[10], grads[11], grads[12], grads[13])
```

```python
import math

import jax
import jax.numpy as jnp
from jax import lax
from jax.experimental import pallas as pl
from jax.experimental.pallas import tpu as pltpu
from jax.sharding import PartitionSpec as P

HEAD_DIM = 64
CAP = 96


EPSILON = 1e-06
NEGATIVE = -1e30
HIGH = lax.Precision.HIGHEST


def block_rows(total_rows):
    for candidate in (512, 384, 256, 128):
        return candidate
    return total_rows


def document_ids(positions, starts):
    return jnp.sum((starts[None, :] <= positions[:, None]).astype(jnp.int32), axis=1) - 1


def rotary(values, positions, direction):
    half_dim = values.shape[-1] // 2
    frequency = jnp.exp(
        jnp.arange(half_dim, dtype=jnp.float32) * (-2.0 * math.log(10000.0) / values.shape[-1])
    )
    angles = positions.astype(jnp.float32)[:, None] * frequency[None, :]
    cosine = jnp.cos(angles)[:, None, :]
    sine_part = direction * jnp.sin(angles)[:, None, :]
    leading = values[..., :half_dim]
    trailing = values[..., half_dim:]
    return jnp.concatenate(
        [leading * cosine - trailing * sine_part, trailing * cosine + leading * sine_part], axis=-1
    )


def scores_and_mask(queries, key_block, query_pos, query_doc, key_pos, key_doc):
    scores = jnp.einsum(
        "qhd,khd->qhk", queries, key_block, preferred_element_type=jnp.float32
    ) * HEAD_DIM ** (-0.5)
    allowed = (query_doc[:, None] == key_doc[None, :]) & (key_pos[None, :] <= query_pos[:, None])
    return (scores, allowed[:, None, :])


def pair_grads(
    queries,
    output_grad,
    log_total,
    row_delta,
    query_pos,
    query_doc,
    key_block,
    value_block,
    key_pos,
    key_doc,
):
    scores, allowed = scores_and_mask(queries, key_block, query_pos, query_doc, key_pos, key_doc)
    weights = jnp.where(allowed, jnp.exp(scores - log_total[..., None]), 0.0)
    weight_grad = jnp.einsum(
        "qhd,khd->qhk", output_grad, value_block, preferred_element_type=jnp.float32
    )
    score_grad = (weights * (weight_grad - row_delta[..., None]) * HEAD_DIM ** (-0.5)).astype(
        jnp.bfloat16
    )
    return (weights.astype(jnp.bfloat16), score_grad)


def over_blocks(function, state, total_rows):
    block_size = block_rows(total_rows)

    def advance(carried, block_index):
        return (function(carried, block_index * block_size, block_size), None)

    state, unused = lax.scan(advance, state, jnp.arange(total_rows // block_size, dtype=jnp.int32))
    return state


def bits_of(axis):
    bits, bit = [], 1
    while bit < lax.axis_size(axis):
        bits.append(bit)
        bit *= 2
    return bits


def swap(values, axis, bit):
    return lax.ppermute(values, axis, [(i, i ^ bit) for i in range(lax.axis_size(axis))])


def halve(values, axis, bit, dim):
    own = (lax.axis_index(axis) // bit) % 2
    kept = lax.dynamic_index_in_dim(values, own, dim, keepdims=False)
    sent = lax.dynamic_index_in_dim(values, 1 - own, dim, keepdims=False)
    total = kept.astype(jnp.float32) + swap(sent, axis, bit).astype(jnp.float32)
    return total.astype(jnp.bfloat16)


def scatter_sum(values, axis):
    bits = bits_of(axis)
    values = values.reshape((2,) * len(bits) + values.shape[1:])
    for place, bit in enumerate(bits):
        values = halve(values, axis, bit, len(bits) - 1 - place)
    return values


def exchange(blocks, direction, ranks, name):
    exchange_size, group_size, spread = ranks
    count = exchange_size * group_size

    def kernel(*refs):
        arrays = len(blocks)
        sources, targets = refs[:arrays], refs[arrays : 2 * arrays]
        send_sem, recv_sem, local_sem = refs[2 * arrays :]
        exp_index, ctx_index = lax.axis_index("exp"), lax.axis_index("ctx")
        inner = lax.rem(ctx_index, spread)

        def member(shift):
            far, near = shift // group_size, shift % group_size
            other = lax.rem(exp_index + far, exchange_size)
            return {
                "exp": other,
                "ctx": lax.rem(ctx_index // spread + near, group_size) * spread + inner,
            }

        def back(shift):
            far, near = shift // group_size, shift % group_size
            return (exchange_size - far) % exchange_size * group_size + (
                group_size - near
            ) % group_size

        barrier = pltpu.get_barrier_semaphore()
        for shift in range(1, count):
            pl.semaphore_signal(
                barrier, inc=1, device_id=member(shift), device_id_type=pl.DeviceIdType.MESH
            )
        pl.semaphore_wait(barrier, count - 1)
        copies = []
        for index in range(arrays):
            for shift in range(1, count):
                copy = pltpu.make_async_remote_copy(
                    src_ref=sources[index].at[shift],
                    dst_ref=targets[index].at[shift],
                    send_sem=send_sem.at[index, shift],
                    recv_sem=recv_sem.at[index, shift],
                    device_id=member(shift if direction > 0 else back(shift)),
                    device_id_type=pl.DeviceIdType.MESH,
                )
                copy.start()
                copies.append(copy)
            copy = pltpu.make_async_copy(
                sources[index].at[0], targets[index].at[0], local_sem.at[index]
            )
            copy.start()
            copies.append(copy)
        for copy in copies:
            copy.wait()

    return pl.pallas_call(
        kernel,
        out_shape=[jax.ShapeDtypeStruct(block.shape, block.dtype) for block in blocks],
        in_specs=[pl.BlockSpec(memory_space=pl.ANY)] * len(blocks),
        out_specs=[pl.BlockSpec(memory_space=pl.ANY)] * len(blocks),
        scratch_shapes=[
            pltpu.SemaphoreType.DMA((len(blocks), count)),
            pltpu.SemaphoreType.DMA((len(blocks), count)),
            pltpu.SemaphoreType.DMA((len(blocks),)),
        ],
        compiler_params=pltpu.CompilerParams(
            collective_id=0 if direction > 0 else 1, has_side_effects=True
        ),
        name=name,
    )(*blocks)


def local(
    tokens,
    cotangent,
    previous,
    routes,
    boundaries,
    norm_first,
    query_weight,
    key_weight,
    value_weight,
    output_weight,
    norm_second,
    router,
    gate_carry,
    constant_map,
    constant_vector,
    expert_gate,
    expert_linear,
    expert_down,
):
    row_count = tokens.shape[1]
    model_width = tokens.shape[2]
    head_count = model_width // HEAD_DIM
    heads_shape = (row_count, head_count, HEAD_DIM)
    starts = boundaries[0]
    positions = lax.axis_index("ctx") * row_count + jnp.arange(row_count, dtype=jnp.int32)
    documents = document_ids(positions, starts)
    inputs = tokens[0].astype(jnp.float32)
    upstream = cotangent[0].astype(jnp.float32)
    prior = previous[0]
    chosen_routes = routes[0]
    inverse_first = lax.rsqrt(jnp.mean(inputs * inputs, axis=-1, keepdims=True) + EPSILON)
    unit_first = inputs * inverse_first
    gain_first = norm_first.astype(jnp.float32)
    normed = (unit_first * gain_first).astype(jnp.bfloat16)
    query_heads = rotary(
        jnp.dot(normed, query_weight, preferred_element_type=jnp.float32).reshape(heads_shape),
        positions,
        1.0,
    ).astype(jnp.bfloat16)
    key_heads = rotary(
        jnp.dot(normed, key_weight, preferred_element_type=jnp.float32).reshape(heads_shape),
        positions,
        1.0,
    ).astype(jnp.bfloat16)
    value_flat = jnp.dot(normed, value_weight, preferred_element_type=jnp.float32).astype(
        jnp.bfloat16
    )
    key_flat = key_heads.reshape(row_count, model_width)

    def attend(totals, shards):
        key_rows, value_rows = shards
        key_count = key_rows.shape[0]
        key_positions = jnp.arange(key_count, dtype=jnp.int32)

        def visit(state, begin, block_size):
            running_max, running_sum, accumulated = state
            key_block = lax.dynamic_slice_in_dim(key_rows, begin, block_size, 0).reshape(
                block_size, head_count, HEAD_DIM
            )
            value_block = lax.dynamic_slice_in_dim(value_rows, begin, block_size, 0).reshape(
                block_size, head_count, HEAD_DIM
            )
            key_pos = lax.dynamic_slice_in_dim(key_positions, begin, block_size, 0)
            scores, allowed = scores_and_mask(
                query_heads, key_block, positions, documents, key_pos, document_ids(key_pos, starts)
            )
            new_max = jnp.maximum(
                running_max, jnp.max(jnp.where(allowed, scores, NEGATIVE), axis=-1)
            )
            weights = jnp.where(allowed, jnp.exp(scores - new_max[..., None]), 0.0)
            factor = jnp.exp(running_max - new_max)
            running_sum = running_sum * factor + jnp.sum(weights, axis=-1)
            accumulated = accumulated * factor[..., None] + jnp.einsum(
                "qhk,khd->qhd",
                weights.astype(jnp.bfloat16),
                value_block,
                preferred_element_type=jnp.float32,
            )
            return (new_max, running_sum, accumulated)

        return over_blocks(visit, totals, key_count)

    start_state = (
        jnp.full((row_count, head_count), NEGATIVE, jnp.float32),
        jnp.zeros((row_count, head_count), jnp.float32),
        jnp.zeros(heads_shape, jnp.float32),
    )
    running_max, running_sum, accumulated = attend(
        start_state,
        (
            lax.all_gather(key_flat, "ctx", axis=0, tiled=True),
            lax.all_gather(value_flat, "ctx", axis=0, tiled=True),
        ),
    )
    attended = accumulated / running_sum[..., None]
    log_total = running_max + jnp.log(running_sum)
    attended_low = attended.reshape(row_count, model_width).astype(jnp.bfloat16)
    middle = inputs + jnp.dot(attended_low, output_weight, preferred_element_type=jnp.float32)
    inverse_second = lax.rsqrt(jnp.mean(middle * middle, axis=-1, keepdims=True) + EPSILON)
    unit_second = middle * inverse_second
    gain_second = norm_second.astype(jnp.float32)
    second = unit_second * gain_second
    second_low = second.astype(jnp.bfloat16)
    logits = jnp.dot(second_low, router, preferred_element_type=jnp.float32) + jnp.dot(
        prior, gate_carry.astype(jnp.float32), precision=HIGH
    )
    gate_probs = jax.nn.softmax(logits, axis=-1)
    expert_count = gate_probs.shape[1]
    route_hits = (
        chosen_routes[:, :, None] == jnp.arange(expert_count, dtype=jnp.int32)[None, None, :]
    ).astype(jnp.float32)
    chosen_mask = jnp.sum(route_hits, axis=1)
    gate_weights = gate_probs * chosen_mask
    route_weights = jnp.sum(route_hits * gate_probs[:, None, :], axis=-1)
    local_experts = expert_gate.shape[0]
    exchange_count = lax.axis_size("exp")
    ffn_count = local_experts * exchange_count
    group_size = local_experts
    spread = lax.axis_size("ctx") // group_size
    ranks = (exchange_count, group_size, spread)
    ctx_index = lax.axis_index("ctx")
    far = (chosen_routes // group_size - lax.axis_index("exp")) % exchange_count
    near = (chosen_routes % group_size - ctx_index // spread) % group_size
    relative = far * group_size + near
    ffn_hits = route_hits[:, :, :ffn_count].reshape(row_count * 2, ffn_count)
    earlier = jnp.cumsum(ffn_hits, axis=0) - ffn_hits
    slot_rank = jnp.sum(earlier * ffn_hits, axis=-1).astype(jnp.int32).reshape(row_count, 2)
    is_ffn = chosen_routes < ffn_count
    targets = jnp.where(is_ffn, relative * CAP + slot_rank, -1)
    safe_targets = jnp.maximum(targets, 0)
    slot_total = ffn_count * CAP
    slot_ids = jnp.arange(slot_total, dtype=jnp.int32)
    dispatch_first = (slot_ids[:, None] == targets[None, :, 0]).astype(jnp.bfloat16)
    dispatch_second = (slot_ids[:, None] == targets[None, :, 1]).astype(jnp.bfloat16)
    slot_shape = (ffn_count, CAP, model_width)
    outgoing = (
        jnp.dot(dispatch_first + dispatch_second, second_low, preferred_element_type=jnp.float32)
        .astype(jnp.bfloat16)
        .reshape(slot_shape)
    )
    route_grads = (route_weights[:, :, None] * upstream[:, None, :]).astype(jnp.bfloat16)
    sending_back = (
        (
            jnp.dot(dispatch_first, route_grads[:, 0], preferred_element_type=jnp.float32)
            + jnp.dot(dispatch_second, route_grads[:, 1], preferred_element_type=jnp.float32)
        )
        .astype(jnp.bfloat16)
        .reshape(slot_shape)
    )
    received, grads_in = exchange((outgoing, sending_back), 1, ranks, "to_experts")
    received = received.reshape(slot_total, model_width)
    grads_in = grads_in.reshape(slot_total, model_width)
    own_expert = ctx_index // spread
    gate_matrix = lax.dynamic_index_in_dim(expert_gate, own_expert, 0, keepdims=False)
    linear_matrix = lax.dynamic_index_in_dim(expert_linear, own_expert, 0, keepdims=False)
    down_matrix = lax.dynamic_index_in_dim(expert_down, own_expert, 0, keepdims=False)
    gate_part = jnp.dot(received, gate_matrix, preferred_element_type=jnp.float32)
    linear_part = jnp.dot(received, linear_matrix, preferred_element_type=jnp.float32)
    hidden_grad = jnp.dot(grads_in, down_matrix.T, preferred_element_type=jnp.float32)
    gate_sigmoid = jax.nn.sigmoid(gate_part)
    hidden = (gate_part * gate_sigmoid * linear_part).astype(jnp.bfloat16)
    gate_low = (
        hidden_grad * linear_part * gate_sigmoid * (1.0 + gate_part * (1.0 - gate_sigmoid))
    ).astype(jnp.bfloat16)
    linear_low = (hidden_grad * gate_part * gate_sigmoid).astype(jnp.bfloat16)
    dp_size = lax.axis_size("dp")
    share_width = gate_low.shape[1] // dp_size
    split = (slot_total, dp_size, share_width)
    down_terms = jnp.dot(hidden.T, grads_in, preferred_element_type=jnp.float32)
    down_terms = down_terms.astype(jnp.bfloat16).reshape(dp_size, share_width, model_width)
    gate_terms = jnp.einsum(
        "sd,sgf->gdf", received, gate_low.reshape(split), preferred_element_type=jnp.float32
    ).astype(jnp.bfloat16)
    linear_terms = jnp.einsum(
        "sd,sgf->gdf", received, linear_low.reshape(split), preferred_element_type=jnp.float32
    ).astype(jnp.bfloat16)
    produced = jnp.dot(hidden, down_matrix, preferred_element_type=jnp.float32)
    input_back = jnp.dot(
        gate_low, gate_matrix.T, preferred_element_type=jnp.float32
    ) + jnp.dot(linear_low, linear_matrix.T, preferred_element_type=jnp.float32)
    returned, home_grads = exchange(
        (
            produced.astype(jnp.bfloat16).reshape(slot_shape),
            input_back.astype(jnp.bfloat16).reshape(slot_shape),
        ),
        -1,
        ranks,
        "from_experts",
    )
    returned = returned.reshape(slot_total, model_width)
    home_grads = home_grads.reshape(slot_total, model_width)

    def collect(terms):
        share = scatter_sum(terms, "dp")
        bit = 1
        while bit < spread:
            share = (
                share.astype(jnp.float32) + swap(share, "ctx", bit).astype(jnp.float32)
            ).astype(jnp.bfloat16)
            bit *= 2
        parts, order = [share], [0]
        while bit < lax.axis_size("ctx"):
            bit *= 2
        while bit > spread:
            bit //= 2
            parts = parts + [swap(part, "ctx", bit) for part in parts]
            order = order + [place ^ (bit // spread) for place in order]
        stacked = jnp.stack(parts)
        places = jnp.array(order, jnp.int32) ^ own_expert
        inverse = jnp.argsort(places)
        return stacked[inverse].astype(jnp.float32)

    experts = (collect(gate_terms), collect(linear_terms), collect(down_terms))
    route_outputs = jnp.where(is_ffn[:, :, None], returned[safe_targets].astype(jnp.float32), 0.0)
    copy_index = ffn_count + 1
    combined = jnp.sum(route_weights[:, :, None] * route_outputs, axis=1)
    combined = combined + gate_weights[:, copy_index : copy_index + 1] * second
    mixing = jax.nn.softmax(
        jnp.einsum("td,jdc->tjc", second_low, constant_map, preferred_element_type=jnp.float32),
        axis=-1,
    )
    vectors = constant_vector.astype(jnp.float32)
    constant_terms = (
        mixing[:, :, 0:1] * second[:, None, :] + mixing[:, :, 1:2] * vectors[None, :, :]
    )
    constant_gates = gate_weights[:, ffn_count + 2 : ffn_count + 4]
    combined = combined + jnp.sum(constant_gates[:, :, None] * constant_terms, axis=1)
    result = (middle + combined).astype(jnp.bfloat16)
    ffn_weight_grad = jnp.sum(upstream[:, None, :] * route_outputs, axis=-1)
    copy_grad = jnp.sum(upstream * second, axis=-1)
    constant_weight_grad = jnp.sum(upstream[:, None, :] * constant_terms, axis=-1)
    ffn_columns = jnp.sum(route_hits[:, :, :ffn_count] * ffn_weight_grad[:, :, None], axis=1)
    gate_grad = jnp.concatenate(
        [
            ffn_columns,
            jnp.zeros((row_count, 1), jnp.float32),
            copy_grad[:, None],
            constant_weight_grad,
        ],
        axis=1,
    )
    prob_grad = gate_grad * chosen_mask
    logit_grad = gate_probs * (prob_grad - jnp.sum(gate_probs * prob_grad, axis=-1, keepdims=True))
    carry_grad = jnp.dot(prior.T, logit_grad, precision=HIGH)
    logit_low = logit_grad.astype(jnp.bfloat16)
    router_grad = jnp.dot(second_low.T, logit_low, preferred_element_type=jnp.float32)
    second_grad = jnp.dot(logit_low, router.T, preferred_element_type=jnp.float32)
    second_grad = second_grad + gate_weights[:, copy_index : copy_index + 1] * upstream
    term_grad = constant_gates[:, :, None] * upstream[:, None, :]
    second_grad = second_grad + jnp.sum(term_grad * mixing[:, :, 0:1], axis=1)
    vector_grad = jnp.sum(term_grad * mixing[:, :, 1:2], axis=0)
    mixing_grad = jnp.stack(
        [
            jnp.sum(term_grad * second[:, None, :], axis=-1),
            jnp.sum(term_grad * vectors[None, :, :], axis=-1),
        ],
        axis=-1,
    )
    map_low = (
        mixing * (mixing_grad - jnp.sum(mixing * mixing_grad, axis=-1, keepdims=True))
    ).astype(jnp.bfloat16)
    map_grad = jnp.einsum("td,tjc->jdc", second_low, map_low, preferred_element_type=jnp.float32)
    second_grad = second_grad + jnp.einsum(
        "tjc,jdc->td", map_low, constant_map, preferred_element_type=jnp.float32
    )
    second_grad = second_grad + jnp.sum(
        jnp.where(is_ffn[:, :, None], home_grads[safe_targets].astype(jnp.float32), 0.0), axis=1
    )
    second_unit_grad = second_grad * gain_second
    second_gain_grad = jnp.sum(second_grad * unit_second, axis=0)
    middle_grad = upstream + inverse_second * (
        second_unit_grad
        - unit_second * jnp.mean(second_unit_grad * unit_second, axis=-1, keepdims=True)
    )
    middle_low = middle_grad.astype(jnp.bfloat16)
    output_grad = jnp.dot(attended_low.T, middle_low, preferred_element_type=jnp.float32)
    attended_grad = (
        jnp.dot(middle_low, output_weight.T, preferred_element_type=jnp.float32)
        .astype(jnp.bfloat16)
        .reshape(heads_shape)
    )
    row_delta = jnp.sum(attended_grad.astype(jnp.float32) * attended, axis=-1)
    zero_heads = jnp.zeros(heads_shape, jnp.float32)
    key_rows, value_rows = (
        lax.all_gather(key_flat, "ctx", axis=0, tiled=True),
        lax.all_gather(value_flat, "ctx", axis=0, tiled=True),
    )
    key_count = key_rows.shape[0]
    block_size = block_rows(key_count)
    key_positions = jnp.arange(key_count, dtype=jnp.int32)

    def visit(query_sum, block_index):
        begin = block_index * block_size
        key_block = lax.dynamic_slice_in_dim(key_rows, begin, block_size, 0).reshape(
            block_size, head_count, HEAD_DIM
        )
        value_block = lax.dynamic_slice_in_dim(value_rows, begin, block_size, 0).reshape(
            block_size, head_count, HEAD_DIM
        )
        key_pos = lax.dynamic_slice_in_dim(key_positions, begin, block_size, 0)
        weights_low, score_grad = pair_grads(
            query_heads,
            attended_grad,
            log_total,
            row_delta,
            positions,
            documents,
            key_block,
            value_block,
            key_pos,
            document_ids(key_pos, starts),
        )
        query_sum = query_sum + jnp.einsum(
            "qhk,khd->qhd", score_grad, key_block, preferred_element_type=jnp.float32
        )
        key_part = jnp.einsum(
            "qhk,qhd->khd", score_grad, query_heads, preferred_element_type=jnp.float32
        ).reshape(block_size, model_width)
        value_part = jnp.einsum(
            "qhk,qhd->khd", weights_low, attended_grad, preferred_element_type=jnp.float32
        ).reshape(block_size, model_width)
        return (query_sum, jnp.concatenate([key_part, value_part], axis=1))

    query_grad, key_terms = lax.scan(
        visit, zero_heads, jnp.arange(key_count // block_size, dtype=jnp.int32)
    )
    summed = lax.psum_scatter(
        key_terms.reshape(key_count, 2 * model_width).astype(jnp.bfloat16),
        "ctx",
        scatter_dimension=0,
        tiled=True,
    ).astype(jnp.float32)
    key_grad = summed[:, :model_width].reshape(heads_shape)
    value_grad = summed[:, model_width:].reshape(heads_shape)
    query_low = (
        rotary(query_grad, positions, -1.0).reshape(row_count, model_width).astype(jnp.bfloat16)
    )
    key_low = rotary(key_grad, positions, -1.0).reshape(row_count, model_width).astype(jnp.bfloat16)
    value_low = value_grad.reshape(row_count, model_width).astype(jnp.bfloat16)
    query_sum_grad = jnp.dot(normed.T, query_low, preferred_element_type=jnp.float32)
    key_sum_grad = jnp.dot(normed.T, key_low, preferred_element_type=jnp.float32)
    value_sum_grad = jnp.dot(normed.T, value_low, preferred_element_type=jnp.float32)
    first_grad = (
        jnp.dot(query_low, query_weight.T, preferred_element_type=jnp.float32)
        + jnp.dot(key_low, key_weight.T, preferred_element_type=jnp.float32)
        + jnp.dot(value_low, value_weight.T, preferred_element_type=jnp.float32)
    )
    first_unit_grad = first_grad * gain_first
    first_gain_grad = jnp.sum(first_grad * unit_first, axis=0)
    token_grad = middle_grad + inverse_first * (
        first_unit_grad
        - unit_first * jnp.mean(first_unit_grad * unit_first, axis=-1, keepdims=True)
    )
    steps = [(axis, bit) for axis in ("ctx", "exp", "dp") for bit in bits_of(axis)]
    units = 2 ** len(steps)
    wide = jnp.concatenate([query_sum_grad, key_sum_grad, value_sum_grad, output_grad], axis=0)
    small_terms = (first_gain_grad, second_gain_grad, router_grad, carry_grad, map_grad, vector_grad)
    flat = jnp.concatenate([term.reshape(-1) for term in small_terms])
    small_rows = -(-flat.size // (units * model_width))
    wide_rows = wide.shape[0] // units
    unit_rows = -(-(small_rows + wide_rows) // 16) * 16
    flat = jnp.pad(flat, (0, units * small_rows * model_width - flat.size))
    packed = jnp.concatenate(
        [
            wide.reshape(units, wide_rows, model_width).astype(jnp.bfloat16),
            flat.reshape(units, small_rows, model_width).astype(jnp.bfloat16),
            jnp.zeros((units, unit_rows - wide_rows - small_rows, model_width), jnp.bfloat16),
        ],
        axis=1,
    )
    for axis, bit in steps:
        packed = packed.reshape((2, -1) + packed.shape[1:])
        packed = halve(packed, axis, bit, 0)
    for axis, bit in steps[::-1]:
        other = swap(packed, axis, bit)
        own = (lax.axis_index(axis) // bit) % 2
        packed = jnp.concatenate(
            [jnp.where(own == 0, packed, other), jnp.where(own == 0, other, packed)], axis=0
        )
    packed = packed.astype(jnp.float32)
    wide = packed[:, :wide_rows].reshape(4, model_width, model_width)
    flat = packed[:, wide_rows : wide_rows + small_rows].reshape(-1)
    smalls, begin = [], 0
    for term in small_terms:
        smalls.append(flat[begin : begin + term.size].reshape(term.shape))
        begin += term.size
    dense = (smalls[0], wide[0], wide[1], wide[2], wide[3]) + tuple(smalls[1:])
    return (
        result[None],
        token_grad[None],
        dense[0],
        dense[1],
        dense[2],
        dense[3],
        dense[4],
        dense[5],
        dense[6],
        dense[7],
        dense[8],
        dense[9],
        experts[0],
        experts[1],
        experts[2],
    )


def solution(mesh):
    return jax.shard_map(
        local,
        mesh=mesh,
        in_specs=(
            P(("dp", "exp"), "ctx", None),
            P(("dp", "exp"), "ctx", None),
            P(("dp", "exp"), "ctx", None),
            P(("dp", "exp"), "ctx", None),
            P(("dp", "exp"), None),
            P(),
            P(),
            P(),
            P(),
            P(),
            P(),
            P(),
            P(),
            P(),
            P(),
            P("exp", None, None),
            P("exp", None, None),
            P("exp", None, None),
        ),
        out_specs=(
            P(("dp", "exp"), "ctx", None),
            P(("dp", "exp"), "ctx", None),
            P(),
            P(),
            P(),
            P(),
            P(),
            P(),
            P(),
            P(),
            P(),
            P(),
            P("exp", None, "dp"),
            P("exp", None, "dp"),
            P("exp", "dp", None),
        ),
        check_vma=False,
    )
```

```python
import math

import jax
import jax.numpy as jnp
from jax import lax
from jax.experimental import pallas as pl
from jax.experimental.pallas import tpu as pltpu
from jax.sharding import PartitionSpec as P

HEAD_DIM = 64
CAP = 96


EPSILON = 1e-06
NEGATIVE = -1e30
HIGH = lax.Precision.HIGHEST


def block_rows(total_rows):
    for candidate in (512, 384, 256, 128):
        return candidate
    return total_rows


def document_ids(positions, starts):
    return jnp.sum((starts[None, :] <= positions[:, None]).astype(jnp.int32), axis=1) - 1


def rotary(values, positions, direction):
    half_dim = values.shape[-1] // 2
    frequency = jnp.exp(
        jnp.arange(half_dim, dtype=jnp.float32) * (-2.0 * math.log(10000.0) / values.shape[-1])
    )
    angles = positions.astype(jnp.float32)[:, None] * frequency[None, :]
    cosine = jnp.cos(angles)[:, None, :]
    sine_part = direction * jnp.sin(angles)[:, None, :]
    leading = values[..., :half_dim]
    trailing = values[..., half_dim:]
    return jnp.concatenate(
        [leading * cosine - trailing * sine_part, trailing * cosine + leading * sine_part], axis=-1
    )


def scores_and_mask(queries, key_block, query_pos, query_doc, key_pos, key_doc):
    scores = jnp.einsum(
        "qhd,khd->qhk", queries, key_block, preferred_element_type=jnp.float32
    ) * HEAD_DIM ** (-0.5)
    allowed = (query_doc[:, None] == key_doc[None, :]) & (key_pos[None, :] <= query_pos[:, None])
    return (scores, allowed[:, None, :])


def pair_grads(
    queries,
    output_grad,
    log_total,
    row_delta,
    query_pos,
    query_doc,
    key_block,
    value_block,
    key_pos,
    key_doc,
):
    scores, allowed = scores_and_mask(queries, key_block, query_pos, query_doc, key_pos, key_doc)
    weights = jnp.where(allowed, jnp.exp(scores - log_total[..., None]), 0.0)
    weight_grad = jnp.einsum(
        "qhd,khd->qhk", output_grad, value_block, preferred_element_type=jnp.float32
    )
    score_grad = (weights * (weight_grad - row_delta[..., None]) * HEAD_DIM ** (-0.5)).astype(
        jnp.bfloat16
    )
    return (weights.astype(jnp.bfloat16), score_grad)


def over_blocks(function, state, total_rows):
    block_size = block_rows(total_rows)

    def advance(carried, block_index):
        return (function(carried, block_index * block_size, block_size), None)

    state, unused = lax.scan(advance, state, jnp.arange(total_rows // block_size, dtype=jnp.int32))
    return state


def bits_of(axis):
    bits, bit = [], 1
    while bit < lax.axis_size(axis):
        bits.append(bit)
        bit *= 2
    return bits


def swap(values, axis, bit):
    return lax.ppermute(values, axis, [(i, i ^ bit) for i in range(lax.axis_size(axis))])


def halve(values, axis, bit, dim):
    own = (lax.axis_index(axis) // bit) % 2
    kept = lax.dynamic_index_in_dim(values, own, dim, keepdims=False)
    sent = lax.dynamic_index_in_dim(values, 1 - own, dim, keepdims=False)
    total = kept.astype(jnp.float32) + swap(sent, axis, bit).astype(jnp.float32)
    return total.astype(jnp.bfloat16)


def scatter_sum(values, axis):
    bits = bits_of(axis)
    values = values.reshape((2,) * len(bits) + values.shape[1:])
    for place, bit in enumerate(bits):
        values = halve(values, axis, bit, len(bits) - 1 - place)
    return values


def mesh_id(exp_index, ctx_index):
    return {"exp": exp_index, "ctx": ctx_index}


def dot(left, right):
    return jnp.dot(left, right, preferred_element_type=jnp.float32)


def dot_nt(left, right):
    return lax.dot_general(
        left, right, (((1,), (1,)), ((), ())), preferred_element_type=jnp.float32
    )


def dot_tn(left, right):
    return lax.dot_general(
        left, right, (((0,), (0,)), ((), ())), preferred_element_type=jnp.float32
    )


def member_of(shift, ranks):
    exchange_size, group_size, spread = ranks
    exp_index, ctx_index = lax.axis_index("exp"), lax.axis_index("ctx")
    far, near = shift // group_size, shift % group_size
    place = jnp.bitwise_xor(ctx_index // spread, near) * spread + lax.rem(ctx_index, spread)
    return mesh_id(jnp.bitwise_xor(exp_index, far), place)


def greet(count, ranks):
    barrier = pltpu.get_barrier_semaphore()
    for shift in range(1, count):
        pl.semaphore_signal(
            barrier, inc=1, device_id=member_of(shift, ranks), device_id_type=pl.DeviceIdType.MESH
        )
    pl.semaphore_wait(barrier, count - 1)


def send_block(source, target, shift, ranks, send_sem, recv_sem):
    return pltpu.make_async_remote_copy(
        src_ref=source.at[shift],
        dst_ref=target.at[shift],
        send_sem=send_sem.at[shift],
        recv_sem=recv_sem.at[shift],
        device_id=member_of(shift, ranks),
        device_id_type=pl.DeviceIdType.MESH,
    )


def exchange(block, ranks, collective_id, name):
    count = ranks[0] * ranks[1]

    def kernel(source, target, send_sem, recv_sem, local_sem):
        greet(count, ranks)
        copies = [
            send_block(source, target, shift, ranks, send_sem, recv_sem)
            for shift in range(1, count)
        ]
        copies.append(pltpu.make_async_copy(source.at[0], target.at[0], local_sem))
        for copy in copies:
            copy.start()
        for copy in copies:
            copy.wait()

    return pl.pallas_call(
        kernel,
        out_shape=jax.ShapeDtypeStruct(block.shape, block.dtype),
        in_specs=[pl.BlockSpec(memory_space=pl.ANY)],
        out_specs=pl.BlockSpec(memory_space=pl.ANY),
        scratch_shapes=[
            pltpu.SemaphoreType.DMA((count,)),
            pltpu.SemaphoreType.DMA((count,)),
            pltpu.SemaphoreType.DMA,
        ],
        compiler_params=pltpu.CompilerParams(collective_id=collective_id, has_side_effects=True),
        name=name,
    )(block)


def expert_layer(outgoing, gates, grads, weights, ranks, shares):
    count, cap, width = outgoing.shape
    hidden_units = weights[0].shape[2]
    rows = count * cap
    share = hidden_units // shares
    spread = ranks[2]

    def kernel(
        outgoing_ref,
        gates_ref,
        grads_ref,
        gate_hbm,
        linear_hbm,
        down_hbm,
        back_ref,
        output_ref,
        dots_ref,
        gate_terms,
        linear_terms,
        down_terms,
        received,
        received_gates,
        gate_w,
        linear_w,
        down_w,
        hidden_grad,
        hidden,
        gate_low,
        linear_low,
        rows_t,
        scaled,
        gate_column,
        out_total,
        in_total,
        out_send,
        in_send,
        dots_send,
        terms,
        weight_sem,
        send_sem,
        recv_sem,
        local_sem,
        terms_sem,
    ):
        own = lax.axis_index("ctx") // spread
        loads = [
            pltpu.make_async_copy(source.at[own], target, weight_sem.at[index])
            for index, (source, target) in enumerate(
                ((down_hbm, down_w), (gate_hbm, gate_w), (linear_hbm, linear_w))
            )
        ]
        for load in loads:
            load.start()
        greet(count, ranks)

        def send_all(source, target, index):
            copies = [
                send_block(source, target, shift, ranks, send_sem.at[index], recv_sem.at[index])
                for shift in range(1, count)
            ]
            copies.append(
                pltpu.make_async_copy(source.at[0], target.at[0], local_sem.at[index])
            )
            for copy in copies:
                copy.start()
            return copies

        incoming = send_all(gates_ref, received_gates, 0) + send_all(outgoing_ref, received, 1)
        loads[0].wait()

        def backward_in(index, carry):
            part = pl.ds(pl.multiple_of(index * share, share), share)
            hidden_grad[:, part] = dot_nt(grads_ref[...], down_w[part, :])
            return carry

        lax.fori_loop(0, shares, backward_in, 0)
        for copy in incoming + loads[1:]:
            copy.wait()
        for shift in range(count):
            column = jnp.transpose(received_gates[shift])[:cap, 0:1]
            block = pl.ds(shift * cap, cap)
            gate_column[block, :] = jnp.broadcast_to(column, (cap, 128))
            scaled[block, :] = (column * grads_ref[block, :].astype(jnp.float32)).astype(
                jnp.bfloat16
            )
        tokens = received[...].reshape(rows, width)
        rows_t[...] = jnp.transpose(tokens)

        def through(index, carry):
            part = pl.ds(pl.multiple_of(index * share, share), share)
            tokens = received[...].reshape(rows, width)
            gate_part = dot(tokens, gate_w[:, part])
            linear_part = dot(tokens, linear_w[:, part])
            sigmoid = 1.0 / (1.0 + jnp.exp(-gate_part))
            silu = gate_part * sigmoid
            low = (silu * linear_part).astype(jnp.bfloat16)
            hidden[:, part] = low
            upper = hidden_grad[:, part] * gate_column[:, 0:1]
            low_gate = (
                upper * linear_part * sigmoid * (1.0 + gate_part * (1.0 - sigmoid))
            ).astype(jnp.bfloat16)
            gate_low[:, part] = low_gate
            low_linear = (upper * silu).astype(jnp.bfloat16)
            linear_low[:, part] = low_linear
            out = dot(low, down_w[part, :])
            back = dot_nt(low_gate, gate_w[:, part]) + dot_nt(low_linear, linear_w[:, part])

            @pl.when(index == 0)
            def _():
                out_total[...] = out
                in_total[...] = back

            @pl.when(index > 0)
            def _():
                out_total[...] += out
                in_total[...] += back

            return carry

        lax.fori_loop(0, shares, through, 0)
        in_send[...] = in_total[...].astype(jnp.bfloat16).reshape(count, cap, width)
        going = send_all(in_send, back_ref, 2)
        low = out_total[...].astype(jnp.bfloat16)
        out_send[...] = low.reshape(count, cap, width)
        dots = jnp.sum(
            low.astype(jnp.float32) * grads_ref[...].astype(jnp.float32), axis=1, keepdims=True
        )
        for shift in range(count):
            column = jnp.broadcast_to(dots[shift * cap : (shift + 1) * cap], (cap, 128))
            dots_send[shift, :, 0:cap] = jnp.transpose(column)[0:8, :]
            dots_send[shift, :, cap:] = jnp.zeros((8, 128 - cap), jnp.float32)
        going = going + send_all(dots_send, dots_ref, 3) + send_all(out_send, output_ref, 4)

        def term_copy(which, index):
            target = (down_terms, gate_terms, linear_terms)[which]
            return pltpu.make_async_copy(
                terms[which].at[index], target.at[index], terms_sem.at[which, index]
            )

        def weigh(index, carry):
            part = pl.ds(pl.multiple_of(index * share, share), share)
            terms[0][index] = dot_tn(hidden[:, part], scaled[...]).astype(jnp.bfloat16)
            term_copy(0, index).start()
            terms[1][index] = dot(rows_t[...], gate_low[:, part]).astype(jnp.bfloat16)
            term_copy(1, index).start()
            terms[2][index] = dot(rows_t[...], linear_low[:, part]).astype(jnp.bfloat16)
            term_copy(2, index).start()
            return carry

        lax.fori_loop(0, shares, weigh, 0)
        for which in range(3):
            for index in range(shares):
                term_copy(which, index).wait()
        for copy in going:
            copy.wait()

    low, full = jnp.bfloat16, jnp.float32
    columns, lines = (shares, width, share), (shares, share, width)
    any_space = pl.BlockSpec(memory_space=pl.ANY)
    in_vmem = pl.BlockSpec(memory_space=pltpu.VMEM)
    return pl.pallas_call(
        kernel,
        out_shape=[
            jax.ShapeDtypeStruct(outgoing.shape, low),
            jax.ShapeDtypeStruct(outgoing.shape, low),
            jax.ShapeDtypeStruct(gates.shape, full),
            jax.ShapeDtypeStruct(columns, low),
            jax.ShapeDtypeStruct(columns, low),
            jax.ShapeDtypeStruct(lines, low),
        ],
        in_specs=[in_vmem, in_vmem, in_vmem, any_space, any_space, any_space],
        out_specs=[any_space] * 6,
        scratch_shapes=[
            pltpu.VMEM(outgoing.shape, low),
            pltpu.VMEM(gates.shape, full),
            pltpu.VMEM((width, hidden_units), low),
            pltpu.VMEM((width, hidden_units), low),
            pltpu.VMEM((hidden_units, width), low),
            pltpu.VMEM((rows, hidden_units), full),
            pltpu.VMEM((rows, hidden_units), low),
            pltpu.VMEM((rows, hidden_units), low),
            pltpu.VMEM((rows, hidden_units), low),
            pltpu.VMEM((width, rows), low),
            pltpu.VMEM((rows, width), low),
            pltpu.VMEM((rows, 128), full),
            pltpu.VMEM((rows, width), full),
            pltpu.VMEM((rows, width), full),
            pltpu.VMEM(outgoing.shape, low),
            pltpu.VMEM(outgoing.shape, low),
            pltpu.VMEM(gates.shape, full),
            [pltpu.VMEM(lines, low), pltpu.VMEM(columns, low), pltpu.VMEM(columns, low)],
            pltpu.SemaphoreType.DMA((3,)),
            pltpu.SemaphoreType.DMA((5, count)),
            pltpu.SemaphoreType.DMA((5, count)),
            pltpu.SemaphoreType.DMA((5,)),
            pltpu.SemaphoreType.DMA((3, shares)),
        ],
        compiler_params=pltpu.CompilerParams(
            collective_id=1, has_side_effects=True, vmem_limit_bytes=60 * 2**20
        ),
        cost_estimate=pl.CostEstimate(
            flops=18 * rows * width * hidden_units,
            bytes_accessed=12 * width * hidden_units + 12 * rows * width,
            transcendentals=rows * hidden_units,
        ),
        name="experts",
    )(outgoing, gates, grads, *weights)


def local(
    tokens,
    cotangent,
    previous,
    routes,
    boundaries,
    norm_first,
    query_weight,
    key_weight,
    value_weight,
    output_weight,
    norm_second,
    router,
    gate_carry,
    constant_map,
    constant_vector,
    expert_gate,
    expert_linear,
    expert_down,
):
    row_count = tokens.shape[1]
    model_width = tokens.shape[2]
    head_count = model_width // HEAD_DIM
    heads_shape = (row_count, head_count, HEAD_DIM)
    starts = boundaries[0]
    positions = lax.axis_index("ctx") * row_count + jnp.arange(row_count, dtype=jnp.int32)
    documents = document_ids(positions, starts)
    inputs = tokens[0].astype(jnp.float32)
    upstream = cotangent[0].astype(jnp.float32)
    prior = previous[0]
    chosen_routes = routes[0]
    inverse_first = lax.rsqrt(jnp.mean(inputs * inputs, axis=-1, keepdims=True) + EPSILON)
    unit_first = inputs * inverse_first
    gain_first = norm_first.astype(jnp.float32)
    normed = (unit_first * gain_first).astype(jnp.bfloat16)
    query_heads = rotary(
        jnp.dot(normed, query_weight, preferred_element_type=jnp.float32).reshape(heads_shape),
        positions,
        1.0,
    ).astype(jnp.bfloat16)
    key_heads = rotary(
        jnp.dot(normed, key_weight, preferred_element_type=jnp.float32).reshape(heads_shape),
        positions,
        1.0,
    ).astype(jnp.bfloat16)
    value_flat = jnp.dot(normed, value_weight, preferred_element_type=jnp.float32).astype(
        jnp.bfloat16
    )
    key_flat = key_heads.reshape(row_count, model_width)

    def attend(totals, shards):
        key_rows, value_rows = shards
        key_count = key_rows.shape[0]
        key_positions = jnp.arange(key_count, dtype=jnp.int32)

        def visit(state, begin, block_size):
            running_max, running_sum, accumulated = state
            key_block = lax.dynamic_slice_in_dim(key_rows, begin, block_size, 0).reshape(
                block_size, head_count, HEAD_DIM
            )
            value_block = lax.dynamic_slice_in_dim(value_rows, begin, block_size, 0).reshape(
                block_size, head_count, HEAD_DIM
            )
            key_pos = lax.dynamic_slice_in_dim(key_positions, begin, block_size, 0)
            scores, allowed = scores_and_mask(
                query_heads, key_block, positions, documents, key_pos, document_ids(key_pos, starts)
            )
            new_max = jnp.maximum(
                running_max, jnp.max(jnp.where(allowed, scores, NEGATIVE), axis=-1)
            )
            weights = jnp.where(allowed, jnp.exp(scores - new_max[..., None]), 0.0)
            factor = jnp.exp(running_max - new_max)
            running_sum = running_sum * factor + jnp.sum(weights, axis=-1)
            accumulated = accumulated * factor[..., None] + jnp.einsum(
                "qhk,khd->qhd",
                weights.astype(jnp.bfloat16),
                value_block,
                preferred_element_type=jnp.float32,
            )
            return (new_max, running_sum, accumulated)

        return over_blocks(visit, totals, key_count)

    start_state = (
        jnp.full((row_count, head_count), NEGATIVE, jnp.float32),
        jnp.zeros((row_count, head_count), jnp.float32),
        jnp.zeros(heads_shape, jnp.float32),
    )
    running_max, running_sum, accumulated = attend(
        start_state,
        (
            lax.all_gather(key_flat, "ctx", axis=0, tiled=True),
            lax.all_gather(value_flat, "ctx", axis=0, tiled=True),
        ),
    )
    attended = accumulated / running_sum[..., None]
    log_total = running_max + jnp.log(running_sum)
    attended_low = attended.reshape(row_count, model_width).astype(jnp.bfloat16)
    middle = inputs + jnp.dot(attended_low, output_weight, preferred_element_type=jnp.float32)
    inverse_second = lax.rsqrt(jnp.mean(middle * middle, axis=-1, keepdims=True) + EPSILON)
    unit_second = middle * inverse_second
    gain_second = norm_second.astype(jnp.float32)
    second = unit_second * gain_second
    second_low = second.astype(jnp.bfloat16)
    logits = jnp.dot(second_low, router, preferred_element_type=jnp.float32) + jnp.dot(
        prior, gate_carry.astype(jnp.float32), precision=HIGH
    )
    gate_probs = jax.nn.softmax(logits, axis=-1)
    expert_count = gate_probs.shape[1]
    route_hits = (
        chosen_routes[:, :, None] == jnp.arange(expert_count, dtype=jnp.int32)[None, None, :]
    ).astype(jnp.float32)
    chosen_mask = jnp.sum(route_hits, axis=1)
    gate_weights = gate_probs * chosen_mask
    route_weights = jnp.sum(route_hits * gate_probs[:, None, :], axis=-1)
    local_experts = expert_gate.shape[0]
    exchange_count = lax.axis_size("exp")
    ffn_count = local_experts * exchange_count
    group_size = local_experts
    spread = lax.axis_size("ctx") // group_size
    ranks = (exchange_count, group_size, spread)
    ctx_index = lax.axis_index("ctx")
    far = jnp.bitwise_xor(chosen_routes // group_size, lax.axis_index("exp"))
    near = jnp.bitwise_xor(chosen_routes % group_size, ctx_index // spread)
    relative = far * group_size + near
    ffn_hits = route_hits[:, :, :ffn_count].reshape(row_count * 2, ffn_count)
    earlier = jnp.cumsum(ffn_hits, axis=0) - ffn_hits
    slot_rank = jnp.sum(earlier * ffn_hits, axis=-1).astype(jnp.int32).reshape(row_count, 2)
    is_ffn = chosen_routes < ffn_count
    targets = jnp.where(is_ffn, relative * CAP + slot_rank, -1)
    safe_targets = jnp.maximum(targets, 0)
    slot_total = ffn_count * CAP
    slot_ids = jnp.arange(slot_total, dtype=jnp.int32)
    dispatch_first = (slot_ids[:, None] == targets[None, :, 0]).astype(jnp.bfloat16)
    dispatch_second = (slot_ids[:, None] == targets[None, :, 1]).astype(jnp.bfloat16)
    slot_shape = (ffn_count, CAP, model_width)
    outgoing = (
        jnp.dot(dispatch_first + dispatch_second, second_low, preferred_element_type=jnp.float32)
        .astype(jnp.bfloat16)
        .reshape(slot_shape)
    )
    sending_grads = (
        jnp.dot(dispatch_first + dispatch_second, cotangent[0], preferred_element_type=jnp.float32)
        .astype(jnp.bfloat16)
        .reshape(slot_shape)
    )
    grads_in = exchange(sending_grads, ranks, 0, "grads_to_experts")
    weights_first = jnp.where(
        slot_ids[:, None] == targets[None, :, 0], route_weights[None, :, 0], 0.0
    )
    weights_second = jnp.where(
        slot_ids[:, None] == targets[None, :, 1], route_weights[None, :, 1], 0.0
    )
    slot_gates = jnp.sum(weights_first + weights_second, axis=1).reshape(ffn_count, 1, CAP)
    slot_gates = jnp.broadcast_to(
        jnp.pad(slot_gates, ((0, 0), (0, 0), (0, 128 - CAP))), (ffn_count, 8, 128)
    )
    own_expert = ctx_index // spread
    home_grads, returned, dots, gate_terms, linear_terms, down_terms = expert_layer(
        outgoing,
        slot_gates,
        grads_in.reshape(slot_total, model_width),
        (expert_gate, expert_linear, expert_down),
        ranks,
        lax.axis_size("dp"),
    )
    returned = returned.reshape(slot_total, model_width)
    home_grads = home_grads.reshape(slot_total, model_width)
    slot_dots = dots[:, 0, :CAP].reshape(slot_total)

    def collect(terms):
        share = scatter_sum(terms, "dp")
        bit = 1
        while bit < spread:
            share = (
                share.astype(jnp.float32) + swap(share, "ctx", bit).astype(jnp.float32)
            ).astype(jnp.bfloat16)
            bit *= 2
        parts, order = [share], [0]
        while bit < lax.axis_size("ctx"):
            bit *= 2
        while bit > spread:
            bit //= 2
            parts = parts + [swap(part, "ctx", bit) for part in parts]
            order = order + [place ^ (bit // spread) for place in order]
        stacked = jnp.stack(parts)
        places = jnp.array(order, jnp.int32) ^ own_expert
        inverse = jnp.argsort(places)
        return stacked[inverse].astype(jnp.float32)

    experts = (collect(gate_terms), collect(linear_terms), collect(down_terms))
    route_outputs = jnp.where(is_ffn[:, :, None], returned[safe_targets].astype(jnp.float32), 0.0)
    copy_index = ffn_count + 1
    combined = jnp.sum(route_weights[:, :, None] * route_outputs, axis=1)
    combined = combined + gate_weights[:, copy_index : copy_index + 1] * second
    mixing = jax.nn.softmax(
        jnp.einsum("td,jdc->tjc", second_low, constant_map, preferred_element_type=jnp.float32),
        axis=-1,
    )
    vectors = constant_vector.astype(jnp.float32)
    constant_terms = (
        mixing[:, :, 0:1] * second[:, None, :] + mixing[:, :, 1:2] * vectors[None, :, :]
    )
    constant_gates = gate_weights[:, ffn_count + 2 : ffn_count + 4]
    combined = combined + jnp.sum(constant_gates[:, :, None] * constant_terms, axis=1)
    result = (middle + combined).astype(jnp.bfloat16)
    ffn_weight_grad = jnp.where(is_ffn, slot_dots[safe_targets], 0.0)
    copy_grad = jnp.sum(upstream * second, axis=-1)
    constant_weight_grad = jnp.sum(upstream[:, None, :] * constant_terms, axis=-1)
    ffn_columns = jnp.sum(route_hits[:, :, :ffn_count] * ffn_weight_grad[:, :, None], axis=1)
    gate_grad = jnp.concatenate(
        [
            ffn_columns,
            jnp.zeros((row_count, 1), jnp.float32),
            copy_grad[:, None],
            constant_weight_grad,
        ],
        axis=1,
    )
    prob_grad = gate_grad * chosen_mask
    logit_grad = gate_probs * (prob_grad - jnp.sum(gate_probs * prob_grad, axis=-1, keepdims=True))
    carry_grad = jnp.dot(prior.T, logit_grad, precision=HIGH)
    logit_low = logit_grad.astype(jnp.bfloat16)
    router_grad = jnp.dot(second_low.T, logit_low, preferred_element_type=jnp.float32)
    second_grad = jnp.dot(logit_low, router.T, preferred_element_type=jnp.float32)
    second_grad = second_grad + gate_weights[:, copy_index : copy_index + 1] * upstream
    term_grad = constant_gates[:, :, None] * upstream[:, None, :]
    second_grad = second_grad + jnp.sum(term_grad * mixing[:, :, 0:1], axis=1)
    vector_grad = jnp.sum(term_grad * mixing[:, :, 1:2], axis=0)
    mixing_grad = jnp.stack(
        [
            jnp.sum(term_grad * second[:, None, :], axis=-1),
            jnp.sum(term_grad * vectors[None, :, :], axis=-1),
        ],
        axis=-1,
    )
    map_low = (
        mixing * (mixing_grad - jnp.sum(mixing * mixing_grad, axis=-1, keepdims=True))
    ).astype(jnp.bfloat16)
    map_grad = jnp.einsum("td,tjc->jdc", second_low, map_low, preferred_element_type=jnp.float32)
    second_grad = second_grad + jnp.einsum(
        "tjc,jdc->td", map_low, constant_map, preferred_element_type=jnp.float32
    )
    second_grad = second_grad + jnp.sum(
        jnp.where(is_ffn[:, :, None], home_grads[safe_targets].astype(jnp.float32), 0.0), axis=1
    )
    second_unit_grad = second_grad * gain_second
    second_gain_grad = jnp.sum(second_grad * unit_second, axis=0)
    middle_grad = upstream + inverse_second * (
        second_unit_grad
        - unit_second * jnp.mean(second_unit_grad * unit_second, axis=-1, keepdims=True)
    )
    middle_low = middle_grad.astype(jnp.bfloat16)
    output_grad = jnp.dot(attended_low.T, middle_low, preferred_element_type=jnp.float32)
    attended_grad = (
        jnp.dot(middle_low, output_weight.T, preferred_element_type=jnp.float32)
        .astype(jnp.bfloat16)
        .reshape(heads_shape)
    )
    row_delta = jnp.sum(attended_grad.astype(jnp.float32) * attended, axis=-1)
    zero_heads = jnp.zeros(heads_shape, jnp.float32)
    key_rows, value_rows = (
        lax.all_gather(key_flat, "ctx", axis=0, tiled=True),
        lax.all_gather(value_flat, "ctx", axis=0, tiled=True),
    )
    key_count = key_rows.shape[0]
    block_size = block_rows(key_count)
    key_positions = jnp.arange(key_count, dtype=jnp.int32)

    def visit(query_sum, block_index):
        begin = block_index * block_size
        key_block = lax.dynamic_slice_in_dim(key_rows, begin, block_size, 0).reshape(
            block_size, head_count, HEAD_DIM
        )
        value_block = lax.dynamic_slice_in_dim(value_rows, begin, block_size, 0).reshape(
            block_size, head_count, HEAD_DIM
        )
        key_pos = lax.dynamic_slice_in_dim(key_positions, begin, block_size, 0)
        weights_low, score_grad = pair_grads(
            query_heads,
            attended_grad,
            log_total,
            row_delta,
            positions,
            documents,
            key_block,
            value_block,
            key_pos,
            document_ids(key_pos, starts),
        )
        query_sum = query_sum + jnp.einsum(
            "qhk,khd->qhd", score_grad, key_block, preferred_element_type=jnp.float32
        )
        key_part = jnp.einsum(
            "qhk,qhd->khd", score_grad, query_heads, preferred_element_type=jnp.float32
        ).reshape(block_size, model_width)
        value_part = jnp.einsum(
            "qhk,qhd->khd", weights_low, attended_grad, preferred_element_type=jnp.float32
        ).reshape(block_size, model_width)
        return (query_sum, jnp.concatenate([key_part, value_part], axis=1))

    query_grad, key_terms = lax.scan(
        visit, zero_heads, jnp.arange(key_count // block_size, dtype=jnp.int32)
    )
    summed = lax.psum_scatter(
        key_terms.reshape(key_count, 2 * model_width).astype(jnp.bfloat16),
        "ctx",
        scatter_dimension=0,
        tiled=True,
    ).astype(jnp.float32)
    key_grad = summed[:, :model_width].reshape(heads_shape)
    value_grad = summed[:, model_width:].reshape(heads_shape)
    query_low = (
        rotary(query_grad, positions, -1.0).reshape(row_count, model_width).astype(jnp.bfloat16)
    )
    key_low = rotary(key_grad, positions, -1.0).reshape(row_count, model_width).astype(jnp.bfloat16)
    value_low = value_grad.reshape(row_count, model_width).astype(jnp.bfloat16)
    query_sum_grad = jnp.dot(normed.T, query_low, preferred_element_type=jnp.float32)
    key_sum_grad = jnp.dot(normed.T, key_low, preferred_element_type=jnp.float32)
    value_sum_grad = jnp.dot(normed.T, value_low, preferred_element_type=jnp.float32)
    first_grad = (
        jnp.dot(query_low, query_weight.T, preferred_element_type=jnp.float32)
        + jnp.dot(key_low, key_weight.T, preferred_element_type=jnp.float32)
        + jnp.dot(value_low, value_weight.T, preferred_element_type=jnp.float32)
    )
    first_unit_grad = first_grad * gain_first
    first_gain_grad = jnp.sum(first_grad * unit_first, axis=0)
    token_grad = middle_grad + inverse_first * (
        first_unit_grad
        - unit_first * jnp.mean(first_unit_grad * unit_first, axis=-1, keepdims=True)
    )
    steps = [(axis, bit) for axis in ("ctx", "exp", "dp") for bit in bits_of(axis)]
    units = 2 ** len(steps)
    wide = jnp.concatenate([query_sum_grad, key_sum_grad, value_sum_grad, output_grad], axis=0)
    small_terms = (first_gain_grad, second_gain_grad, router_grad, carry_grad, map_grad, vector_grad)
    flat = jnp.concatenate([term.reshape(-1) for term in small_terms])
    small_rows = -(-flat.size // (units * model_width))
    wide_rows = wide.shape[0] // units
    unit_rows = -(-(small_rows + wide_rows) // 16) * 16
    flat = jnp.pad(flat, (0, units * small_rows * model_width - flat.size))
    packed = jnp.concatenate(
        [
            wide.reshape(units, wide_rows, model_width).astype(jnp.bfloat16),
            flat.reshape(units, small_rows, model_width).astype(jnp.bfloat16),
            jnp.zeros((units, unit_rows - wide_rows - small_rows, model_width), jnp.bfloat16),
        ],
        axis=1,
    )
    for axis, bit in steps:
        packed = packed.reshape((2, -1) + packed.shape[1:])
        packed = halve(packed, axis, bit, 0)
    for axis, bit in steps[::-1]:
        other = swap(packed, axis, bit)
        own = (lax.axis_index(axis) // bit) % 2
        packed = jnp.concatenate(
            [jnp.where(own == 0, packed, other), jnp.where(own == 0, other, packed)], axis=0
        )
    packed = packed.astype(jnp.float32)
    wide = packed[:, :wide_rows].reshape(4, model_width, model_width)
    flat = packed[:, wide_rows : wide_rows + small_rows].reshape(-1)
    smalls, begin = [], 0
    for term in small_terms:
        smalls.append(flat[begin : begin + term.size].reshape(term.shape))
        begin += term.size
    dense = (smalls[0], wide[0], wide[1], wide[2], wide[3]) + tuple(smalls[1:])
    return (
        result[None],
        token_grad[None],
        dense[0],
        dense[1],
        dense[2],
        dense[3],
        dense[4],
        dense[5],
        dense[6],
        dense[7],
        dense[8],
        dense[9],
        experts[0],
        experts[1],
        experts[2],
    )


def solution(mesh):
    return jax.shard_map(
        local,
        mesh=mesh,
        in_specs=(
            P(("dp", "exp"), "ctx", None),
            P(("dp", "exp"), "ctx", None),
            P(("dp", "exp"), "ctx", None),
            P(("dp", "exp"), "ctx", None),
            P(("dp", "exp"), None),
            P(),
            P(),
            P(),
            P(),
            P(),
            P(),
            P(),
            P(),
            P(),
            P(),
            P("exp", None, None),
            P("exp", None, None),
            P("exp", None, None),
        ),
        out_specs=(
            P(("dp", "exp"), "ctx", None),
            P(("dp", "exp"), "ctx", None),
            P(),
            P(),
            P(),
            P(),
            P(),
            P(),
            P(),
            P(),
            P(),
            P(),
            P("exp", None, "dp"),
            P("exp", None, "dp"),
            P("exp", "dp", None),
        ),
        check_vma=False,
    )
```

```python
import math

import jax
import jax.numpy as jnp
import numpy as np
from jax import lax
from jax.experimental import pallas as pl
from jax.experimental.pallas import tpu as pltpu
from jax.sharding import PartitionSpec as P

HEAD_DIM = 64
CAP = 96


EPSILON = 1e-06
NEGATIVE = -1e30
HIGH = lax.Precision.HIGHEST


def bits_of(axis):
    bits, bit = [], 1
    while bit < lax.axis_size(axis):
        bits.append(bit)
        bit *= 2
    return bits


def swap(values, axis, bit):
    return lax.ppermute(values, axis, [(i, i ^ bit) for i in range(lax.axis_size(axis))])


def halve(values, axis, bit, dim):
    own = (lax.axis_index(axis) // bit) % 2
    kept = lax.dynamic_index_in_dim(values, own, dim, keepdims=False)
    sent = lax.dynamic_index_in_dim(values, 1 - own, dim, keepdims=False)
    total = kept.astype(jnp.float32) + swap(sent, axis, bit).astype(jnp.float32)
    return total.astype(jnp.bfloat16)


def scatter_sum(values, axis):
    bits = bits_of(axis)
    values = values.reshape((2,) * len(bits) + values.shape[1:])
    for place, bit in enumerate(bits):
        values = halve(values, axis, bit, len(bits) - 1 - place)
    return values


def mesh_id(exp_index, ctx_index):
    return {"exp": exp_index, "ctx": ctx_index}


def dot(left, right):
    return jnp.dot(left, right, preferred_element_type=jnp.float32)


def dot_nt(left, right):
    return lax.dot_general(
        left, right, (((1,), (1,)), ((), ())), preferred_element_type=jnp.float32
    )


def dot_tn(left, right):
    return lax.dot_general(
        left, right, (((0,), (0,)), ((), ())), preferred_element_type=jnp.float32
    )


def member_of(shift, ranks):
    exchange_size, group_size, spread = ranks
    exp_index, ctx_index = lax.axis_index("exp"), lax.axis_index("ctx")
    far, near = shift // group_size, shift % group_size
    place = jnp.bitwise_xor(ctx_index // spread, near) * spread + lax.rem(ctx_index, spread)
    return mesh_id(jnp.bitwise_xor(exp_index, far), place)


def greet(count, ranks):
    barrier = pltpu.get_barrier_semaphore()
    for shift in range(1, count):
        pl.semaphore_signal(
            barrier, inc=1, device_id=member_of(shift, ranks), device_id_type=pl.DeviceIdType.MESH
        )
    pl.semaphore_wait(barrier, count - 1)


def send_block(source, target, shift, ranks, send_sem, recv_sem):
    return pltpu.make_async_remote_copy(
        src_ref=source.at[shift],
        dst_ref=target.at[shift],
        send_sem=send_sem.at[shift],
        recv_sem=recv_sem.at[shift],
        device_id=member_of(shift, ranks),
        device_id_type=pl.DeviceIdType.MESH,
    )


def expert_layer(outgoing, gates, grads, weights, ranks, shares):
    count, cap, width = outgoing.shape
    hidden_units = weights[0].shape[2]
    rows = count * cap
    share = hidden_units // shares
    spread = ranks[2]

    def kernel(
        outgoing_ref,
        gates_ref,
        grads_ref,
        gate_hbm,
        linear_hbm,
        down_hbm,
        back_ref,
        output_ref,
        dots_ref,
        gate_terms,
        linear_terms,
        down_terms,
        received,
        received_gates,
        gate_w,
        linear_w,
        down_w,
        hidden_grad,
        hidden,
        gate_low,
        linear_low,
        rows_t,
        scaled,
        gate_column,
        out_total,
        in_total,
        out_send,
        in_send,
        dots_send,
        terms,
        weight_sem,
        send_sem,
        recv_sem,
        local_sem,
        terms_sem,
    ):
        own = lax.axis_index("ctx") // spread
        loads = [
            pltpu.make_async_copy(source.at[own], target, weight_sem.at[index])
            for index, (source, target) in enumerate(
                ((down_hbm, down_w), (gate_hbm, gate_w), (linear_hbm, linear_w))
            )
        ]
        for load in loads:
            load.start()
        greet(count, ranks)

        def send_all(source, target, index):
            copies = [
                send_block(source, target, shift, ranks, send_sem.at[index], recv_sem.at[index])
                for shift in range(1, count)
            ]
            copies.append(
                pltpu.make_async_copy(source.at[0], target.at[0], local_sem.at[index])
            )
            for copy in copies:
                copy.start()
            return copies

        incoming = send_all(gates_ref, received_gates, 0) + send_all(outgoing_ref, received, 1)
        loads[0].wait()

        def backward_in(index, carry):
            part = pl.ds(pl.multiple_of(index * share, share), share)
            hidden_grad[:, part] = dot_nt(grads_ref[...], down_w[part, :])
            return carry

        lax.fori_loop(0, shares, backward_in, 0)
        for copy in incoming + loads[1:]:
            copy.wait()
        for shift in range(count):
            column = jnp.transpose(received_gates[shift])[:cap, 0:1]
            block = pl.ds(shift * cap, cap)
            gate_column[block, :] = jnp.broadcast_to(column, (cap, 128))
            scaled[block, :] = (column * grads_ref[block, :].astype(jnp.float32)).astype(
                jnp.bfloat16
            )
        tokens = received[...].reshape(rows, width)
        rows_t[...] = jnp.transpose(tokens)

        def through(index, carry):
            part = pl.ds(pl.multiple_of(index * share, share), share)
            tokens = received[...].reshape(rows, width)
            gate_part = dot(tokens, gate_w[:, part])
            linear_part = dot(tokens, linear_w[:, part])
            sigmoid = 1.0 / (1.0 + jnp.exp(-gate_part))
            silu = gate_part * sigmoid
            low = (silu * linear_part).astype(jnp.bfloat16)
            hidden[:, part] = low
            upper = hidden_grad[:, part] * gate_column[:, 0:1]
            low_gate = (
                upper * linear_part * sigmoid * (1.0 + gate_part * (1.0 - sigmoid))
            ).astype(jnp.bfloat16)
            gate_low[:, part] = low_gate
            low_linear = (upper * silu).astype(jnp.bfloat16)
            linear_low[:, part] = low_linear
            out = dot(low, down_w[part, :])
            back = dot_nt(low_gate, gate_w[:, part]) + dot_nt(low_linear, linear_w[:, part])

            @pl.when(index == 0)
            def _():
                out_total[...] = out
                in_total[...] = back

            @pl.when(index > 0)
            def _():
                out_total[...] += out
                in_total[...] += back

            return carry

        lax.fori_loop(0, shares, through, 0)
        in_send[...] = in_total[...].astype(jnp.bfloat16).reshape(count, cap, width)
        going = send_all(in_send, back_ref, 2)
        low = out_total[...].astype(jnp.bfloat16)
        out_send[...] = low.reshape(count, cap, width)
        dots = jnp.sum(
            low.astype(jnp.float32) * grads_ref[...].astype(jnp.float32), axis=1, keepdims=True
        )
        for shift in range(count):
            column = jnp.broadcast_to(dots[shift * cap : (shift + 1) * cap], (cap, 128))
            dots_send[shift, :, 0:cap] = jnp.transpose(column)[0:8, :]
            dots_send[shift, :, cap:] = jnp.zeros((8, 128 - cap), jnp.float32)
        going = going + send_all(dots_send, dots_ref, 3) + send_all(out_send, output_ref, 4)

        def term_copy(which, index):
            target = (down_terms, gate_terms, linear_terms)[which]
            return pltpu.make_async_copy(
                terms[which].at[index], target.at[index], terms_sem.at[which, index]
            )

        def weigh(index, carry):
            part = pl.ds(pl.multiple_of(index * share, share), share)
            terms[0][index] = dot_tn(hidden[:, part], scaled[...]).astype(jnp.bfloat16)
            term_copy(0, index).start()
            terms[1][index] = dot(rows_t[...], gate_low[:, part]).astype(jnp.bfloat16)
            term_copy(1, index).start()
            terms[2][index] = dot(rows_t[...], linear_low[:, part]).astype(jnp.bfloat16)
            term_copy(2, index).start()
            return carry

        lax.fori_loop(0, shares, weigh, 0)
        for which in range(3):
            for index in range(shares):
                term_copy(which, index).wait()
        for copy in going:
            copy.wait()

    low, full = jnp.bfloat16, jnp.float32
    columns, lines = (shares, width, share), (shares, share, width)
    any_space = pl.BlockSpec(memory_space=pl.ANY)
    in_vmem = pl.BlockSpec(memory_space=pltpu.VMEM)
    return pl.pallas_call(
        kernel,
        out_shape=[
            jax.ShapeDtypeStruct(outgoing.shape, low),
            jax.ShapeDtypeStruct(outgoing.shape, low),
            jax.ShapeDtypeStruct(gates.shape, full),
            jax.ShapeDtypeStruct(columns, low),
            jax.ShapeDtypeStruct(columns, low),
            jax.ShapeDtypeStruct(lines, low),
        ],
        in_specs=[in_vmem, in_vmem, in_vmem, any_space, any_space, any_space],
        out_specs=[any_space] * 6,
        scratch_shapes=[
            pltpu.VMEM(outgoing.shape, low),
            pltpu.VMEM(gates.shape, full),
            pltpu.VMEM((width, hidden_units), low),
            pltpu.VMEM((width, hidden_units), low),
            pltpu.VMEM((hidden_units, width), low),
            pltpu.VMEM((rows, hidden_units), full),
            pltpu.VMEM((rows, hidden_units), low),
            pltpu.VMEM((rows, hidden_units), low),
            pltpu.VMEM((rows, hidden_units), low),
            pltpu.VMEM((width, rows), low),
            pltpu.VMEM((rows, width), low),
            pltpu.VMEM((rows, 128), full),
            pltpu.VMEM((rows, width), full),
            pltpu.VMEM((rows, width), full),
            pltpu.VMEM(outgoing.shape, low),
            pltpu.VMEM(outgoing.shape, low),
            pltpu.VMEM(gates.shape, full),
            [pltpu.VMEM(lines, low), pltpu.VMEM(columns, low), pltpu.VMEM(columns, low)],
            pltpu.SemaphoreType.DMA((3,)),
            pltpu.SemaphoreType.DMA((5, count)),
            pltpu.SemaphoreType.DMA((5, count)),
            pltpu.SemaphoreType.DMA((5,)),
            pltpu.SemaphoreType.DMA((3, shares)),
        ],
        compiler_params=pltpu.CompilerParams(
            collective_id=1, has_side_effects=True, vmem_limit_bytes=60 * 2**20
        ),
        cost_estimate=pl.CostEstimate(
            flops=18 * rows * width * hidden_units,
            bytes_accessed=12 * width * hidden_units + 12 * rows * width,
            transcendentals=rows * hidden_units,
        ),
        name="experts",
    )(outgoing, gates, grads, *weights)


def rope_tables(row_count):
    half = HEAD_DIM // 2
    frequency = np.exp(
        np.arange(half, dtype=np.float32) * np.float32(-2.0 * math.log(10000.0) / HEAD_DIM)
    ).astype(np.float32)
    angles = np.arange(row_count, dtype=np.float32)[:, None] * frequency[None, :]
    cosine, sine = np.cos(angles).astype(np.float32), np.sin(angles).astype(np.float32)
    return (
        np.concatenate([cosine] * 4, axis=1),
        np.concatenate([-sine, sine, -sine, sine], axis=1),
    )


def rotate(values, cosine, sine):
    lane = lax.broadcasted_iota(jnp.int32, cosine.shape, 1)
    leading = jnp.bitwise_and(lane, HEAD_DIM - 1) < HEAD_DIM // 2
    parts = []
    for begin in range(0, values.shape[1], 128):
        part = values[:, begin : begin + 128]
        ahead = pltpu.roll(part, 128 - HEAD_DIM // 2, 1)
        behind = pltpu.roll(part, HEAD_DIM // 2, 1)
        parts.append(part * cosine + jnp.where(leading, ahead, behind) * sine)
    return jnp.concatenate(parts, axis=1)


def inverse_norm(values):
    return lax.rsqrt(jnp.mean(values * values, axis=1, keepdims=True) + EPSILON)


def head_masks(rows):
    first = lax.broadcasted_iota(jnp.int32, (rows, 128), 1) < HEAD_DIM
    return first, jnp.logical_not(first)


def start_of(positions, starts):
    first = jnp.zeros_like(positions)
    for index in range(starts.shape[1]):
        begin = starts[0, index]
        first = jnp.where(begin <= positions, jnp.maximum(first, begin), first)
    return first


def gather_steps(size):
    bits, held, steps = [], [0], []
    bit = size // 2
    while bit >= 1:
        steps.append((bit, list(held)))
        held = held + [place ^ bit for place in held]
        bit //= 2
    return steps


def peer(far, near):
    return {
        "exp": jnp.bitwise_xor(lax.axis_index("exp"), far),
        "ctx": jnp.bitwise_xor(lax.axis_index("ctx"), near),
    }


def greet_all(places):
    barrier = pltpu.get_barrier_semaphore()
    for far, near in places:
        pl.semaphore_signal(
            barrier, inc=1, device_id=peer(far, near), device_id_type=pl.DeviceIdType.MESH
        )
    pl.semaphore_wait(barrier, len(places))


def group_places(ranks):
    return [
        (shift // ranks[1], shift % ranks[1] * ranks[2]) for shift in range(1, ranks[0] * ranks[1])
    ]


def ring_places(size):
    return [(0, bit) for bit, _ in gather_steps(size)]


def places_of(ranks, size):
    places = group_places(ranks)
    return places + [place for place in ring_places(size) if place not in places]


class Gather:
    def __init__(self, buffers, size, send_sem, recv_sem):
        self.buffers, self.size = buffers, size
        self.send_sem, self.recv_sem = send_sem, recv_sem
        self.steps = gather_steps(size)
        self.started = []

    def copy(self, place, bit, index):
        block = jnp.bitwise_xor(lax.axis_index("ctx"), place)
        buffer = self.buffers[index]
        return pltpu.make_async_remote_copy(
            src_ref=buffer.at[block],
            dst_ref=buffer.at[block],
            send_sem=self.send_sem.at[index, place ^ bit],
            recv_sem=self.recv_sem.at[index, place ^ bit],
            device_id=peer(0, bit),
            device_id_type=pl.DeviceIdType.MESH,
        )

    def forward(self, place):
        for bit, held in self.steps:
            if place in held:
                for index in range(len(self.buffers)):
                    copy = self.copy(place, bit, index)
                    copy.start()
                    self.started.append(copy)

    def arrive(self, place):
        bit = place & -place
        for index in range(len(self.buffers)):
            self.copy(place ^ bit, bit, index).wait_recv()
        self.forward(place)

    def finish(self):
        for copy in self.started:
            copy.wait_send()


def slot_targets(routes, ranks, cap):
    exchange_size, group_size, spread = ranks
    rows = routes.shape[1]
    experts = exchange_size * group_size
    expert = lax.broadcasted_iota(jnp.int32, (16, rows), 0)
    hits = [(expert == routes[k : k + 1]).astype(jnp.float32) for k in range(2)]
    before = lax.broadcasted_iota(jnp.int32, (rows, rows), 0) < lax.broadcasted_iota(
        jnp.int32, (rows, rows), 1
    )
    earlier = dot(
        (hits[0] + hits[1]).astype(jnp.bfloat16), before.astype(jnp.float32).astype(jnp.bfloat16)
    )
    targets = []
    for k in range(2):
        route = routes[k : k + 1]
        rank = jnp.sum(hits[k] * earlier, axis=0, keepdims=True)
        far = jnp.bitwise_xor(route // group_size, lax.axis_index("exp"))
        near = jnp.bitwise_xor(route % group_size, lax.axis_index("ctx") // spread)
        place = ((far * group_size + near) * cap).astype(jnp.float32)
        targets.append(jnp.where(route < experts, place + rank, -1.0))
    return targets


def attend_layer(
    tokens, cotangent, previous, routes, starts, weights, norms, heads, carry, ranks, cap, size
):
    rows, width = tokens.shape
    count = ranks[0] * ranks[1]
    slots = count * cap
    pairs = width // 128
    tables = rope_tables(size * rows)
    low, full = jnp.bfloat16, jnp.float32

    def kernel(
        tokens_ref,
        cotangent_ref,
        previous_ref,
        routes_ref,
        starts_ref,
        query_hbm,
        key_hbm,
        value_hbm,
        output_hbm,
        first_ref,
        second_ref,
        heads_ref,
        carry_ref,
        cosine_hbm,
        sine_hbm,
        queries_out,
        keys_out,
        values_out,
        attended_ref,
        lse_ref,
        middle_ref,
        probs_ref,
        targets_ref,
        outgoing_ref,
        gates_ref,
        grads_ref,
        stream,
        queries,
        keys,
        values,
        query_w,
        key_w,
        value_w,
        output_w,
        cosine,
        sine,
        bias,
        totals,
        highest,
        slot_grads,
        load_sem,
        gather_send,
        gather_recv,
        grad_send,
        grad_recv,
        keep_sem,
    ):
        own = lax.axis_index("ctx")
        loads = [
            pltpu.make_async_copy(source, target, load_sem.at[index])
            for index, (source, target) in enumerate(
                (
                    (query_hbm, query_w),
                    (key_hbm, key_w),
                    (value_hbm, value_w),
                    (cosine_hbm, cosine),
                    (sine_hbm, sine),
                    (output_hbm, output_w),
                )
            )
        ]
        for load in loads:
            load.start()
        stream[own] = tokens_ref[...]
        greet_all(places_of(ranks, size))
        gather = Gather([stream], size, gather_send, gather_recv)
        gather.forward(0)

        targets = slot_targets(routes_ref[...], ranks, cap)
        slot = lax.broadcasted_iota(jnp.int32, (slots, rows), 0).astype(full)
        picked = jnp.logical_or(slot == targets[0], slot == targets[1])
        picked = picked.astype(full).astype(low)
        slot_grads[...] = dot(picked, cotangent_ref[...]).astype(low).reshape(count, cap, width)
        grad_copies = [
            send_block(slot_grads, grads_ref, shift, ranks, grad_send, grad_recv)
            for shift in range(1, count)
        ]
        grad_copies.append(pltpu.make_async_copy(slot_grads.at[0], grads_ref.at[0], keep_sem.at[0]))

        for load in loads[:5]:
            load.wait()
        gain = first_ref[...].astype(full)

        def project(block, wanted):
            line = pl.ds(pl.multiple_of(block * rows, rows), rows)
            values_in = stream[block].astype(full)
            normed = (values_in * inverse_norm(values_in) * gain).astype(low)
            if "q" in wanted:
                turned = rotate(dot(normed, query_w[...]), cosine[line, :], sine[line, :])
                queries[block] = (turned.astype(low).astype(full) * HEAD_DIM**-0.5).astype(low)
            if "k" in wanted:
                turned = rotate(dot(normed, key_w[...]), cosine[line, :], sine[line, :])
                keys[block] = turned.astype(low)
                values[block] = dot(normed, value_w[...]).astype(low)

        masks = head_masks(rows)
        query_pos = own * rows + lax.broadcasted_iota(jnp.int32, (rows, rows), 0)
        document_start = start_of(query_pos[:, 0:128], starts_ref)

        def attend(block):
            key_pos = block * rows + lax.broadcasted_iota(jnp.int32, (rows, rows), 1)
            allowed = jnp.logical_and(key_pos >= document_start[:, 0:1], key_pos <= query_pos)
            bias[...] = jnp.where(allowed, 0.0, NEGATIVE)

            def pair(index, carried):
                lanes = pl.ds(pl.multiple_of(index * 128, 128), 128)
                query, key, value = queries[own, :, lanes], keys[block, :, lanes], values[block, :, lanes]
                for head in range(2):
                    scores = dot_nt(jnp.where(masks[head], query, 0), key) + bias[...]
                    old = highest[index, head][:, 0:1]
                    new = jnp.maximum(old, jnp.max(scores, axis=1, keepdims=True))
                    weight = jnp.exp(scores - new).astype(low)
                    factor = jnp.exp(old - new)
                    totals[index, head] = totals[index, head] * factor + dot(
                        weight, jnp.where(masks[head], value, 1)
                    )
                    highest[index, head] = jnp.broadcast_to(new, (rows, 128))
                return carried

            lax.fori_loop(0, pairs, pair, 0)

        totals[...] = jnp.zeros_like(totals)
        highest[...] = jnp.full(highest.shape, NEGATIVE, full)
        project(own, "qk")
        attend(own)
        for place in range(1, size):
            gather.arrive(place)
            if place == size // 2:
                for copy in grad_copies:
                    copy.start()
            block = jnp.bitwise_xor(own, place)

            @pl.when(block < own)
            def _():
                project(block, "k")
                attend(block)

            @pl.when(block > own)
            def _():
                project(block, "q")

        keep = [
            pltpu.make_async_copy(source, target, keep_sem.at[index + 1])
            for index, (source, target) in enumerate(
                ((queries, queries_out), (keys, keys_out), (values, values_out))
            )
        ]
        for copy in keep:
            copy.start()

        lane = lax.broadcasted_iota(jnp.int32, (rows, 128), 1)
        lse_ref[...] = jnp.zeros_like(lse_ref)
        for index in range(pairs):
            halves = []
            for head in range(2):
                total = totals[index, head]
                column = HEAD_DIM if head == 0 else 0
                weight_sum = total[:, column : column + 1]
                halves.append(total / weight_sum)
                lse = highest[index, head][:, 0:1] + jnp.log(weight_sum)
                lse_ref[...] = jnp.where(lane == 2 * index + head, lse, lse_ref[...])
            attended_ref[:, index * 128 : index * 128 + 128] = jnp.where(
                masks[0], halves[0], halves[1]
            )
        loads[5].wait()
        middle = tokens_ref[...].astype(full) + dot(attended_ref[...].astype(low), output_w[...])
        middle_ref[...] = middle
        second = middle * inverse_norm(middle) * second_ref[...].astype(full)
        second_low = second.astype(low)
        outgoing_ref[...] = dot(picked, second_low).astype(low).reshape(count, cap, width)

        experts = previous_ref.shape[1]
        logits = dot(second_low, heads_ref[...])[:, 0:experts] + jnp.dot(
            previous_ref[...], carry_ref[...].astype(full), precision=HIGH
        )
        logits = logits - jnp.max(logits, axis=1, keepdims=True)
        powers = jnp.exp(logits)
        probs_ref[...] = jnp.zeros_like(probs_ref)
        probs_ref[:, 0:experts] = powers / jnp.sum(powers, axis=1, keepdims=True)
        turned = jnp.transpose(probs_ref[...])[0:16]
        expert = lax.broadcasted_iota(jnp.int32, (16, rows), 0)
        weighted = jnp.zeros((slots, rows), full)
        for k in range(2):
            route = routes_ref[k : k + 1, :]
            gate = jnp.sum(jnp.where(expert == route, turned, 0.0), axis=0, keepdims=True)
            weighted = jnp.where(slot == targets[k], gate, weighted)
        gate_column = jnp.sum(weighted, axis=1, keepdims=True)
        for shift in range(count):
            column = jnp.broadcast_to(gate_column[shift * cap : (shift + 1) * cap], (cap, 128))
            gates_ref[shift] = jnp.zeros((8, 128), full)
            gates_ref[shift, :, 0:cap] = jnp.transpose(column)[0:8, :]
        pad = jnp.zeros((6, rows), full)
        target_rows = jnp.concatenate([targets[0], targets[1], pad], axis=0)
        target_rows = jnp.concatenate([target_rows] + [jnp.zeros((120, rows), full)], axis=0)
        targets_ref[...] = jnp.transpose(target_rows)

        gather.finish()
        for copy in keep + grad_copies:
            copy.wait()

    stream_shape = (size, rows, width)
    any_space = pl.BlockSpec(memory_space=pl.ANY)
    in_vmem = pl.BlockSpec(memory_space=pltpu.VMEM)
    square = (width, width)
    return pl.pallas_call(
        kernel,
        out_shape=[
            jax.ShapeDtypeStruct(stream_shape, low),
            jax.ShapeDtypeStruct(stream_shape, low),
            jax.ShapeDtypeStruct(stream_shape, low),
            jax.ShapeDtypeStruct((rows, width), full),
            jax.ShapeDtypeStruct((rows, 128), full),
            jax.ShapeDtypeStruct((rows, width), full),
            jax.ShapeDtypeStruct((rows, 128), full),
            jax.ShapeDtypeStruct((rows, 128), full),
            jax.ShapeDtypeStruct((count, cap, width), low),
            jax.ShapeDtypeStruct((count, 8, 128), full),
            jax.ShapeDtypeStruct((count, cap, width), low),
        ],
        in_specs=[in_vmem] * 4
        + [pl.BlockSpec(memory_space=pltpu.SMEM)]
        + [any_space] * 4
        + [in_vmem] * 4
        + [any_space] * 2,
        out_specs=[any_space] * 3 + [in_vmem] * 7 + [any_space],
        scratch_shapes=[
            pltpu.VMEM(stream_shape, low),
            pltpu.VMEM(stream_shape, low),
            pltpu.VMEM(stream_shape, low),
            pltpu.VMEM(stream_shape, low),
            pltpu.VMEM(square, low),
            pltpu.VMEM(square, low),
            pltpu.VMEM(square, low),
            pltpu.VMEM(square, low),
            pltpu.VMEM((size * rows, 128), full),
            pltpu.VMEM((size * rows, 128), full),
            pltpu.VMEM((rows, rows), full),
            pltpu.VMEM((pairs, 2, rows, 128), full),
            pltpu.VMEM((pairs, 2, rows, 128), full),
            pltpu.VMEM((count, cap, width), low),
            pltpu.SemaphoreType.DMA((6,)),
            pltpu.SemaphoreType.DMA((1, size)),
            pltpu.SemaphoreType.DMA((1, size)),
            pltpu.SemaphoreType.DMA((count,)),
            pltpu.SemaphoreType.DMA((count,)),
            pltpu.SemaphoreType.DMA((4,)),
        ],
        compiler_params=pltpu.CompilerParams(
            collective_id=0, has_side_effects=True, vmem_limit_bytes=60 * 2**20
        ),
        cost_estimate=pl.CostEstimate(
            flops=2 * size * rows * width * width * 3 + 16 * size * rows * rows * width,
            bytes_accessed=20 * 2**20,
            transcendentals=size * rows * rows * 12,
        ),
        name="attend",
    )(
        tokens,
        cotangent,
        previous,
        routes,
        starts,
        *weights,
        *norms,
        heads,
        carry,
        jnp.asarray(tables[0]),
        jnp.asarray(tables[1]),
    )


def column_of(values, index):
    return values[:, index : index + 1]


def backward_layer(
    tokens,
    cotangent,
    previous,
    routes,
    starts,
    forward,
    returns,
    weights,
    norms,
    heads,
    vectors,
    ranks,
    cap,
    size,
):
    rows, width = tokens.shape
    count = ranks[0] * ranks[1]
    slots = count * cap
    pairs = width // 128
    tables = rope_tables(size * rows)
    low, full = jnp.bfloat16, jnp.float32
    experts = previous.shape[1]
    copy_index = count + 1
    stat_rows = 16

    def kernel(
        tokens_ref,
        cotangent_ref,
        previous_ref,
        routes_ref,
        starts_ref,
        attended_ref,
        lse_ref,
        middle_ref,
        probs_ref,
        targets_ref,
        queries_hbm,
        keys_hbm,
        values_hbm,
        back_ref,
        output_ref,
        dots_ref,
        query_hbm,
        key_hbm,
        value_hbm,
        output_hbm,
        first_ref,
        second_ref,
        heads_ref,
        vectors_ref,
        cosine_hbm,
        sine_hbm,
        result_ref,
        token_grads_ref,
        wide_ref,
        small_ref,
        queries,
        keys,
        values,
        query_w,
        key_w,
        value_w,
        output_w,
        cosine,
        sine,
        bias,
        out_grads,
        stats,
        delta,
        middle_grad,
        query_total,
        key_total,
        value_total,
        load_sem,
        gather_send,
        gather_recv,
    ):
        own = lax.axis_index("ctx")
        line = pl.ds(pl.multiple_of(own * rows, rows), rows)
        loads = [
            pltpu.make_async_copy(source, target, load_sem.at[index])
            for index, (source, target) in enumerate(
                (
                    (output_hbm, output_w),
                    (queries_hbm, queries),
                    (keys_hbm, keys),
                    (values_hbm, values),
                    (cosine_hbm.at[line], cosine),
                    (sine_hbm.at[line], sine),
                    (query_hbm, query_w),
                    (key_hbm, key_w),
                    (value_hbm, value_w),
                )
            )
        ]
        for load in loads:
            load.start()
        greet_all(ring_places(size))

        lane = lax.broadcasted_iota(jnp.int32, (rows, 128), 1)
        upstream = cotangent_ref[...].astype(full)
        middle = middle_ref[...]
        inverse_second = inverse_norm(middle)
        unit_second = middle * inverse_second
        gain_second = second_ref[...].astype(full)
        second = unit_second * gain_second
        second_low = second.astype(low)
        heads_in = heads_ref[...]
        mixed = dot(second_low, heads_in)
        probs = probs_ref[...]
        route = [column_of(routes_ref[...], k) for k in range(2)]
        chosen = jnp.logical_or(lane == route[0], lane == route[1])
        gates = jnp.where(chosen, probs, 0.0)
        target = [column_of(targets_ref[...], k) for k in range(2)]

        gate_grad = jnp.zeros((rows, 128), full)
        place = lane.astype(full)
        for k in range(2):
            found = jnp.zeros((rows, 128), full)
            for shift in range(count):
                found = found + jnp.where(
                    jnp.logical_and(target[k] - shift * cap == place, lane < cap),
                    dots_ref[shift, 0:1, :],
                    0.0,
                )
            gate_grad = gate_grad + jnp.where(
                lane == route[k], jnp.sum(found, axis=1, keepdims=True), 0.0
            )
        copy_grad = jnp.sum(upstream * second, axis=1, keepdims=True)
        gate_grad = jnp.where(lane == copy_index, copy_grad, gate_grad)
        direct = column_of(gates, copy_index)
        constants = []
        for index in range(2):
            vector = vectors_ref[index : index + 1, :].astype(full)
            vector_dot = jnp.sum(upstream * vector, axis=1, keepdims=True)
            begin = experts + 2 * index
            spread_of = column_of(mixed, begin + 1) - column_of(mixed, begin)
            mixing = (1.0 / (1.0 + jnp.exp(spread_of)), 1.0 / (1.0 + jnp.exp(-spread_of)))
            gate = column_of(gates, copy_index + 1 + index)
            term = mixing[0] * copy_grad + mixing[1] * vector_dot
            gate_grad = jnp.where(lane == copy_index + 1 + index, term, gate_grad)
            direct = direct + gate * mixing[0]
            constants.append((gate, mixing, vector, vector_dot))
        prob_grad = jnp.where(chosen, gate_grad, 0.0)
        logit_grad = probs * (prob_grad - jnp.sum(probs * prob_grad, axis=1, keepdims=True))
        head_grad = logit_grad
        for index, (gate, mixing, vector, vector_dot) in enumerate(constants):
            mixing_grad = (gate * copy_grad, gate * vector_dot)
            mean = mixing[0] * mixing_grad[0] + mixing[1] * mixing_grad[1]
            for part in range(2):
                head_grad = jnp.where(
                    lane == experts + 2 * index + part,
                    mixing[part] * (mixing_grad[part] - mean),
                    head_grad,
                )
        head_low = head_grad.astype(low)

        slot = lax.broadcasted_iota(jnp.int32, (rows, slots), 1).astype(full)
        picked = [(slot == target[k]).astype(full).astype(low) for k in range(2)]
        second_grad = (
            dot_nt(head_low, heads_in) + direct * upstream + dot(picked[0] + picked[1], back_ref[...])
        )
        normal_grad = second_grad * gain_second
        middle_total = upstream + inverse_second * (
            normal_grad - unit_second * jnp.mean(normal_grad * unit_second, axis=1, keepdims=True)
        )
        middle_grad[...] = middle_total
        middle_low = middle_total.astype(low)
        loads[0].wait()
        out_grad = dot_nt(middle_low, output_w[...]).astype(low)
        out_grads[own] = out_grad
        product = out_grad.astype(full) * attended_ref[...]
        masks = head_masks(rows)
        deltas = jnp.zeros((rows, 128), full)
        for index in range(pairs):
            part = product[:, index * 128 : index * 128 + 128]
            for head in range(2):
                total = jnp.sum(jnp.where(masks[head], part, 0.0), axis=1, keepdims=True)
                deltas = jnp.where(lane == 2 * index + head, total, deltas)
        delta[...] = deltas
        stats[own, 0:stat_rows] = jnp.transpose(lse_ref[...])[0:stat_rows]
        stats[own, stat_rows:] = jnp.transpose(deltas)[0:stat_rows]
        gather = Gather([out_grads, stats], size, gather_send, gather_recv)
        gather.forward(0)

        chosen_out = second * direct
        for k in range(2):
            weight = jnp.sum(jnp.where(lane == route[k], probs, 0.0), axis=1, keepdims=True)
            chosen_out = chosen_out + weight * dot(picked[k], output_ref[...])
        for gate, mixing, vector, vector_dot in constants:
            chosen_out = chosen_out + gate * mixing[1] * vector
        result_ref[...] = (middle + chosen_out).astype(low)
        small_ref[...] = jnp.zeros_like(small_ref)
        small_ref[1:2, :] = jnp.sum(second_grad * unit_second, axis=0, keepdims=True)
        for index, (gate, mixing, vector, vector_dot) in enumerate(constants):
            small_ref[2 + index : 3 + index, :] = jnp.sum(
                gate * mixing[1] * upstream, axis=0, keepdims=True
            )
        small_ref[8:24, :] = dot_tn(head_low, second_low)[0:16]
        carry_grad = lax.dot_general(
            jnp.transpose(logit_grad), previous_ref[...], (((1,), (0,)), ((), ())), precision=HIGH
        )
        small_ref[24:40, 0:experts] = carry_grad[0:16]
        wide_ref[3] = dot_tn(attended_ref[...].astype(low), middle_low).astype(low)

        for load in loads[1:4]:
            load.wait()
        query_total[...] = jnp.zeros_like(query_total)
        key_total[...] = jnp.zeros_like(key_total)
        value_total[...] = jnp.zeros_like(value_total)
        column = lax.broadcasted_iota(jnp.int32, (rows, rows), 0)
        row = lax.broadcasted_iota(jnp.int32, (rows, rows), 1)

        def key_side(block, diagonal):
            key_pos, query_pos = own * rows + column, block * rows + row
            first = start_of(query_pos[0:8], starts_ref)[0:1]
            allowed = jnp.logical_and(key_pos >= first, key_pos <= query_pos)
            bias[...] = jnp.where(allowed, 0.0, NEGATIVE)

            def pair(index, carried):
                lanes = pl.ds(pl.multiple_of(index * 128, 128), 128)
                query, key, value = queries[block, :, lanes], keys[own, :, lanes], values[own, :, lanes]
                grad = out_grads[block, :, lanes]
                key_sum, value_sum = key_total[:, lanes], value_total[:, lanes]
                if diagonal:
                    query_sum = query_total[:, lanes]
                for head in range(2):
                    lse = stats[block, pl.ds(2 * index + head, 1), :]
                    mean = stats[block, pl.ds(stat_rows + 2 * index + head, 1), :]
                    own_key = jnp.where(masks[head], key, 0)
                    weight = jnp.exp(dot_nt(own_key, query) + bias[...] - lse)
                    weight_grad = dot_nt(jnp.where(masks[head], value, 0), grad)
                    score = (weight * (weight_grad - mean)).astype(low)
                    value_sum = value_sum + dot(weight.astype(low), jnp.where(masks[head], grad, 0))
                    key_sum = key_sum + dot(score, jnp.where(masks[head], query, 0))
                    if diagonal:
                        query_sum = query_sum + dot_tn(score, own_key)
                key_total[:, lanes] = key_sum
                value_total[:, lanes] = value_sum
                if diagonal:
                    query_total[:, lanes] = query_sum
                return carried

            lax.fori_loop(0, pairs, pair, 0)

        def query_side(block):
            key_pos, query_pos = block * rows + row, own * rows + column
            first = start_of(query_pos[:, 0:128], starts_ref)[:, 0:1]
            allowed = jnp.logical_and(key_pos >= first, key_pos <= query_pos)
            bias[...] = jnp.where(allowed, 0.0, NEGATIVE)

            def pair(index, carried):
                lanes = pl.ds(pl.multiple_of(index * 128, 128), 128)
                query, key, value = queries[own, :, lanes], keys[block, :, lanes], values[block, :, lanes]
                grad = out_grads[own, :, lanes]
                query_sum = query_total[:, lanes]
                for head in range(2):
                    here = lane == 2 * index + head
                    lse = jnp.sum(jnp.where(here, lse_ref[...], 0.0), axis=1, keepdims=True)
                    mean = jnp.sum(jnp.where(here, delta[...], 0.0), axis=1, keepdims=True)
                    other_key = jnp.where(masks[head], key, 0)
                    weight = jnp.exp(dot_nt(query, other_key) + bias[...] - lse)
                    weight_grad = dot_nt(grad, jnp.where(masks[head], value, 0))
                    score = (weight * (weight_grad - mean)).astype(low)
                    query_sum = query_sum + dot(score, other_key)
                query_total[:, lanes] = query_sum
                return carried

            lax.fori_loop(0, pairs, pair, 0)

        key_side(own, True)
        for place in range(1, size):
            block = jnp.bitwise_xor(own, place)

            @pl.when(block < own)
            def _():
                query_side(block)

        for place in range(1, size):
            gather.arrive(place)
            block = jnp.bitwise_xor(own, place)

            @pl.when(block > own)
            def _():
                key_side(block, False)

        for load in loads[4:]:
            load.wait()
        inputs = tokens_ref[...].astype(full)
        inverse_first = inverse_norm(inputs)
        unit_first = inputs * inverse_first
        gain_first = first_ref[...].astype(full)
        normed = (unit_first * gain_first).astype(low)
        turn = -sine[...]
        query_low = rotate(query_total[...] * HEAD_DIM**-0.5, cosine[...], turn).astype(low)
        key_low = rotate(key_total[...], cosine[...], turn).astype(low)
        value_low = value_total[...].astype(low)
        first_grad = (
            dot_nt(query_low, query_w[...])
            + dot_nt(key_low, key_w[...])
            + dot_nt(value_low, value_w[...])
        )
        for index, part in enumerate((query_low, key_low, value_low)):
            wide_ref[index] = dot_tn(normed, part).astype(low)
        small_ref[0:1, :] = jnp.sum(first_grad * unit_first, axis=0, keepdims=True)
        normal_grad = first_grad * gain_first
        token_grads_ref[...] = middle_grad[...] + inverse_first * (
            normal_grad - unit_first * jnp.mean(normal_grad * unit_first, axis=1, keepdims=True)
        )
        gather.finish()

    stream_shape = (size, rows, width)
    any_space = pl.BlockSpec(memory_space=pl.ANY)
    in_vmem = pl.BlockSpec(memory_space=pltpu.VMEM)
    square = (width, width)
    return pl.pallas_call(
        kernel,
        out_shape=[
            jax.ShapeDtypeStruct((rows, width), low),
            jax.ShapeDtypeStruct((rows, width), full),
            jax.ShapeDtypeStruct((4,) + square, low),
            jax.ShapeDtypeStruct((40, width), full),
        ],
        in_specs=[in_vmem] * 4
        + [pl.BlockSpec(memory_space=pltpu.SMEM)]
        + [in_vmem] * 5
        + [any_space] * 3
        + [in_vmem] * 3
        + [any_space] * 4
        + [in_vmem] * 4
        + [any_space] * 2,
        out_specs=[in_vmem] * 4,
        scratch_shapes=[
            pltpu.VMEM(stream_shape, low),
            pltpu.VMEM(stream_shape, low),
            pltpu.VMEM(stream_shape, low),
            pltpu.VMEM(square, low),
            pltpu.VMEM(square, low),
            pltpu.VMEM(square, low),
            pltpu.VMEM(square, low),
            pltpu.VMEM((rows, 128), full),
            pltpu.VMEM((rows, 128), full),
            pltpu.VMEM((rows, rows), full),
            pltpu.VMEM(stream_shape, low),
            pltpu.VMEM((size, 2 * stat_rows, rows), full),
            pltpu.VMEM((rows, 128), full),
            pltpu.VMEM((rows, width), full),
            pltpu.VMEM((rows, width), full),
            pltpu.VMEM((rows, width), full),
            pltpu.VMEM((rows, width), full),
            pltpu.SemaphoreType.DMA((9,)),
            pltpu.SemaphoreType.DMA((2, size)),
            pltpu.SemaphoreType.DMA((2, size)),
        ],
        compiler_params=pltpu.CompilerParams(
            collective_id=2, has_side_effects=True, vmem_limit_bytes=60 * 2**20
        ),
        cost_estimate=pl.CostEstimate(
            flops=14 * rows * width * width * 2 + 20 * size * rows * rows * width,
            bytes_accessed=30 * 2**20,
            transcendentals=size * rows * rows * 12,
        ),
        name="backward",
    )(
        tokens,
        cotangent,
        previous,
        routes,
        starts,
        *forward,
        *returns,
        *weights,
        *norms,
        heads,
        vectors,
        jnp.asarray(tables[0]),
        jnp.asarray(tables[1]),
    )


def local(
    tokens,
    cotangent,
    previous,
    routes,
    boundaries,
    norm_first,
    query_weight,
    key_weight,
    value_weight,
    output_weight,
    norm_second,
    router,
    gate_carry,
    constant_map,
    constant_vector,
    expert_gate,
    expert_linear,
    expert_down,
):
    model_width = tokens.shape[2]
    ring = lax.axis_size("ctx")
    group_size = expert_gate.shape[0]
    exchange_count = lax.axis_size("exp")
    spread = ring // group_size
    ranks = (exchange_count, group_size, spread)
    slot_total = exchange_count * group_size * CAP
    expert_total = router.shape[1]
    heads = jnp.concatenate([router, constant_map[0], constant_map[1]], axis=1)
    head_count = heads.shape[1]
    heads = jnp.pad(heads, ((0, 0), (0, 128 - head_count)))
    norms = (norm_first[None], norm_second[None])
    weights = (query_weight, key_weight, value_weight, output_weight)
    (
        queries,
        keys,
        values,
        attended,
        lse,
        middle,
        probs,
        targets,
        outgoing,
        slot_gates,
        grads_in,
    ) = attend_layer(
        tokens[0],
        cotangent[0],
        previous[0],
        routes[0].T,
        boundaries,
        weights,
        norms,
        heads,
        gate_carry,
        ranks,
        CAP,
        ring,
    )
    home_grads, returned, dots, gate_terms, linear_terms, down_terms = expert_layer(
        outgoing,
        slot_gates,
        grads_in.reshape(slot_total, model_width),
        (expert_gate, expert_linear, expert_down),
        ranks,
        lax.axis_size("dp"),
    )
    result, token_grads, wide, small = backward_layer(
        tokens[0],
        cotangent[0],
        previous[0],
        routes[0],
        boundaries,
        (attended, lse, middle, probs, targets, queries, keys, values),
        (
            home_grads.reshape(slot_total, model_width),
            returned.reshape(slot_total, model_width),
            dots,
        ),
        weights,
        norms,
        heads,
        constant_vector,
        ranks,
        CAP,
        ring,
    )
    own_expert = lax.axis_index("ctx") // spread

    def collect(terms):
        share = scatter_sum(terms, "dp")
        bit = 1
        while bit < spread:
            share = (
                share.astype(jnp.float32) + swap(share, "ctx", bit).astype(jnp.float32)
            ).astype(jnp.bfloat16)
            bit *= 2
        parts, order = [share], [0]
        while bit < lax.axis_size("ctx"):
            bit *= 2
        while bit > spread:
            bit //= 2
            parts = parts + [swap(part, "ctx", bit) for part in parts]
            order = order + [place ^ (bit // spread) for place in order]
        stacked = jnp.stack(parts)
        places = jnp.array(order, jnp.int32) ^ own_expert
        inverse = jnp.argsort(places)
        return stacked[inverse].astype(jnp.float32)

    experts = (collect(gate_terms), collect(linear_terms), collect(down_terms))
    steps = [(axis, bit) for axis in ("ctx", "exp", "dp") for bit in bits_of(axis)]
    units = 2 ** len(steps)
    wide = wide.reshape(4 * model_width, model_width)
    flat = small.reshape(-1)
    small_rows = -(-flat.size // (units * model_width))
    wide_rows = wide.shape[0] // units
    unit_rows = -(-(small_rows + wide_rows) // 16) * 16
    flat = jnp.pad(flat, (0, units * small_rows * model_width - flat.size))
    packed = jnp.concatenate(
        [
            wide.reshape(units, wide_rows, model_width).astype(jnp.bfloat16),
            flat.reshape(units, small_rows, model_width).astype(jnp.bfloat16),
            jnp.zeros((units, unit_rows - wide_rows - small_rows, model_width), jnp.bfloat16),
        ],
        axis=1,
    )
    for axis, bit in steps:
        packed = packed.reshape((2, -1) + packed.shape[1:])
        packed = halve(packed, axis, bit, 0)
    for axis, bit in steps[::-1]:
        other = swap(packed, axis, bit)
        own = (lax.axis_index(axis) // bit) % 2
        packed = jnp.concatenate(
            [jnp.where(own == 0, packed, other), jnp.where(own == 0, other, packed)], axis=0
        )
    packed = packed.astype(jnp.float32)
    wide = packed[:, :wide_rows].reshape(4, model_width, model_width)
    flat = packed[:, wide_rows : wide_rows + small_rows].reshape(-1)
    small = flat[: small.size].reshape(small.shape)
    head_grads = small[8 : 8 + head_count].T
    return (
        result[None],
        token_grads[None],
        small[0],
        wide[0],
        wide[1],
        wide[2],
        wide[3],
        small[1],
        head_grads[:, :expert_total],
        small[24 : 24 + expert_total, :expert_total].T,
        jnp.stack(
            [head_grads[:, expert_total : expert_total + 2], head_grads[:, expert_total + 2 :]]
        ),
        small[2:4],
        experts[0],
        experts[1],
        experts[2],
    )


def solution(mesh):
    return jax.shard_map(
        local,
        mesh=mesh,
        in_specs=(
            P(("dp", "exp"), "ctx", None),
            P(("dp", "exp"), "ctx", None),
            P(("dp", "exp"), "ctx", None),
            P(("dp", "exp"), "ctx", None),
            P(("dp", "exp"), None),
            P(),
            P(),
            P(),
            P(),
            P(),
            P(),
            P(),
            P(),
            P(),
            P(),
            P("exp", None, None),
            P("exp", None, None),
            P("exp", None, None),
        ),
        out_specs=(
            P(("dp", "exp"), "ctx", None),
            P(("dp", "exp"), "ctx", None),
            P(),
            P(),
            P(),
            P(),
            P(),
            P(),
            P(),
            P(),
            P(),
            P(),
            P("exp", None, "dp"),
            P("exp", None, "dp"),
            P("exp", "dp", None),
        ),
        check_vma=False,
    )
```

```python
import math

import jax
import jax.numpy as jnp
import numpy as np
from jax import lax
from jax.experimental import pallas as pl
from jax.experimental.pallas import tpu as pltpu
from jax.sharding import PartitionSpec as P

HEAD_DIM = 64
CAP = 96


EPSILON = 1e-06
NEGATIVE = -1e30
HIGH = lax.Precision.HIGHEST


HEAD_ROWS = 16


def mesh_id(exp_index, ctx_index):
    return {"exp": exp_index, "ctx": ctx_index}


def dot(left, right):
    return jnp.dot(left, right, preferred_element_type=jnp.float32)


def dot_nt(left, right):
    return lax.dot_general(
        left, right, (((1,), (1,)), ((), ())), preferred_element_type=jnp.float32
    )


def dot_tn(left, right):
    return lax.dot_general(
        left, right, (((0,), (0,)), ((), ())), preferred_element_type=jnp.float32
    )


def member_of(shift, ranks):
    exchange_size, group_size, spread = ranks
    exp_index, ctx_index = lax.axis_index("exp"), lax.axis_index("ctx")
    far, near = shift // group_size, shift % group_size
    place = jnp.bitwise_xor(ctx_index // spread, near) * spread + lax.rem(ctx_index, spread)
    return mesh_id(jnp.bitwise_xor(exp_index, far), place)


def greet(count, ranks):
    barrier = pltpu.get_barrier_semaphore()
    for shift in range(1, count):
        pl.semaphore_signal(
            barrier, inc=1, device_id=member_of(shift, ranks), device_id_type=pl.DeviceIdType.MESH
        )
    pl.semaphore_wait(barrier, count - 1)


def send_block(source, target, shift, ranks, send_sem, recv_sem):
    return pltpu.make_async_remote_copy(
        src_ref=source.at[shift],
        dst_ref=target.at[shift],
        send_sem=send_sem.at[shift],
        recv_sem=recv_sem.at[shift],
        device_id=member_of(shift, ranks),
        device_id_type=pl.DeviceIdType.MESH,
    )


def expert_layer(outgoing, gates, grads, weights, ranks, shares):
    count, cap, width = outgoing.shape
    hidden_units = weights[0].shape[2]
    rows = count * cap
    share = hidden_units // shares
    spread = ranks[2]

    def kernel(
        outgoing_hbm,
        gates_ref,
        grads_ref,
        gate_hbm,
        linear_hbm,
        down_hbm,
        back_ref,
        output_ref,
        dots_ref,
        gate_terms,
        linear_terms,
        down_terms,
        received,
        received_gates,
        gate_w,
        linear_w,
        down_w,
        hidden_grad,
        hidden,
        gate_low,
        linear_low,
        rows_t,
        scaled,
        gate_column,
        out_total,
        in_total,
        in_send,
        dots_send,
        terms,
        weight_sem,
        send_sem,
        recv_sem,
        local_sem,
        terms_sem,
    ):
        own = lax.axis_index("ctx") // spread
        loads = [
            pltpu.make_async_copy(source.at[own], target, weight_sem.at[index])
            for index, (source, target) in enumerate(
                ((down_hbm, down_w), (gate_hbm, gate_w), (linear_hbm, linear_w))
            )
        ]
        for load in loads:
            load.start()
        greet(count, ranks)

        def send_some(source, target, index, shifts):
            copies = []
            for shift in shifts:
                if shift:
                    copies.append(
                        send_block(
                            source, target, shift, ranks, send_sem.at[index], recv_sem.at[index]
                        )
                    )
                else:
                    copies.append(
                        pltpu.make_async_copy(source.at[0], target.at[0], local_sem.at[index])
                    )
            for copy in copies:
                copy.start()
            return copies

        every = range(count)
        gates_in = send_some(gates_ref, received_gates, 0, every)
        incoming = send_some(outgoing_hbm, received, 1, every)
        loads[0].wait()

        def backward_in(index, carry):
            part = pl.ds(pl.multiple_of(index * share, share), share)
            hidden_grad[:, part] = dot_nt(grads_ref[...], down_w[part, :])
            return carry

        lax.fori_loop(0, shares, backward_in, 0)
        for copy in gates_in:
            copy.wait()
        for shift in every:
            column = jnp.transpose(received_gates[shift])[:cap, 0:1]
            block = pl.ds(shift * cap, cap)
            gate_column[block, :] = jnp.broadcast_to(column, (cap, 128))
            scaled[block, :] = (column * grads_ref[block, :].astype(jnp.float32)).astype(
                jnp.bfloat16
            )
        for load in loads[1:]:
            load.wait()

        going = []
        batches = 2
        members = count // batches
        lines = rows // batches
        for batch in range(batches):
            chunks = range(batch * members, (batch + 1) * members)
            for shift in chunks:
                incoming[shift].wait()
            block = pl.ds(batch * lines, lines)

            def through(index, carry):
                part = pl.ds(pl.multiple_of(index * share, share), share)
                tokens = received[batch * members : (batch + 1) * members].reshape(lines, width)
                gate_part = dot(tokens, gate_w[:, part])
                linear_part = dot(tokens, linear_w[:, part])
                sigmoid = 1.0 / (1.0 + jnp.exp(-gate_part))
                silu = gate_part * sigmoid
                low = (silu * linear_part).astype(jnp.bfloat16)
                hidden[block, part] = low
                upper = hidden_grad[block, part] * gate_column[block, 0:1]
                low_gate = (
                    upper * linear_part * sigmoid * (1.0 + gate_part * (1.0 - sigmoid))
                ).astype(jnp.bfloat16)
                gate_low[block, part] = low_gate
                low_linear = (upper * silu).astype(jnp.bfloat16)
                linear_low[block, part] = low_linear
                out = dot(low, down_w[part, :])
                back = dot_nt(low_gate, gate_w[:, part]) + dot_nt(low_linear, linear_w[:, part])

                @pl.when(index == 0)
                def _():
                    out_total[block, :] = out
                    in_total[block, :] = back

                @pl.when(index > 0)
                def _():
                    out_total[block, :] += out
                    in_total[block, :] += back

                return carry

            lax.fori_loop(0, shares, through, 0)
            in_send[batch * members : (batch + 1) * members] = (
                in_total[block, :].astype(jnp.bfloat16).reshape(members, cap, width)
            )
            going += send_some(in_send, back_ref, 2, chunks)
            low = out_total[block, :].astype(jnp.bfloat16)
            output_ref[batch * members : (batch + 1) * members] = low.reshape(members, cap, width)
            dots = jnp.sum(
                low.astype(jnp.float32) * grads_ref[block, :].astype(jnp.float32),
                axis=1,
                keepdims=True,
            )
            for place, shift in enumerate(chunks):
                column = jnp.broadcast_to(dots[place * cap : (place + 1) * cap], (cap, 128))
                dots_send[shift, :, 0:cap] = jnp.transpose(column)[0:8, :]
                dots_send[shift, :, cap:] = jnp.zeros((8, 128 - cap), jnp.float32)
            going += send_some(dots_send, dots_ref, 3, chunks)
            rows_t[:, batch * lines : (batch + 1) * lines] = jnp.transpose(
                received[batch * members : (batch + 1) * members].reshape(lines, width)
            )

        def term_copy(which, index):
            target = (down_terms, gate_terms, linear_terms)[which]
            return pltpu.make_async_copy(
                terms[which].at[index], target.at[index], terms_sem.at[which, index]
            )

        def weigh(index, carry):
            part = pl.ds(pl.multiple_of(index * share, share), share)
            terms[0][index] = dot_tn(hidden[:, part], scaled[...]).astype(jnp.bfloat16)
            term_copy(0, index).start()
            terms[1][index] = dot(rows_t[...], gate_low[:, part]).astype(jnp.bfloat16)
            term_copy(1, index).start()
            terms[2][index] = dot(rows_t[...], linear_low[:, part]).astype(jnp.bfloat16)
            term_copy(2, index).start()
            return carry

        lax.fori_loop(0, shares, weigh, 0)
        for which in range(3):
            for index in range(shares):
                term_copy(which, index).wait()
        for copy in going:
            copy.wait()

    low, full = jnp.bfloat16, jnp.float32
    columns, lines = (shares, width, share), (shares, share, width)
    any_space = pl.BlockSpec(memory_space=pl.ANY)
    in_vmem = pl.BlockSpec(memory_space=pltpu.VMEM)
    return pl.pallas_call(
        kernel,
        out_shape=[
            jax.ShapeDtypeStruct(outgoing.shape, low),
            jax.ShapeDtypeStruct(outgoing.shape, low),
            jax.ShapeDtypeStruct(gates.shape, full),
            jax.ShapeDtypeStruct(columns, low),
            jax.ShapeDtypeStruct(columns, low),
            jax.ShapeDtypeStruct(lines, low),
        ],
        in_specs=[any_space, in_vmem, in_vmem, any_space, any_space, any_space],
        out_specs=[any_space, in_vmem] + [any_space] * 4,
        scratch_shapes=[
            pltpu.VMEM(outgoing.shape, low),
            pltpu.VMEM(gates.shape, full),
            pltpu.VMEM((width, hidden_units), low),
            pltpu.VMEM((width, hidden_units), low),
            pltpu.VMEM((hidden_units, width), low),
            pltpu.VMEM((rows, hidden_units), full),
            pltpu.VMEM((rows, hidden_units), low),
            pltpu.VMEM((rows, hidden_units), low),
            pltpu.VMEM((rows, hidden_units), low),
            pltpu.VMEM((width, rows), low),
            pltpu.VMEM((rows, width), low),
            pltpu.VMEM((rows, 128), full),
            pltpu.VMEM((rows, width), full),
            pltpu.VMEM((rows, width), full),
            pltpu.VMEM(outgoing.shape, low),
            pltpu.VMEM(gates.shape, full),
            [pltpu.VMEM(lines, low), pltpu.VMEM(columns, low), pltpu.VMEM(columns, low)],
            pltpu.SemaphoreType.DMA((3,)),
            pltpu.SemaphoreType.DMA((4, count)),
            pltpu.SemaphoreType.DMA((4, count)),
            pltpu.SemaphoreType.DMA((4,)),
            pltpu.SemaphoreType.DMA((3, shares)),
        ],
        compiler_params=pltpu.CompilerParams(
            collective_id=1, has_side_effects=True, vmem_limit_bytes=60 * 2**20
        ),
        cost_estimate=pl.CostEstimate(
            flops=18 * rows * width * hidden_units,
            bytes_accessed=12 * width * hidden_units + 12 * rows * width,
            transcendentals=rows * hidden_units,
        ),
        name="experts",
    )(outgoing, gates, grads, *weights)


def rope_tables(row_count):
    half = HEAD_DIM // 2
    frequency = np.exp(
        np.arange(half, dtype=np.float32) * np.float32(-2.0 * math.log(10000.0) / HEAD_DIM)
    ).astype(np.float32)
    angles = np.arange(row_count, dtype=np.float32)[:, None] * frequency[None, :]
    cosine, sine = np.cos(angles).astype(np.float32), np.sin(angles).astype(np.float32)
    return (
        np.concatenate([cosine] * 4, axis=1),
        np.concatenate([-sine, sine, -sine, sine], axis=1),
    )


def rotate(values, cosine, sine):
    lane = lax.broadcasted_iota(jnp.int32, cosine.shape, 1)
    leading = jnp.bitwise_and(lane, HEAD_DIM - 1) < HEAD_DIM // 2
    parts = []
    for begin in range(0, values.shape[1], 128):
        part = values[:, begin : begin + 128]
        ahead = pltpu.roll(part, 128 - HEAD_DIM // 2, 1)
        behind = pltpu.roll(part, HEAD_DIM // 2, 1)
        parts.append(part * cosine + jnp.where(leading, ahead, behind) * sine)
    return jnp.concatenate(parts, axis=1)


def inverse_norm(values):
    return lax.rsqrt(jnp.mean(values * values, axis=1, keepdims=True) + EPSILON)


def head_masks(rows):
    first = lax.broadcasted_iota(jnp.int32, (rows, 128), 1) < HEAD_DIM
    return first, jnp.logical_not(first)


def start_of(positions, starts):
    first = jnp.zeros_like(positions)
    for index in range(starts.shape[1]):
        begin = starts[0, index]
        first = jnp.where(begin <= positions, jnp.maximum(first, begin), first)
    return first


def gather_steps(size):
    bits, held, steps = [], [0], []
    bit = size // 2
    while bit >= 1:
        steps.append((bit, list(held)))
        held = held + [place ^ bit for place in held]
        bit //= 2
    return steps


def peer_at(deep, far, near):
    return {
        "dp": jnp.bitwise_xor(lax.axis_index("dp"), deep),
        "exp": jnp.bitwise_xor(lax.axis_index("exp"), far),
        "ctx": jnp.bitwise_xor(lax.axis_index("ctx"), near),
    }


def peer(far, near):
    return peer_at(0, far, near)


def greet_places(places):
    barrier = pltpu.get_barrier_semaphore()
    for place in places:
        pl.semaphore_signal(
            barrier, inc=1, device_id=peer_at(*place), device_id_type=pl.DeviceIdType.MESH
        )
    pl.semaphore_wait(barrier, len(places))


def greet_all(places):
    greet_places([(0,) + place for place in places])


def group_places(ranks):
    return [
        (shift // ranks[1], shift % ranks[1] * ranks[2]) for shift in range(1, ranks[0] * ranks[1])
    ]


def ring_places(size):
    return [(0, bit) for bit, _ in gather_steps(size)]


def places_of(ranks, size):
    places = group_places(ranks)
    return places + [place for place in ring_places(size) if place not in places]


class Gather:
    def __init__(self, buffers, size, send_sem, recv_sem, sources=None):
        self.buffers, self.sources = buffers, sources
        self.send_sem, self.recv_sem = send_sem, recv_sem
        self.steps = gather_steps(size)
        self.started = []

    def copy(self, place, bit, index):
        block = jnp.bitwise_xor(lax.axis_index("ctx"), place)
        buffer = self.buffers[index]
        straight = self.sources is not None and place == 0
        return pltpu.make_async_remote_copy(
            src_ref=self.sources[index] if straight else buffer.at[block],
            dst_ref=buffer.at[block],
            send_sem=self.send_sem.at[index, place ^ bit],
            recv_sem=self.recv_sem.at[index, place ^ bit],
            device_id=peer(0, bit),
            device_id_type=pl.DeviceIdType.MESH,
        )

    def forward(self, place):
        for bit, held in self.steps:
            if place in held:
                for index in range(len(self.buffers)):
                    copy = self.copy(place, bit, index)
                    copy.start()
                    self.started.append(copy)

    def arrive(self, place):
        bit = place & -place
        for index in range(len(self.buffers)):
            self.copy(place ^ bit, bit, index).wait_recv()
        self.forward(place)

    def finish(self):
        for copy in self.started:
            copy.wait_send()


def slot_targets(routes, ranks, cap):
    exchange_size, group_size, spread = ranks
    rows = routes.shape[1]
    experts = exchange_size * group_size
    expert = lax.broadcasted_iota(jnp.int32, (16, rows), 0)
    hits = [(expert == routes[k : k + 1]).astype(jnp.float32) for k in range(2)]
    before = lax.broadcasted_iota(jnp.int32, (rows, rows), 0) < lax.broadcasted_iota(
        jnp.int32, (rows, rows), 1
    )
    earlier = dot(
        (hits[0] + hits[1]).astype(jnp.bfloat16), before.astype(jnp.float32).astype(jnp.bfloat16)
    )
    targets = []
    for k in range(2):
        route = routes[k : k + 1]
        rank = jnp.sum(hits[k] * earlier, axis=0, keepdims=True)
        far = jnp.bitwise_xor(route // group_size, lax.axis_index("exp"))
        near = jnp.bitwise_xor(route % group_size, lax.axis_index("ctx") // spread)
        place = ((far * group_size + near) * cap).astype(jnp.float32)
        targets.append(jnp.where(route < experts, place + rank, -1.0))
    return targets


def attend_layer(
    tokens, cotangent, previous, routes, starts, weights, pack, carry, ranks, cap, size
):
    rows, width = tokens.shape
    count = ranks[0] * ranks[1]
    slots = count * cap
    pairs = width // 128
    tables = rope_tables(size * rows)
    low, full = jnp.bfloat16, jnp.float32

    def kernel(
        tokens_hbm,
        cotangent_ref,
        previous_ref,
        routes_ref,
        starts_ref,
        query_hbm,
        key_hbm,
        value_hbm,
        output_hbm,
        pack_ref,
        carry_ref,
        cosine_hbm,
        sine_hbm,
        queries_out,
        keys_out,
        values_out,
        attended_ref,
        lse_ref,
        middle_ref,
        probs_ref,
        targets_ref,
        outgoing_ref,
        gates_ref,
        grads_ref,
        stream,
        queries,
        keys,
        values,
        query_w,
        key_w,
        value_w,
        output_w,
        cosine,
        sine,
        bias,
        totals,
        highest,
        slot_grads,
        load_sem,
        gather_send,
        gather_recv,
        grad_send,
        grad_recv,
        keep_sem,
    ):
        own = lax.axis_index("ctx")
        bring = pltpu.make_async_copy(tokens_hbm, stream.at[own], load_sem.at[6])
        bring.start()
        loads = [
            pltpu.make_async_copy(source, target, load_sem.at[index])
            for index, (source, target) in enumerate(
                (
                    (query_hbm, query_w),
                    (key_hbm, key_w),
                    (value_hbm, value_w),
                    (cosine_hbm, cosine),
                    (sine_hbm, sine),
                    (output_hbm, output_w),
                )
            )
        ]
        for load in loads:
            load.start()
        greet_all(places_of(ranks, size))
        gather = Gather([stream], size, gather_send, gather_recv, [tokens_hbm])
        gather.forward(0)

        targets = slot_targets(routes_ref[...], ranks, cap)
        slot = lax.broadcasted_iota(jnp.int32, (slots, rows), 0).astype(full)
        picked = jnp.logical_or(slot == targets[0], slot == targets[1])
        picked = picked.astype(full).astype(low)
        slot_grads[...] = dot(picked, cotangent_ref[...]).astype(low).reshape(count, cap, width)
        grad_copies = [
            send_block(slot_grads, grads_ref, shift, ranks, grad_send, grad_recv)
            for shift in range(1, count)
        ]
        grad_copies.append(pltpu.make_async_copy(slot_grads.at[0], grads_ref.at[0], keep_sem.at[0]))

        bring.wait()
        for load in loads[:5]:
            load.wait()
        gain = pack_ref[HEAD_ROWS : HEAD_ROWS + 1, :].astype(full)

        def project(block, wanted):
            line = pl.ds(pl.multiple_of(block * rows, rows), rows)
            values_in = stream[block].astype(full)
            normed = (values_in * inverse_norm(values_in) * gain).astype(low)
            if "q" in wanted:
                turned = rotate(dot(normed, query_w[...]), cosine[line, :], sine[line, :])
                queries[block] = (turned.astype(low).astype(full) * HEAD_DIM**-0.5).astype(low)
            if "k" in wanted:
                turned = rotate(dot(normed, key_w[...]), cosine[line, :], sine[line, :])
                keys[block] = turned.astype(low)
                values[block] = dot(normed, value_w[...]).astype(low)

        masks = head_masks(rows)
        query_pos = own * rows + lax.broadcasted_iota(jnp.int32, (rows, rows), 1)
        document_start = start_of(query_pos[0:8], starts_ref)[0:1]

        def attend(block):
            key_pos = block * rows + lax.broadcasted_iota(jnp.int32, (rows, rows), 0)
            allowed = jnp.logical_and(key_pos >= document_start, key_pos <= query_pos)
            bias[...] = jnp.where(allowed, 0.0, NEGATIVE)

            def pair(index, carried):
                lanes = pl.ds(pl.multiple_of(index * 128, 128), 128)
                query, key, value = queries[own, :, lanes], keys[block, :, lanes], values[block, :, lanes]
                scores = [dot_nt(jnp.where(mask, key, 0), query) + bias[...] for mask in masks]
                old = [highest[index, head][0:1, :] for head in range(2)]
                new = [
                    jnp.maximum(old[head], jnp.max(scores[head], axis=0, keepdims=True))
                    for head in range(2)
                ]
                weight = [jnp.exp(scores[head] - new[head]).astype(low) for head in range(2)]
                for head in range(2):
                    totals[index, head] = totals[index, head] * jnp.exp(old[head] - new[head]) + dot_tn(
                        jnp.where(masks[head], value, 1), weight[head]
                    )
                    highest[index, head] = jnp.broadcast_to(new[head], (8, rows))
                return carried

            lax.fori_loop(0, pairs, pair, 0)

        totals[...] = jnp.zeros_like(totals)
        highest[...] = jnp.full(highest.shape, NEGATIVE, full)
        project(own, "qk")
        attend(own)
        for place in range(1, size):
            gather.arrive(place)
            if place == size // 2:
                for copy in grad_copies:
                    copy.start()
            block = jnp.bitwise_xor(own, place)

            @pl.when(block < own)
            def _():
                project(block, "k")
                attend(block)

            @pl.when(block > own)
            def _():
                project(block, "q")

        keep = [
            pltpu.make_async_copy(source, target, keep_sem.at[index + 1])
            for index, (source, target) in enumerate(
                ((queries, queries_out), (keys, keys_out), (values, values_out))
            )
        ]
        for copy in keep:
            copy.start()

        lse_ref[...] = jnp.zeros_like(lse_ref)
        upper = lax.broadcasted_iota(jnp.int32, (128, rows), 0) < HEAD_DIM
        for index in range(pairs):
            halves = []
            for head in range(2):
                total = totals[index, head]
                line = HEAD_DIM if head == 0 else 0
                weight_sum = total[line : line + 1, :]
                halves.append(total / weight_sum)
                lse_ref[2 * index + head : 2 * index + head + 1, :] = highest[index, head][
                    0:1, :
                ] + jnp.log(weight_sum)
            attended_ref[:, index * 128 : index * 128 + 128] = jnp.transpose(
                jnp.where(upper, halves[0], halves[1])
            )
        loads[5].wait()
        middle = stream[own].astype(full) + dot(attended_ref[...].astype(low), output_w[...])
        middle_ref[...] = middle
        second = (
            middle
            * inverse_norm(middle)
            * pack_ref[HEAD_ROWS + 1 : HEAD_ROWS + 2, :].astype(full)
        )
        second_low = second.astype(low)
        outgoing_ref[...] = dot(picked, second_low).astype(low).reshape(count, cap, width)

        experts = previous_ref.shape[0]
        logits = dot_nt(second_low, pack_ref[0:HEAD_ROWS, :])[:, 0:experts] + lax.dot_general(
            previous_ref[...],
            carry_ref[...].astype(full),
            (((0,), (0,)), ((), ())),
            precision=HIGH,
        )
        logits = logits - jnp.max(logits, axis=1, keepdims=True)
        powers = jnp.exp(logits)
        probs_ref[...] = jnp.zeros_like(probs_ref)
        probs_ref[:, 0:experts] = powers / jnp.sum(powers, axis=1, keepdims=True)
        turned = jnp.transpose(probs_ref[...])[0:16]
        expert = lax.broadcasted_iota(jnp.int32, (16, rows), 0)
        weighted = jnp.zeros((slots, rows), full)
        for k in range(2):
            route = routes_ref[k : k + 1, :]
            gate = jnp.sum(jnp.where(expert == route, turned, 0.0), axis=0, keepdims=True)
            weighted = jnp.where(slot == targets[k], gate, weighted)
        gate_column = jnp.sum(weighted, axis=1, keepdims=True)
        for shift in range(count):
            column = jnp.broadcast_to(gate_column[shift * cap : (shift + 1) * cap], (cap, 128))
            gates_ref[shift] = jnp.zeros((8, 128), full)
            gates_ref[shift, :, 0:cap] = jnp.transpose(column)[0:8, :]
        pad = jnp.zeros((6, rows), full)
        target_rows = jnp.concatenate([targets[0], targets[1], pad], axis=0)
        target_rows = jnp.concatenate([target_rows] + [jnp.zeros((120, rows), full)], axis=0)
        targets_ref[...] = jnp.transpose(target_rows)

        gather.finish()
        for copy in keep + grad_copies:
            copy.wait()

    stream_shape = (size, rows, width)
    any_space = pl.BlockSpec(memory_space=pl.ANY)
    in_vmem = pl.BlockSpec(memory_space=pltpu.VMEM)
    square = (width, width)
    return pl.pallas_call(
        kernel,
        out_shape=[
            jax.ShapeDtypeStruct(stream_shape, low),
            jax.ShapeDtypeStruct(stream_shape, low),
            jax.ShapeDtypeStruct(stream_shape, low),
            jax.ShapeDtypeStruct((rows, width), full),
            jax.ShapeDtypeStruct((16, rows), full),
            jax.ShapeDtypeStruct((rows, width), full),
            jax.ShapeDtypeStruct((rows, 128), full),
            jax.ShapeDtypeStruct((rows, 128), full),
            jax.ShapeDtypeStruct((count, cap, width), low),
            jax.ShapeDtypeStruct((count, 8, 128), full),
            jax.ShapeDtypeStruct((count, cap, width), low),
        ],
        in_specs=[any_space]
        + [in_vmem] * 3
        + [pl.BlockSpec(memory_space=pltpu.SMEM)]
        + [any_space] * 4
        + [in_vmem] * 2
        + [any_space] * 2,
        out_specs=[any_space] * 3 + [in_vmem] * 7 + [any_space],
        scratch_shapes=[
            pltpu.VMEM(stream_shape, low),
            pltpu.VMEM(stream_shape, low),
            pltpu.VMEM(stream_shape, low),
            pltpu.VMEM(stream_shape, low),
            pltpu.VMEM(square, low),
            pltpu.VMEM(square, low),
            pltpu.VMEM(square, low),
            pltpu.VMEM(square, low),
            pltpu.VMEM((size * rows, 128), full),
            pltpu.VMEM((size * rows, 128), full),
            pltpu.VMEM((rows, rows), full),
            pltpu.VMEM((pairs, 2, 128, rows), full),
            pltpu.VMEM((pairs, 2, 8, rows), full),
            pltpu.VMEM((count, cap, width), low),
            pltpu.SemaphoreType.DMA((7,)),
            pltpu.SemaphoreType.DMA((1, size)),
            pltpu.SemaphoreType.DMA((1, size)),
            pltpu.SemaphoreType.DMA((count,)),
            pltpu.SemaphoreType.DMA((count,)),
            pltpu.SemaphoreType.DMA((4,)),
        ],
        compiler_params=pltpu.CompilerParams(
            collective_id=0, has_side_effects=True, vmem_limit_bytes=60 * 2**20
        ),
        cost_estimate=pl.CostEstimate(
            flops=2 * size * rows * width * width * 3 + 16 * size * rows * rows * width,
            bytes_accessed=20 * 2**20,
            transcendentals=size * rows * rows * 12,
        ),
        name="attend",
    )(
        tokens,
        cotangent,
        previous,
        routes,
        starts,
        *weights,
        pack,
        carry,
        jnp.asarray(tables[0]),
        jnp.asarray(tables[1]),
    )


def column_of(values, index):
    return values[:, index : index + 1]


def backward_layer(
    tokens,
    cotangent,
    previous,
    routes,
    starts,
    forward,
    returns,
    weights,
    pack,
    terms,
    ranks,
    cap,
    size,
    shares,
):
    rows, width = tokens.shape
    count = ranks[0] * ranks[1]
    slots = count * cap
    pairs = width // 128
    tables = rope_tables(size * rows)
    low, full = jnp.bfloat16, jnp.float32
    experts = previous.shape[0]
    copy_index = count + 1
    stat_rows = 16
    kinds = len(terms)

    def kernel(
        tokens_ref,
        cotangent_ref,
        previous_ref,
        routes_ref,
        starts_ref,
        attended_ref,
        lse_ref,
        middle_ref,
        probs_ref,
        targets_ref,
        queries_hbm,
        keys_hbm,
        values_hbm,
        back_ref,
        produced_hbm,
        dots_ref,
        query_hbm,
        key_hbm,
        value_hbm,
        output_hbm,
        pack_ref,
        cosine_hbm,
        sine_hbm,
        *rest,
    ):
        term_refs, rest = rest[:kinds], rest[kinds:]
        result_ref, token_grads_ref, wide_ref, small_ref = rest[:4]
        first_refs, rest = rest[4 : 4 + kinds], rest[4 + kinds :]
        (
            queries,
            keys,
            values,
            query_w,
            key_w,
            value_w,
            output_w,
            cosine,
            sine,
            bias,
            out_grads,
            stats,
            outputs,
            middle_grad,
            query_total,
            key_total,
            value_total,
            load_sem,
            gather_send,
            gather_recv,
            first_send,
            first_recv,
            out_send,
            out_recv,
            out_keep,
        ) = rest
        own = lax.axis_index("ctx")
        line = pl.ds(pl.multiple_of(own * rows, rows), rows)
        loads = [
            pltpu.make_async_copy(source, target, load_sem.at[index])
            for index, (source, target) in enumerate(
                (
                    (output_hbm, output_w),
                    (queries_hbm, queries),
                    (keys_hbm, keys),
                    (values_hbm, values),
                    (cosine_hbm.at[line], cosine),
                    (sine_hbm.at[line], sine),
                    (query_hbm, query_w),
                    (key_hbm, key_w),
                    (value_hbm, value_w),
                )
            )
        ]
        for load in loads:
            load.start()
        greet_places([(0,) + place for place in places_of(ranks, size)] + [(1, 0, 0)])
        first_copies = [
            pltpu.make_async_remote_copy(
                src_ref=term_refs[kind].at[jnp.bitwise_xor(lax.axis_index("dp"), shares - 1)],
                dst_ref=first_refs[kind],
                send_sem=first_send.at[kind],
                recv_sem=first_recv.at[kind],
                device_id=peer_at(1, 0, 0),
                device_id_type=pl.DeviceIdType.MESH,
            )
            for kind in range(kinds)
        ]
        for copy in first_copies:
            copy.start()

        output_copies = [
            send_block(produced_hbm, outputs, shift, ranks, out_send, out_recv)
            for shift in range(1, count)
        ]
        output_copies.append(pltpu.make_async_copy(produced_hbm.at[0], outputs.at[0], out_keep))

        def keep_wide(index, value):
            half = width // 2
            for part in range(2):
                wide_ref[part, index * width : (index + 1) * width, :] = value[
                    :, part * half : (part + 1) * half
                ].astype(low)

        lane = lax.broadcasted_iota(jnp.int32, (rows, 128), 1)
        upstream = cotangent_ref[...].astype(full)
        middle = middle_ref[...]
        inverse_second = inverse_norm(middle)
        unit_second = middle * inverse_second
        gain_second = pack_ref[HEAD_ROWS + 1 : HEAD_ROWS + 2, :].astype(full)
        second = unit_second * gain_second
        second_low = second.astype(low)
        heads_in = jnp.concatenate(
            [pack_ref[0:HEAD_ROWS, :], jnp.zeros((128 - HEAD_ROWS, width), low)], axis=0
        )
        mixed = dot_nt(second_low, heads_in)
        probs = probs_ref[...]
        route_rows = jnp.concatenate(
            [routes_ref[...].astype(full), jnp.zeros((126, rows), full)], axis=0
        )
        route_columns = jnp.transpose(route_rows).astype(jnp.int32)
        route = [column_of(route_columns, k) for k in range(2)]
        chosen = jnp.logical_or(lane == route[0], lane == route[1])
        gates = jnp.where(chosen, probs, 0.0)
        target = [column_of(targets_ref[...], k) for k in range(2)]

        gate_grad = jnp.zeros((rows, 128), full)
        place = lane.astype(full)
        for k in range(2):
            found = jnp.zeros((rows, 128), full)
            for shift in range(count):
                found = found + jnp.where(
                    jnp.logical_and(target[k] - shift * cap == place, lane < cap),
                    dots_ref[shift, 0:1, :],
                    0.0,
                )
            gate_grad = gate_grad + jnp.where(
                lane == route[k], jnp.sum(found, axis=1, keepdims=True), 0.0
            )
        copy_grad = jnp.sum(upstream * second, axis=1, keepdims=True)
        gate_grad = jnp.where(lane == copy_index, copy_grad, gate_grad)
        direct = column_of(gates, copy_index)
        constants = []
        for index in range(2):
            vector = pack_ref[HEAD_ROWS + 2 + index : HEAD_ROWS + 3 + index, :].astype(full)
            vector_dot = jnp.sum(upstream * vector, axis=1, keepdims=True)
            begin = experts + 2 * index
            spread_of = column_of(mixed, begin + 1) - column_of(mixed, begin)
            mixing = (1.0 / (1.0 + jnp.exp(spread_of)), 1.0 / (1.0 + jnp.exp(-spread_of)))
            gate = column_of(gates, copy_index + 1 + index)
            term = mixing[0] * copy_grad + mixing[1] * vector_dot
            gate_grad = jnp.where(lane == copy_index + 1 + index, term, gate_grad)
            direct = direct + gate * mixing[0]
            constants.append((gate, mixing, vector, vector_dot))
        prob_grad = jnp.where(chosen, gate_grad, 0.0)
        logit_grad = probs * (prob_grad - jnp.sum(probs * prob_grad, axis=1, keepdims=True))
        head_grad = logit_grad
        for index, (gate, mixing, vector, vector_dot) in enumerate(constants):
            mixing_grad = (gate * copy_grad, gate * vector_dot)
            mean = mixing[0] * mixing_grad[0] + mixing[1] * mixing_grad[1]
            for part in range(2):
                head_grad = jnp.where(
                    lane == experts + 2 * index + part,
                    mixing[part] * (mixing_grad[part] - mean),
                    head_grad,
                )
        head_low = head_grad.astype(low)

        slot = lax.broadcasted_iota(jnp.int32, (rows, slots), 1).astype(full)
        picked = [(slot == target[k]).astype(full).astype(low) for k in range(2)]
        second_grad = (
            dot(head_low, heads_in) + direct * upstream + dot(picked[0] + picked[1], back_ref[...])
        )
        normal_grad = second_grad * gain_second
        middle_total = upstream + inverse_second * (
            normal_grad - unit_second * jnp.mean(normal_grad * unit_second, axis=1, keepdims=True)
        )
        middle_grad[...] = middle_total
        middle_low = middle_total.astype(low)
        loads[0].wait()
        out_grad = dot_nt(middle_low, output_w[...]).astype(low)
        out_grads[own] = out_grad
        product = out_grad.astype(full) * attended_ref[...]
        masks = head_masks(rows)
        deltas = jnp.zeros((rows, 128), full)
        for index in range(pairs):
            part = product[:, index * 128 : index * 128 + 128]
            for head in range(2):
                total = jnp.sum(jnp.where(masks[head], part, 0.0), axis=1, keepdims=True)
                deltas = jnp.where(lane == 2 * index + head, total, deltas)
        stats[own, 0:stat_rows] = lse_ref[...]
        stats[own, stat_rows:] = jnp.transpose(deltas)[0:stat_rows]
        gather = Gather([out_grads, stats], size, gather_send, gather_recv)
        gather.forward(0)
        for copy in output_copies:
            copy.start()

        chosen_out = second * direct
        for gate, mixing, vector, vector_dot in constants:
            chosen_out = chosen_out + gate * mixing[1] * vector
        base = middle + chosen_out
        small_ref[...] = jnp.zeros_like(small_ref)
        small_ref[1:2, :] = jnp.sum(second_grad * unit_second, axis=0, keepdims=True)
        for index, (gate, mixing, vector, vector_dot) in enumerate(constants):
            small_ref[2 + index : 3 + index, :] = jnp.sum(
                gate * mixing[1] * upstream, axis=0, keepdims=True
            )
        small_ref[8:24, :] = dot_tn(head_low, second_low)[0:16]
        carry_grad = lax.dot_general(
            jnp.transpose(logit_grad)[0:16],
            previous_ref[...],
            (((1,), (1,)), ((), ())),
            precision=HIGH,
        )
        small_ref[24:40, 0:experts] = carry_grad
        keep_wide(3, dot_tn(attended_ref[...].astype(low), middle_low))

        for load in loads[1:4]:
            load.wait()
        query_total[...] = jnp.zeros_like(query_total)
        key_total[...] = jnp.zeros_like(key_total)
        value_total[...] = jnp.zeros_like(value_total)
        column = lax.broadcasted_iota(jnp.int32, (rows, rows), 0)
        row = lax.broadcasted_iota(jnp.int32, (rows, rows), 1)

        def block_side(block, as_query, as_key):
            key_block, query_block = (own if as_key else block), (own if as_query else block)
            key_pos, query_pos = key_block * rows + column, query_block * rows + row
            first = start_of(query_pos[0:8], starts_ref)[0:1]
            allowed = jnp.logical_and(key_pos >= first, key_pos <= query_pos)
            bias[...] = jnp.where(allowed, 0.0, NEGATIVE)

            def pair(index, carried):
                lanes = pl.ds(pl.multiple_of(index * 128, 128), 128)
                query, grad = queries[query_block, :, lanes], out_grads[query_block, :, lanes]
                key, value = keys[key_block, :, lanes], values[key_block, :, lanes]
                one_key = [jnp.where(mask, key, 0) for mask in masks]
                scores = [dot_nt(one_key[head], query) for head in range(2)]
                weight_grad = [dot_nt(jnp.where(mask, value, 0), grad) for mask in masks]
                weight, score = [], []
                for head in range(2):
                    lse = stats[query_block, pl.ds(2 * index + head, 1), :]
                    mean = stats[query_block, pl.ds(stat_rows + 2 * index + head, 1), :]
                    weight.append(jnp.exp(scores[head] + bias[...] - lse))
                    score.append((weight[head] * (weight_grad[head] - mean)).astype(low))
                if as_key:
                    value_total[:, lanes] += dot(
                        weight[0].astype(low), jnp.where(masks[0], grad, 0)
                    ) + dot(weight[1].astype(low), jnp.where(masks[1], grad, 0))
                    key_total[:, lanes] += dot(score[0], jnp.where(masks[0], query, 0)) + dot(
                        score[1], jnp.where(masks[1], query, 0)
                    )
                if as_query:
                    query_total[lanes, :] += dot_tn(one_key[0], score[0]) + dot_tn(
                        one_key[1], score[1]
                    )
                return carried

            lax.fori_loop(0, pairs, pair, 0)

        block_side(own, True, True)
        for place in range(1, size):
            block = jnp.bitwise_xor(own, place)

            @pl.when(block < own)
            def _():
                block_side(block, True, False)

        for place in range(1, size):
            gather.arrive(place)
            block = jnp.bitwise_xor(own, place)

            @pl.when(block > own)
            def _():
                block_side(block, False, True)

        for load in loads[4:]:
            load.wait()
        inputs = tokens_ref[...].astype(full)
        inverse_first = inverse_norm(inputs)
        unit_first = inputs * inverse_first
        gain_first = pack_ref[HEAD_ROWS : HEAD_ROWS + 1, :].astype(full)
        normed = (unit_first * gain_first).astype(low)
        turn = -sine[...]
        query_grad = jnp.transpose(query_total[...]) * HEAD_DIM**-0.5
        query_low = rotate(query_grad, cosine[...], turn).astype(low)
        key_low = rotate(key_total[...], cosine[...], turn).astype(low)
        value_low = value_total[...].astype(low)
        first_grad = (
            dot_nt(query_low, query_w[...])
            + dot_nt(key_low, key_w[...])
            + dot_nt(value_low, value_w[...])
        )
        for index, part in enumerate((query_low, key_low, value_low)):
            keep_wide(index, dot_tn(normed, part))
        small_ref[0:1, :] = jnp.sum(first_grad * unit_first, axis=0, keepdims=True)
        normal_grad = first_grad * gain_first
        token_grads_ref[...] = middle_grad[...] + inverse_first * (
            normal_grad - unit_first * jnp.mean(normal_grad * unit_first, axis=1, keepdims=True)
        )
        for copy in output_copies:
            copy.wait()
        for k in range(2):
            weight = jnp.sum(jnp.where(lane == route[k], probs, 0.0), axis=1, keepdims=True)
            base = base + weight * dot(picked[k], outputs[...].reshape(slots, width))
        result_ref[...] = base.astype(low)
        gather.finish()
        for copy in first_copies:
            copy.wait()

    stream_shape = (size, rows, width)
    any_space = pl.BlockSpec(memory_space=pl.ANY)
    in_vmem = pl.BlockSpec(memory_space=pltpu.VMEM)
    square = (width, width)
    return pl.pallas_call(
        kernel,
        out_shape=[
            jax.ShapeDtypeStruct((rows, width), low),
            jax.ShapeDtypeStruct((rows, width), full),
            jax.ShapeDtypeStruct((2, 4 * width, width // 2), low),
            jax.ShapeDtypeStruct((64, width), full),
        ]
        + [jax.ShapeDtypeStruct(term.shape[1:], low) for term in terms],
        in_specs=[in_vmem] * 4
        + [pl.BlockSpec(memory_space=pltpu.SMEM)]
        + [in_vmem] * 5
        + [any_space] * 3
        + [in_vmem, any_space, in_vmem]
        + [any_space] * 4
        + [in_vmem]
        + [any_space] * (2 + kinds),
        out_specs=[in_vmem] * 4 + [any_space] * kinds,
        scratch_shapes=[
            pltpu.VMEM(stream_shape, low),
            pltpu.VMEM(stream_shape, low),
            pltpu.VMEM(stream_shape, low),
            pltpu.VMEM(square, low),
            pltpu.VMEM(square, low),
            pltpu.VMEM(square, low),
            pltpu.VMEM(square, low),
            pltpu.VMEM((rows, 128), full),
            pltpu.VMEM((rows, 128), full),
            pltpu.VMEM((rows, rows), full),
            pltpu.VMEM(stream_shape, low),
            pltpu.VMEM((size, 2 * stat_rows, rows), full),
            pltpu.VMEM((count, cap, width), low),
            pltpu.VMEM((rows, width), full),
            pltpu.VMEM((width, rows), full),
            pltpu.VMEM((rows, width), full),
            pltpu.VMEM((rows, width), full),
            pltpu.SemaphoreType.DMA((9,)),
            pltpu.SemaphoreType.DMA((2, size)),
            pltpu.SemaphoreType.DMA((2, size)),
            pltpu.SemaphoreType.DMA((kinds,)),
            pltpu.SemaphoreType.DMA((kinds,)),
            pltpu.SemaphoreType.DMA((count,)),
            pltpu.SemaphoreType.DMA((count,)),
            pltpu.SemaphoreType.DMA,
        ],
        compiler_params=pltpu.CompilerParams(
            collective_id=2, has_side_effects=True, vmem_limit_bytes=60 * 2**20
        ),
        cost_estimate=pl.CostEstimate(
            flops=14 * rows * width * width * 2 + 20 * size * rows * rows * width,
            bytes_accessed=30 * 2**20,
            transcendentals=size * rows * rows * 12,
        ),
        name="backward",
    )(
        tokens,
        cotangent,
        previous,
        routes,
        starts,
        *forward,
        *returns,
        *weights,
        pack,
        jnp.asarray(tables[0]),
        jnp.asarray(tables[1]),
        *terms,
    )


PIECES = 2
DENSE_TIMES = (7, 24, 34, 48, 62, 77, 91, 101, 118, 125, 132)
EXPERT_TIMES = (19, 14, 19, 4, 11, 2)


def halving_steps(size):
    steps, step = [], 0
    while 1 << step < size:
        bit = 1 << step
        steps += [(step, place) for place in range(size - bit, 0, -2 * bit)]
        step += 1
    return steps


def needed_before(step, place):
    return {(earlier, place | 1 << earlier) for earlier in range(step)}


def add_into(target, source):
    rows = target.shape[0]
    piece = 96 if rows % 96 == 0 else (64 if rows % 64 == 0 else rows)

    def body(index, carried):
        part = pl.ds(pl.multiple_of(index * piece, piece), piece)
        total = target[part, :].astype(jnp.float32) + source[part, :].astype(jnp.float32)
        target[part, :] = total.astype(target.dtype)
        return carried

    lax.fori_loop(0, rows // piece, body, 0)


def reduce_layer(terms, firsts, wide, small, spread, shares, ring, exchange_size):
    low, full = jnp.bfloat16, jnp.float32
    steps = halving_steps(shares)
    first_step, later = steps[0], steps[1:]
    kinds = len(terms)
    blocks = [term.shape[1:] for term in terms]
    members = ring // spread
    groups = 3
    near_bits = [1 << step for step in range(ring.bit_length() - 1)]
    far_bits = [1 << step for step in range(exchange_size.bit_length() - 1)]
    deep_bits = [1 << step for step in range(shares.bit_length() - 1)]
    near = [(0, 0, bit) for bit in near_bits]
    far = [(0, bit, 0) for bit in far_bits]
    deep = [(bit, 0, 0) for bit in deep_bits]
    orders = [near + far + deep, near[:1] + far + near[1:] + deep, near + far + deep]
    places = near + far + deep
    bit_count = len(places)
    group_rows = [wide.shape[1], wide.shape[1], small.shape[0]]
    tile = [16, 16, 8]
    plans = []
    for group in range(groups):
        length, plan = group_rows[group], []
        for _ in range(bit_count):
            halved = (length // 2) % tile[group] == 0
            length = length // 2 if halved else length
            plan.append((halved, length))
        plans.append(plan)

    def kernel(*refs):
        refs = list(refs)

        def take(number):
            taken = refs[:number]
            del refs[:number]
            return taken

        term_refs, first_refs = take(kinds), take(kinds)
        (wide_hbm, small_hbm) = take(2)
        gathered = take(kinds)
        (wide_out, small_out) = take(2)
        sums, landed = take(kinds), take(kinds)
        (halves, smalls) = take(2)
        group_landed = take(groups)
        (load_sem, step_send, step_recv, own_sem, ring_send, ring_recv) = take(6)
        (dense_send, dense_recv, dense_load) = take(3)
        share = lax.axis_index("dp")
        mine = lax.axis_index("ctx") // spread

        dense_in = [
            pltpu.make_async_copy(wide_hbm, halves, dense_load.at[0]),
            pltpu.make_async_copy(small_hbm, smalls, dense_load.at[1]),
        ]
        for copy in dense_in:
            copy.start()
        loads = []
        for kind in range(kinds):
            copies = [
                pltpu.make_async_copy(
                    first_refs[kind], landed[kind].at[0], load_sem.at[kind, shares // 2]
                )
            ]
            for place in range(shares - 2, -1, -2):
                copies.append(
                    pltpu.make_async_copy(
                        term_refs[kind].at[jnp.bitwise_xor(share, place)],
                        sums[kind].at[place // 2],
                        load_sem.at[kind, place // 2],
                    )
                )
            for copy in copies:
                copy.start()
            loads.append(copies)
        greet_places(places)

        def expert_chain(kind, piece):
            period, odd_wait, even_wait, near_wait, far_wait, last_wait = EXPERT_TIMES
            begin = time = period * (kind * PIECES + piece)
            slots = {step: index for index, step in enumerate(steps)}
            lines = blocks[kind][0] // PIECES
            window = pl.ds(piece * lines, lines)
            one = kind * PIECES + piece

            def transfer(step, place):
                index = slots[step, place]
                if place % 2 == 1:
                    source = term_refs[kind].at[jnp.bitwise_xor(share, place), window]
                else:
                    source = sums[kind].at[place // 2, window]
                return pltpu.make_async_remote_copy(
                    src_ref=source,
                    dst_ref=landed[kind].at[index, window],
                    send_sem=step_send.at[one, index],
                    recv_sem=step_recv.at[one, index],
                    device_id=peer_at(1 << step, 0, 0),
                    device_id_type=pl.DeviceIdType.MESH,
                )

            yield begin
            if piece == 0:
                for copy in loads[kind]:
                    copy.wait()
            add_into(
                sums[kind].at[(shares - 2) // 2, window], landed[kind].at[0, window]
            )
            arrived, started, waiting = {first_step}, [], list(later)
            while True:
                for op in list(waiting):
                    if needed_before(*op) <= arrived:
                        transfer(*op).start()
                        started.append(op)
                        waiting.remove(op)
                if not started:
                    break
                op = started.pop(0)
                yield time + (even_wait if op[0] else odd_wait)
                transfer(*op).wait()
                arrived.add(op)
                add_into(
                    sums[kind].at[(op[1] ^ 1 << op[0]) // 2, window],
                    landed[kind].at[slots[op], window],
                )
            time += even_wait
            index = len(steps)
            bit = 1
            while bit < spread:
                copy = pltpu.make_async_remote_copy(
                    src_ref=sums[kind].at[0, window],
                    dst_ref=landed[kind].at[index, window],
                    send_sem=step_send.at[one, index],
                    recv_sem=step_recv.at[one, index],
                    device_id=peer_at(0, 0, bit),
                    device_id_type=pl.DeviceIdType.MESH,
                )
                copy.start()
                time += near_wait
                yield time
                copy.wait()
                add_into(sums[kind].at[0, window], landed[kind].at[index, window])
                index += 1
                bit *= 2
            keep = pltpu.make_async_copy(
                sums[kind].at[0, window], gathered[kind].at[mine, window], own_sem.at[one]
            )
            keep.start()
            sent = []

            def pass_on(place, bit):
                block = jnp.bitwise_xor(mine, place)
                target = gathered[kind].at[block, window]
                return pltpu.make_async_remote_copy(
                    src_ref=sums[kind].at[0, window] if place == 0 else target,
                    dst_ref=target,
                    send_sem=ring_send.at[one, place ^ bit],
                    recv_sem=ring_recv.at[one, place ^ bit],
                    device_id=peer_at(0, 0, bit * spread),
                    device_id_type=pl.DeviceIdType.MESH,
                )

            def forward(place):
                for bit, held in gather_steps(members):
                    if place in held:
                        copy = pass_on(place, bit)
                        copy.start()
                        sent.append(copy)

            forward(0)
            for place in range(1, members):
                wait = near_wait if place == 1 else far_wait if place & (place - 1) == 0 else last_wait
                yield time + wait + (far_wait if wait == last_wait else 0)
                bit = place & -place
                pass_on(place ^ bit, bit).wait_recv()
                forward(place)
            yield 1000
            keep.wait()
            for copy in sent:
                copy.wait_send()

        def bit_of(place):
            deep_bit, far_bit, near_bit = place
            axis, bit = ("dp", deep_bit) if deep_bit else ("exp", far_bit) if far_bit else ("ctx", near_bit)
            return lax.rem(lax.axis_index(axis) // bit, 2)

        def dense_chain(times):
            times = iter(times + tuple(range(times[-1] + 8, 900, 8)))
            buffers = [halves.at[0], halves.at[1], smalls]
            yield 0
            for copy in dense_in:
                copy.wait()
            begins = [0] * groups
            trail = []

            def window(begin, length, group):
                if isinstance(begin, int):
                    return pl.ds(begin, length)
                return pl.ds(pl.multiple_of(begin, tile[group]), length)

            def exchange_rows(group, step, source, target):
                return pltpu.make_async_remote_copy(
                    src_ref=source,
                    dst_ref=target,
                    send_sem=dense_send.at[group, step],
                    recv_sem=dense_recv.at[group, step],
                    device_id=peer_at(*orders[group][step % bit_count]),
                    device_id_type=pl.DeviceIdType.MESH,
                )

            for step in range(bit_count):
                copies = []
                for group in range(groups):
                    halved, length = plans[group][step]
                    upper = bit_of(orders[group][step])
                    if halved:
                        sent = begins[group] + (1 - upper) * length
                        begins[group] = begins[group] + upper * length
                    else:
                        sent = begins[group]
                    at = sum(size for _, size in plans[group][:step])
                    copy = exchange_rows(
                        group,
                        step,
                        buffers[group].at[window(sent, length, group)],
                        group_landed[group].at[pl.ds(at, length)],
                    )
                    copy.start()
                    copies.append((copy, at, length))
                trail.append(list(begins))
                yield next(times)
                for group, (copy, at, length) in enumerate(copies):
                    copy.wait()
                    add_into(
                        buffers[group].at[window(begins[group], length, group)],
                        group_landed[group].at[pl.ds(at, length)],
                    )
            outputs = [wide_out.at[0], wide_out.at[1], small_out]
            keeps = []
            for group in range(groups):
                part = window(begins[group], plans[group][-1][1], group)
                keep = pltpu.make_async_copy(
                    buffers[group].at[part], outputs[group].at[part], dense_load.at[group]
                )
                keep.start()
                keeps.append(keep)
            for keep in keeps:
                keep.wait()
            for step in range(bit_count - 1, -1, -1):
                copies = []
                for group in range(groups):
                    halved, length = plans[group][step]
                    if halved:
                        part = outputs[group].at[window(trail[step][group], length, group)]
                        copy = exchange_rows(group, bit_count + step, part, part)
                        copy.start()
                        copies.append(copy)
                if copies:
                    yield next(times)
                for copy in copies:
                    copy.wait()

        chains = [dense_chain(DENSE_TIMES)] + [
            expert_chain(kind, piece) for kind in range(kinds) for piece in range(PIECES)
        ]
        due = [(next(chain), index) for index, chain in enumerate(chains)]
        while due:
            due.sort()
            _, index = due.pop(0)
            time = next(chains[index], None)
            if time is not None:
                due.append((time, index))

    any_space = pl.BlockSpec(memory_space=pl.ANY)
    extra = len(steps) + spread.bit_length() - 1
    return pl.pallas_call(
        kernel,
        out_shape=[jax.ShapeDtypeStruct((members,) + block, low) for block in blocks]
        + [jax.ShapeDtypeStruct(wide.shape, low), jax.ShapeDtypeStruct(small.shape, full)],
        in_specs=[any_space] * (2 * kinds + 2),
        out_specs=[any_space] * (kinds + 2),
        scratch_shapes=[pltpu.VMEM((shares // 2,) + block, low) for block in blocks]
        + [pltpu.VMEM((extra,) + block, low) for block in blocks]
        + [pltpu.VMEM(wide.shape, low), pltpu.VMEM(small.shape, full)]
        + [
            pltpu.VMEM(
                (sum(length for _, length in plans[group]), (wide, wide, small)[group].shape[-1]),
                (low, low, full)[group],
            )
            for group in range(groups)
        ]
        + [
            pltpu.SemaphoreType.DMA((kinds, shares // 2 + 1)),
            pltpu.SemaphoreType.DMA((kinds * PIECES, extra)),
            pltpu.SemaphoreType.DMA((kinds * PIECES, extra)),
            pltpu.SemaphoreType.DMA((kinds * PIECES,)),
            pltpu.SemaphoreType.DMA((kinds * PIECES, members)),
            pltpu.SemaphoreType.DMA((kinds * PIECES, members)),
            pltpu.SemaphoreType.DMA((groups, 2 * bit_count)),
            pltpu.SemaphoreType.DMA((groups, 2 * bit_count)),
            pltpu.SemaphoreType.DMA((3,)),
        ],
        compiler_params=pltpu.CompilerParams(
            collective_id=3, has_side_effects=True, vmem_limit_bytes=60 * 2**20
        ),
        name="reduce",
    )(*terms, *firsts, wide, small)


def widen_layer(parts, wide, small, experts):
    members = parts[0].shape[0]
    pieces = 4
    steps = members * pieces
    squares = wide.shape[1] // (2 * wide.shape[2])
    width = 2 * wide.shape[2]
    lines = wide.shape[1] // steps
    turns = width // lines
    full = jnp.float32
    kinds = len(parts)

    def kernel(*refs):
        sources, wide_ref, small_ref = refs[:kinds], refs[kinds], refs[kinds + 1]
        targets = refs[kinds + 2 : 2 * kinds + 2]
        square_refs = refs[2 * kinds + 2 : 2 * kinds + 2 + squares]
        head_ref, map_ref, carry_ref, vector_ref, gains_ref = refs[2 * kinds + 2 + squares :]
        step = pl.program_id(0) * pieces + pl.program_id(1)
        for source, target in zip(sources, targets):
            target[...] = source[...].astype(full)
        for index in range(squares):

            @pl.when(step // turns == index)
            def _():
                square_refs[index][:, 0 : width // 2] = wide_ref[0].astype(full)
                square_refs[index][:, width // 2 :] = wide_ref[1].astype(full)

        @pl.when(step == 0)
        def _():
            head_ref[...] = small_ref[8 : 8 + experts, :]
            for index in range(2):
                begin = 8 + experts + 2 * index
                map_ref[index] = small_ref[begin : begin + 2, :]
            carry_ref[...] = jnp.transpose(small_ref[24:40, 0:128])[0:experts, 0:experts]
            vector_ref[...] = small_ref[2:4, :]
            gains_ref[...] = small_ref[0:2, :]

    def chunk(part):
        return pl.BlockSpec(
            (1, part.shape[1] // pieces, part.shape[2]), lambda member, piece: (member, piece, 0)
        )

    def square(index):
        return pl.BlockSpec(
            (lines, width),
            lambda member, piece: (
                jnp.clip(member * pieces + piece - index * turns, 0, turns - 1),
                0,
            ),
        )

    def whole(*shape):
        return pl.BlockSpec(shape, lambda member, piece: (0,) * len(shape))

    smalls = [(experts, width), (2, 2, width), (experts, experts), (2, width), (2, width)]
    return pl.pallas_call(
        kernel,
        out_shape=[jax.ShapeDtypeStruct(part.shape, full) for part in parts]
        + [jax.ShapeDtypeStruct((width, width), full)] * squares
        + [jax.ShapeDtypeStruct(shape, full) for shape in smalls],
        grid=(members, pieces),
        in_specs=[chunk(part) for part in parts]
        + [
            pl.BlockSpec(
                (2, lines, width // 2), lambda member, piece: (0, member * pieces + piece, 0)
            ),
            whole(*small.shape),
        ],
        out_specs=[chunk(part) for part in parts]
        + [square(index) for index in range(squares)]
        + [whole(*shape) for shape in smalls],
        compiler_params=pltpu.CompilerParams(vmem_limit_bytes=48 * 2**20),
        name="widen",
    )(*parts, wide, small)


def local(
    tokens,
    cotangent,
    previous,
    routes,
    boundaries,
    norm_first,
    query_weight,
    key_weight,
    value_weight,
    output_weight,
    norm_second,
    router,
    gate_carry,
    constant_map,
    constant_vector,
    expert_gate,
    expert_linear,
    expert_down,
):
    model_width = tokens.shape[2]
    ring = lax.axis_size("ctx")
    group_size = expert_gate.shape[0]
    exchange_count = lax.axis_size("exp")
    spread = ring // group_size
    ranks = (exchange_count, group_size, spread)
    slot_total = exchange_count * group_size * CAP
    expert_total = router.shape[1]
    pack = jnp.concatenate(
        [
            router.T,
            constant_map[0].T,
            constant_map[1].T,
            norm_first[None],
            norm_second[None],
            constant_vector,
        ],
        axis=0,
    )
    pack = jnp.pad(pack, ((0, 32 - pack.shape[0]), (0, 0)))
    weights = (query_weight, key_weight, value_weight, output_weight)
    (
        queries,
        keys,
        values,
        attended,
        lse,
        middle,
        probs,
        targets,
        outgoing,
        slot_gates,
        grads_in,
    ) = attend_layer(
        tokens[0],
        cotangent[0],
        previous[0].T,
        routes[0].T,
        boundaries,
        weights,
        pack,
        gate_carry,
        ranks,
        CAP,
        ring,
    )
    home_grads, produced, dots, gate_terms, linear_terms, down_terms = expert_layer(
        outgoing,
        slot_gates,
        grads_in.reshape(slot_total, model_width),
        (expert_gate, expert_linear, expert_down),
        ranks,
        lax.axis_size("dp"),
    )
    terms = (down_terms, gate_terms, linear_terms)
    shares = lax.axis_size("dp")
    result, token_grads, wide, small, *firsts = backward_layer(
        tokens[0],
        cotangent[0],
        previous[0].T,
        routes[0].T,
        boundaries,
        (attended, lse, middle, probs, targets, queries, keys, values),
        (home_grads.reshape(slot_total, model_width), produced, dots),
        weights,
        pack,
        terms,
        ranks,
        CAP,
        ring,
        shares,
    )
    *parts, wide, small = reduce_layer(
        terms, firsts, wide, small, spread, shares, ring, exchange_count
    )
    (
        down_grads,
        gate_grads,
        linear_grads,
        query_grads,
        key_grads,
        value_grads,
        output_grads,
        router_grads,
        map_grads,
        carry_grads,
        vector_grads,
        gain_grads,
    ) = widen_layer(parts, wide, small, expert_total)
    return (
        result[None],
        token_grads[None],
        gain_grads[0],
        query_grads,
        key_grads,
        value_grads,
        output_grads,
        gain_grads[1],
        router_grads.T,
        carry_grads,
        jnp.transpose(map_grads, (0, 2, 1)),
        vector_grads,
        gate_grads,
        linear_grads,
        down_grads,
    )


def solution(mesh):
    return jax.shard_map(
        local,
        mesh=mesh,
        in_specs=(
            P(("dp", "exp"), "ctx", None),
            P(("dp", "exp"), "ctx", None),
            P(("dp", "exp"), "ctx", None),
            P(("dp", "exp"), "ctx", None),
            P(("dp", "exp"), None),
            P(),
            P(),
            P(),
            P(),
            P(),
            P(),
            P(),
            P(),
            P(),
            P(),
            P("exp", None, None),
            P("exp", None, None),
            P("exp", None, None),
        ),
        out_specs=(
            P(("dp", "exp"), "ctx", None),
            P(("dp", "exp"), "ctx", None),
            P(),
            P(),
            P(),
            P(),
            P(),
            P(),
            P(),
            P(),
            P(),
            P(),
            P("exp", None, "dp"),
            P("exp", None, "dp"),
            P("exp", "dp", None),
        ),
        check_vma=False,
    )
```

```python
import math

import jax
import jax.numpy as jnp
import numpy as np
from jax import lax
from jax.experimental import pallas as pl
from jax.experimental.pallas import tpu as pltpu
from jax.sharding import PartitionSpec as P

HEAD_DIM = 64
CAP = 96


EPSILON = 1e-06
NEGATIVE = -1e30
HIGH = lax.Precision.HIGHEST


HEAD_ROWS = 16


def mesh_id(exp_index, ctx_index):
    return {"exp": exp_index, "ctx": ctx_index}


def dot(left, right):
    return jnp.dot(left, right, preferred_element_type=jnp.float32)


def dot_nt(left, right):
    return lax.dot_general(
        left, right, (((1,), (1,)), ((), ())), preferred_element_type=jnp.float32
    )


def dot_tn(left, right):
    return lax.dot_general(
        left, right, (((0,), (0,)), ((), ())), preferred_element_type=jnp.float32
    )


def member_of(shift, ranks):
    exchange_size, group_size, spread = ranks
    exp_index, ctx_index = lax.axis_index("exp"), lax.axis_index("ctx")
    far, near = shift // group_size, shift % group_size
    place = jnp.bitwise_xor(ctx_index // spread, near) * spread + lax.rem(ctx_index, spread)
    return mesh_id(jnp.bitwise_xor(exp_index, far), place)


def greet(count, ranks):
    barrier = pltpu.get_barrier_semaphore()
    for shift in range(1, count):
        pl.semaphore_signal(
            barrier, inc=1, device_id=member_of(shift, ranks), device_id_type=pl.DeviceIdType.MESH
        )
    pl.semaphore_wait(barrier, count - 1)


def send_block(source, target, shift, ranks, send_sem, recv_sem):
    return pltpu.make_async_remote_copy(
        src_ref=source.at[shift],
        dst_ref=target.at[shift],
        send_sem=send_sem.at[shift],
        recv_sem=recv_sem.at[shift],
        device_id=member_of(shift, ranks),
        device_id_type=pl.DeviceIdType.MESH,
    )


def expert_layer(outgoing, gates, grads, weights, ranks, shares):
    count, cap, width = outgoing.shape
    hidden_units = weights[0].shape[2]
    rows = count * cap
    share = hidden_units // shares
    spread = ranks[2]

    def kernel(
        outgoing_hbm,
        gates_ref,
        grads_ref,
        gate_hbm,
        linear_hbm,
        down_hbm,
        back_ref,
        output_ref,
        dots_ref,
        gate_terms,
        linear_terms,
        down_terms,
        first_ref,
        received,
        received_gates,
        gate_w,
        linear_w,
        down_w,
        hidden_grad,
        hidden,
        gate_low,
        linear_low,
        rows_t,
        scaled,
        gate_column,
        out_total,
        in_total,
        in_send,
        dots_send,
        terms,
        weight_sem,
        send_sem,
        recv_sem,
        local_sem,
        terms_sem,
        first_send,
        first_recv,
    ):
        own = lax.axis_index("ctx") // spread
        loads = [
            pltpu.make_async_copy(source.at[own], target, weight_sem.at[index])
            for index, (source, target) in enumerate(
                ((down_hbm, down_w), (gate_hbm, gate_w), (linear_hbm, linear_w))
            )
        ]
        for load in loads:
            load.start()
        greet_places([(0,) + place for place in group_places(ranks)] + [(1, 0, 0)])

        def send_some(source, target, index, shifts):
            copies = []
            for shift in shifts:
                if shift:
                    copies.append(
                        send_block(
                            source, target, shift, ranks, send_sem.at[index], recv_sem.at[index]
                        )
                    )
                else:
                    copies.append(
                        pltpu.make_async_copy(source.at[0], target.at[0], local_sem.at[index])
                    )
            for copy in copies:
                copy.start()
            return copies

        every = range(count)
        gates_in = send_some(gates_ref, received_gates, 0, every)
        incoming = send_some(outgoing_hbm, received, 1, every)
        loads[0].wait()

        def backward_in(index, carry):
            part = pl.ds(pl.multiple_of(index * share, share), share)
            hidden_grad[:, part] = dot_nt(grads_ref[...], down_w[part, :])
            return carry

        lax.fori_loop(0, shares, backward_in, 0)
        for copy in gates_in:
            copy.wait()
        for shift in every:
            column = jnp.transpose(received_gates[shift])[:cap, 0:1]
            block = pl.ds(shift * cap, cap)
            gate_column[block, :] = jnp.broadcast_to(column, (cap, 128))
            scaled[block, :] = (column * grads_ref[block, :].astype(jnp.float32)).astype(
                jnp.bfloat16
            )
        for load in loads[1:]:
            load.wait()

        going = []
        batches = 2
        members = count // batches
        lines = rows // batches
        for batch in range(batches):
            chunks = range(batch * members, (batch + 1) * members)
            for shift in chunks:
                incoming[shift].wait()
            block = pl.ds(batch * lines, lines)

            def through(index, carry):
                part = pl.ds(pl.multiple_of(index * share, share), share)
                tokens = received[batch * members : (batch + 1) * members].reshape(lines, width)
                gate_part = dot(tokens, gate_w[:, part])
                linear_part = dot(tokens, linear_w[:, part])
                sigmoid = 1.0 / (1.0 + jnp.exp(-gate_part))
                silu = gate_part * sigmoid
                low = (silu * linear_part).astype(jnp.bfloat16)
                hidden[block, part] = low
                upper = hidden_grad[block, part] * gate_column[block, 0:1]
                low_gate = (
                    upper * linear_part * sigmoid * (1.0 + gate_part * (1.0 - sigmoid))
                ).astype(jnp.bfloat16)
                gate_low[block, part] = low_gate
                low_linear = (upper * silu).astype(jnp.bfloat16)
                linear_low[block, part] = low_linear
                out = dot(low, down_w[part, :])
                back = dot_nt(low_gate, gate_w[:, part]) + dot_nt(low_linear, linear_w[:, part])

                @pl.when(index == 0)
                def _():
                    out_total[block, :] = out
                    in_total[block, :] = back

                @pl.when(index > 0)
                def _():
                    out_total[block, :] += out
                    in_total[block, :] += back

                return carry

            lax.fori_loop(0, shares, through, 0)
            in_send[batch * members : (batch + 1) * members] = (
                in_total[block, :].astype(jnp.bfloat16).reshape(members, cap, width)
            )
            going += send_some(in_send, back_ref, 2, chunks)
            low = out_total[block, :].astype(jnp.bfloat16)
            output_ref[batch * members : (batch + 1) * members] = low.reshape(members, cap, width)
            dots = jnp.sum(
                low.astype(jnp.float32) * grads_ref[block, :].astype(jnp.float32),
                axis=1,
                keepdims=True,
            )
            for place, shift in enumerate(chunks):
                column = jnp.broadcast_to(dots[place * cap : (place + 1) * cap], (cap, 128))
                dots_send[shift, :, 0:cap] = jnp.transpose(column)[0:8, :]
                dots_send[shift, :, cap:] = jnp.zeros((8, 128 - cap), jnp.float32)
            going += send_some(dots_send, dots_ref, 3, chunks)
            rows_t[:, batch * lines : (batch + 1) * lines] = jnp.transpose(
                received[batch * members : (batch + 1) * members].reshape(lines, width)
            )

        def term_copy(which, index):
            target = (down_terms, gate_terms, linear_terms)[which]
            return pltpu.make_async_copy(
                terms[which].at[index], target.at[index], terms_sem.at[which, index]
            )

        def weigh(which, turn):
            index = jnp.bitwise_xor(lax.axis_index("dp"), shares - 1 - turn)
            part = pl.ds(pl.multiple_of(index * share, share), share)
            if which == 0:
                value = dot_tn(hidden[:, part], scaled[...])
            else:
                value = dot(rows_t[...], (gate_low if which == 1 else linear_low)[:, part])
            terms[which][index] = value.astype(jnp.bfloat16)
            term_copy(which, index).start()
            return index

        index = weigh(0, 0)
        first = pltpu.make_async_remote_copy(
            src_ref=terms[0].at[index],
            dst_ref=first_ref,
            send_sem=first_send,
            recv_sem=first_recv,
            device_id=peer_at(1, 0, 0),
            device_id_type=pl.DeviceIdType.MESH,
        )
        first.start()

        def weigh_rest(turn, carry):
            weigh(1, turn)
            weigh(2, turn)

            @pl.when(turn > 0)
            def _():
                weigh(0, turn)

            return carry

        lax.fori_loop(0, shares, weigh_rest, 0)
        for which in range(3):
            for index in range(shares):
                term_copy(which, index).wait()
        for copy in going:
            copy.wait()
        first.wait()

    low, full = jnp.bfloat16, jnp.float32
    columns, lines = (shares, width, share), (shares, share, width)
    any_space = pl.BlockSpec(memory_space=pl.ANY)
    in_vmem = pl.BlockSpec(memory_space=pltpu.VMEM)
    return pl.pallas_call(
        kernel,
        out_shape=[
            jax.ShapeDtypeStruct(outgoing.shape, low),
            jax.ShapeDtypeStruct(outgoing.shape, low),
            jax.ShapeDtypeStruct(gates.shape, full),
            jax.ShapeDtypeStruct(columns, low),
            jax.ShapeDtypeStruct(columns, low),
            jax.ShapeDtypeStruct(lines, low),
            jax.ShapeDtypeStruct(lines[1:], low),
        ],
        in_specs=[any_space, in_vmem, in_vmem, any_space, any_space, any_space],
        out_specs=[any_space, in_vmem] + [any_space] * 5,
        scratch_shapes=[
            pltpu.VMEM(outgoing.shape, low),
            pltpu.VMEM(gates.shape, full),
            pltpu.VMEM((width, hidden_units), low),
            pltpu.VMEM((width, hidden_units), low),
            pltpu.VMEM((hidden_units, width), low),
            pltpu.VMEM((rows, hidden_units), full),
            pltpu.VMEM((rows, hidden_units), low),
            pltpu.VMEM((rows, hidden_units), low),
            pltpu.VMEM((rows, hidden_units), low),
            pltpu.VMEM((width, rows), low),
            pltpu.VMEM((rows, width), low),
            pltpu.VMEM((rows, 128), full),
            pltpu.VMEM((rows, width), full),
            pltpu.VMEM((rows, width), full),
            pltpu.VMEM(outgoing.shape, low),
            pltpu.VMEM(gates.shape, full),
            [pltpu.VMEM(lines, low), pltpu.VMEM(columns, low), pltpu.VMEM(columns, low)],
            pltpu.SemaphoreType.DMA((3,)),
            pltpu.SemaphoreType.DMA((4, count)),
            pltpu.SemaphoreType.DMA((4, count)),
            pltpu.SemaphoreType.DMA((4,)),
            pltpu.SemaphoreType.DMA((3, shares)),
            pltpu.SemaphoreType.DMA,
            pltpu.SemaphoreType.DMA,
        ],
        compiler_params=pltpu.CompilerParams(
            collective_id=1, has_side_effects=True, vmem_limit_bytes=60 * 2**20
        ),
        cost_estimate=pl.CostEstimate(
            flops=18 * rows * width * hidden_units,
            bytes_accessed=12 * width * hidden_units + 12 * rows * width,
            transcendentals=rows * hidden_units,
        ),
        name="experts",
    )(outgoing, gates, grads, *weights)


def rope_tables(row_count):
    half = HEAD_DIM // 2
    frequency = np.exp(
        np.arange(half, dtype=np.float32) * np.float32(-2.0 * math.log(10000.0) / HEAD_DIM)
    ).astype(np.float32)
    angles = np.arange(row_count, dtype=np.float32)[:, None] * frequency[None, :]
    cosine, sine = np.cos(angles).astype(np.float32), np.sin(angles).astype(np.float32)
    return (
        np.concatenate([cosine] * 4, axis=1),
        np.concatenate([-sine, sine, -sine, sine], axis=1),
    )


def rotate(values, cosine, sine):
    lane = lax.broadcasted_iota(jnp.int32, cosine.shape, 1)
    leading = jnp.bitwise_and(lane, HEAD_DIM - 1) < HEAD_DIM // 2
    parts = []
    for begin in range(0, values.shape[1], 128):
        part = values[:, begin : begin + 128]
        ahead = pltpu.roll(part, 128 - HEAD_DIM // 2, 1)
        behind = pltpu.roll(part, HEAD_DIM // 2, 1)
        parts.append(part * cosine + jnp.where(leading, ahead, behind) * sine)
    return jnp.concatenate(parts, axis=1)


def inverse_norm(values):
    return lax.rsqrt(jnp.mean(values * values, axis=1, keepdims=True) + EPSILON)


def head_masks(rows):
    first = lax.broadcasted_iota(jnp.int32, (rows, 128), 1) < HEAD_DIM
    return first, jnp.logical_not(first)


def start_of(positions, starts):
    first = jnp.zeros_like(positions)
    for index in range(starts.shape[1]):
        begin = starts[0, index]
        first = jnp.where(begin <= positions, jnp.maximum(first, begin), first)
    return first


def gather_steps(size):
    bits, held, steps = [], [0], []
    bit = size // 2
    while bit >= 1:
        steps.append((bit, list(held)))
        held = held + [place ^ bit for place in held]
        bit //= 2
    return steps


def peer_at(deep, far, near):
    return {
        "dp": jnp.bitwise_xor(lax.axis_index("dp"), deep),
        "exp": jnp.bitwise_xor(lax.axis_index("exp"), far),
        "ctx": jnp.bitwise_xor(lax.axis_index("ctx"), near),
    }


def peer(far, near):
    return peer_at(0, far, near)


def greet_places(places):
    barrier = pltpu.get_barrier_semaphore()
    for place in places:
        pl.semaphore_signal(
            barrier, inc=1, device_id=peer_at(*place), device_id_type=pl.DeviceIdType.MESH
        )
    pl.semaphore_wait(barrier, len(places))


def greet_all(places):
    greet_places([(0,) + place for place in places])


def group_places(ranks):
    return [
        (shift // ranks[1], shift % ranks[1] * ranks[2]) for shift in range(1, ranks[0] * ranks[1])
    ]


def ring_places(size):
    return [(0, bit) for bit, _ in gather_steps(size)]


def places_of(ranks, size):
    places = group_places(ranks)
    return places + [place for place in ring_places(size) if place not in places]


class Gather:
    def __init__(self, buffers, size, send_sem, recv_sem, sources=None):
        self.buffers, self.sources = buffers, sources
        self.send_sem, self.recv_sem = send_sem, recv_sem
        self.steps = gather_steps(size)
        self.started = []

    def copy(self, place, bit, index):
        block = jnp.bitwise_xor(lax.axis_index("ctx"), place)
        buffer = self.buffers[index]
        straight = self.sources is not None and place == 0
        return pltpu.make_async_remote_copy(
            src_ref=self.sources[index] if straight else buffer.at[block],
            dst_ref=buffer.at[block],
            send_sem=self.send_sem.at[index, place ^ bit],
            recv_sem=self.recv_sem.at[index, place ^ bit],
            device_id=peer(0, bit),
            device_id_type=pl.DeviceIdType.MESH,
        )

    def forward(self, place):
        for bit, held in self.steps:
            if place in held:
                for index in range(len(self.buffers)):
                    copy = self.copy(place, bit, index)
                    copy.start()
                    self.started.append(copy)

    def arrive(self, place):
        bit = place & -place
        for index in range(len(self.buffers)):
            self.copy(place ^ bit, bit, index).wait_recv()
        self.forward(place)

    def finish(self):
        for copy in self.started:
            copy.wait_send()


def slot_targets(routes, ranks, cap):
    exchange_size, group_size, spread = ranks
    rows = routes.shape[1]
    experts = exchange_size * group_size
    expert = lax.broadcasted_iota(jnp.int32, (16, rows), 0)
    hits = [(expert == routes[k : k + 1]).astype(jnp.float32) for k in range(2)]
    before = lax.broadcasted_iota(jnp.int32, (rows, rows), 0) < lax.broadcasted_iota(
        jnp.int32, (rows, rows), 1
    )
    earlier = dot(
        (hits[0] + hits[1]).astype(jnp.bfloat16), before.astype(jnp.float32).astype(jnp.bfloat16)
    )
    targets = []
    for k in range(2):
        route = routes[k : k + 1]
        rank = jnp.sum(hits[k] * earlier, axis=0, keepdims=True)
        far = jnp.bitwise_xor(route // group_size, lax.axis_index("exp"))
        near = jnp.bitwise_xor(route % group_size, lax.axis_index("ctx") // spread)
        place = ((far * group_size + near) * cap).astype(jnp.float32)
        targets.append(jnp.where(route < experts, place + rank, -1.0))
    return targets


def attend_layer(
    tokens, cotangent, previous, routes, starts, weights, pack, carry, ranks, cap, size
):
    rows, width = tokens.shape
    count = ranks[0] * ranks[1]
    slots = count * cap
    pairs = width // 128
    tables = rope_tables(size * rows)
    low, full = jnp.bfloat16, jnp.float32

    def kernel(
        tokens_hbm,
        cotangent_ref,
        previous_ref,
        routes_ref,
        starts_ref,
        query_hbm,
        key_hbm,
        value_hbm,
        output_hbm,
        pack_ref,
        carry_ref,
        cosine_hbm,
        sine_hbm,
        queries_out,
        keys_out,
        values_out,
        attended_ref,
        lse_ref,
        middle_ref,
        probs_ref,
        targets_ref,
        outgoing_ref,
        gates_ref,
        grads_ref,
        stream,
        queries,
        keys,
        values,
        query_w,
        key_w,
        value_w,
        output_w,
        cosine,
        sine,
        bias,
        totals,
        highest,
        slot_grads,
        load_sem,
        gather_send,
        gather_recv,
        grad_send,
        grad_recv,
        keep_sem,
    ):
        own = lax.axis_index("ctx")
        bring = pltpu.make_async_copy(tokens_hbm, stream.at[own], load_sem.at[6])
        bring.start()
        loads = [
            pltpu.make_async_copy(source, target, load_sem.at[index])
            for index, (source, target) in enumerate(
                (
                    (query_hbm, query_w),
                    (key_hbm, key_w),
                    (value_hbm, value_w),
                    (cosine_hbm, cosine),
                    (sine_hbm, sine),
                    (output_hbm, output_w),
                )
            )
        ]
        for load in loads:
            load.start()
        greet_all(places_of(ranks, size))
        gather = Gather([stream], size, gather_send, gather_recv, [tokens_hbm])
        gather.forward(0)

        targets = slot_targets(routes_ref[...], ranks, cap)
        slot = lax.broadcasted_iota(jnp.int32, (slots, rows), 0).astype(full)
        picked = jnp.logical_or(slot == targets[0], slot == targets[1])
        picked = picked.astype(full).astype(low)
        slot_grads[...] = dot(picked, cotangent_ref[...]).astype(low).reshape(count, cap, width)
        grad_copies = [
            send_block(slot_grads, grads_ref, shift, ranks, grad_send, grad_recv)
            for shift in range(1, count)
        ]
        grad_copies.append(pltpu.make_async_copy(slot_grads.at[0], grads_ref.at[0], keep_sem.at[0]))

        bring.wait()
        for load in loads[:5]:
            load.wait()
        gain = pack_ref[HEAD_ROWS : HEAD_ROWS + 1, :].astype(full)

        def project(block, wanted):
            line = pl.ds(pl.multiple_of(block * rows, rows), rows)
            values_in = stream[block].astype(full)
            normed = (values_in * inverse_norm(values_in) * gain).astype(low)
            if "q" in wanted:
                turned = rotate(dot(normed, query_w[...]), cosine[line, :], sine[line, :])
                queries[block] = (turned.astype(low).astype(full) * HEAD_DIM**-0.5).astype(low)
            if "k" in wanted:
                turned = rotate(dot(normed, key_w[...]), cosine[line, :], sine[line, :])
                keys[block] = turned.astype(low)
                values[block] = dot(normed, value_w[...]).astype(low)

        masks = head_masks(rows)
        query_pos = own * rows + lax.broadcasted_iota(jnp.int32, (rows, rows), 1)
        document_start = start_of(query_pos[0:8], starts_ref)[0:1]

        def attend(block):
            key_pos = block * rows + lax.broadcasted_iota(jnp.int32, (rows, rows), 0)
            allowed = jnp.logical_and(key_pos >= document_start, key_pos <= query_pos)
            bias[...] = jnp.where(allowed, 0.0, NEGATIVE)

            def pair(index, carried):
                lanes = pl.ds(pl.multiple_of(index * 128, 128), 128)
                query, key, value = queries[own, :, lanes], keys[block, :, lanes], values[block, :, lanes]
                scores = [dot_nt(jnp.where(mask, key, 0), query) + bias[...] for mask in masks]
                old = [highest[index, head][0:1, :] for head in range(2)]
                new = [
                    jnp.maximum(old[head], jnp.max(scores[head], axis=0, keepdims=True))
                    for head in range(2)
                ]
                weight = [jnp.exp(scores[head] - new[head]).astype(low) for head in range(2)]
                for head in range(2):
                    totals[index, head] = totals[index, head] * jnp.exp(old[head] - new[head]) + dot_tn(
                        jnp.where(masks[head], value, 1), weight[head]
                    )
                    highest[index, head] = jnp.broadcast_to(new[head], (8, rows))
                return carried

            lax.fori_loop(0, pairs, pair, 0)

        totals[...] = jnp.zeros_like(totals)
        highest[...] = jnp.full(highest.shape, NEGATIVE, full)
        project(own, "qk")
        attend(own)
        for place in range(1, size):
            gather.arrive(place)
            if place == size // 2:
                for copy in grad_copies:
                    copy.start()
            block = jnp.bitwise_xor(own, place)

            @pl.when(block < own)
            def _():
                project(block, "k")
                attend(block)

            @pl.when(block > own)
            def _():
                project(block, "q")

        keep = [
            pltpu.make_async_copy(source, target, keep_sem.at[index + 1])
            for index, (source, target) in enumerate(
                ((queries, queries_out), (keys, keys_out), (values, values_out))
            )
        ]
        for copy in keep:
            copy.start()

        lse_ref[...] = jnp.zeros_like(lse_ref)
        upper = lax.broadcasted_iota(jnp.int32, (128, rows), 0) < HEAD_DIM
        for index in range(pairs):
            halves = []
            for head in range(2):
                total = totals[index, head]
                line = HEAD_DIM if head == 0 else 0
                weight_sum = total[line : line + 1, :]
                halves.append(total / weight_sum)
                lse_ref[2 * index + head : 2 * index + head + 1, :] = highest[index, head][
                    0:1, :
                ] + jnp.log(weight_sum)
            attended_ref[:, index * 128 : index * 128 + 128] = jnp.transpose(
                jnp.where(upper, halves[0], halves[1])
            )
        loads[5].wait()
        middle = stream[own].astype(full) + dot(attended_ref[...].astype(low), output_w[...])
        middle_ref[...] = middle
        second = (
            middle
            * inverse_norm(middle)
            * pack_ref[HEAD_ROWS + 1 : HEAD_ROWS + 2, :].astype(full)
        )
        second_low = second.astype(low)
        outgoing_ref[...] = dot(picked, second_low).astype(low).reshape(count, cap, width)

        experts = previous_ref.shape[0]
        logits = dot_nt(second_low, pack_ref[0:HEAD_ROWS, :])[:, 0:experts] + lax.dot_general(
            previous_ref[...],
            carry_ref[...].astype(full),
            (((0,), (0,)), ((), ())),
            precision=HIGH,
        )
        logits = logits - jnp.max(logits, axis=1, keepdims=True)
        powers = jnp.exp(logits)
        probs_ref[...] = jnp.zeros_like(probs_ref)
        probs_ref[:, 0:experts] = powers / jnp.sum(powers, axis=1, keepdims=True)
        turned = jnp.transpose(probs_ref[...])[0:16]
        expert = lax.broadcasted_iota(jnp.int32, (16, rows), 0)
        weighted = jnp.zeros((slots, rows), full)
        for k in range(2):
            route = routes_ref[k : k + 1, :]
            gate = jnp.sum(jnp.where(expert == route, turned, 0.0), axis=0, keepdims=True)
            weighted = jnp.where(slot == targets[k], gate, weighted)
        gate_column = jnp.sum(weighted, axis=1, keepdims=True)
        for shift in range(count):
            column = jnp.broadcast_to(gate_column[shift * cap : (shift + 1) * cap], (cap, 128))
            gates_ref[shift] = jnp.zeros((8, 128), full)
            gates_ref[shift, :, 0:cap] = jnp.transpose(column)[0:8, :]
        pad = jnp.zeros((6, rows), full)
        target_rows = jnp.concatenate([targets[0], targets[1], pad], axis=0)
        target_rows = jnp.concatenate([target_rows] + [jnp.zeros((120, rows), full)], axis=0)
        targets_ref[...] = jnp.transpose(target_rows)

        gather.finish()
        for copy in keep + grad_copies:
            copy.wait()

    stream_shape = (size, rows, width)
    any_space = pl.BlockSpec(memory_space=pl.ANY)
    in_vmem = pl.BlockSpec(memory_space=pltpu.VMEM)
    square = (width, width)
    return pl.pallas_call(
        kernel,
        out_shape=[
            jax.ShapeDtypeStruct(stream_shape, low),
            jax.ShapeDtypeStruct(stream_shape, low),
            jax.ShapeDtypeStruct(stream_shape, low),
            jax.ShapeDtypeStruct((rows, width), full),
            jax.ShapeDtypeStruct((16, rows), full),
            jax.ShapeDtypeStruct((rows, width), full),
            jax.ShapeDtypeStruct((rows, 128), full),
            jax.ShapeDtypeStruct((rows, 128), full),
            jax.ShapeDtypeStruct((count, cap, width), low),
            jax.ShapeDtypeStruct((count, 8, 128), full),
            jax.ShapeDtypeStruct((count, cap, width), low),
        ],
        in_specs=[any_space]
        + [in_vmem] * 3
        + [pl.BlockSpec(memory_space=pltpu.SMEM)]
        + [any_space] * 4
        + [in_vmem] * 2
        + [any_space] * 2,
        out_specs=[any_space] * 3 + [in_vmem] * 7 + [any_space],
        scratch_shapes=[
            pltpu.VMEM(stream_shape, low),
            pltpu.VMEM(stream_shape, low),
            pltpu.VMEM(stream_shape, low),
            pltpu.VMEM(stream_shape, low),
            pltpu.VMEM(square, low),
            pltpu.VMEM(square, low),
            pltpu.VMEM(square, low),
            pltpu.VMEM(square, low),
            pltpu.VMEM((size * rows, 128), full),
            pltpu.VMEM((size * rows, 128), full),
            pltpu.VMEM((rows, rows), full),
            pltpu.VMEM((pairs, 2, 128, rows), full),
            pltpu.VMEM((pairs, 2, 8, rows), full),
            pltpu.VMEM((count, cap, width), low),
            pltpu.SemaphoreType.DMA((7,)),
            pltpu.SemaphoreType.DMA((1, size)),
            pltpu.SemaphoreType.DMA((1, size)),
            pltpu.SemaphoreType.DMA((count,)),
            pltpu.SemaphoreType.DMA((count,)),
            pltpu.SemaphoreType.DMA((4,)),
        ],
        compiler_params=pltpu.CompilerParams(
            collective_id=0, has_side_effects=True, vmem_limit_bytes=60 * 2**20
        ),
        cost_estimate=pl.CostEstimate(
            flops=2 * size * rows * width * width * 3 + 16 * size * rows * rows * width,
            bytes_accessed=20 * 2**20,
            transcendentals=size * rows * rows * 12,
        ),
        name="attend",
    )(
        tokens,
        cotangent,
        previous,
        routes,
        starts,
        *weights,
        pack,
        carry,
        jnp.asarray(tables[0]),
        jnp.asarray(tables[1]),
    )


def add_into(target, source):
    rows = target.shape[0]
    piece = 96 if rows % 96 == 0 else (64 if rows % 64 == 0 else rows)

    def body(index, carried):
        part = pl.ds(pl.multiple_of(index * piece, piece), piece)
        total = target[part, :].astype(jnp.float32) + source[part, :].astype(jnp.float32)
        target[part, :] = total.astype(target.dtype)
        return carried

    lax.fori_loop(0, rows // piece, body, 0)


def column_of(values, index):
    return values[:, index : index + 1]


def backward_layer(
    tokens,
    cotangent,
    previous,
    routes,
    starts,
    forward,
    returns,
    weights,
    pack,
    terms,
    first,
    ranks,
    cap,
    size,
    shares,
):
    rows, width = tokens.shape
    count = ranks[0] * ranks[1]
    slots = count * cap
    pairs = width // 128
    tables = rope_tables(size * rows)
    low, full = jnp.bfloat16, jnp.float32
    experts = previous.shape[0]
    copy_index = count + 1
    stat_rows = 16
    kinds = len(terms)

    def kernel(
        tokens_ref,
        cotangent_ref,
        previous_ref,
        routes_ref,
        starts_ref,
        attended_ref,
        lse_ref,
        middle_ref,
        probs_ref,
        targets_ref,
        queries_hbm,
        keys_hbm,
        values_hbm,
        back_ref,
        produced_hbm,
        dots_ref,
        query_hbm,
        key_hbm,
        value_hbm,
        output_hbm,
        pack_ref,
        cosine_hbm,
        sine_hbm,
        *rest,
    ):
        term_refs, first_hbm, rest = rest[:kinds], rest[kinds], rest[kinds + 1 :]
        result_ref, token_grads_ref, wide_ref, small_ref = rest[:4]
        first_refs, rest = rest[4 : 4 + kinds], rest[4 + kinds :]
        (
            queries,
            keys,
            values,
            query_w,
            key_w,
            value_w,
            output_w,
            cosine,
            sine,
            bias,
            out_grads,
            stats,
            outputs,
            middle_grad,
            query_total,
            key_total,
            value_total,
            load_sem,
            gather_send,
            gather_recv,
            first_send,
            first_recv,
            out_send,
            out_recv,
            out_keep,
            sum_part,
            first_part,
            sum_load,
        ) = rest
        own = lax.axis_index("ctx")
        line = pl.ds(pl.multiple_of(own * rows, rows), rows)
        loads = [
            pltpu.make_async_copy(source, target, load_sem.at[index])
            for index, (source, target) in enumerate(
                (
                    (output_hbm, output_w),
                    (queries_hbm, queries),
                    (keys_hbm, keys),
                    (values_hbm, values),
                    (cosine_hbm.at[line], cosine),
                    (sine_hbm.at[line], sine),
                    (query_hbm, query_w),
                    (key_hbm, key_w),
                    (value_hbm, value_w),
                )
            )
        ]
        for load in loads:
            load.start()
        share = lax.axis_index("dp")
        sum_loads = [
            pltpu.make_async_copy(
                term_refs[0].at[jnp.bitwise_xor(share, shares - 2)], sum_part, sum_load.at[0]
            ),
            pltpu.make_async_copy(first_hbm, first_part, sum_load.at[1]),
        ]
        for copy in sum_loads:
            copy.start()
        greet_places(
            [(0,) + place for place in places_of(ranks, size)] + [(1, 0, 0), (2, 0, 0)]
        )
        first_copies = [
            pltpu.make_async_remote_copy(
                src_ref=(
                    term_refs[kind].at[jnp.bitwise_xor(share, shares - 1)] if kind else sum_part
                ),
                dst_ref=first_refs[kind],
                send_sem=first_send.at[kind],
                recv_sem=first_recv.at[kind],
                device_id=peer_at(1 if kind else 2, 0, 0),
                device_id_type=pl.DeviceIdType.MESH,
            )
            for kind in range(kinds)
        ]
        for copy in first_copies[1:]:
            copy.start()
        for copy in sum_loads:
            copy.wait()
        add_into(sum_part, first_part)
        first_copies[0].start()
        output_copies = [
            send_block(produced_hbm, outputs, shift, ranks, out_send, out_recv)
            for shift in range(1, count)
        ]
        output_copies.append(pltpu.make_async_copy(produced_hbm.at[0], outputs.at[0], out_keep))

        def keep_wide(index, value):
            half = width // 2
            for part in range(2):
                wide_ref[part, index * width : (index + 1) * width, :] = value[
                    :, part * half : (part + 1) * half
                ].astype(low)

        lane = lax.broadcasted_iota(jnp.int32, (rows, 128), 1)
        upstream = cotangent_ref[...].astype(full)
        middle = middle_ref[...]
        inverse_second = inverse_norm(middle)
        unit_second = middle * inverse_second
        gain_second = pack_ref[HEAD_ROWS + 1 : HEAD_ROWS + 2, :].astype(full)
        second = unit_second * gain_second
        second_low = second.astype(low)
        heads_in = jnp.concatenate(
            [pack_ref[0:HEAD_ROWS, :], jnp.zeros((128 - HEAD_ROWS, width), low)], axis=0
        )
        mixed = dot_nt(second_low, heads_in)
        probs = probs_ref[...]
        route_rows = jnp.concatenate(
            [routes_ref[...].astype(full), jnp.zeros((126, rows), full)], axis=0
        )
        route_columns = jnp.transpose(route_rows).astype(jnp.int32)
        route = [column_of(route_columns, k) for k in range(2)]
        chosen = jnp.logical_or(lane == route[0], lane == route[1])
        gates = jnp.where(chosen, probs, 0.0)
        target = [column_of(targets_ref[...], k) for k in range(2)]

        gate_grad = jnp.zeros((rows, 128), full)
        place = lane.astype(full)
        for k in range(2):
            found = jnp.zeros((rows, 128), full)
            for shift in range(count):
                found = found + jnp.where(
                    jnp.logical_and(target[k] - shift * cap == place, lane < cap),
                    dots_ref[shift, 0:1, :],
                    0.0,
                )
            gate_grad = gate_grad + jnp.where(
                lane == route[k], jnp.sum(found, axis=1, keepdims=True), 0.0
            )
        copy_grad = jnp.sum(upstream * second, axis=1, keepdims=True)
        gate_grad = jnp.where(lane == copy_index, copy_grad, gate_grad)
        direct = column_of(gates, copy_index)
        constants = []
        for index in range(2):
            vector = pack_ref[HEAD_ROWS + 2 + index : HEAD_ROWS + 3 + index, :].astype(full)
            vector_dot = jnp.sum(upstream * vector, axis=1, keepdims=True)
            begin = experts + 2 * index
            spread_of = column_of(mixed, begin + 1) - column_of(mixed, begin)
            mixing = (1.0 / (1.0 + jnp.exp(spread_of)), 1.0 / (1.0 + jnp.exp(-spread_of)))
            gate = column_of(gates, copy_index + 1 + index)
            term = mixing[0] * copy_grad + mixing[1] * vector_dot
            gate_grad = jnp.where(lane == copy_index + 1 + index, term, gate_grad)
            direct = direct + gate * mixing[0]
            constants.append((gate, mixing, vector, vector_dot))
        prob_grad = jnp.where(chosen, gate_grad, 0.0)
        logit_grad = probs * (prob_grad - jnp.sum(probs * prob_grad, axis=1, keepdims=True))
        head_grad = logit_grad
        for index, (gate, mixing, vector, vector_dot) in enumerate(constants):
            mixing_grad = (gate * copy_grad, gate * vector_dot)
            mean = mixing[0] * mixing_grad[0] + mixing[1] * mixing_grad[1]
            for part in range(2):
                head_grad = jnp.where(
                    lane == experts + 2 * index + part,
                    mixing[part] * (mixing_grad[part] - mean),
                    head_grad,
                )
        head_low = head_grad.astype(low)

        slot = lax.broadcasted_iota(jnp.int32, (rows, slots), 1).astype(full)
        picked = [(slot == target[k]).astype(full).astype(low) for k in range(2)]
        second_grad = (
            dot(head_low, heads_in) + direct * upstream + dot(picked[0] + picked[1], back_ref[...])
        )
        normal_grad = second_grad * gain_second
        middle_total = upstream + inverse_second * (
            normal_grad - unit_second * jnp.mean(normal_grad * unit_second, axis=1, keepdims=True)
        )
        middle_grad[...] = middle_total
        middle_low = middle_total.astype(low)
        loads[0].wait()
        out_grad = dot_nt(middle_low, output_w[...]).astype(low)
        out_grads[own] = out_grad
        product = out_grad.astype(full) * attended_ref[...]
        masks = head_masks(rows)
        deltas = jnp.zeros((rows, 128), full)
        for index in range(pairs):
            part = product[:, index * 128 : index * 128 + 128]
            for head in range(2):
                total = jnp.sum(jnp.where(masks[head], part, 0.0), axis=1, keepdims=True)
                deltas = jnp.where(lane == 2 * index + head, total, deltas)
        stats[own, 0:stat_rows] = lse_ref[...]
        stats[own, stat_rows:] = jnp.transpose(deltas)[0:stat_rows]
        gather = Gather([out_grads, stats], size, gather_send, gather_recv)
        gather.forward(0)
        for copy in output_copies:
            copy.start()

        chosen_out = second * direct
        for gate, mixing, vector, vector_dot in constants:
            chosen_out = chosen_out + gate * mixing[1] * vector
        base = middle + chosen_out
        small_ref[...] = jnp.zeros_like(small_ref)
        small_ref[1:2, :] = jnp.sum(second_grad * unit_second, axis=0, keepdims=True)
        for index, (gate, mixing, vector, vector_dot) in enumerate(constants):
            small_ref[2 + index : 3 + index, :] = jnp.sum(
                gate * mixing[1] * upstream, axis=0, keepdims=True
            )
        small_ref[8:24, :] = dot_tn(head_low, second_low)[0:16]
        carry_grad = lax.dot_general(
            jnp.transpose(logit_grad)[0:16],
            previous_ref[...],
            (((1,), (1,)), ((), ())),
            precision=HIGH,
        )
        small_ref[24:40, 0:experts] = carry_grad
        keep_wide(3, dot_tn(attended_ref[...].astype(low), middle_low))

        for load in loads[1:4]:
            load.wait()
        query_total[...] = jnp.zeros_like(query_total)
        key_total[...] = jnp.zeros_like(key_total)
        value_total[...] = jnp.zeros_like(value_total)
        column = lax.broadcasted_iota(jnp.int32, (rows, rows), 0)
        row = lax.broadcasted_iota(jnp.int32, (rows, rows), 1)

        def block_side(block, as_query, as_key):
            key_block, query_block = (own if as_key else block), (own if as_query else block)
            key_pos, query_pos = key_block * rows + column, query_block * rows + row
            first = start_of(query_pos[0:8], starts_ref)[0:1]
            allowed = jnp.logical_and(key_pos >= first, key_pos <= query_pos)
            bias[...] = jnp.where(allowed, 0.0, NEGATIVE)

            def pair(index, carried):
                lanes = pl.ds(pl.multiple_of(index * 128, 128), 128)
                query, grad = queries[query_block, :, lanes], out_grads[query_block, :, lanes]
                key, value = keys[key_block, :, lanes], values[key_block, :, lanes]
                one_key = [jnp.where(mask, key, 0) for mask in masks]
                scores = [dot_nt(one_key[head], query) for head in range(2)]
                weight_grad = [dot_nt(jnp.where(mask, value, 0), grad) for mask in masks]
                weight, score = [], []
                for head in range(2):
                    lse = stats[query_block, pl.ds(2 * index + head, 1), :]
                    mean = stats[query_block, pl.ds(stat_rows + 2 * index + head, 1), :]
                    weight.append(jnp.exp(scores[head] + bias[...] - lse))
                    score.append((weight[head] * (weight_grad[head] - mean)).astype(low))
                if as_key:
                    value_total[:, lanes] += dot(
                        weight[0].astype(low), jnp.where(masks[0], grad, 0)
                    ) + dot(weight[1].astype(low), jnp.where(masks[1], grad, 0))
                    key_total[:, lanes] += dot(score[0], jnp.where(masks[0], query, 0)) + dot(
                        score[1], jnp.where(masks[1], query, 0)
                    )
                if as_query:
                    query_total[lanes, :] += dot_tn(one_key[0], score[0]) + dot_tn(
                        one_key[1], score[1]
                    )
                return carried

            lax.fori_loop(0, pairs, pair, 0)

        block_side(own, True, True)
        for place in range(1, size):
            block = jnp.bitwise_xor(own, place)

            @pl.when(block < own)
            def _():
                block_side(block, True, False)

        for place in range(1, size):
            gather.arrive(place)
            block = jnp.bitwise_xor(own, place)

            @pl.when(block > own)
            def _():
                block_side(block, False, True)

        for load in loads[4:]:
            load.wait()
        inputs = tokens_ref[...].astype(full)
        inverse_first = inverse_norm(inputs)
        unit_first = inputs * inverse_first
        gain_first = pack_ref[HEAD_ROWS : HEAD_ROWS + 1, :].astype(full)
        normed = (unit_first * gain_first).astype(low)
        turn = -sine[...]
        query_grad = jnp.transpose(query_total[...]) * HEAD_DIM**-0.5
        query_low = rotate(query_grad, cosine[...], turn).astype(low)
        key_low = rotate(key_total[...], cosine[...], turn).astype(low)
        value_low = value_total[...].astype(low)
        first_grad = (
            dot_nt(query_low, query_w[...])
            + dot_nt(key_low, key_w[...])
            + dot_nt(value_low, value_w[...])
        )
        for index, part in enumerate((query_low, key_low, value_low)):
            keep_wide(index, dot_tn(normed, part))
        small_ref[0:1, :] = jnp.sum(first_grad * unit_first, axis=0, keepdims=True)
        normal_grad = first_grad * gain_first
        token_grads_ref[...] = middle_grad[...] + inverse_first * (
            normal_grad - unit_first * jnp.mean(normal_grad * unit_first, axis=1, keepdims=True)
        )
        for copy in output_copies:
            copy.wait()
        for k in range(2):
            weight = jnp.sum(jnp.where(lane == route[k], probs, 0.0), axis=1, keepdims=True)
            base = base + weight * dot(picked[k], outputs[...].reshape(slots, width))
        result_ref[...] = base.astype(low)
        gather.finish()
        for copy in first_copies:
            copy.wait()

    stream_shape = (size, rows, width)
    any_space = pl.BlockSpec(memory_space=pl.ANY)
    in_vmem = pl.BlockSpec(memory_space=pltpu.VMEM)
    square = (width, width)
    return pl.pallas_call(
        kernel,
        out_shape=[
            jax.ShapeDtypeStruct((rows, width), low),
            jax.ShapeDtypeStruct((rows, width), full),
            jax.ShapeDtypeStruct((2, 4 * width, width // 2), low),
            jax.ShapeDtypeStruct((64, width), full),
        ]
        + [jax.ShapeDtypeStruct(term.shape[1:], low) for term in terms],
        in_specs=[in_vmem] * 4
        + [pl.BlockSpec(memory_space=pltpu.SMEM)]
        + [in_vmem] * 5
        + [any_space] * 3
        + [in_vmem, any_space, in_vmem]
        + [any_space] * 4
        + [in_vmem]
        + [any_space] * (3 + kinds),
        out_specs=[in_vmem] * 4 + [any_space] * kinds,
        scratch_shapes=[
            pltpu.VMEM(stream_shape, low),
            pltpu.VMEM(stream_shape, low),
            pltpu.VMEM(stream_shape, low),
            pltpu.VMEM(square, low),
            pltpu.VMEM(square, low),
            pltpu.VMEM(square, low),
            pltpu.VMEM(square, low),
            pltpu.VMEM((rows, 128), full),
            pltpu.VMEM((rows, 128), full),
            pltpu.VMEM((rows, rows), full),
            pltpu.VMEM(stream_shape, low),
            pltpu.VMEM((size, 2 * stat_rows, rows), full),
            pltpu.VMEM((count, cap, width), low),
            pltpu.VMEM((rows, width), full),
            pltpu.VMEM((width, rows), full),
            pltpu.VMEM((rows, width), full),
            pltpu.VMEM((rows, width), full),
            pltpu.SemaphoreType.DMA((9,)),
            pltpu.SemaphoreType.DMA((2, size)),
            pltpu.SemaphoreType.DMA((2, size)),
            pltpu.SemaphoreType.DMA((kinds,)),
            pltpu.SemaphoreType.DMA((kinds,)),
            pltpu.SemaphoreType.DMA((count,)),
            pltpu.SemaphoreType.DMA((count,)),
            pltpu.SemaphoreType.DMA,
            pltpu.VMEM(terms[0].shape[1:], low),
            pltpu.VMEM(terms[0].shape[1:], low),
            pltpu.SemaphoreType.DMA((2,)),
        ],
        compiler_params=pltpu.CompilerParams(
            collective_id=2, has_side_effects=True, vmem_limit_bytes=60 * 2**20
        ),
        cost_estimate=pl.CostEstimate(
            flops=14 * rows * width * width * 2 + 20 * size * rows * rows * width,
            bytes_accessed=30 * 2**20,
            transcendentals=size * rows * rows * 12,
        ),
        name="backward",
    )(
        tokens,
        cotangent,
        previous,
        routes,
        starts,
        *forward,
        *returns,
        *weights,
        pack,
        jnp.asarray(tables[0]),
        jnp.asarray(tables[1]),
        *terms,
        first,
    )


PIECES = 2
ORDER = (
    1, 0, 3, 2, 0, 4, 0, 2, 1, 5, 0, 0, 4, 2, 4,
    4, 5, 3, 3, 0, 4, 1, 5, 3, 0, 0, 6, 5, 4, 2,
    1, 3, 2, 0, 6, 6, 3, 0, 1, 6, 5, 6, 0, 5, 6,
)
DENSE_TIMES = (7, 24, 34, 48, 62, 77, 91, 101, 118, 125, 132)
EXPERT_TIMES = (19, 14, 19, 4, 11, 2)


def halving_steps(size):
    steps, step = [], 0
    while 1 << step < size:
        bit = 1 << step
        steps += [(step, place) for place in range(size - bit, 0, -2 * bit)]
        step += 1
    return steps


def needed_before(step, place):
    return {(earlier, place | 1 << earlier) for earlier in range(step)}


def reduce_layer(terms, firsts, wide, small, spread, shares, ring, exchange_size):
    low, full = jnp.bfloat16, jnp.float32
    steps = halving_steps(shares)
    done = [[(0, shares - 1), (1, shares - 2)]] + [[(0, shares - 1)]] * (len(terms) - 1)
    kinds = len(terms)
    blocks = [term.shape[1:] for term in terms]
    members = ring // spread
    groups = 3
    near_bits = [1 << step for step in range(ring.bit_length() - 1)]
    far_bits = [1 << step for step in range(exchange_size.bit_length() - 1)]
    deep_bits = [1 << step for step in range(shares.bit_length() - 1)]
    near = [(0, 0, bit) for bit in near_bits]
    far = [(0, bit, 0) for bit in far_bits]
    deep = [(bit, 0, 0) for bit in deep_bits]
    orders = [near + far + deep, near[:1] + far + near[1:] + deep, near + far + deep]
    places = near + far + deep
    bit_count = len(places)
    group_rows = [wide.shape[1], wide.shape[1], small.shape[0]]
    tile = [16, 16, 8]
    plans = []
    for group in range(groups):
        length, plan = group_rows[group], []
        for _ in range(bit_count):
            halved = (length // 2) % tile[group] == 0
            length = length // 2 if halved else length
            plan.append((halved, length))
        plans.append(plan)

    def kernel(*refs):
        refs = list(refs)

        def take(number):
            taken = refs[:number]
            del refs[:number]
            return taken

        term_refs, first_refs = take(kinds), take(kinds)
        (wide_hbm, small_hbm) = take(2)
        gathered = take(kinds)
        (wide_out, small_out) = take(2)
        sums, landed = take(kinds), take(kinds)
        (halves, smalls) = take(2)
        group_landed = take(groups)
        (load_sem, step_send, step_recv, own_sem, ring_send, ring_recv) = take(6)
        (dense_send, dense_recv, dense_load) = take(3)
        share = lax.axis_index("dp")
        mine = lax.axis_index("ctx") // spread

        dense_in = [
            pltpu.make_async_copy(wide_hbm, halves, dense_load.at[0]),
            pltpu.make_async_copy(small_hbm, smalls, dense_load.at[1]),
        ]
        for copy in dense_in:
            copy.start()
        loads = []
        for kind in range(kinds):
            copies = [
                pltpu.make_async_copy(
                    first_refs[kind],
                    landed[kind].at[steps.index(done[kind][-1])],
                    load_sem.at[kind, shares // 2],
                )
            ]
            for place in range(shares - 2, -1, -2):
                copies.append(
                    pltpu.make_async_copy(
                        term_refs[kind].at[jnp.bitwise_xor(share, place)],
                        sums[kind].at[place // 2],
                        load_sem.at[kind, place // 2],
                    )
                )
            for copy in copies:
                copy.start()
            loads.append(copies)
        greet_places(places)

        def expert_chain(kind, piece):
            period, odd_wait, even_wait, near_wait, far_wait, last_wait = EXPERT_TIMES
            begin = time = period * (kind * PIECES + piece)
            slots = {step: index for index, step in enumerate(steps)}
            lines = blocks[kind][0] // PIECES
            window = pl.ds(piece * lines, lines)
            one = kind * PIECES + piece

            def transfer(step, place):
                index = slots[step, place]
                if place % 2 == 1:
                    source = term_refs[kind].at[jnp.bitwise_xor(share, place), window]
                else:
                    source = sums[kind].at[place // 2, window]
                return pltpu.make_async_remote_copy(
                    src_ref=source,
                    dst_ref=landed[kind].at[index, window],
                    send_sem=step_send.at[one, index],
                    recv_sem=step_recv.at[one, index],
                    device_id=peer_at(1 << step, 0, 0),
                    device_id_type=pl.DeviceIdType.MESH,
                )

            yield begin
            while loads[kind]:
                loads[kind].pop().wait()
            step, place = done[kind][-1]
            add_into(
                sums[kind].at[(place ^ 1 << step) // 2, window],
                landed[kind].at[slots[step, place], window],
            )
            arrived, started = set(done[kind]), []
            waiting = [op for op in steps if op not in arrived]
            while True:
                for op in list(waiting):
                    if needed_before(*op) <= arrived:
                        transfer(*op).start()
                        started.append(op)
                        waiting.remove(op)
                if not started:
                    break
                op = started.pop(0)
                yield time + (even_wait if op[0] else odd_wait)
                transfer(*op).wait()
                arrived.add(op)
                add_into(
                    sums[kind].at[(op[1] ^ 1 << op[0]) // 2, window],
                    landed[kind].at[slots[op], window],
                )
            time += even_wait
            index = len(steps)
            bit = 1
            while bit < spread:
                copy = pltpu.make_async_remote_copy(
                    src_ref=sums[kind].at[0, window],
                    dst_ref=landed[kind].at[index, window],
                    send_sem=step_send.at[one, index],
                    recv_sem=step_recv.at[one, index],
                    device_id=peer_at(0, 0, bit),
                    device_id_type=pl.DeviceIdType.MESH,
                )
                copy.start()
                time += near_wait
                yield time
                copy.wait()
                add_into(sums[kind].at[0, window], landed[kind].at[index, window])
                index += 1
                bit *= 2
            keep = pltpu.make_async_copy(
                sums[kind].at[0, window], gathered[kind].at[mine, window], own_sem.at[one]
            )
            keep.start()
            sent = []

            def pass_on(place, bit):
                block = jnp.bitwise_xor(mine, place)
                target = gathered[kind].at[block, window]
                return pltpu.make_async_remote_copy(
                    src_ref=sums[kind].at[0, window] if place == 0 else target,
                    dst_ref=target,
                    send_sem=ring_send.at[one, place ^ bit],
                    recv_sem=ring_recv.at[one, place ^ bit],
                    device_id=peer_at(0, 0, bit * spread),
                    device_id_type=pl.DeviceIdType.MESH,
                )

            def forward(place):
                for bit, held in gather_steps(members):
                    if place in held:
                        copy = pass_on(place, bit)
                        copy.start()
                        sent.append(copy)

            forward(0)
            for place in range(1, members):
                wait = near_wait if place == 1 else far_wait if place & (place - 1) == 0 else last_wait
                yield time + wait + (far_wait if wait == last_wait else 0)
                bit = place & -place
                pass_on(place ^ bit, bit).wait_recv()
                forward(place)
            yield 1000
            keep.wait()
            for copy in sent:
                copy.wait_send()

        def bit_of(place):
            deep_bit, far_bit, near_bit = place
            axis, bit = ("dp", deep_bit) if deep_bit else ("exp", far_bit) if far_bit else ("ctx", near_bit)
            return lax.rem(lax.axis_index(axis) // bit, 2)

        def dense_chain(times):
            times = iter(times + tuple(range(times[-1] + 8, 900, 8)))
            buffers = [halves.at[0], halves.at[1], smalls]
            yield 0
            for copy in dense_in:
                copy.wait()
            begins = [0] * groups
            trail = []

            def window(begin, length, group):
                if isinstance(begin, int):
                    return pl.ds(begin, length)
                return pl.ds(pl.multiple_of(begin, tile[group]), length)

            def exchange_rows(group, step, source, target):
                return pltpu.make_async_remote_copy(
                    src_ref=source,
                    dst_ref=target,
                    send_sem=dense_send.at[group, step],
                    recv_sem=dense_recv.at[group, step],
                    device_id=peer_at(*orders[group][step % bit_count]),
                    device_id_type=pl.DeviceIdType.MESH,
                )

            for step in range(bit_count):
                copies = []
                for group in range(groups):
                    halved, length = plans[group][step]
                    upper = bit_of(orders[group][step])
                    if halved:
                        sent = begins[group] + (1 - upper) * length
                        begins[group] = begins[group] + upper * length
                    else:
                        sent = begins[group]
                    at = sum(size for _, size in plans[group][:step])
                    copy = exchange_rows(
                        group,
                        step,
                        buffers[group].at[window(sent, length, group)],
                        group_landed[group].at[pl.ds(at, length)],
                    )
                    copy.start()
                    copies.append((copy, at, length))
                trail.append(list(begins))
                yield next(times)
                for group, (copy, at, length) in enumerate(copies):
                    copy.wait()
                    add_into(
                        buffers[group].at[window(begins[group], length, group)],
                        group_landed[group].at[pl.ds(at, length)],
                    )
            outputs = [wide_out.at[0], wide_out.at[1], small_out]
            keeps = []
            for group in range(groups):
                part = window(begins[group], plans[group][-1][1], group)
                keep = pltpu.make_async_copy(
                    buffers[group].at[part], outputs[group].at[part], dense_load.at[group]
                )
                keep.start()
                keeps.append(keep)
            for keep in keeps:
                keep.wait()
            for step in range(bit_count - 1, -1, -1):
                copies = []
                for group in range(groups):
                    halved, length = plans[group][step]
                    if halved:
                        part = outputs[group].at[window(trail[step][group], length, group)]
                        copy = exchange_rows(group, bit_count + step, part, part)
                        copy.start()
                        copies.append(copy)
                if copies:
                    yield next(times)
                for copy in copies:
                    copy.wait()

        chains = [dense_chain(DENSE_TIMES)] + [
            expert_chain(kind, piece) for kind in range(kinds) for piece in range(PIECES)
        ]
        due = dict(enumerate(next(chain) for chain in chains))
        planned = list(ORDER) if (shares, ring, exchange_size) == (4, 4, 2) else []
        while due:
            index = planned.pop(0) if planned else min(due, key=lambda one: (due[one], one))
            time = next(chains[index], None)
            if time is None:
                del due[index]
            else:
                due[index] = time

    any_space = pl.BlockSpec(memory_space=pl.ANY)
    extra = len(steps) + spread.bit_length() - 1
    return pl.pallas_call(
        kernel,
        out_shape=[jax.ShapeDtypeStruct((members,) + block, low) for block in blocks]
        + [jax.ShapeDtypeStruct(wide.shape, low), jax.ShapeDtypeStruct(small.shape, full)],
        in_specs=[any_space] * (2 * kinds + 2),
        out_specs=[any_space] * (kinds + 2),
        scratch_shapes=[pltpu.VMEM((shares // 2,) + block, low) for block in blocks]
        + [pltpu.VMEM((extra,) + block, low) for block in blocks]
        + [pltpu.VMEM(wide.shape, low), pltpu.VMEM(small.shape, full)]
        + [
            pltpu.VMEM(
                (sum(length for _, length in plans[group]), (wide, wide, small)[group].shape[-1]),
                (low, low, full)[group],
            )
            for group in range(groups)
        ]
        + [
            pltpu.SemaphoreType.DMA((kinds, shares // 2 + 1)),
            pltpu.SemaphoreType.DMA((kinds * PIECES, extra)),
            pltpu.SemaphoreType.DMA((kinds * PIECES, extra)),
            pltpu.SemaphoreType.DMA((kinds * PIECES,)),
            pltpu.SemaphoreType.DMA((kinds * PIECES, members)),
            pltpu.SemaphoreType.DMA((kinds * PIECES, members)),
            pltpu.SemaphoreType.DMA((groups, 2 * bit_count)),
            pltpu.SemaphoreType.DMA((groups, 2 * bit_count)),
            pltpu.SemaphoreType.DMA((3,)),
        ],
        compiler_params=pltpu.CompilerParams(
            collective_id=3, has_side_effects=True, vmem_limit_bytes=60 * 2**20
        ),
        name="reduce",
    )(*terms, *firsts, wide, small)


def widen_layer(parts, wide, small, experts):
    members = parts[0].shape[0]
    pieces = 4
    steps = members * pieces
    squares = wide.shape[1] // (2 * wide.shape[2])
    width = 2 * wide.shape[2]
    lines = wide.shape[1] // steps
    turns = width // lines
    full = jnp.float32
    kinds = len(parts)

    def kernel(*refs):
        sources, wide_ref, small_ref = refs[:kinds], refs[kinds], refs[kinds + 1]
        targets = refs[kinds + 2 : 2 * kinds + 2]
        square_refs = refs[2 * kinds + 2 : 2 * kinds + 2 + squares]
        head_ref, map_ref, carry_ref, vector_ref, gains_ref = refs[2 * kinds + 2 + squares :]
        step = pl.program_id(0) * pieces + pl.program_id(1)
        for source, target in zip(sources, targets):
            target[...] = source[...].astype(full)
        for index in range(squares):

            @pl.when(step // turns == index)
            def _():
                square_refs[index][:, 0 : width // 2] = wide_ref[0].astype(full)
                square_refs[index][:, width // 2 :] = wide_ref[1].astype(full)

        @pl.when(step == 0)
        def _():
            head_ref[...] = small_ref[8 : 8 + experts, :]
            for index in range(2):
                begin = 8 + experts + 2 * index
                map_ref[index] = small_ref[begin : begin + 2, :]
            carry_ref[...] = jnp.transpose(small_ref[24:40, 0:128])[0:experts, 0:experts]
            vector_ref[...] = small_ref[2:4, :]
            gains_ref[...] = small_ref[0:2, :]

    def chunk(part):
        return pl.BlockSpec(
            (1, part.shape[1] // pieces, part.shape[2]), lambda member, piece: (member, piece, 0)
        )

    def square(index):
        return pl.BlockSpec(
            (lines, width),
            lambda member, piece: (
                jnp.clip(member * pieces + piece - index * turns, 0, turns - 1),
                0,
            ),
        )

    def whole(*shape):
        return pl.BlockSpec(shape, lambda member, piece: (0,) * len(shape))

    smalls = [(experts, width), (2, 2, width), (experts, experts), (2, width), (2, width)]
    return pl.pallas_call(
        kernel,
        out_shape=[jax.ShapeDtypeStruct(part.shape, full) for part in parts]
        + [jax.ShapeDtypeStruct((width, width), full)] * squares
        + [jax.ShapeDtypeStruct(shape, full) for shape in smalls],
        grid=(members, pieces),
        in_specs=[chunk(part) for part in parts]
        + [
            pl.BlockSpec(
                (2, lines, width // 2), lambda member, piece: (0, member * pieces + piece, 0)
            ),
            whole(*small.shape),
        ],
        out_specs=[chunk(part) for part in parts]
        + [square(index) for index in range(squares)]
        + [whole(*shape) for shape in smalls],
        compiler_params=pltpu.CompilerParams(vmem_limit_bytes=48 * 2**20),
        name="widen",
    )(*parts, wide, small)


def local(
    tokens,
    cotangent,
    previous,
    routes,
    boundaries,
    norm_first,
    query_weight,
    key_weight,
    value_weight,
    output_weight,
    norm_second,
    router,
    gate_carry,
    constant_map,
    constant_vector,
    expert_gate,
    expert_linear,
    expert_down,
):
    model_width = tokens.shape[2]
    ring = lax.axis_size("ctx")
    group_size = expert_gate.shape[0]
    exchange_count = lax.axis_size("exp")
    spread = ring // group_size
    ranks = (exchange_count, group_size, spread)
    slot_total = exchange_count * group_size * CAP
    expert_total = router.shape[1]
    pack = jnp.concatenate(
        [
            router.T,
            constant_map[0].T,
            constant_map[1].T,
            norm_first[None],
            norm_second[None],
            constant_vector,
        ],
        axis=0,
    )
    pack = jnp.pad(pack, ((0, 32 - pack.shape[0]), (0, 0)))
    weights = (query_weight, key_weight, value_weight, output_weight)
    (
        queries,
        keys,
        values,
        attended,
        lse,
        middle,
        probs,
        targets,
        outgoing,
        slot_gates,
        grads_in,
    ) = attend_layer(
        tokens[0],
        cotangent[0],
        previous[0].T,
        routes[0].T,
        boundaries,
        weights,
        pack,
        gate_carry,
        ranks,
        CAP,
        ring,
    )
    home_grads, produced, dots, gate_terms, linear_terms, down_terms, first = expert_layer(
        outgoing,
        slot_gates,
        grads_in.reshape(slot_total, model_width),
        (expert_gate, expert_linear, expert_down),
        ranks,
        lax.axis_size("dp"),
    )
    terms = (down_terms, gate_terms, linear_terms)
    shares = lax.axis_size("dp")
    result, token_grads, wide, small, *firsts = backward_layer(
        tokens[0],
        cotangent[0],
        previous[0].T,
        routes[0].T,
        boundaries,
        (attended, lse, middle, probs, targets, queries, keys, values),
        (home_grads.reshape(slot_total, model_width), produced, dots),
        weights,
        pack,
        terms,
        first,
        ranks,
        CAP,
        ring,
        shares,
    )
    *parts, wide, small = reduce_layer(
        terms, firsts, wide, small, spread, shares, ring, exchange_count
    )
    (
        down_grads,
        gate_grads,
        linear_grads,
        query_grads,
        key_grads,
        value_grads,
        output_grads,
        router_grads,
        map_grads,
        carry_grads,
        vector_grads,
        gain_grads,
    ) = widen_layer(parts, wide, small, expert_total)
    return (
        result[None],
        token_grads[None],
        gain_grads[0],
        query_grads,
        key_grads,
        value_grads,
        output_grads,
        gain_grads[1],
        router_grads.T,
        carry_grads,
        jnp.transpose(map_grads, (0, 2, 1)),
        vector_grads,
        gate_grads,
        linear_grads,
        down_grads,
    )


def solution(mesh):
    return jax.shard_map(
        local,
        mesh=mesh,
        in_specs=(
            P(("dp", "exp"), "ctx", None),
            P(("dp", "exp"), "ctx", None),
            P(("dp", "exp"), "ctx", None),
            P(("dp", "exp"), "ctx", None),
            P(("dp", "exp"), None),
            P(),
            P(),
            P(),
            P(),
            P(),
            P(),
            P(),
            P(),
            P(),
            P(),
            P("exp", None, None),
            P("exp", None, None),
            P("exp", None, None),
        ),
        out_specs=(
            P(("dp", "exp"), "ctx", None),
            P(("dp", "exp"), "ctx", None),
            P(),
            P(),
            P(),
            P(),
            P(),
            P(),
            P(),
            P(),
            P(),
            P(),
            P("exp", None, "dp"),
            P("exp", None, "dp"),
            P("exp", "dp", None),
        ),
        check_vma=False,
    )
```

```python
import math

import jax
import jax.numpy as jnp
import numpy as np
from jax import lax
from jax.experimental import pallas as pl
from jax.experimental.pallas import tpu as pltpu
from jax.sharding import PartitionSpec as P

HEAD_DIM = 64
CAP = 96


EPSILON = 1e-06
NEGATIVE = -1e30
HIGH = lax.Precision.HIGHEST


HEAD_ROWS = 16


def mesh_id(exp_index, ctx_index):
    return {"exp": exp_index, "ctx": ctx_index}


def dot(left, right):
    return jnp.dot(left, right, preferred_element_type=jnp.float32)


def dot_nt(left, right):
    return lax.dot_general(
        left, right, (((1,), (1,)), ((), ())), preferred_element_type=jnp.float32
    )


def dot_tn(left, right):
    return lax.dot_general(
        left, right, (((0,), (0,)), ((), ())), preferred_element_type=jnp.float32
    )


def member_of(shift, ranks):
    exchange_size, group_size, spread = ranks
    exp_index, ctx_index = lax.axis_index("exp"), lax.axis_index("ctx")
    far, near = shift // group_size, shift % group_size
    place = jnp.bitwise_xor(ctx_index // spread, near) * spread + lax.rem(ctx_index, spread)
    return mesh_id(jnp.bitwise_xor(exp_index, far), place)


def greet(count, ranks):
    barrier = pltpu.get_barrier_semaphore()
    for shift in range(1, count):
        pl.semaphore_signal(
            barrier, inc=1, device_id=member_of(shift, ranks), device_id_type=pl.DeviceIdType.MESH
        )
    pl.semaphore_wait(barrier, count - 1)


def block_of(shift, count):
    return (shift + count - count // 4) % count


def own_block(count):
    return block_of(0, count)


def send_block(source, target, block, ranks, send_sem, recv_sem):
    count = ranks[0] * ranks[1]
    return pltpu.make_async_remote_copy(
        src_ref=source.at[block],
        dst_ref=target.at[block],
        send_sem=send_sem.at[block],
        recv_sem=recv_sem.at[block],
        device_id=member_of((block + count // 4) % count, ranks),
        device_id_type=pl.DeviceIdType.MESH,
    )


def keep_block(source, target, count, sem):
    block = own_block(count)
    return pltpu.make_async_copy(source.at[block], target.at[block], sem)


def other_blocks(count):
    return [block for block in range(count) if block != own_block(count)]


def expert_layer(outgoing, gates, grads, weights, ranks, shares):
    count, cap, width = outgoing.shape
    hidden_units = weights[0].shape[2]
    rows = count * cap
    share = hidden_units // shares
    spread = ranks[2]

    def kernel(
        outgoing_hbm,
        gates_ref,
        grads_ref,
        gate_hbm,
        linear_hbm,
        down_hbm,
        back_ref,
        output_ref,
        dots_ref,
        gate_terms,
        linear_terms,
        down_terms,
        first_ref,
        received,
        received_gates,
        gate_w,
        linear_w,
        down_w,
        hidden_grad,
        hidden,
        gate_low,
        linear_low,
        rows_t,
        scaled,
        gate_column,
        out_total,
        in_total,
        in_send,
        dots_send,
        terms,
        weight_sem,
        send_sem,
        recv_sem,
        local_sem,
        terms_sem,
        first_send,
        first_recv,
    ):
        own = lax.axis_index("ctx") // spread
        loads = [
            pltpu.make_async_copy(source.at[own], target, weight_sem.at[index])
            for index, (source, target) in enumerate(
                ((down_hbm, down_w), (gate_hbm, gate_w), (linear_hbm, linear_w))
            )
        ]
        for load in loads:
            load.start()
        greet_places([(0,) + place for place in group_places(ranks)] + [(1, 0, 0)])

        def send_some(source, target, index, shifts):
            copies = []
            for shift in shifts:
                if shift == own_block(count):
                    copies.append(keep_block(source, target, count, local_sem.at[index]))
                else:
                    copies.append(
                        send_block(
                            source, target, shift, ranks, send_sem.at[index], recv_sem.at[index]
                        )
                    )
            for copy in copies:
                copy.start()
            return copies

        every = range(count)
        gates_in = send_some(gates_ref, received_gates, 0, every)
        soon = [block for block in every if not count // 2 <= block < count - count // 4]
        incoming = dict(zip(soon, send_some(outgoing_hbm, received, 1, soon)))
        loads[0].wait()

        def backward_in(index, carry):
            part = pl.ds(pl.multiple_of(index * share, share), share)
            hidden_grad[:, part] = dot_nt(grads_ref[...], down_w[part, :])
            return carry

        lax.fori_loop(0, shares, backward_in, 0)
        for copy in gates_in:
            copy.wait()
        for shift in every:
            column = jnp.transpose(received_gates[shift])[:cap, 0:1]
            block = pl.ds(shift * cap, cap)
            gate_column[block, :] = jnp.broadcast_to(column, (cap, 128))
            scaled[block, :] = (column * grads_ref[block, :].astype(jnp.float32)).astype(
                jnp.bfloat16
            )
        for load in loads[1:]:
            load.wait()

        going = []
        batches = 2
        members = count // batches
        lines = rows // batches
        for batch in range(batches):
            chunks = range(batch * members, (batch + 1) * members)
            for shift in chunks:
                incoming[shift].wait()
            if batch == 0:
                late = [block for block in every if block not in soon]
                incoming.update(zip(late, send_some(outgoing_hbm, received, 1, late)))
            block = pl.ds(batch * lines, lines)

            def through(index, carry):
                part = pl.ds(pl.multiple_of(index * share, share), share)
                tokens = received[batch * members : (batch + 1) * members].reshape(lines, width)
                gate_part = dot(tokens, gate_w[:, part])
                linear_part = dot(tokens, linear_w[:, part])
                sigmoid = 1.0 / (1.0 + jnp.exp(-gate_part))
                silu = gate_part * sigmoid
                low = (silu * linear_part).astype(jnp.bfloat16)
                hidden[block, part] = low
                upper = hidden_grad[block, part] * gate_column[block, 0:1]
                low_gate = (
                    upper * linear_part * sigmoid * (1.0 + gate_part * (1.0 - sigmoid))
                ).astype(jnp.bfloat16)
                gate_low[block, part] = low_gate
                low_linear = (upper * silu).astype(jnp.bfloat16)
                linear_low[block, part] = low_linear
                out = dot(low, down_w[part, :])
                back = dot_nt(low_gate, gate_w[:, part]) + dot_nt(low_linear, linear_w[:, part])

                @pl.when(index == 0)
                def _():
                    out_total[block, :] = out
                    in_total[block, :] = back

                @pl.when(index > 0)
                def _():
                    out_total[block, :] += out
                    in_total[block, :] += back

                return carry

            lax.fori_loop(0, shares, through, 0)
            in_send[batch * members : (batch + 1) * members] = (
                in_total[block, :].astype(jnp.bfloat16).reshape(members, cap, width)
            )
            going += send_some(in_send, back_ref, 2, chunks)
            low = out_total[block, :].astype(jnp.bfloat16)
            output_ref[batch * members : (batch + 1) * members] = low.reshape(members, cap, width)
            dots = jnp.sum(
                low.astype(jnp.float32) * grads_ref[block, :].astype(jnp.float32),
                axis=1,
                keepdims=True,
            )
            for place, shift in enumerate(chunks):
                column = jnp.broadcast_to(dots[place * cap : (place + 1) * cap], (cap, 128))
                dots_send[shift, :, 0:cap] = jnp.transpose(column)[0:8, :]
                dots_send[shift, :, cap:] = jnp.zeros((8, 128 - cap), jnp.float32)
            going += send_some(dots_send, dots_ref, 3, chunks)
            rows_t[:, batch * lines : (batch + 1) * lines] = jnp.transpose(
                received[batch * members : (batch + 1) * members].reshape(lines, width)
            )

        def term_copy(which, index):
            target = (down_terms, gate_terms, linear_terms)[which]
            return pltpu.make_async_copy(
                terms[which].at[index], target.at[index], terms_sem.at[which, index]
            )

        def weigh(which, turn):
            index = jnp.bitwise_xor(lax.axis_index("dp"), shares - 1 - turn)
            part = pl.ds(pl.multiple_of(index * share, share), share)
            if which == 0:
                value = dot_tn(hidden[:, part], scaled[...])
            else:
                value = dot(rows_t[...], (gate_low if which == 1 else linear_low)[:, part])
            terms[which][index] = value.astype(jnp.bfloat16)
            term_copy(which, index).start()
            return index

        index = weigh(0, 0)
        first = pltpu.make_async_remote_copy(
            src_ref=terms[0].at[index],
            dst_ref=first_ref,
            send_sem=first_send,
            recv_sem=first_recv,
            device_id=peer_at(1, 0, 0),
            device_id_type=pl.DeviceIdType.MESH,
        )
        first.start()

        def weigh_rest(turn, carry):
            weigh(1, turn)
            weigh(2, turn)

            @pl.when(turn > 0)
            def _():
                weigh(0, turn)

            return carry

        lax.fori_loop(0, shares, weigh_rest, 0)
        for which in range(3):
            for index in range(shares):
                term_copy(which, index).wait()
        for copy in going:
            copy.wait()
        first.wait()

    low, full = jnp.bfloat16, jnp.float32
    columns, lines = (shares, width, share), (shares, share, width)
    any_space = pl.BlockSpec(memory_space=pl.ANY)
    in_vmem = pl.BlockSpec(memory_space=pltpu.VMEM)
    return pl.pallas_call(
        kernel,
        out_shape=[
            jax.ShapeDtypeStruct(outgoing.shape, low),
            jax.ShapeDtypeStruct(outgoing.shape, low),
            jax.ShapeDtypeStruct(gates.shape, full),
            jax.ShapeDtypeStruct(columns, low),
            jax.ShapeDtypeStruct(columns, low),
            jax.ShapeDtypeStruct(lines, low),
            jax.ShapeDtypeStruct(lines[1:], low),
        ],
        in_specs=[any_space, in_vmem, in_vmem, any_space, any_space, any_space],
        out_specs=[any_space, in_vmem] + [any_space] * 5,
        scratch_shapes=[
            pltpu.VMEM(outgoing.shape, low),
            pltpu.VMEM(gates.shape, full),
            pltpu.VMEM((width, hidden_units), low),
            pltpu.VMEM((width, hidden_units), low),
            pltpu.VMEM((hidden_units, width), low),
            pltpu.VMEM((rows, hidden_units), full),
            pltpu.VMEM((rows, hidden_units), low),
            pltpu.VMEM((rows, hidden_units), low),
            pltpu.VMEM((rows, hidden_units), low),
            pltpu.VMEM((width, rows), low),
            pltpu.VMEM((rows, width), low),
            pltpu.VMEM((rows, 128), full),
            pltpu.VMEM((rows, width), full),
            pltpu.VMEM((rows, width), full),
            pltpu.VMEM(outgoing.shape, low),
            pltpu.VMEM(gates.shape, full),
            [pltpu.VMEM(lines, low), pltpu.VMEM(columns, low), pltpu.VMEM(columns, low)],
            pltpu.SemaphoreType.DMA((3,)),
            pltpu.SemaphoreType.DMA((4, count)),
            pltpu.SemaphoreType.DMA((4, count)),
            pltpu.SemaphoreType.DMA((4,)),
            pltpu.SemaphoreType.DMA((3, shares)),
            pltpu.SemaphoreType.DMA,
            pltpu.SemaphoreType.DMA,
        ],
        compiler_params=pltpu.CompilerParams(
            collective_id=1, has_side_effects=True, vmem_limit_bytes=60 * 2**20
        ),
        cost_estimate=pl.CostEstimate(
            flops=18 * rows * width * hidden_units,
            bytes_accessed=12 * width * hidden_units + 12 * rows * width,
            transcendentals=rows * hidden_units,
        ),
        name="experts",
    )(outgoing, gates, grads, *weights)


def rope_tables(row_count):
    half = HEAD_DIM // 2
    frequency = np.exp(
        np.arange(half, dtype=np.float32) * np.float32(-2.0 * math.log(10000.0) / HEAD_DIM)
    ).astype(np.float32)
    angles = np.arange(row_count, dtype=np.float32)[:, None] * frequency[None, :]
    cosine, sine = np.cos(angles).astype(np.float32), np.sin(angles).astype(np.float32)
    return (
        np.concatenate([cosine] * 4, axis=1),
        np.concatenate([-sine, sine, -sine, sine], axis=1),
    )


def rotate(values, cosine, sine):
    lane = lax.broadcasted_iota(jnp.int32, cosine.shape, 1)
    leading = jnp.bitwise_and(lane, HEAD_DIM - 1) < HEAD_DIM // 2
    parts = []
    for begin in range(0, values.shape[1], 128):
        part = values[:, begin : begin + 128]
        ahead = pltpu.roll(part, 128 - HEAD_DIM // 2, 1)
        behind = pltpu.roll(part, HEAD_DIM // 2, 1)
        parts.append(part * cosine + jnp.where(leading, ahead, behind) * sine)
    return jnp.concatenate(parts, axis=1)


def inverse_norm(values):
    return lax.rsqrt(jnp.mean(values * values, axis=1, keepdims=True) + EPSILON)


def head_masks(rows):
    first = lax.broadcasted_iota(jnp.int32, (rows, 128), 1) < HEAD_DIM
    return first, jnp.logical_not(first)


def start_of(positions, starts):
    first = jnp.zeros_like(positions)
    for index in range(starts.shape[1]):
        begin = starts[0, index]
        first = jnp.where(begin <= positions, jnp.maximum(first, begin), first)
    return first


def gather_steps(size):
    bits, held, steps = [], [0], []
    bit = size // 2
    while bit >= 1:
        steps.append((bit, list(held)))
        held = held + [place ^ bit for place in held]
        bit //= 2
    return steps


def peer_at(deep, far, near):
    return {
        "dp": jnp.bitwise_xor(lax.axis_index("dp"), deep),
        "exp": jnp.bitwise_xor(lax.axis_index("exp"), far),
        "ctx": jnp.bitwise_xor(lax.axis_index("ctx"), near),
    }


def peer(far, near):
    return peer_at(0, far, near)


def greet_places(places):
    barrier = pltpu.get_barrier_semaphore()
    for place in places:
        pl.semaphore_signal(
            barrier, inc=1, device_id=peer_at(*place), device_id_type=pl.DeviceIdType.MESH
        )
    pl.semaphore_wait(barrier, len(places))


def greet_all(places):
    greet_places([(0,) + place for place in places])


def group_places(ranks):
    return [
        (shift // ranks[1], shift % ranks[1] * ranks[2]) for shift in range(1, ranks[0] * ranks[1])
    ]


def ring_places(size):
    return [(0, bit) for bit, _ in gather_steps(size)]


def places_of(ranks, size):
    places = group_places(ranks)
    return places + [place for place in ring_places(size) if place not in places]


class Gather:
    def __init__(self, buffers, size, send_sem, recv_sem, sources=None):
        self.buffers, self.sources = buffers, sources
        self.send_sem, self.recv_sem = send_sem, recv_sem
        self.steps = gather_steps(size)

    def copy(self, place, bit, index):
        block = jnp.bitwise_xor(lax.axis_index("ctx"), place)
        buffer = self.buffers[index]
        straight = self.sources is not None and place == 0
        return pltpu.make_async_remote_copy(
            src_ref=self.sources[index] if straight else buffer.at[block],
            dst_ref=buffer.at[block],
            send_sem=self.send_sem.at[index, place ^ bit],
            recv_sem=self.recv_sem.at[index, place ^ bit],
            device_id=peer(0, bit),
            device_id_type=pl.DeviceIdType.MESH,
        )

    def forward(self, place):
        for bit, held in self.steps:
            if place in held:
                for index in range(len(self.buffers)):
                    self.copy(place, bit, index).start()

    def arrive(self, place):
        bit = place & -place
        for index in range(len(self.buffers)):
            self.copy(place ^ bit, bit, index).wait_recv()
        self.forward(place)

    def finish(self):
        for bit, held in self.steps:
            for place in held:
                for index in range(len(self.buffers)):
                    self.copy(place, bit, index).wait_send()


def fill_rows(pack, prior, router_ref, map_ref, first_ref, second_ref, vector_ref, previous_ref):
    full = jnp.float32
    experts = router_ref.shape[0]
    width = router_ref.shape[1]
    pack[0:experts, :] = router_ref[...].astype(full)
    for index in range(2):
        pack[experts + 2 * index : experts + 2 * index + 2, :] = map_ref[index].astype(full)
    pack[HEAD_ROWS : HEAD_ROWS + 1, :] = first_ref[...].astype(full).reshape(1, width)
    pack[HEAD_ROWS + 1 : HEAD_ROWS + 2, :] = second_ref[...].astype(full).reshape(1, width)
    pack[HEAD_ROWS + 2 : HEAD_ROWS + 4, :] = vector_ref[...].astype(full)
    for index in range(experts):
        prior[index : index + 1, :] = previous_ref[index]


def slot_targets(routes, ranks, cap):
    exchange_size, group_size, spread = ranks
    rows = routes.shape[1]
    experts = exchange_size * group_size
    expert = lax.broadcasted_iota(jnp.int32, (16, rows), 0)
    hits = [(expert == routes[k : k + 1]).astype(jnp.float32) for k in range(2)]
    before = lax.broadcasted_iota(jnp.int32, (rows, rows), 0) < lax.broadcasted_iota(
        jnp.int32, (rows, rows), 1
    )
    earlier = dot(
        (hits[0] + hits[1]).astype(jnp.bfloat16), before.astype(jnp.float32).astype(jnp.bfloat16)
    )
    targets = []
    for k in range(2):
        route = routes[k : k + 1]
        rank = jnp.sum(hits[k] * earlier, axis=0, keepdims=True)
        far = jnp.bitwise_xor(route // group_size, lax.axis_index("exp"))
        near = jnp.bitwise_xor(route % group_size, lax.axis_index("ctx") // spread)
        count = exchange_size * group_size
        block = jnp.bitwise_and(far * group_size + near + count - count // 4, count - 1)
        place = (block * cap).astype(jnp.float32)
        targets.append(jnp.where(route < experts, place + rank, -1.0))
    return targets


def attend_layer(
    tokens, cotangent, previous, routes, starts, weights, params, carry, ranks, cap, size
):
    rows, width = tokens.shape
    count = ranks[0] * ranks[1]
    slots = count * cap
    pairs = width // 128
    tables = rope_tables(size * rows)
    low, full = jnp.bfloat16, jnp.float32

    def kernel(
        tokens_hbm,
        cotangent_ref,
        previous_ref,
        routes_ref,
        starts_ref,
        query_hbm,
        key_hbm,
        value_hbm,
        output_hbm,
        router_ref,
        map_ref,
        first_ref,
        second_ref,
        vector_ref,
        carry_ref,
        cosine_hbm,
        sine_hbm,
        queries_out,
        keys_out,
        values_out,
        attended_ref,
        lse_ref,
        middle_ref,
        probs_ref,
        targets_ref,
        outgoing_ref,
        gates_ref,
        grads_ref,
        stream,
        queries,
        keys,
        values,
        query_w,
        key_w,
        value_w,
        output_w,
        cosine,
        sine,
        bias,
        totals,
        highest,
        slot_grads,
        load_sem,
        gather_send,
        gather_recv,
        grad_send,
        grad_recv,
        keep_sem,
        pack,
        prior,
    ):
        own = lax.axis_index("ctx")
        bring = pltpu.make_async_copy(tokens_hbm, stream.at[own], load_sem.at[6])
        bring.start()
        loads = [
            pltpu.make_async_copy(source, target, load_sem.at[index])
            for index, (source, target) in enumerate(
                (
                    (query_hbm, query_w),
                    (key_hbm, key_w),
                    (value_hbm, value_w),
                    (cosine_hbm, cosine),
                    (sine_hbm, sine),
                    (output_hbm, output_w),
                )
            )
        ]
        for load in loads:
            load.start()
        greet_all(places_of(ranks, size))
        gather = Gather([stream], size, gather_send, gather_recv, [tokens_hbm])
        gather.forward(0)

        fill_rows(
            pack, prior, router_ref, map_ref, first_ref, second_ref, vector_ref, previous_ref
        )
        targets = slot_targets(routes_ref[...], ranks, cap)
        slot = lax.broadcasted_iota(jnp.int32, (slots, rows), 0).astype(full)
        picked = jnp.logical_or(slot == targets[0], slot == targets[1])
        picked = picked.astype(full).astype(low)
        slot_grads[...] = dot(picked, cotangent_ref[...]).astype(low).reshape(count, cap, width)
        grad_copies = [
            send_block(slot_grads, grads_ref, block, ranks, grad_send, grad_recv)
            for block in other_blocks(count)
        ]
        grad_copies.append(keep_block(slot_grads, grads_ref, count, keep_sem.at[0]))

        bring.wait()
        for load in loads[:5]:
            load.wait()
        gain = pack[HEAD_ROWS : HEAD_ROWS + 1, :]

        def project(block, wanted):
            line = pl.ds(pl.multiple_of(block * rows, rows), rows)
            values_in = stream[block].astype(full)
            normed = (values_in * inverse_norm(values_in) * gain).astype(low)
            if "q" in wanted:
                turned = rotate(dot(normed, query_w[...]), cosine[line, :], sine[line, :])
                queries[block] = (turned.astype(low).astype(full) * HEAD_DIM**-0.5).astype(low)
            if "k" in wanted:
                turned = rotate(dot(normed, key_w[...]), cosine[line, :], sine[line, :])
                keys[block] = turned.astype(low)
                values[block] = dot(normed, value_w[...]).astype(low)

        masks = head_masks(rows)
        query_pos = own * rows + lax.broadcasted_iota(jnp.int32, (rows, rows), 1)
        document_start = start_of(query_pos[0:8], starts_ref)[0:1]

        def attend(block):
            key_pos = block * rows + lax.broadcasted_iota(jnp.int32, (rows, rows), 0)
            allowed = jnp.logical_and(key_pos >= document_start, key_pos <= query_pos)
            bias[...] = jnp.where(allowed, 0.0, NEGATIVE)

            def pair(index, carried):
                lanes = pl.ds(pl.multiple_of(index * 128, 128), 128)
                query, key, value = queries[own, :, lanes], keys[block, :, lanes], values[block, :, lanes]
                scores = [dot_nt(jnp.where(mask, key, 0), query) + bias[...] for mask in masks]
                old = [highest[index, head][0:1, :] for head in range(2)]
                new = [
                    jnp.maximum(old[head], jnp.max(scores[head], axis=0, keepdims=True))
                    for head in range(2)
                ]
                weight = [jnp.exp(scores[head] - new[head]).astype(low) for head in range(2)]
                for head in range(2):
                    totals[index, head] = totals[index, head] * jnp.exp(old[head] - new[head]) + dot_tn(
                        jnp.where(masks[head], value, 1), weight[head]
                    )
                    highest[index, head] = jnp.broadcast_to(new[head], (8, rows))
                return carried

            lax.fori_loop(0, pairs, pair, 0)

        totals[...] = jnp.zeros_like(totals)
        highest[...] = jnp.full(highest.shape, NEGATIVE, full)
        project(own, "qk")
        attend(own)
        def others(place, carried):
            for one in range(1, size):

                @pl.when(place == one)
                def _():
                    gather.arrive(one)
                    if one == size // 2:
                        for copy in grad_copies:
                            copy.start()

            block = jnp.bitwise_xor(own, place)

            @pl.when(block < own)
            def _():
                project(block, "k")
                attend(block)

            @pl.when(block > own)
            def _():
                project(block, "q")

            return carried

        lax.fori_loop(1, size, others, 0)
        keep = [
            pltpu.make_async_copy(source, target, keep_sem.at[index + 1])
            for index, (source, target) in enumerate(
                ((queries, queries_out), (keys, keys_out), (values, values_out))
            )
        ]
        for copy in keep:
            copy.start()

        lse_ref[...] = jnp.zeros_like(lse_ref)
        upper = lax.broadcasted_iota(jnp.int32, (128, rows), 0) < HEAD_DIM
        for index in range(pairs):
            halves = []
            for head in range(2):
                total = totals[index, head]
                line = HEAD_DIM if head == 0 else 0
                weight_sum = total[line : line + 1, :]
                halves.append(total / weight_sum)
                lse_ref[2 * index + head : 2 * index + head + 1, :] = highest[index, head][
                    0:1, :
                ] + jnp.log(weight_sum)
            attended_ref[:, index * 128 : index * 128 + 128] = jnp.transpose(
                jnp.where(upper, halves[0], halves[1])
            )
        loads[5].wait()
        middle = stream[own].astype(full) + dot(attended_ref[...].astype(low), output_w[...])
        middle_ref[...] = middle
        second = (
            middle
            * inverse_norm(middle)
            * pack[HEAD_ROWS + 1 : HEAD_ROWS + 2, :]
        )
        second_low = second.astype(low)
        outgoing_ref[...] = dot(picked, second_low).astype(low).reshape(count, cap, width)

        experts = previous_ref.shape[0]
        logits = dot_nt(second_low, pack[0:HEAD_ROWS, :].astype(low))[:, 0:experts] + lax.dot_general(
            prior[0:experts, :],
            carry_ref[...].astype(full),
            (((0,), (0,)), ((), ())),
            precision=HIGH,
        )
        logits = logits - jnp.max(logits, axis=1, keepdims=True)
        powers = jnp.exp(logits)
        probs_ref[...] = jnp.zeros_like(probs_ref)
        probs_ref[:, 0:experts] = powers / jnp.sum(powers, axis=1, keepdims=True)
        turned = jnp.transpose(probs_ref[...])[0:16]
        expert = lax.broadcasted_iota(jnp.int32, (16, rows), 0)
        weighted = jnp.zeros((slots, rows), full)
        for k in range(2):
            route = routes_ref[k : k + 1, :]
            gate = jnp.sum(jnp.where(expert == route, turned, 0.0), axis=0, keepdims=True)
            weighted = jnp.where(slot == targets[k], gate, weighted)
        gate_column = jnp.sum(weighted, axis=1, keepdims=True)
        for shift in range(count):
            column = jnp.broadcast_to(gate_column[shift * cap : (shift + 1) * cap], (cap, 128))
            gates_ref[shift] = jnp.zeros((8, 128), full)
            gates_ref[shift, :, 0:cap] = jnp.transpose(column)[0:8, :]
        pad = jnp.zeros((6, rows), full)
        target_rows = jnp.concatenate([targets[0], targets[1], pad], axis=0)
        target_rows = jnp.concatenate([target_rows] + [jnp.zeros((120, rows), full)], axis=0)
        targets_ref[...] = jnp.transpose(target_rows)

        gather.finish()
        for copy in keep + grad_copies:
            copy.wait()

    stream_shape = (size, rows, width)
    any_space = pl.BlockSpec(memory_space=pl.ANY)
    in_vmem = pl.BlockSpec(memory_space=pltpu.VMEM)
    square = (width, width)
    return pl.pallas_call(
        kernel,
        out_shape=[
            jax.ShapeDtypeStruct(stream_shape, low),
            jax.ShapeDtypeStruct(stream_shape, low),
            jax.ShapeDtypeStruct(stream_shape, low),
            jax.ShapeDtypeStruct((rows, width), full),
            jax.ShapeDtypeStruct((16, rows), full),
            jax.ShapeDtypeStruct((rows, width), full),
            jax.ShapeDtypeStruct((rows, 128), full),
            jax.ShapeDtypeStruct((rows, 128), full),
            jax.ShapeDtypeStruct((count, cap, width), low),
            jax.ShapeDtypeStruct((count, 8, 128), full),
            jax.ShapeDtypeStruct((count, cap, width), low),
        ],
        in_specs=[any_space]
        + [in_vmem] * 3
        + [pl.BlockSpec(memory_space=pltpu.SMEM)]
        + [any_space] * 4
        + [in_vmem] * 6
        + [any_space] * 2,
        out_specs=[any_space] * 3 + [in_vmem] * 7 + [any_space],
        scratch_shapes=[
            pltpu.VMEM(stream_shape, low),
            pltpu.VMEM(stream_shape, low),
            pltpu.VMEM(stream_shape, low),
            pltpu.VMEM(stream_shape, low),
            pltpu.VMEM(square, low),
            pltpu.VMEM(square, low),
            pltpu.VMEM(square, low),
            pltpu.VMEM(square, low),
            pltpu.VMEM((size * rows, 128), full),
            pltpu.VMEM((size * rows, 128), full),
            pltpu.VMEM((rows, rows), full),
            pltpu.VMEM((pairs, 2, 128, rows), full),
            pltpu.VMEM((pairs, 2, 8, rows), full),
            pltpu.VMEM((count, cap, width), low),
            pltpu.SemaphoreType.DMA((7,)),
            pltpu.SemaphoreType.DMA((1, size)),
            pltpu.SemaphoreType.DMA((1, size)),
            pltpu.SemaphoreType.DMA((count,)),
            pltpu.SemaphoreType.DMA((count,)),
            pltpu.SemaphoreType.DMA((4,)),
            pltpu.VMEM((24, width), full),
            pltpu.VMEM((16, rows), full),
        ],
        compiler_params=pltpu.CompilerParams(
            collective_id=0, has_side_effects=True, vmem_limit_bytes=60 * 2**20
        ),
        cost_estimate=pl.CostEstimate(
            flops=2 * size * rows * width * width * 3 + 16 * size * rows * rows * width,
            bytes_accessed=20 * 2**20,
            transcendentals=size * rows * rows * 12,
        ),
        name="attend",
    )(
        tokens,
        cotangent,
        previous,
        routes,
        starts,
        *weights,
        *params,
        carry,
        jnp.asarray(tables[0]),
        jnp.asarray(tables[1]),
    )


def add_into(target, source):
    rows = target.shape[0]
    piece = 96 if rows % 96 == 0 else (64 if rows % 64 == 0 else rows)

    def body(index, carried):
        part = pl.ds(pl.multiple_of(index * piece, piece), piece)
        total = target[part, :].astype(jnp.float32) + source[part, :].astype(jnp.float32)
        target[part, :] = total.astype(target.dtype)
        return carried

    lax.fori_loop(0, rows // piece, body, 0)


def column_of(values, index):
    return values[:, index : index + 1]


def backward_layer(
    tokens,
    cotangent,
    previous,
    routes,
    starts,
    forward,
    returns,
    weights,
    params,
    terms,
    first,
    ranks,
    cap,
    size,
    shares,
):
    rows, width = tokens.shape
    count = ranks[0] * ranks[1]
    slots = count * cap
    pairs = width // 128
    tables = rope_tables(size * rows)
    low, full = jnp.bfloat16, jnp.float32
    experts = previous.shape[0]
    copy_index = count + 1
    stat_rows = 16
    kinds = len(terms)

    def kernel(
        tokens_ref,
        cotangent_ref,
        previous_ref,
        routes_ref,
        starts_ref,
        attended_ref,
        lse_ref,
        middle_ref,
        probs_ref,
        targets_ref,
        queries_hbm,
        keys_hbm,
        values_hbm,
        back_ref,
        produced_hbm,
        dots_ref,
        query_hbm,
        key_hbm,
        value_hbm,
        output_hbm,
        router_ref,
        map_ref,
        first_gain_ref,
        second_gain_ref,
        vector_ref,
        cosine_hbm,
        sine_hbm,
        *rest,
    ):
        term_refs, first_hbm, rest = rest[:kinds], rest[kinds], rest[kinds + 1 :]
        result_ref, token_grads_ref, wide_ref, small_ref = rest[:4]
        first_refs, rest = rest[4 : 4 + kinds], rest[4 + kinds :]
        (
            queries,
            keys,
            values,
            query_w,
            key_w,
            value_w,
            output_w,
            cosine,
            sine,
            bias,
            out_grads,
            stats,
            outputs,
            middle_grad,
            query_total,
            key_total,
            value_total,
            load_sem,
            gather_send,
            gather_recv,
            first_send,
            first_recv,
            out_send,
            out_recv,
            out_keep,
            sum_part,
            first_part,
            sum_load,
            pack,
            prior,
        ) = rest
        own = lax.axis_index("ctx")
        line = pl.ds(pl.multiple_of(own * rows, rows), rows)
        loads = [
            pltpu.make_async_copy(source, target, load_sem.at[index])
            for index, (source, target) in enumerate(
                (
                    (output_hbm, output_w),
                    (queries_hbm, queries),
                    (keys_hbm, keys),
                    (values_hbm, values),
                    (cosine_hbm.at[line], cosine),
                    (sine_hbm.at[line], sine),
                    (query_hbm, query_w),
                    (key_hbm, key_w),
                    (value_hbm, value_w),
                )
            )
        ]
        for load in loads:
            load.start()
        share = lax.axis_index("dp")
        sum_loads = [
            pltpu.make_async_copy(
                term_refs[0].at[jnp.bitwise_xor(share, shares - 2)], sum_part, sum_load.at[0]
            ),
            pltpu.make_async_copy(first_hbm, first_part, sum_load.at[1]),
        ]
        for copy in sum_loads:
            copy.start()
        greet_places(
            [(0,) + place for place in places_of(ranks, size)] + [(1, 0, 0), (2, 0, 0)]
        )
        first_copies = [
            pltpu.make_async_remote_copy(
                src_ref=(
                    term_refs[kind].at[jnp.bitwise_xor(share, shares - 1)] if kind else sum_part
                ),
                dst_ref=first_refs[kind],
                send_sem=first_send.at[kind],
                recv_sem=first_recv.at[kind],
                device_id=peer_at(1 if kind else 2, 0, 0),
                device_id_type=pl.DeviceIdType.MESH,
            )
            for kind in range(kinds)
        ]
        for copy in first_copies[1:]:
            copy.start()
        for copy in sum_loads:
            copy.wait()
        add_into(sum_part, first_part)
        first_copies[0].start()
        output_copies = [
            send_block(produced_hbm, outputs, block, ranks, out_send, out_recv)
            for block in other_blocks(count)
        ]
        output_copies.append(keep_block(produced_hbm, outputs, count, out_keep))

        def keep_wide(index, value):
            half = width // 2
            for part in range(2):
                wide_ref[part, index * width : (index + 1) * width, :] = value[
                    :, part * half : (part + 1) * half
                ].astype(low)

        fill_rows(
            pack,
            prior,
            router_ref,
            map_ref,
            first_gain_ref,
            second_gain_ref,
            vector_ref,
            previous_ref,
        )
        lane = lax.broadcasted_iota(jnp.int32, (rows, 128), 1)
        upstream = cotangent_ref[...].astype(full)
        middle = middle_ref[...]
        inverse_second = inverse_norm(middle)
        unit_second = middle * inverse_second
        gain_second = pack[HEAD_ROWS + 1 : HEAD_ROWS + 2, :]
        second = unit_second * gain_second
        second_low = second.astype(low)
        heads_in = jnp.concatenate(
            [pack[0:HEAD_ROWS, :].astype(low), jnp.zeros((128 - HEAD_ROWS, width), low)], axis=0
        )
        mixed = dot_nt(second_low, heads_in)
        probs = probs_ref[...]
        route_rows = jnp.concatenate(
            [routes_ref[...].astype(full), jnp.zeros((126, rows), full)], axis=0
        )
        route_columns = jnp.transpose(route_rows).astype(jnp.int32)
        route = [column_of(route_columns, k) for k in range(2)]
        chosen = jnp.logical_or(lane == route[0], lane == route[1])
        gates = jnp.where(chosen, probs, 0.0)
        target = [column_of(targets_ref[...], k) for k in range(2)]

        gate_grad = jnp.zeros((rows, 128), full)
        place = lane.astype(full)
        for k in range(2):
            found = jnp.zeros((rows, 128), full)
            for shift in range(count):
                found = found + jnp.where(
                    jnp.logical_and(target[k] - shift * cap == place, lane < cap),
                    dots_ref[shift, 0:1, :],
                    0.0,
                )
            gate_grad = gate_grad + jnp.where(
                lane == route[k], jnp.sum(found, axis=1, keepdims=True), 0.0
            )
        copy_grad = jnp.sum(upstream * second, axis=1, keepdims=True)
        gate_grad = jnp.where(lane == copy_index, copy_grad, gate_grad)
        direct = column_of(gates, copy_index)
        constants = []
        for index in range(2):
            vector = pack[HEAD_ROWS + 2 + index : HEAD_ROWS + 3 + index, :]
            vector_dot = jnp.sum(upstream * vector, axis=1, keepdims=True)
            begin = experts + 2 * index
            spread_of = column_of(mixed, begin + 1) - column_of(mixed, begin)
            mixing = (1.0 / (1.0 + jnp.exp(spread_of)), 1.0 / (1.0 + jnp.exp(-spread_of)))
            gate = column_of(gates, copy_index + 1 + index)
            term = mixing[0] * copy_grad + mixing[1] * vector_dot
            gate_grad = jnp.where(lane == copy_index + 1 + index, term, gate_grad)
            direct = direct + gate * mixing[0]
            constants.append((gate, mixing, vector, vector_dot))
        prob_grad = jnp.where(chosen, gate_grad, 0.0)
        logit_grad = probs * (prob_grad - jnp.sum(probs * prob_grad, axis=1, keepdims=True))
        head_grad = logit_grad
        for index, (gate, mixing, vector, vector_dot) in enumerate(constants):
            mixing_grad = (gate * copy_grad, gate * vector_dot)
            mean = mixing[0] * mixing_grad[0] + mixing[1] * mixing_grad[1]
            for part in range(2):
                head_grad = jnp.where(
                    lane == experts + 2 * index + part,
                    mixing[part] * (mixing_grad[part] - mean),
                    head_grad,
                )
        head_low = head_grad.astype(low)

        slot = lax.broadcasted_iota(jnp.int32, (rows, slots), 1).astype(full)
        picked = [(slot == target[k]).astype(full).astype(low) for k in range(2)]
        second_grad = (
            dot(head_low, heads_in) + direct * upstream + dot(picked[0] + picked[1], back_ref[...])
        )
        normal_grad = second_grad * gain_second
        middle_total = upstream + inverse_second * (
            normal_grad - unit_second * jnp.mean(normal_grad * unit_second, axis=1, keepdims=True)
        )
        middle_grad[...] = middle_total
        middle_low = middle_total.astype(low)
        loads[0].wait()
        out_grad = dot_nt(middle_low, output_w[...]).astype(low)
        out_grads[own] = out_grad
        product = out_grad.astype(full) * attended_ref[...]
        masks = head_masks(rows)
        deltas = jnp.zeros((rows, 128), full)
        for index in range(pairs):
            part = product[:, index * 128 : index * 128 + 128]
            for head in range(2):
                total = jnp.sum(jnp.where(masks[head], part, 0.0), axis=1, keepdims=True)
                deltas = jnp.where(lane == 2 * index + head, total, deltas)
        stats[own, 0:stat_rows] = lse_ref[...]
        stats[own, stat_rows:] = jnp.transpose(deltas)[0:stat_rows]
        gather = Gather([out_grads, stats], size, gather_send, gather_recv)
        gather.forward(0)
        for copy in output_copies:
            copy.start()

        chosen_out = second * direct
        for gate, mixing, vector, vector_dot in constants:
            chosen_out = chosen_out + gate * mixing[1] * vector
        base = middle + chosen_out
        small_ref[...] = jnp.zeros_like(small_ref)
        small_ref[1:2, :] = jnp.sum(second_grad * unit_second, axis=0, keepdims=True)
        for index, (gate, mixing, vector, vector_dot) in enumerate(constants):
            small_ref[2 + index : 3 + index, :] = jnp.sum(
                gate * mixing[1] * upstream, axis=0, keepdims=True
            )
        small_ref[8:24, :] = dot_tn(head_low, second_low)[0:16]
        carry_grad = lax.dot_general(
            jnp.transpose(logit_grad)[0:16],
            prior[0:experts, :],
            (((1,), (1,)), ((), ())),
            precision=HIGH,
        )
        small_ref[24:40, 0:experts] = carry_grad
        keep_wide(3, dot_tn(attended_ref[...].astype(low), middle_low))

        for load in loads[1:4]:
            load.wait()
        query_total[...] = jnp.zeros_like(query_total)
        key_total[...] = jnp.zeros_like(key_total)
        value_total[...] = jnp.zeros_like(value_total)
        column = lax.broadcasted_iota(jnp.int32, (rows, rows), 0)
        row = lax.broadcasted_iota(jnp.int32, (rows, rows), 1)

        def block_side(block, as_query, as_key):
            key_block, query_block = (own if as_key else block), (own if as_query else block)
            key_pos, query_pos = key_block * rows + column, query_block * rows + row
            first = start_of(query_pos[0:8], starts_ref)[0:1]
            allowed = jnp.logical_and(key_pos >= first, key_pos <= query_pos)
            bias[...] = jnp.where(allowed, 0.0, NEGATIVE)

            def pair(index, carried):
                lanes = pl.ds(pl.multiple_of(index * 128, 128), 128)
                query, grad = queries[query_block, :, lanes], out_grads[query_block, :, lanes]
                key, value = keys[key_block, :, lanes], values[key_block, :, lanes]
                one_key = [jnp.where(mask, key, 0) for mask in masks]
                scores = [dot_nt(one_key[head], query) for head in range(2)]
                weight_grad = [dot_nt(jnp.where(mask, value, 0), grad) for mask in masks]
                weight, score = [], []
                for head in range(2):
                    lse = stats[query_block, pl.ds(2 * index + head, 1), :]
                    mean = stats[query_block, pl.ds(stat_rows + 2 * index + head, 1), :]
                    weight.append(jnp.exp(scores[head] + bias[...] - lse))
                    score.append((weight[head] * (weight_grad[head] - mean)).astype(low))
                if as_key:
                    value_total[:, lanes] += dot(
                        weight[0].astype(low), jnp.where(masks[0], grad, 0)
                    ) + dot(weight[1].astype(low), jnp.where(masks[1], grad, 0))
                    key_total[:, lanes] += dot(score[0], jnp.where(masks[0], query, 0)) + dot(
                        score[1], jnp.where(masks[1], query, 0)
                    )
                if as_query:
                    query_total[lanes, :] += dot_tn(one_key[0], score[0]) + dot_tn(
                        one_key[1], score[1]
                    )
                return carried

            lax.fori_loop(0, pairs, pair, 0)

        block_side(own, True, True)
        def earlier(place, carried):
            block = jnp.bitwise_xor(own, place)

            @pl.when(block < own)
            def _():
                block_side(block, True, False)

            return carried

        def later(place, carried):
            for one in range(1, size):

                @pl.when(place == one)
                def _():
                    gather.arrive(one)

            block = jnp.bitwise_xor(own, place)

            @pl.when(block > own)
            def _():
                block_side(block, False, True)

            return carried

        lax.fori_loop(1, size, earlier, 0)
        lax.fori_loop(1, size, later, 0)
        for load in loads[4:]:
            load.wait()
        inputs = tokens_ref[...].astype(full)
        inverse_first = inverse_norm(inputs)
        unit_first = inputs * inverse_first
        gain_first = pack[HEAD_ROWS : HEAD_ROWS + 1, :]
        normed = (unit_first * gain_first).astype(low)
        turn = -sine[...]
        query_grad = jnp.transpose(query_total[...]) * HEAD_DIM**-0.5
        query_low = rotate(query_grad, cosine[...], turn).astype(low)
        key_low = rotate(key_total[...], cosine[...], turn).astype(low)
        value_low = value_total[...].astype(low)
        first_grad = (
            dot_nt(query_low, query_w[...])
            + dot_nt(key_low, key_w[...])
            + dot_nt(value_low, value_w[...])
        )
        for index, part in enumerate((query_low, key_low, value_low)):
            keep_wide(index, dot_tn(normed, part))
        small_ref[0:1, :] = jnp.sum(first_grad * unit_first, axis=0, keepdims=True)
        normal_grad = first_grad * gain_first
        token_grads_ref[...] = middle_grad[...] + inverse_first * (
            normal_grad - unit_first * jnp.mean(normal_grad * unit_first, axis=1, keepdims=True)
        )
        for copy in output_copies:
            copy.wait()
        for k in range(2):
            weight = jnp.sum(jnp.where(lane == route[k], probs, 0.0), axis=1, keepdims=True)
            base = base + weight * dot(picked[k], outputs[...].reshape(slots, width))
        result_ref[...] = base.astype(low)
        gather.finish()
        for copy in first_copies:
            copy.wait()

    stream_shape = (size, rows, width)
    any_space = pl.BlockSpec(memory_space=pl.ANY)
    in_vmem = pl.BlockSpec(memory_space=pltpu.VMEM)
    square = (width, width)
    return pl.pallas_call(
        kernel,
        out_shape=[
            jax.ShapeDtypeStruct((rows, width), low),
            jax.ShapeDtypeStruct((rows, width), full),
            jax.ShapeDtypeStruct((2, 4 * width, width // 2), low),
            jax.ShapeDtypeStruct((64, width), full),
        ]
        + [jax.ShapeDtypeStruct(term.shape[1:], low) for term in terms],
        in_specs=[in_vmem] * 4
        + [pl.BlockSpec(memory_space=pltpu.SMEM)]
        + [in_vmem] * 5
        + [any_space] * 3
        + [in_vmem, any_space, in_vmem]
        + [any_space] * 4
        + [in_vmem] * 5
        + [any_space] * (3 + kinds),
        out_specs=[in_vmem] * 4 + [any_space] * kinds,
        scratch_shapes=[
            pltpu.VMEM(stream_shape, low),
            pltpu.VMEM(stream_shape, low),
            pltpu.VMEM(stream_shape, low),
            pltpu.VMEM(square, low),
            pltpu.VMEM(square, low),
            pltpu.VMEM(square, low),
            pltpu.VMEM(square, low),
            pltpu.VMEM((rows, 128), full),
            pltpu.VMEM((rows, 128), full),
            pltpu.VMEM((rows, rows), full),
            pltpu.VMEM(stream_shape, low),
            pltpu.VMEM((size, 2 * stat_rows, rows), full),
            pltpu.VMEM((count, cap, width), low),
            pltpu.VMEM((rows, width), full),
            pltpu.VMEM((width, rows), full),
            pltpu.VMEM((rows, width), full),
            pltpu.VMEM((rows, width), full),
            pltpu.SemaphoreType.DMA((9,)),
            pltpu.SemaphoreType.DMA((2, size)),
            pltpu.SemaphoreType.DMA((2, size)),
            pltpu.SemaphoreType.DMA((kinds,)),
            pltpu.SemaphoreType.DMA((kinds,)),
            pltpu.SemaphoreType.DMA((count,)),
            pltpu.SemaphoreType.DMA((count,)),
            pltpu.SemaphoreType.DMA,
            pltpu.VMEM(terms[0].shape[1:], low),
            pltpu.VMEM(terms[0].shape[1:], low),
            pltpu.SemaphoreType.DMA((2,)),
            pltpu.VMEM((24, width), full),
            pltpu.VMEM((16, rows), full),
        ],
        compiler_params=pltpu.CompilerParams(
            collective_id=2, has_side_effects=True, vmem_limit_bytes=60 * 2**20
        ),
        cost_estimate=pl.CostEstimate(
            flops=14 * rows * width * width * 2 + 20 * size * rows * rows * width,
            bytes_accessed=30 * 2**20,
            transcendentals=size * rows * rows * 12,
        ),
        name="backward",
    )(
        tokens,
        cotangent,
        previous,
        routes,
        starts,
        *forward,
        *returns,
        *weights,
        *params,
        jnp.asarray(tables[0]),
        jnp.asarray(tables[1]),
        *terms,
        first,
    )


PIECES = 4
ORDER = (
    6, 7, 11, 0, 5, 6, 1, 0, 0, 7, 11, 7, 6, 11, 0,
    3, 0, 2, 4, 5, 5, 2, 0, 10, 7, 1, 0, 6, 4, 10,
    3, 2, 10, 8, 7, 0, 4, 10, 8, 1, 6, 5, 8, 1, 3,
    10, 9, 2, 12, 4, 0, 10, 5, 4, 2, 3, 8, 6, 9, 9,
    9, 11, 5, 12, 12, 0, 9, 11, 8, 0, 8, 12, 9, 12, 11,
    1, 3, 7, 12,
)
DENSE_TIMES = (7, 24, 34, 48, 62, 77, 91, 101, 118, 125, 132)
EXPERT_TIMES = (19, 14, 19, 4, 11, 2)


def halving_steps(size):
    steps, step = [], 0
    while 1 << step < size:
        bit = 1 << step
        steps += [(step, place) for place in range(size - bit, 0, -2 * bit)]
        step += 1
    return steps


def needed_before(step, place):
    return {(earlier, place | 1 << earlier) for earlier in range(step)}


def reduce_layer(terms, firsts, wide, small, spread, shares, ring, exchange_size):
    low, full = jnp.bfloat16, jnp.float32
    steps = halving_steps(shares)
    done = [[(0, shares - 1), (1, shares - 2)]] + [[(0, shares - 1)]] * (len(terms) - 1)
    kinds = len(terms)
    blocks = [term.shape[1:] for term in terms]
    members = ring // spread
    groups = 3
    near_bits = [1 << step for step in range(ring.bit_length() - 1)]
    far_bits = [1 << step for step in range(exchange_size.bit_length() - 1)]
    deep_bits = [1 << step for step in range(shares.bit_length() - 1)]
    near = [(0, 0, bit) for bit in near_bits]
    far = [(0, bit, 0) for bit in far_bits]
    deep = [(bit, 0, 0) for bit in deep_bits]
    orders = [near + far + deep, near[:1] + far + near[1:] + deep, near + far + deep]
    places = near + far + deep
    bit_count = len(places)
    group_rows = [wide.shape[1], wide.shape[1], small.shape[0]]
    tile = [16, 16, 8]
    plans = []
    for group in range(groups):
        length, plan = group_rows[group], []
        for _ in range(bit_count):
            halved = (length // 2) % tile[group] == 0
            length = length // 2 if halved else length
            plan.append((halved, length))
        plans.append(plan)

    def kernel(*refs):
        refs = list(refs)

        def take(number):
            taken = refs[:number]
            del refs[:number]
            return taken

        term_refs, first_refs = take(kinds), take(kinds)
        (wide_hbm, small_hbm) = take(2)
        gathered = take(kinds)
        (wide_out, small_out) = take(2)
        sums, landed = take(kinds), take(kinds)
        (halves, smalls) = take(2)
        group_landed = take(groups)
        (load_sem, step_send, step_recv, own_sem, ring_send, ring_recv) = take(6)
        (dense_send, dense_recv, dense_load) = take(3)
        share = lax.axis_index("dp")
        mine = lax.axis_index("ctx") // spread

        dense_in = [
            pltpu.make_async_copy(wide_hbm, halves, dense_load.at[0]),
            pltpu.make_async_copy(small_hbm, smalls, dense_load.at[1]),
        ]
        for copy in dense_in:
            copy.start()
        loads = []
        for kind in range(kinds):
            copies = [
                pltpu.make_async_copy(
                    first_refs[kind],
                    landed[kind].at[steps.index(done[kind][-1])],
                    load_sem.at[kind, shares // 2],
                )
            ]
            for place in range(shares - 2, -1, -2):
                copies.append(
                    pltpu.make_async_copy(
                        term_refs[kind].at[jnp.bitwise_xor(share, place)],
                        sums[kind].at[place // 2],
                        load_sem.at[kind, place // 2],
                    )
                )
            for copy in copies:
                copy.start()
            loads.append(copies)
        greet_places(places)

        def expert_chain(kind, piece):
            period, odd_wait, even_wait, near_wait, far_wait, last_wait = EXPERT_TIMES
            begin = time = period * (kind * PIECES + piece)
            slots = {step: index for index, step in enumerate(steps)}
            lines = blocks[kind][0] // PIECES
            window = pl.ds(piece * lines, lines)
            one = kind * PIECES + piece

            def transfer(step, place):
                index = slots[step, place]
                if place % 2 == 1:
                    source = term_refs[kind].at[jnp.bitwise_xor(share, place), window]
                else:
                    source = sums[kind].at[place // 2, window]
                return pltpu.make_async_remote_copy(
                    src_ref=source,
                    dst_ref=landed[kind].at[index, window],
                    send_sem=step_send.at[one, index],
                    recv_sem=step_recv.at[one, index],
                    device_id=peer_at(1 << step, 0, 0),
                    device_id_type=pl.DeviceIdType.MESH,
                )

            yield begin
            while loads[kind]:
                loads[kind].pop().wait()
            step, place = done[kind][-1]
            add_into(
                sums[kind].at[(place ^ 1 << step) // 2, window],
                landed[kind].at[slots[step, place], window],
            )
            arrived, started = set(done[kind]), []
            waiting = [op for op in steps if op not in arrived]
            while True:
                for op in list(waiting):
                    if needed_before(*op) <= arrived:
                        transfer(*op).start()
                        started.append(op)
                        waiting.remove(op)
                if not started:
                    break
                op = started.pop(0)
                yield time + (even_wait if op[0] else odd_wait)
                transfer(*op).wait()
                arrived.add(op)
                add_into(
                    sums[kind].at[(op[1] ^ 1 << op[0]) // 2, window],
                    landed[kind].at[slots[op], window],
                )
            time += even_wait
            index = len(steps)
            bit = 1
            while bit < spread:
                copy = pltpu.make_async_remote_copy(
                    src_ref=sums[kind].at[0, window],
                    dst_ref=landed[kind].at[index, window],
                    send_sem=step_send.at[one, index],
                    recv_sem=step_recv.at[one, index],
                    device_id=peer_at(0, 0, bit),
                    device_id_type=pl.DeviceIdType.MESH,
                )
                copy.start()
                time += near_wait
                yield time
                copy.wait()
                add_into(sums[kind].at[0, window], landed[kind].at[index, window])
                index += 1
                bit *= 2
            keep = pltpu.make_async_copy(
                sums[kind].at[0, window], gathered[kind].at[mine, window], own_sem.at[one]
            )
            keep.start()
            sent = []

            def pass_on(place, bit):
                block = jnp.bitwise_xor(mine, place)
                target = gathered[kind].at[block, window]
                return pltpu.make_async_remote_copy(
                    src_ref=sums[kind].at[0, window] if place == 0 else target,
                    dst_ref=target,
                    send_sem=ring_send.at[one, place ^ bit],
                    recv_sem=ring_recv.at[one, place ^ bit],
                    device_id=peer_at(0, 0, bit * spread),
                    device_id_type=pl.DeviceIdType.MESH,
                )

            def forward(place):
                for bit, held in gather_steps(members):
                    if place in held:
                        copy = pass_on(place, bit)
                        copy.start()
                        sent.append(copy)

            forward(0)
            for place in range(1, members):
                wait = near_wait if place == 1 else far_wait if place & (place - 1) == 0 else last_wait
                yield time + wait + (far_wait if wait == last_wait else 0)
                bit = place & -place
                pass_on(place ^ bit, bit).wait_recv()
                forward(place)
            yield 1000
            keep.wait()
            for copy in sent:
                copy.wait_send()

        def bit_of(place):
            deep_bit, far_bit, near_bit = place
            axis, bit = ("dp", deep_bit) if deep_bit else ("exp", far_bit) if far_bit else ("ctx", near_bit)
            return lax.rem(lax.axis_index(axis) // bit, 2)

        def dense_chain(times):
            times = iter(times + tuple(range(times[-1] + 8, 900, 8)))
            buffers = [halves.at[0], halves.at[1], smalls]
            yield 0
            for copy in dense_in:
                copy.wait()
            begins = [0] * groups
            trail = []

            def window(begin, length, group):
                if isinstance(begin, int):
                    return pl.ds(begin, length)
                return pl.ds(pl.multiple_of(begin, tile[group]), length)

            def exchange_rows(group, step, source, target):
                return pltpu.make_async_remote_copy(
                    src_ref=source,
                    dst_ref=target,
                    send_sem=dense_send.at[group, step],
                    recv_sem=dense_recv.at[group, step],
                    device_id=peer_at(*orders[group][step % bit_count]),
                    device_id_type=pl.DeviceIdType.MESH,
                )

            for step in range(bit_count):
                copies = []
                for group in range(groups):
                    halved, length = plans[group][step]
                    upper = bit_of(orders[group][step])
                    if halved:
                        sent = begins[group] + (1 - upper) * length
                        begins[group] = begins[group] + upper * length
                    else:
                        sent = begins[group]
                    at = sum(size for _, size in plans[group][:step])
                    copy = exchange_rows(
                        group,
                        step,
                        buffers[group].at[window(sent, length, group)],
                        group_landed[group].at[pl.ds(at, length)],
                    )
                    copy.start()
                    copies.append((copy, at, length))
                trail.append(list(begins))
                yield next(times)
                for group, (copy, at, length) in enumerate(copies):
                    copy.wait()
                    add_into(
                        buffers[group].at[window(begins[group], length, group)],
                        group_landed[group].at[pl.ds(at, length)],
                    )
            outputs = [wide_out.at[0], wide_out.at[1], small_out]
            keeps = []
            for group in range(groups):
                part = window(begins[group], plans[group][-1][1], group)
                keep = pltpu.make_async_copy(
                    buffers[group].at[part], outputs[group].at[part], dense_load.at[group]
                )
                keep.start()
                keeps.append(keep)
            for keep in keeps:
                keep.wait()
            for step in range(bit_count - 1, -1, -1):
                copies = []
                for group in range(groups):
                    halved, length = plans[group][step]
                    if halved:
                        part = outputs[group].at[window(trail[step][group], length, group)]
                        copy = exchange_rows(group, bit_count + step, part, part)
                        copy.start()
                        copies.append(copy)
                if copies:
                    yield next(times)
                for copy in copies:
                    copy.wait()

        chains = [dense_chain(DENSE_TIMES)] + [
            expert_chain(kind, piece) for kind in range(kinds) for piece in range(PIECES)
        ]
        due = dict(enumerate(next(chain) for chain in chains))
        planned = list(ORDER) if (shares, ring, exchange_size) == (4, 4, 2) else []
        while due:
            index = planned.pop(0) if planned else min(due, key=lambda one: (due[one], one))
            time = next(chains[index], None)
            if time is None:
                del due[index]
            else:
                due[index] = time

    any_space = pl.BlockSpec(memory_space=pl.ANY)
    extra = len(steps) + spread.bit_length() - 1
    return pl.pallas_call(
        kernel,
        out_shape=[jax.ShapeDtypeStruct((members,) + block, low) for block in blocks]
        + [jax.ShapeDtypeStruct(wide.shape, low), jax.ShapeDtypeStruct(small.shape, full)],
        in_specs=[any_space] * (2 * kinds + 2),
        out_specs=[any_space] * (kinds + 2),
        scratch_shapes=[pltpu.VMEM((shares // 2,) + block, low) for block in blocks]
        + [pltpu.VMEM((extra,) + block, low) for block in blocks]
        + [pltpu.VMEM(wide.shape, low), pltpu.VMEM(small.shape, full)]
        + [
            pltpu.VMEM(
                (sum(length for _, length in plans[group]), (wide, wide, small)[group].shape[-1]),
                (low, low, full)[group],
            )
            for group in range(groups)
        ]
        + [
            pltpu.SemaphoreType.DMA((kinds, shares // 2 + 1)),
            pltpu.SemaphoreType.DMA((kinds * PIECES, extra)),
            pltpu.SemaphoreType.DMA((kinds * PIECES, extra)),
            pltpu.SemaphoreType.DMA((kinds * PIECES,)),
            pltpu.SemaphoreType.DMA((kinds * PIECES, members)),
            pltpu.SemaphoreType.DMA((kinds * PIECES, members)),
            pltpu.SemaphoreType.DMA((groups, 2 * bit_count)),
            pltpu.SemaphoreType.DMA((groups, 2 * bit_count)),
            pltpu.SemaphoreType.DMA((3,)),
        ],
        compiler_params=pltpu.CompilerParams(
            collective_id=3, has_side_effects=True, vmem_limit_bytes=60 * 2**20
        ),
        name="reduce",
    )(*terms, *firsts, wide, small)


def widen_layer(parts, wide, small, experts):
    members = parts[0].shape[0]
    pieces = 4
    steps = members * pieces
    squares = wide.shape[1] // (2 * wide.shape[2])
    width = 2 * wide.shape[2]
    lines = wide.shape[1] // steps
    turns = width // lines
    full = jnp.float32
    kinds = len(parts)

    def kernel(*refs):
        sources, wide_ref, small_ref = refs[:kinds], refs[kinds], refs[kinds + 1]
        targets = refs[kinds + 2 : 2 * kinds + 2]
        square_refs = refs[2 * kinds + 2 : 2 * kinds + 2 + squares]
        head_ref, map_ref, carry_ref, vector_ref, gains_ref = refs[2 * kinds + 2 + squares :]
        step = pl.program_id(0) * pieces + pl.program_id(1)
        for source, target in zip(sources, targets):
            target[...] = source[...].astype(full)
        for index in range(squares):

            @pl.when(step // turns == index)
            def _():
                square_refs[index][:, 0 : width // 2] = wide_ref[0].astype(full)
                square_refs[index][:, width // 2 :] = wide_ref[1].astype(full)

        @pl.when(step == 0)
        def _():
            head_ref[...] = small_ref[8 : 8 + experts, :]
            for index in range(2):
                begin = 8 + experts + 2 * index
                map_ref[index] = small_ref[begin : begin + 2, :]
            carry_ref[...] = jnp.transpose(small_ref[24:40, 0:128])[0:experts, 0:experts]
            vector_ref[...] = small_ref[2:4, :]
            gains_ref[...] = small_ref[0:2, :]

    def chunk(part):
        return pl.BlockSpec(
            (1, part.shape[1] // pieces, part.shape[2]), lambda member, piece: (member, piece, 0)
        )

    def square(index):
        return pl.BlockSpec(
            (lines, width),
            lambda member, piece: (
                jnp.clip(member * pieces + piece - index * turns, 0, turns - 1),
                0,
            ),
        )

    def whole(*shape):
        return pl.BlockSpec(shape, lambda member, piece: (0,) * len(shape))

    smalls = [(experts, width), (2, 2, width), (experts, experts), (2, width), (2, width)]
    return pl.pallas_call(
        kernel,
        out_shape=[jax.ShapeDtypeStruct(part.shape, full) for part in parts]
        + [jax.ShapeDtypeStruct((width, width), full)] * squares
        + [jax.ShapeDtypeStruct(shape, full) for shape in smalls],
        grid=(members, pieces),
        in_specs=[chunk(part) for part in parts]
        + [
            pl.BlockSpec(
                (2, lines, width // 2), lambda member, piece: (0, member * pieces + piece, 0)
            ),
            whole(*small.shape),
        ],
        out_specs=[chunk(part) for part in parts]
        + [square(index) for index in range(squares)]
        + [whole(*shape) for shape in smalls],
        compiler_params=pltpu.CompilerParams(vmem_limit_bytes=60 * 2**20),
        name="widen",
    )(*parts, wide, small)


def local(
    tokens,
    cotangent,
    previous,
    routes,
    boundaries,
    norm_first,
    query_weight,
    key_weight,
    value_weight,
    output_weight,
    norm_second,
    router,
    gate_carry,
    constant_map,
    constant_vector,
    expert_gate,
    expert_linear,
    expert_down,
):
    model_width = tokens.shape[2]
    ring = lax.axis_size("ctx")
    group_size = expert_gate.shape[0]
    exchange_count = lax.axis_size("exp")
    spread = ring // group_size
    ranks = (exchange_count, group_size, spread)
    slot_total = exchange_count * group_size * CAP
    expert_total = router.shape[1]
    params = (
        router.T,
        jnp.transpose(constant_map, (0, 2, 1)),
        norm_first,
        norm_second,
        constant_vector,
    )
    prior = jnp.transpose(previous, (2, 0, 1))
    weights = (query_weight, key_weight, value_weight, output_weight)
    (
        queries,
        keys,
        values,
        attended,
        lse,
        middle,
        probs,
        targets,
        outgoing,
        slot_gates,
        grads_in,
    ) = attend_layer(
        tokens[0],
        cotangent[0],
        prior,
        routes[0].T,
        boundaries,
        weights,
        params,
        gate_carry,
        ranks,
        CAP,
        ring,
    )
    home_grads, produced, dots, gate_terms, linear_terms, down_terms, first = expert_layer(
        outgoing,
        slot_gates,
        grads_in.reshape(slot_total, model_width),
        (expert_gate, expert_linear, expert_down),
        ranks,
        lax.axis_size("dp"),
    )
    terms = (down_terms, gate_terms, linear_terms)
    shares = lax.axis_size("dp")
    result, token_grads, wide, small, *firsts = backward_layer(
        tokens[0],
        cotangent[0],
        prior,
        routes[0].T,
        boundaries,
        (attended, lse, middle, probs, targets, queries, keys, values),
        (home_grads.reshape(slot_total, model_width), produced, dots),
        weights,
        params,
        terms,
        first,
        ranks,
        CAP,
        ring,
        shares,
    )
    *parts, wide, small = reduce_layer(
        terms, firsts, wide, small, spread, shares, ring, exchange_count
    )
    (
        down_grads,
        gate_grads,
        linear_grads,
        query_grads,
        key_grads,
        value_grads,
        output_grads,
        router_grads,
        map_grads,
        carry_grads,
        vector_grads,
        gain_grads,
    ) = widen_layer(parts, wide, small, expert_total)
    return (
        result[None],
        token_grads[None],
        gain_grads[0],
        query_grads,
        key_grads,
        value_grads,
        output_grads,
        gain_grads[1],
        router_grads.T,
        carry_grads,
        jnp.transpose(map_grads, (0, 2, 1)),
        vector_grads,
        gate_grads,
        linear_grads,
        down_grads,
    )


def solution(mesh):
    return jax.shard_map(
        local,
        mesh=mesh,
        in_specs=(
            P(("dp", "exp"), "ctx", None),
            P(("dp", "exp"), "ctx", None),
            P(("dp", "exp"), "ctx", None),
            P(("dp", "exp"), "ctx", None),
            P(("dp", "exp"), None),
            P(),
            P(),
            P(),
            P(),
            P(),
            P(),
            P(),
            P(),
            P(),
            P(),
            P("exp", None, None),
            P("exp", None, None),
            P("exp", None, None),
        ),
        out_specs=(
            P(("dp", "exp"), "ctx", None),
            P(("dp", "exp"), "ctx", None),
            P(),
            P(),
            P(),
            P(),
            P(),
            P(),
            P(),
            P(),
            P(),
            P(),
            P("exp", None, "dp"),
            P("exp", None, "dp"),
            P("exp", "dp", None),
        ),
        check_vma=False,
    )
```

```python
import math

import jax
import jax.numpy as jnp
import numpy as np
from jax import lax
from jax.experimental import pallas as pl
from jax.experimental.pallas import tpu as pltpu
from jax.sharding import PartitionSpec as P

HEAD_DIM = 64
CAP = 96


EPSILON = 1e-06
NEGATIVE = -1e30
HIGH = lax.Precision.HIGHEST


HEAD_ROWS = 16


def mesh_id(exp_index, ctx_index):
    return {"exp": exp_index, "ctx": ctx_index}


def dot(left, right):
    return jnp.dot(left, right, preferred_element_type=jnp.float32)


def dot_nt(left, right):
    return lax.dot_general(
        left, right, (((1,), (1,)), ((), ())), preferred_element_type=jnp.float32
    )


def dot_tn(left, right):
    return lax.dot_general(
        left, right, (((0,), (0,)), ((), ())), preferred_element_type=jnp.float32
    )


def member_of(shift, ranks):
    exchange_size, group_size, spread = ranks
    exp_index, ctx_index = lax.axis_index("exp"), lax.axis_index("ctx")
    far, near = shift // group_size, shift % group_size
    place = jnp.bitwise_xor(ctx_index // spread, near) * spread + lax.rem(ctx_index, spread)
    return mesh_id(jnp.bitwise_xor(exp_index, far), place)


def greet(count, ranks):
    barrier = pltpu.get_barrier_semaphore()
    for shift in range(1, count):
        pl.semaphore_signal(
            barrier, inc=1, device_id=member_of(shift, ranks), device_id_type=pl.DeviceIdType.MESH
        )
    pl.semaphore_wait(barrier, count - 1)


def block_of(shift, count):
    return (shift + count - count // 4) % count


def own_block(count):
    return block_of(0, count)


def send_block(source, target, block, ranks, send_sem, recv_sem):
    count = ranks[0] * ranks[1]
    return pltpu.make_async_remote_copy(
        src_ref=source.at[block],
        dst_ref=target.at[block],
        send_sem=send_sem.at[block],
        recv_sem=recv_sem.at[block],
        device_id=member_of((block + count // 4) % count, ranks),
        device_id_type=pl.DeviceIdType.MESH,
    )


def keep_block(source, target, count, sem):
    block = own_block(count)
    return pltpu.make_async_copy(source.at[block], target.at[block], sem)


def other_blocks(count):
    return [block for block in range(count) if block != own_block(count)]


def expert_layer(outgoing, gates, grads, weights, ranks, shares):
    count, cap, width = outgoing.shape
    hidden_units = weights[0].shape[2]
    rows = count * cap
    share = hidden_units // shares
    spread = ranks[2]

    def kernel(
        outgoing_hbm,
        gates_ref,
        grads_ref,
        gate_hbm,
        linear_hbm,
        down_hbm,
        back_ref,
        output_ref,
        dots_ref,
        gate_terms,
        linear_terms,
        down_terms,
        first_ref,
        received,
        received_gates,
        gate_w,
        linear_w,
        down_w,
        hidden_grad,
        hidden,
        gate_low,
        linear_low,
        rows_t,
        scaled,
        gate_column,
        out_total,
        in_total,
        in_send,
        dots_send,
        terms,
        weight_sem,
        send_sem,
        recv_sem,
        local_sem,
        terms_sem,
        first_send,
        first_recv,
    ):
        own = lax.axis_index("ctx") // spread
        loads = [
            pltpu.make_async_copy(source.at[own], target, weight_sem.at[index])
            for index, (source, target) in enumerate(
                ((down_hbm, down_w), (gate_hbm, gate_w), (linear_hbm, linear_w))
            )
        ]
        for load in loads:
            load.start()
        greet_places([(0,) + place for place in group_places(ranks)] + [(1, 0, 0)])

        def send_some(source, target, index, shifts):
            copies = []
            for shift in shifts:
                if shift == own_block(count):
                    copies.append(keep_block(source, target, count, local_sem.at[index]))
                else:
                    copies.append(
                        send_block(
                            source, target, shift, ranks, send_sem.at[index], recv_sem.at[index]
                        )
                    )
            for copy in copies:
                copy.start()
            return copies

        every = range(count)
        gates_in = send_some(gates_ref, received_gates, 0, every)
        soon = [block for block in every if not count // 2 <= block < count - count // 4]
        incoming = dict(zip(soon, send_some(outgoing_hbm, received, 1, soon)))
        loads[0].wait()

        def backward_in(index, carry):
            part = pl.ds(pl.multiple_of(index * share, share), share)
            hidden_grad[:, part] = dot_nt(grads_ref[...], down_w[part, :])
            return carry

        lax.fori_loop(0, shares, backward_in, 0)
        for copy in gates_in:
            copy.wait()
        for shift in every:
            column = jnp.transpose(received_gates[shift])[:cap, 0:1]
            block = pl.ds(shift * cap, cap)
            gate_column[block, :] = jnp.broadcast_to(column, (cap, 128))
            scaled[block, :] = (column * grads_ref[block, :].astype(jnp.float32)).astype(
                jnp.bfloat16
            )
        for load in loads[1:]:
            load.wait()

        going = []
        batches = 2
        members = count // batches
        lines = rows // batches
        for batch in range(batches):
            chunks = range(batch * members, (batch + 1) * members)
            for shift in chunks:
                incoming[shift].wait()
            if batch == 0:
                late = [block for block in every if block not in soon]
                incoming.update(zip(late, send_some(outgoing_hbm, received, 1, late)))
            block = pl.ds(batch * lines, lines)

            def through(index):
                part = pl.ds(index * share, share)
                tokens = received[batch * members : (batch + 1) * members].reshape(lines, width)
                gate_part = dot(tokens, gate_w[:, part])
                linear_part = dot(tokens, linear_w[:, part])
                sigmoid = 1.0 / (1.0 + jnp.exp(-gate_part))
                silu = gate_part * sigmoid
                low = (silu * linear_part).astype(jnp.bfloat16)
                hidden[block, part] = low
                upper = hidden_grad[block, part] * gate_column[block, 0:1]
                low_gate = (
                    upper * linear_part * sigmoid * (1.0 + gate_part * (1.0 - sigmoid))
                ).astype(jnp.bfloat16)
                gate_low[block, part] = low_gate
                low_linear = (upper * silu).astype(jnp.bfloat16)
                linear_low[block, part] = low_linear
                out = dot(low, down_w[part, :])
                back = dot_nt(low_gate, gate_w[:, part]) + dot_nt(low_linear, linear_w[:, part])

                if index == 0:
                    out_total[block, :] = out
                    in_total[block, :] = back
                else:
                    out_total[block, :] += out
                    in_total[block, :] += back

            for tile in range(shares):
                through(tile)
            in_send[batch * members : (batch + 1) * members] = (
                in_total[block, :].astype(jnp.bfloat16).reshape(members, cap, width)
            )
            going += send_some(in_send, back_ref, 2, chunks)
            low = out_total[block, :].astype(jnp.bfloat16)
            output_ref[batch * members : (batch + 1) * members] = low.reshape(members, cap, width)
            dots = jnp.sum(
                low.astype(jnp.float32) * grads_ref[block, :].astype(jnp.float32),
                axis=1,
                keepdims=True,
            )
            for place, shift in enumerate(chunks):
                column = jnp.broadcast_to(dots[place * cap : (place + 1) * cap], (cap, 128))
                dots_send[shift, :, 0:cap] = jnp.transpose(column)[0:8, :]
                dots_send[shift, :, cap:] = jnp.zeros((8, 128 - cap), jnp.float32)
            going += send_some(dots_send, dots_ref, 3, chunks)
            rows_t[:, batch * lines : (batch + 1) * lines] = jnp.transpose(
                received[batch * members : (batch + 1) * members].reshape(lines, width)
            )

        def term_copy(which, index):
            target = (down_terms, gate_terms, linear_terms)[which]
            return pltpu.make_async_copy(
                terms[which].at[index], target.at[index], terms_sem.at[which, index]
            )

        def weigh(which, turn):
            index = jnp.bitwise_xor(lax.axis_index("dp"), shares - 1 - turn)
            part = pl.ds(pl.multiple_of(index * share, share), share)
            if which == 0:
                value = dot_tn(hidden[:, part], scaled[...])
            else:
                value = dot(rows_t[...], (gate_low if which == 1 else linear_low)[:, part])
            terms[which][index] = value.astype(jnp.bfloat16)
            term_copy(which, index).start()
            return index

        index = weigh(0, 0)
        first = pltpu.make_async_remote_copy(
            src_ref=terms[0].at[index],
            dst_ref=first_ref,
            send_sem=first_send,
            recv_sem=first_recv,
            device_id=peer_at(1, 0, 0),
            device_id_type=pl.DeviceIdType.MESH,
        )
        first.start()

        def weigh_rest(turn, carry):
            weigh(1, turn)
            weigh(2, turn)

            @pl.when(turn > 0)
            def _():
                weigh(0, turn)

            return carry

        lax.fori_loop(0, shares, weigh_rest, 0)
        for which in range(3):
            for index in range(shares):
                term_copy(which, index).wait()
        for copy in going:
            copy.wait()
        first.wait()

    low, full = jnp.bfloat16, jnp.float32
    columns, lines = (shares, width, share), (shares, share, width)
    any_space = pl.BlockSpec(memory_space=pl.ANY)
    in_vmem = pl.BlockSpec(memory_space=pltpu.VMEM)
    return pl.pallas_call(
        kernel,
        out_shape=[
            jax.ShapeDtypeStruct(outgoing.shape, low),
            jax.ShapeDtypeStruct(outgoing.shape, low),
            jax.ShapeDtypeStruct(gates.shape, full),
            jax.ShapeDtypeStruct(columns, low),
            jax.ShapeDtypeStruct(columns, low),
            jax.ShapeDtypeStruct(lines, low),
            jax.ShapeDtypeStruct(lines[1:], low),
        ],
        in_specs=[any_space, in_vmem, in_vmem, any_space, any_space, any_space],
        out_specs=[any_space, in_vmem] + [any_space] * 5,
        scratch_shapes=[
            pltpu.VMEM(outgoing.shape, low),
            pltpu.VMEM(gates.shape, full),
            pltpu.VMEM((width, hidden_units), low),
            pltpu.VMEM((width, hidden_units), low),
            pltpu.VMEM((hidden_units, width), low),
            pltpu.VMEM((rows, hidden_units), full),
            pltpu.VMEM((rows, hidden_units), low),
            pltpu.VMEM((rows, hidden_units), low),
            pltpu.VMEM((rows, hidden_units), low),
            pltpu.VMEM((width, rows), low),
            pltpu.VMEM((rows, width), low),
            pltpu.VMEM((rows, 128), full),
            pltpu.VMEM((rows, width), full),
            pltpu.VMEM((rows, width), full),
            pltpu.VMEM(outgoing.shape, low),
            pltpu.VMEM(gates.shape, full),
            [pltpu.VMEM(lines, low), pltpu.VMEM(columns, low), pltpu.VMEM(columns, low)],
            pltpu.SemaphoreType.DMA((3,)),
            pltpu.SemaphoreType.DMA((4, count)),
            pltpu.SemaphoreType.DMA((4, count)),
            pltpu.SemaphoreType.DMA((4,)),
            pltpu.SemaphoreType.DMA((3, shares)),
            pltpu.SemaphoreType.DMA,
            pltpu.SemaphoreType.DMA,
        ],
        compiler_params=pltpu.CompilerParams(
            collective_id=1, has_side_effects=True, vmem_limit_bytes=60 * 2**20
        ),
        cost_estimate=pl.CostEstimate(
            flops=18 * rows * width * hidden_units,
            bytes_accessed=12 * width * hidden_units + 12 * rows * width,
            transcendentals=rows * hidden_units,
        ),
        name="experts",
    )(outgoing, gates, grads, *weights)


def rope_tables(row_count):
    half = HEAD_DIM // 2
    frequency = np.exp(
        np.arange(half, dtype=np.float32) * np.float32(-2.0 * math.log(10000.0) / HEAD_DIM)
    ).astype(np.float32)
    angles = np.arange(row_count, dtype=np.float32)[:, None] * frequency[None, :]
    cosine, sine = np.cos(angles).astype(np.float32), np.sin(angles).astype(np.float32)
    return (
        np.concatenate([cosine] * 4, axis=1),
        np.concatenate([-sine, sine, -sine, sine], axis=1),
    )


def rotate(values, cosine, sine):
    lane = lax.broadcasted_iota(jnp.int32, cosine.shape, 1)
    leading = jnp.bitwise_and(lane, HEAD_DIM - 1) < HEAD_DIM // 2
    parts = []
    for begin in range(0, values.shape[1], 128):
        part = values[:, begin : begin + 128]
        ahead = pltpu.roll(part, 128 - HEAD_DIM // 2, 1)
        behind = pltpu.roll(part, HEAD_DIM // 2, 1)
        parts.append(part * cosine + jnp.where(leading, ahead, behind) * sine)
    return jnp.concatenate(parts, axis=1)


def inverse_norm(values):
    return lax.rsqrt(jnp.mean(values * values, axis=1, keepdims=True) + EPSILON)


def head_masks(rows):
    first = lax.broadcasted_iota(jnp.int32, (rows, 128), 1) < HEAD_DIM
    return first, jnp.logical_not(first)


def start_of(positions, starts):
    first = jnp.zeros_like(positions)
    for index in range(starts.shape[1]):
        begin = starts[0, index]
        first = jnp.where(begin <= positions, jnp.maximum(first, begin), first)
    return first


def gather_steps(size):
    bits, held, steps = [], [0], []
    bit = size // 2
    while bit >= 1:
        steps.append((bit, list(held)))
        held = held + [place ^ bit for place in held]
        bit //= 2
    return steps


def peer_at(deep, far, near):
    return {
        "dp": jnp.bitwise_xor(lax.axis_index("dp"), deep),
        "exp": jnp.bitwise_xor(lax.axis_index("exp"), far),
        "ctx": jnp.bitwise_xor(lax.axis_index("ctx"), near),
    }


def peer(far, near):
    return peer_at(0, far, near)


def greet_places(places):
    barrier = pltpu.get_barrier_semaphore()
    for place in places:
        pl.semaphore_signal(
            barrier, inc=1, device_id=peer_at(*place), device_id_type=pl.DeviceIdType.MESH
        )
    pl.semaphore_wait(barrier, len(places))


def greet_all(places):
    greet_places([(0,) + place for place in places])


def group_places(ranks):
    return [
        (shift // ranks[1], shift % ranks[1] * ranks[2]) for shift in range(1, ranks[0] * ranks[1])
    ]


def ring_places(size):
    return [(0, bit) for bit, _ in gather_steps(size)]


def places_of(ranks, size):
    places = group_places(ranks)
    return places + [place for place in ring_places(size) if place not in places]


class Gather:
    def __init__(self, buffers, size, send_sem, recv_sem, sources=None):
        self.buffers, self.sources = buffers, sources
        self.send_sem, self.recv_sem = send_sem, recv_sem
        self.steps = gather_steps(size)

    def copy(self, place, bit, index):
        block = jnp.bitwise_xor(lax.axis_index("ctx"), place)
        buffer = self.buffers[index]
        straight = self.sources is not None and place == 0
        return pltpu.make_async_remote_copy(
            src_ref=self.sources[index] if straight else buffer.at[block],
            dst_ref=buffer.at[block],
            send_sem=self.send_sem.at[index, place ^ bit],
            recv_sem=self.recv_sem.at[index, place ^ bit],
            device_id=peer(0, bit),
            device_id_type=pl.DeviceIdType.MESH,
        )

    def forward(self, place):
        for bit, held in self.steps:
            if place in held:
                for index in range(len(self.buffers)):
                    self.copy(place, bit, index).start()

    def arrive(self, place):
        bit = place & -place
        for index in range(len(self.buffers)):
            self.copy(place ^ bit, bit, index).wait_recv()
        self.forward(place)

    def finish(self):
        for bit, held in self.steps:
            for place in held:
                for index in range(len(self.buffers)):
                    self.copy(place, bit, index).wait_send()


def fill_rows(pack, prior, router_ref, map_ref, first_ref, second_ref, vector_ref, previous_ref):
    full = jnp.float32
    experts = router_ref.shape[0]
    width = router_ref.shape[1]
    pack[0:experts, :] = router_ref[...].astype(full)
    for index in range(2):
        pack[experts + 2 * index : experts + 2 * index + 2, :] = map_ref[index].astype(full)
    pack[HEAD_ROWS : HEAD_ROWS + 1, :] = first_ref[...].astype(full).reshape(1, width)
    pack[HEAD_ROWS + 1 : HEAD_ROWS + 2, :] = second_ref[...].astype(full).reshape(1, width)
    pack[HEAD_ROWS + 2 : HEAD_ROWS + 4, :] = vector_ref[...].astype(full)
    for index in range(experts):
        prior[index : index + 1, :] = previous_ref[index]


def slot_targets(routes, ranks, cap):
    exchange_size, group_size, spread = ranks
    rows = routes.shape[1]
    experts = exchange_size * group_size
    expert = lax.broadcasted_iota(jnp.int32, (16, rows), 0)
    hits = [(expert == routes[k : k + 1]).astype(jnp.float32) for k in range(2)]
    before = lax.broadcasted_iota(jnp.int32, (rows, rows), 0) < lax.broadcasted_iota(
        jnp.int32, (rows, rows), 1
    )
    earlier = dot(
        (hits[0] + hits[1]).astype(jnp.bfloat16), before.astype(jnp.float32).astype(jnp.bfloat16)
    )
    targets = []
    for k in range(2):
        route = routes[k : k + 1]
        rank = jnp.sum(hits[k] * earlier, axis=0, keepdims=True)
        far = jnp.bitwise_xor(route // group_size, lax.axis_index("exp"))
        near = jnp.bitwise_xor(route % group_size, lax.axis_index("ctx") // spread)
        count = exchange_size * group_size
        block = jnp.bitwise_and(far * group_size + near + count - count // 4, count - 1)
        place = (block * cap).astype(jnp.float32)
        targets.append(jnp.where(route < experts, place + rank, -1.0))
    return targets


def attend_layer(
    tokens, cotangent, previous, routes, starts, weights, params, carry, ranks, cap, size
):
    rows, width = tokens.shape
    count = ranks[0] * ranks[1]
    slots = count * cap
    pairs = width // 128
    tables = rope_tables(size * rows)
    low, full = jnp.bfloat16, jnp.float32

    def kernel(
        tokens_hbm,
        cotangent_ref,
        previous_ref,
        routes_ref,
        starts_ref,
        query_hbm,
        key_hbm,
        value_hbm,
        output_hbm,
        router_ref,
        map_ref,
        first_ref,
        second_ref,
        vector_ref,
        carry_ref,
        cosine_hbm,
        sine_hbm,
        queries_out,
        keys_out,
        values_out,
        attended_ref,
        lse_ref,
        middle_ref,
        probs_ref,
        targets_ref,
        outgoing_ref,
        gates_ref,
        grads_ref,
        stream,
        queries,
        keys,
        values,
        query_w,
        key_w,
        value_w,
        output_w,
        cosine,
        sine,
        bias,
        totals,
        highest,
        slot_grads,
        load_sem,
        gather_send,
        gather_recv,
        grad_send,
        grad_recv,
        keep_sem,
        pack,
        prior,
    ):
        own = lax.axis_index("ctx")
        bring = pltpu.make_async_copy(tokens_hbm, stream.at[own], load_sem.at[6])
        bring.start()
        loads = [
            pltpu.make_async_copy(source, target, load_sem.at[index])
            for index, (source, target) in enumerate(
                (
                    (query_hbm, query_w),
                    (key_hbm, key_w),
                    (value_hbm, value_w),
                    (cosine_hbm, cosine),
                    (sine_hbm, sine),
                    (output_hbm, output_w),
                )
            )
        ]
        for load in loads:
            load.start()
        greet_all(places_of(ranks, size))
        gather = Gather([stream], size, gather_send, gather_recv, [tokens_hbm])
        gather.forward(0)

        fill_rows(
            pack, prior, router_ref, map_ref, first_ref, second_ref, vector_ref, previous_ref
        )
        targets = slot_targets(routes_ref[...], ranks, cap)
        slot = lax.broadcasted_iota(jnp.int32, (slots, rows), 0).astype(full)
        picked = jnp.logical_or(slot == targets[0], slot == targets[1])
        picked = picked.astype(full).astype(low)
        slot_grads[...] = dot(picked, cotangent_ref[...]).astype(low).reshape(count, cap, width)
        grad_copies = [
            send_block(slot_grads, grads_ref, block, ranks, grad_send, grad_recv)
            for block in other_blocks(count)
        ]
        grad_copies.append(keep_block(slot_grads, grads_ref, count, keep_sem.at[0]))

        bring.wait()
        for load in loads[:5]:
            load.wait()
        gain = pack[HEAD_ROWS : HEAD_ROWS + 1, :]

        def project(block, wanted):
            line = pl.ds(pl.multiple_of(block * rows, rows), rows)
            values_in = stream[block].astype(full)
            normed = (values_in * inverse_norm(values_in) * gain).astype(low)
            if "q" in wanted:
                turned = rotate(dot(normed, query_w[...]), cosine[line, :], sine[line, :])
                queries[block] = (turned.astype(low).astype(full) * HEAD_DIM**-0.5).astype(low)
            if "k" in wanted:
                turned = rotate(dot(normed, key_w[...]), cosine[line, :], sine[line, :])
                keys[block] = turned.astype(low)
                values[block] = dot(normed, value_w[...]).astype(low)

        masks = head_masks(rows)
        query_pos = own * rows + lax.broadcasted_iota(jnp.int32, (rows, rows), 1)
        document_start = start_of(query_pos[0:8], starts_ref)[0:1]

        def attend(block):
            key_pos = block * rows + lax.broadcasted_iota(jnp.int32, (rows, rows), 0)
            allowed = jnp.logical_and(key_pos >= document_start, key_pos <= query_pos)
            bias[...] = jnp.where(allowed, 0.0, NEGATIVE)

            def pair(index, carried):
                lanes = pl.ds(pl.multiple_of(index * 128, 128), 128)
                query, key, value = queries[own, :, lanes], keys[block, :, lanes], values[block, :, lanes]
                scores = [dot_nt(jnp.where(mask, key, 0), query) + bias[...] for mask in masks]
                old = [highest[index, head][0:1, :] for head in range(2)]
                new = [
                    jnp.maximum(old[head], jnp.max(scores[head], axis=0, keepdims=True))
                    for head in range(2)
                ]
                weight = [jnp.exp(scores[head] - new[head]).astype(low) for head in range(2)]
                for head in range(2):
                    totals[index, head] = totals[index, head] * jnp.exp(old[head] - new[head]) + dot_tn(
                        jnp.where(masks[head], value, 1), weight[head]
                    )
                    highest[index, head] = jnp.broadcast_to(new[head], (8, rows))
                return carried

            lax.fori_loop(0, pairs, pair, 0)

        totals[...] = jnp.zeros_like(totals)
        highest[...] = jnp.full(highest.shape, NEGATIVE, full)
        project(own, "qk")
        attend(own)
        def others(place, carried):
            for one in range(1, size):

                @pl.when(place == one)
                def _():
                    gather.arrive(one)
                    if one == size // 2:
                        for copy in grad_copies:
                            copy.start()

            block = jnp.bitwise_xor(own, place)

            @pl.when(block < own)
            def _():
                project(block, "k")
                attend(block)

            @pl.when(block > own)
            def _():
                project(block, "q")

            return carried

        lax.fori_loop(1, size, others, 0)
        keep = [
            pltpu.make_async_copy(source, target, keep_sem.at[index + 1])
            for index, (source, target) in enumerate(
                ((queries, queries_out), (keys, keys_out), (values, values_out))
            )
        ]
        for copy in keep:
            copy.start()

        lse_ref[...] = jnp.zeros_like(lse_ref)
        upper = lax.broadcasted_iota(jnp.int32, (128, rows), 0) < HEAD_DIM
        for index in range(pairs):
            halves = []
            for head in range(2):
                total = totals[index, head]
                line = HEAD_DIM if head == 0 else 0
                weight_sum = total[line : line + 1, :]
                halves.append(total / weight_sum)
                lse_ref[2 * index + head : 2 * index + head + 1, :] = highest[index, head][
                    0:1, :
                ] + jnp.log(weight_sum)
            attended_ref[:, index * 128 : index * 128 + 128] = jnp.transpose(
                jnp.where(upper, halves[0], halves[1])
            )
        loads[5].wait()
        middle = stream[own].astype(full) + dot(attended_ref[...].astype(low), output_w[...])
        middle_ref[...] = middle
        second = (
            middle
            * inverse_norm(middle)
            * pack[HEAD_ROWS + 1 : HEAD_ROWS + 2, :]
        )
        second_low = second.astype(low)
        outgoing_ref[...] = dot(picked, second_low).astype(low).reshape(count, cap, width)

        experts = previous_ref.shape[0]
        logits = dot_nt(second_low, pack[0:HEAD_ROWS, :].astype(low))[:, 0:experts] + lax.dot_general(
            prior[0:experts, :],
            carry_ref[...].astype(full),
            (((0,), (0,)), ((), ())),
            precision=HIGH,
        )
        logits = logits - jnp.max(logits, axis=1, keepdims=True)
        powers = jnp.exp(logits)
        probs_ref[...] = jnp.zeros_like(probs_ref)
        probs_ref[:, 0:experts] = powers / jnp.sum(powers, axis=1, keepdims=True)
        turned = jnp.transpose(probs_ref[...])[0:16]
        expert = lax.broadcasted_iota(jnp.int32, (16, rows), 0)
        weighted = jnp.zeros((slots, rows), full)
        for k in range(2):
            route = routes_ref[k : k + 1, :]
            gate = jnp.sum(jnp.where(expert == route, turned, 0.0), axis=0, keepdims=True)
            weighted = jnp.where(slot == targets[k], gate, weighted)
        gate_column = jnp.sum(weighted, axis=1, keepdims=True)
        for shift in range(count):
            column = jnp.broadcast_to(gate_column[shift * cap : (shift + 1) * cap], (cap, 128))
            gates_ref[shift] = jnp.zeros((8, 128), full)
            gates_ref[shift, :, 0:cap] = jnp.transpose(column)[0:8, :]
        pad = jnp.zeros((6, rows), full)
        target_rows = jnp.concatenate([targets[0], targets[1], pad], axis=0)
        target_rows = jnp.concatenate([target_rows] + [jnp.zeros((120, rows), full)], axis=0)
        targets_ref[...] = jnp.transpose(target_rows)

        gather.finish()
        for copy in keep + grad_copies:
            copy.wait()

    stream_shape = (size, rows, width)
    any_space = pl.BlockSpec(memory_space=pl.ANY)
    in_vmem = pl.BlockSpec(memory_space=pltpu.VMEM)
    square = (width, width)
    return pl.pallas_call(
        kernel,
        out_shape=[
            jax.ShapeDtypeStruct(stream_shape, low),
            jax.ShapeDtypeStruct(stream_shape, low),
            jax.ShapeDtypeStruct(stream_shape, low),
            jax.ShapeDtypeStruct((rows, width), full),
            jax.ShapeDtypeStruct((16, rows), full),
            jax.ShapeDtypeStruct((rows, width), full),
            jax.ShapeDtypeStruct((rows, 128), full),
            jax.ShapeDtypeStruct((rows, 128), full),
            jax.ShapeDtypeStruct((count, cap, width), low),
            jax.ShapeDtypeStruct((count, 8, 128), full),
            jax.ShapeDtypeStruct((count, cap, width), low),
        ],
        in_specs=[any_space]
        + [in_vmem] * 3
        + [pl.BlockSpec(memory_space=pltpu.SMEM)]
        + [any_space] * 4
        + [in_vmem] * 6
        + [any_space] * 2,
        out_specs=[any_space] * 3 + [in_vmem] * 7 + [any_space],
        scratch_shapes=[
            pltpu.VMEM(stream_shape, low),
            pltpu.VMEM(stream_shape, low),
            pltpu.VMEM(stream_shape, low),
            pltpu.VMEM(stream_shape, low),
            pltpu.VMEM(square, low),
            pltpu.VMEM(square, low),
            pltpu.VMEM(square, low),
            pltpu.VMEM(square, low),
            pltpu.VMEM((size * rows, 128), full),
            pltpu.VMEM((size * rows, 128), full),
            pltpu.VMEM((rows, rows), full),
            pltpu.VMEM((pairs, 2, 128, rows), full),
            pltpu.VMEM((pairs, 2, 8, rows), full),
            pltpu.VMEM((count, cap, width), low),
            pltpu.SemaphoreType.DMA((7,)),
            pltpu.SemaphoreType.DMA((1, size)),
            pltpu.SemaphoreType.DMA((1, size)),
            pltpu.SemaphoreType.DMA((count,)),
            pltpu.SemaphoreType.DMA((count,)),
            pltpu.SemaphoreType.DMA((4,)),
            pltpu.VMEM((24, width), full),
            pltpu.VMEM((16, rows), full),
        ],
        compiler_params=pltpu.CompilerParams(
            collective_id=0, has_side_effects=True, vmem_limit_bytes=60 * 2**20
        ),
        cost_estimate=pl.CostEstimate(
            flops=2 * size * rows * width * width * 3 + 16 * size * rows * rows * width,
            bytes_accessed=20 * 2**20,
            transcendentals=size * rows * rows * 12,
        ),
        name="attend",
    )(
        tokens,
        cotangent,
        previous,
        routes,
        starts,
        *weights,
        *params,
        carry,
        jnp.asarray(tables[0]),
        jnp.asarray(tables[1]),
    )


def add_into(target, source):
    rows = target.shape[0]
    piece = 96 if rows % 96 == 0 else (64 if rows % 64 == 0 else rows)

    def body(index, carried):
        part = pl.ds(pl.multiple_of(index * piece, piece), piece)
        total = target[part, :].astype(jnp.float32) + source[part, :].astype(jnp.float32)
        target[part, :] = total.astype(target.dtype)
        return carried

    lax.fori_loop(0, rows // piece, body, 0)


def column_of(values, index):
    return values[:, index : index + 1]


def backward_layer(
    tokens,
    cotangent,
    previous,
    routes,
    starts,
    forward,
    returns,
    weights,
    params,
    terms,
    first,
    ranks,
    cap,
    size,
    shares,
):
    rows, width = tokens.shape
    count = ranks[0] * ranks[1]
    slots = count * cap
    pairs = width // 128
    tables = rope_tables(size * rows)
    low, full = jnp.bfloat16, jnp.float32
    experts = previous.shape[0]
    copy_index = count + 1
    stat_rows = 16
    kinds = len(terms)

    def kernel(
        tokens_ref,
        cotangent_ref,
        previous_ref,
        routes_ref,
        starts_ref,
        attended_ref,
        lse_ref,
        middle_ref,
        probs_ref,
        targets_ref,
        queries_hbm,
        keys_hbm,
        values_hbm,
        back_ref,
        produced_hbm,
        dots_ref,
        query_hbm,
        key_hbm,
        value_hbm,
        output_hbm,
        router_ref,
        map_ref,
        first_gain_ref,
        second_gain_ref,
        vector_ref,
        cosine_hbm,
        sine_hbm,
        *rest,
    ):
        term_refs, first_hbm, rest = rest[:kinds], rest[kinds], rest[kinds + 1 :]
        result_ref, token_grads_ref, wide_ref, small_ref = rest[:4]
        first_refs, rest = rest[4 : 4 + kinds], rest[4 + kinds :]
        (
            queries,
            keys,
            values,
            query_w,
            key_w,
            value_w,
            output_w,
            cosine,
            sine,
            bias,
            out_grads,
            stats,
            outputs,
            middle_grad,
            query_total,
            key_total,
            value_total,
            load_sem,
            gather_send,
            gather_recv,
            first_send,
            first_recv,
            out_send,
            out_recv,
            out_keep,
            sum_part,
            first_part,
            sum_load,
            pack,
            prior,
        ) = rest
        own = lax.axis_index("ctx")
        line = pl.ds(pl.multiple_of(own * rows, rows), rows)
        loads = [
            pltpu.make_async_copy(source, target, load_sem.at[index])
            for index, (source, target) in enumerate(
                (
                    (output_hbm, output_w),
                    (queries_hbm, queries),
                    (keys_hbm, keys),
                    (values_hbm, values),
                    (cosine_hbm.at[line], cosine),
                    (sine_hbm.at[line], sine),
                    (query_hbm, query_w),
                    (key_hbm, key_w),
                    (value_hbm, value_w),
                )
            )
        ]
        for load in loads:
            load.start()
        share = lax.axis_index("dp")
        sum_loads = [
            pltpu.make_async_copy(
                term_refs[0].at[jnp.bitwise_xor(share, shares - 2)], sum_part, sum_load.at[0]
            ),
            pltpu.make_async_copy(first_hbm, first_part, sum_load.at[1]),
        ]
        for copy in sum_loads:
            copy.start()
        greet_places(
            [(0,) + place for place in places_of(ranks, size)] + [(1, 0, 0), (2, 0, 0)]
        )
        first_copies = [
            pltpu.make_async_remote_copy(
                src_ref=(
                    term_refs[kind].at[jnp.bitwise_xor(share, shares - 1)] if kind else sum_part
                ),
                dst_ref=first_refs[kind],
                send_sem=first_send.at[kind],
                recv_sem=first_recv.at[kind],
                device_id=peer_at(1 if kind else 2, 0, 0),
                device_id_type=pl.DeviceIdType.MESH,
            )
            for kind in range(kinds)
        ]
        for copy in first_copies[1:]:
            copy.start()
        for copy in sum_loads:
            copy.wait()
        add_into(sum_part, first_part)
        first_copies[0].start()
        output_copies = [
            send_block(produced_hbm, outputs, block, ranks, out_send, out_recv)
            for block in other_blocks(count)
        ]
        output_copies.append(keep_block(produced_hbm, outputs, count, out_keep))

        def keep_wide(index, value):
            half = width // 2
            for part in range(2):
                wide_ref[part, index * width : (index + 1) * width, :] = value[
                    :, part * half : (part + 1) * half
                ].astype(low)

        fill_rows(
            pack,
            prior,
            router_ref,
            map_ref,
            first_gain_ref,
            second_gain_ref,
            vector_ref,
            previous_ref,
        )
        lane = lax.broadcasted_iota(jnp.int32, (rows, 128), 1)
        upstream = cotangent_ref[...].astype(full)
        middle = middle_ref[...]
        inverse_second = inverse_norm(middle)
        unit_second = middle * inverse_second
        gain_second = pack[HEAD_ROWS + 1 : HEAD_ROWS + 2, :]
        second = unit_second * gain_second
        second_low = second.astype(low)
        heads_in = jnp.concatenate(
            [pack[0:HEAD_ROWS, :].astype(low), jnp.zeros((128 - HEAD_ROWS, width), low)], axis=0
        )
        mixed = dot_nt(second_low, heads_in)
        probs = probs_ref[...]
        route_rows = jnp.concatenate(
            [routes_ref[...].astype(full), jnp.zeros((126, rows), full)], axis=0
        )
        route_columns = jnp.transpose(route_rows).astype(jnp.int32)
        route = [column_of(route_columns, k) for k in range(2)]
        chosen = jnp.logical_or(lane == route[0], lane == route[1])
        gates = jnp.where(chosen, probs, 0.0)
        target = [column_of(targets_ref[...], k) for k in range(2)]

        gate_grad = jnp.zeros((rows, 128), full)
        place = lane.astype(full)
        for k in range(2):
            found = jnp.zeros((rows, 128), full)
            for shift in range(count):
                found = found + jnp.where(
                    jnp.logical_and(target[k] - shift * cap == place, lane < cap),
                    dots_ref[shift, 0:1, :],
                    0.0,
                )
            gate_grad = gate_grad + jnp.where(
                lane == route[k], jnp.sum(found, axis=1, keepdims=True), 0.0
            )
        copy_grad = jnp.sum(upstream * second, axis=1, keepdims=True)
        gate_grad = jnp.where(lane == copy_index, copy_grad, gate_grad)
        direct = column_of(gates, copy_index)
        constants = []
        for index in range(2):
            vector = pack[HEAD_ROWS + 2 + index : HEAD_ROWS + 3 + index, :]
            vector_dot = jnp.sum(upstream * vector, axis=1, keepdims=True)
            begin = experts + 2 * index
            spread_of = column_of(mixed, begin + 1) - column_of(mixed, begin)
            mixing = (1.0 / (1.0 + jnp.exp(spread_of)), 1.0 / (1.0 + jnp.exp(-spread_of)))
            gate = column_of(gates, copy_index + 1 + index)
            term = mixing[0] * copy_grad + mixing[1] * vector_dot
            gate_grad = jnp.where(lane == copy_index + 1 + index, term, gate_grad)
            direct = direct + gate * mixing[0]
            constants.append((gate, mixing, vector, vector_dot))
        prob_grad = jnp.where(chosen, gate_grad, 0.0)
        logit_grad = probs * (prob_grad - jnp.sum(probs * prob_grad, axis=1, keepdims=True))
        head_grad = logit_grad
        for index, (gate, mixing, vector, vector_dot) in enumerate(constants):
            mixing_grad = (gate * copy_grad, gate * vector_dot)
            mean = mixing[0] * mixing_grad[0] + mixing[1] * mixing_grad[1]
            for part in range(2):
                head_grad = jnp.where(
                    lane == experts + 2 * index + part,
                    mixing[part] * (mixing_grad[part] - mean),
                    head_grad,
                )
        head_low = head_grad.astype(low)

        slot = lax.broadcasted_iota(jnp.int32, (rows, slots), 1).astype(full)
        picked = [(slot == target[k]).astype(full).astype(low) for k in range(2)]
        second_grad = (
            dot(head_low, heads_in) + direct * upstream + dot(picked[0] + picked[1], back_ref[...])
        )
        normal_grad = second_grad * gain_second
        middle_total = upstream + inverse_second * (
            normal_grad - unit_second * jnp.mean(normal_grad * unit_second, axis=1, keepdims=True)
        )
        middle_grad[...] = middle_total
        middle_low = middle_total.astype(low)
        loads[0].wait()
        out_grad = dot_nt(middle_low, output_w[...]).astype(low)
        out_grads[own] = out_grad
        product = out_grad.astype(full) * attended_ref[...]
        masks = head_masks(rows)
        deltas = jnp.zeros((rows, 128), full)
        for index in range(pairs):
            part = product[:, index * 128 : index * 128 + 128]
            for head in range(2):
                total = jnp.sum(jnp.where(masks[head], part, 0.0), axis=1, keepdims=True)
                deltas = jnp.where(lane == 2 * index + head, total, deltas)
        stats[own, 0:stat_rows] = lse_ref[...]
        stats[own, stat_rows:] = jnp.transpose(deltas)[0:stat_rows]
        gather = Gather([out_grads, stats], size, gather_send, gather_recv)
        gather.forward(0)
        for copy in output_copies:
            copy.start()

        chosen_out = second * direct
        for gate, mixing, vector, vector_dot in constants:
            chosen_out = chosen_out + gate * mixing[1] * vector
        base = middle + chosen_out
        small_ref[...] = jnp.zeros_like(small_ref)
        small_ref[1:2, :] = jnp.sum(second_grad * unit_second, axis=0, keepdims=True)
        for index, (gate, mixing, vector, vector_dot) in enumerate(constants):
            small_ref[2 + index : 3 + index, :] = jnp.sum(
                gate * mixing[1] * upstream, axis=0, keepdims=True
            )
        small_ref[8:24, :] = dot_tn(head_low, second_low)[0:16]
        carry_grad = lax.dot_general(
            jnp.transpose(logit_grad)[0:16],
            prior[0:experts, :],
            (((1,), (1,)), ((), ())),
            precision=HIGH,
        )
        small_ref[24:40, 0:experts] = carry_grad
        keep_wide(3, dot_tn(attended_ref[...].astype(low), middle_low))

        for load in loads[1:4]:
            load.wait()
        query_total[...] = jnp.zeros_like(query_total)
        key_total[...] = jnp.zeros_like(key_total)
        value_total[...] = jnp.zeros_like(value_total)
        column = lax.broadcasted_iota(jnp.int32, (rows, rows), 0)
        row = lax.broadcasted_iota(jnp.int32, (rows, rows), 1)

        def block_side(block, as_query, as_key):
            key_block, query_block = (own if as_key else block), (own if as_query else block)
            key_pos, query_pos = key_block * rows + column, query_block * rows + row
            first = start_of(query_pos[0:8], starts_ref)[0:1]
            allowed = jnp.logical_and(key_pos >= first, key_pos <= query_pos)
            bias[...] = jnp.where(allowed, 0.0, NEGATIVE)

            def pair(index, carried):
                lanes = pl.ds(pl.multiple_of(index * 128, 128), 128)
                query, grad = queries[query_block, :, lanes], out_grads[query_block, :, lanes]
                key, value = keys[key_block, :, lanes], values[key_block, :, lanes]
                one_key = [jnp.where(mask, key, 0) for mask in masks]
                scores = [dot_nt(one_key[head], query) for head in range(2)]
                weight_grad = [dot_nt(jnp.where(mask, value, 0), grad) for mask in masks]
                weight, score = [], []
                for head in range(2):
                    lse = stats[query_block, pl.ds(2 * index + head, 1), :]
                    mean = stats[query_block, pl.ds(stat_rows + 2 * index + head, 1), :]
                    weight.append(jnp.exp(scores[head] + bias[...] - lse))
                    score.append((weight[head] * (weight_grad[head] - mean)).astype(low))
                if as_key:
                    value_total[:, lanes] += dot(
                        weight[0].astype(low), jnp.where(masks[0], grad, 0)
                    ) + dot(weight[1].astype(low), jnp.where(masks[1], grad, 0))
                    key_total[:, lanes] += dot(score[0], jnp.where(masks[0], query, 0)) + dot(
                        score[1], jnp.where(masks[1], query, 0)
                    )
                if as_query:
                    query_total[lanes, :] += dot_tn(one_key[0], score[0]) + dot_tn(
                        one_key[1], score[1]
                    )
                return carried

            lax.fori_loop(0, pairs, pair, 0)

        block_side(own, True, True)
        def earlier(place, carried):
            block = jnp.bitwise_xor(own, place)

            @pl.when(block < own)
            def _():
                block_side(block, True, False)

            return carried

        def later(place, carried):
            for one in range(1, size):

                @pl.when(place == one)
                def _():
                    gather.arrive(one)

            block = jnp.bitwise_xor(own, place)

            @pl.when(block > own)
            def _():
                block_side(block, False, True)

            return carried

        lax.fori_loop(1, size, earlier, 0)
        lax.fori_loop(1, size, later, 0)
        for load in loads[4:]:
            load.wait()
        inputs = tokens_ref[...].astype(full)
        inverse_first = inverse_norm(inputs)
        unit_first = inputs * inverse_first
        gain_first = pack[HEAD_ROWS : HEAD_ROWS + 1, :]
        normed = (unit_first * gain_first).astype(low)
        turn = -sine[...]
        query_grad = jnp.transpose(query_total[...]) * HEAD_DIM**-0.5
        query_low = rotate(query_grad, cosine[...], turn).astype(low)
        key_low = rotate(key_total[...], cosine[...], turn).astype(low)
        value_low = value_total[...].astype(low)
        first_grad = (
            dot_nt(query_low, query_w[...])
            + dot_nt(key_low, key_w[...])
            + dot_nt(value_low, value_w[...])
        )
        for index, part in enumerate((query_low, key_low, value_low)):
            keep_wide(index, dot_tn(normed, part))
        small_ref[0:1, :] = jnp.sum(first_grad * unit_first, axis=0, keepdims=True)
        normal_grad = first_grad * gain_first
        token_grads_ref[...] = middle_grad[...] + inverse_first * (
            normal_grad - unit_first * jnp.mean(normal_grad * unit_first, axis=1, keepdims=True)
        )
        for copy in output_copies:
            copy.wait()
        for k in range(2):
            weight = jnp.sum(jnp.where(lane == route[k], probs, 0.0), axis=1, keepdims=True)
            base = base + weight * dot(picked[k], outputs[...].reshape(slots, width))
        result_ref[...] = base.astype(low)
        gather.finish()
        for copy in first_copies:
            copy.wait()

    stream_shape = (size, rows, width)
    any_space = pl.BlockSpec(memory_space=pl.ANY)
    in_vmem = pl.BlockSpec(memory_space=pltpu.VMEM)
    square = (width, width)
    return pl.pallas_call(
        kernel,
        out_shape=[
            jax.ShapeDtypeStruct((rows, width), low),
            jax.ShapeDtypeStruct((rows, width), full),
            jax.ShapeDtypeStruct((2, 4 * width, width // 2), low),
            jax.ShapeDtypeStruct((64, width), full),
        ]
        + [jax.ShapeDtypeStruct(term.shape[1:], low) for term in terms],
        in_specs=[in_vmem] * 4
        + [pl.BlockSpec(memory_space=pltpu.SMEM)]
        + [in_vmem] * 5
        + [any_space] * 3
        + [in_vmem, any_space, in_vmem]
        + [any_space] * 4
        + [in_vmem] * 5
        + [any_space] * (3 + kinds),
        out_specs=[in_vmem] * 4 + [any_space] * kinds,
        scratch_shapes=[
            pltpu.VMEM(stream_shape, low),
            pltpu.VMEM(stream_shape, low),
            pltpu.VMEM(stream_shape, low),
            pltpu.VMEM(square, low),
            pltpu.VMEM(square, low),
            pltpu.VMEM(square, low),
            pltpu.VMEM(square, low),
            pltpu.VMEM((rows, 128), full),
            pltpu.VMEM((rows, 128), full),
            pltpu.VMEM((rows, rows), full),
            pltpu.VMEM(stream_shape, low),
            pltpu.VMEM((size, 2 * stat_rows, rows), full),
            pltpu.VMEM((count, cap, width), low),
            pltpu.VMEM((rows, width), full),
            pltpu.VMEM((width, rows), full),
            pltpu.VMEM((rows, width), full),
            pltpu.VMEM((rows, width), full),
            pltpu.SemaphoreType.DMA((9,)),
            pltpu.SemaphoreType.DMA((2, size)),
            pltpu.SemaphoreType.DMA((2, size)),
            pltpu.SemaphoreType.DMA((kinds,)),
            pltpu.SemaphoreType.DMA((kinds,)),
            pltpu.SemaphoreType.DMA((count,)),
            pltpu.SemaphoreType.DMA((count,)),
            pltpu.SemaphoreType.DMA,
            pltpu.VMEM(terms[0].shape[1:], low),
            pltpu.VMEM(terms[0].shape[1:], low),
            pltpu.SemaphoreType.DMA((2,)),
            pltpu.VMEM((24, width), full),
            pltpu.VMEM((16, rows), full),
        ],
        compiler_params=pltpu.CompilerParams(
            collective_id=2, has_side_effects=True, vmem_limit_bytes=60 * 2**20
        ),
        cost_estimate=pl.CostEstimate(
            flops=14 * rows * width * width * 2 + 20 * size * rows * rows * width,
            bytes_accessed=30 * 2**20,
            transcendentals=size * rows * rows * 12,
        ),
        name="backward",
    )(
        tokens,
        cotangent,
        previous,
        routes,
        starts,
        *forward,
        *returns,
        *weights,
        *params,
        jnp.asarray(tables[0]),
        jnp.asarray(tables[1]),
        *terms,
        first,
    )


PIECES = 4
ORDER = (
    6, 7, 11, 0, 5, 6, 1, 0, 0, 7, 11, 7, 6, 11, 0,
    3, 0, 2, 4, 5, 5, 2, 0, 10, 7, 1, 0, 6, 4, 10,
    3, 2, 10, 8, 7, 0, 4, 10, 8, 1, 6, 5, 8, 1, 3,
    10, 9, 2, 12, 4, 0, 10, 5, 4, 2, 3, 8, 6, 9, 9,
    9, 11, 5, 12, 12, 0, 9, 11, 8, 0, 8, 12, 9, 12, 11,
    1, 3, 7, 12,
)
DENSE_TIMES = (7, 24, 34, 48, 62, 77, 91, 101, 118, 125, 132)
EXPERT_TIMES = (19, 14, 19, 4, 11, 2)


def halving_steps(size):
    steps, step = [], 0
    while 1 << step < size:
        bit = 1 << step
        steps += [(step, place) for place in range(size - bit, 0, -2 * bit)]
        step += 1
    return steps


def needed_before(step, place):
    return {(earlier, place | 1 << earlier) for earlier in range(step)}


def reduce_layer(terms, firsts, wide, small, spread, shares, ring, exchange_size):
    low, full = jnp.bfloat16, jnp.float32
    steps = halving_steps(shares)
    done = [[(0, shares - 1), (1, shares - 2)]] + [[(0, shares - 1)]] * (len(terms) - 1)
    kinds = len(terms)
    blocks = [term.shape[1:] for term in terms]
    members = ring // spread
    groups = 3
    near_bits = [1 << step for step in range(ring.bit_length() - 1)]
    far_bits = [1 << step for step in range(exchange_size.bit_length() - 1)]
    deep_bits = [1 << step for step in range(shares.bit_length() - 1)]
    near = [(0, 0, bit) for bit in near_bits]
    far = [(0, bit, 0) for bit in far_bits]
    deep = [(bit, 0, 0) for bit in deep_bits]
    orders = [near + far + deep, near[:1] + far + near[1:] + deep, near + far + deep]
    places = near + far + deep
    bit_count = len(places)
    group_rows = [wide.shape[1], wide.shape[1], small.shape[0]]
    tile = [16, 16, 8]
    plans = []
    for group in range(groups):
        length, plan = group_rows[group], []
        for _ in range(bit_count):
            halved = (length // 2) % tile[group] == 0
            length = length // 2 if halved else length
            plan.append((halved, length))
        plans.append(plan)

    def kernel(*refs):
        refs = list(refs)

        def take(number):
            taken = refs[:number]
            del refs[:number]
            return taken

        term_refs, first_refs = take(kinds), take(kinds)
        (wide_hbm, small_hbm) = take(2)
        gathered = take(kinds)
        (wide_out, small_out) = take(2)
        sums, landed = take(kinds), take(kinds)
        (halves, smalls) = take(2)
        group_landed = take(groups)
        (load_sem, step_send, step_recv, own_sem, ring_send, ring_recv) = take(6)
        (dense_send, dense_recv, dense_load) = take(3)
        share = lax.axis_index("dp")
        mine = lax.axis_index("ctx") // spread

        dense_in = [
            pltpu.make_async_copy(wide_hbm, halves, dense_load.at[0]),
            pltpu.make_async_copy(small_hbm, smalls, dense_load.at[1]),
        ]
        for copy in dense_in:
            copy.start()
        loads = []
        for kind in range(kinds):
            copies = [
                pltpu.make_async_copy(
                    first_refs[kind],
                    landed[kind].at[steps.index(done[kind][-1])],
                    load_sem.at[kind, shares // 2],
                )
            ]
            for place in range(shares - 2, -1, -2):
                copies.append(
                    pltpu.make_async_copy(
                        term_refs[kind].at[jnp.bitwise_xor(share, place)],
                        sums[kind].at[place // 2],
                        load_sem.at[kind, place // 2],
                    )
                )
            for copy in copies:
                copy.start()
            loads.append(copies)
        greet_places(places)

        def expert_chain(kind, piece):
            period, odd_wait, even_wait, near_wait, far_wait, last_wait = EXPERT_TIMES
            begin = time = period * (kind * PIECES + piece)
            slots = {step: index for index, step in enumerate(steps)}
            lines = blocks[kind][0] // PIECES
            window = pl.ds(piece * lines, lines)
            one = kind * PIECES + piece

            def transfer(step, place):
                index = slots[step, place]
                if place % 2 == 1:
                    source = term_refs[kind].at[jnp.bitwise_xor(share, place), window]
                else:
                    source = sums[kind].at[place // 2, window]
                return pltpu.make_async_remote_copy(
                    src_ref=source,
                    dst_ref=landed[kind].at[index, window],
                    send_sem=step_send.at[one, index],
                    recv_sem=step_recv.at[one, index],
                    device_id=peer_at(1 << step, 0, 0),
                    device_id_type=pl.DeviceIdType.MESH,
                )

            yield begin
            arrived, started = set(done[kind]), []
            waiting = [op for op in steps if op not in arrived]
            for op in list(waiting):
                if op[0] == 0:
                    transfer(*op).start()
                    started.append(op)
                    waiting.remove(op)
            while loads[kind]:
                loads[kind].pop().wait()
            step, place = done[kind][-1]
            add_into(
                sums[kind].at[(place ^ 1 << step) // 2, window],
                landed[kind].at[slots[step, place], window],
            )
            while True:
                for op in list(waiting):
                    if needed_before(*op) <= arrived:
                        transfer(*op).start()
                        started.append(op)
                        waiting.remove(op)
                if not started:
                    break
                op = started.pop(0)
                yield time + (even_wait if op[0] else odd_wait)
                transfer(*op).wait()
                arrived.add(op)
                add_into(
                    sums[kind].at[(op[1] ^ 1 << op[0]) // 2, window],
                    landed[kind].at[slots[op], window],
                )
            time += even_wait
            index = len(steps)
            bit = 1
            while bit < spread:
                copy = pltpu.make_async_remote_copy(
                    src_ref=sums[kind].at[0, window],
                    dst_ref=landed[kind].at[index, window],
                    send_sem=step_send.at[one, index],
                    recv_sem=step_recv.at[one, index],
                    device_id=peer_at(0, 0, bit),
                    device_id_type=pl.DeviceIdType.MESH,
                )
                copy.start()
                time += near_wait
                yield time
                copy.wait()
                add_into(sums[kind].at[0, window], landed[kind].at[index, window])
                index += 1
                bit *= 2
            keep = pltpu.make_async_copy(
                sums[kind].at[0, window], gathered[kind].at[mine, window], own_sem.at[one]
            )
            keep.start()
            sent = []

            def pass_on(place, bit):
                block = jnp.bitwise_xor(mine, place)
                target = gathered[kind].at[block, window]
                return pltpu.make_async_remote_copy(
                    src_ref=sums[kind].at[0, window] if place == 0 else target,
                    dst_ref=target,
                    send_sem=ring_send.at[one, place ^ bit],
                    recv_sem=ring_recv.at[one, place ^ bit],
                    device_id=peer_at(0, 0, bit * spread),
                    device_id_type=pl.DeviceIdType.MESH,
                )

            def forward(place):
                for bit, held in gather_steps(members):
                    if place in held:
                        copy = pass_on(place, bit)
                        copy.start()
                        sent.append(copy)

            forward(0)
            for place in range(1, members):
                wait = near_wait if place == 1 else far_wait if place & (place - 1) == 0 else last_wait
                yield time + wait + (far_wait if wait == last_wait else 0)
                bit = place & -place
                pass_on(place ^ bit, bit).wait_recv()
                forward(place)
            yield 1000
            keep.wait()
            for copy in sent:
                copy.wait_send()

        def bit_of(place):
            deep_bit, far_bit, near_bit = place
            axis, bit = ("dp", deep_bit) if deep_bit else ("exp", far_bit) if far_bit else ("ctx", near_bit)
            return lax.rem(lax.axis_index(axis) // bit, 2)

        def dense_chain(times):
            times = iter(times + tuple(range(times[-1] + 8, 900, 8)))
            buffers = [halves.at[0], halves.at[1], smalls]
            yield 0
            for copy in dense_in:
                copy.wait()
            begins = [0] * groups
            trail = []

            def window(begin, length, group):
                if isinstance(begin, int):
                    return pl.ds(begin, length)
                return pl.ds(pl.multiple_of(begin, tile[group]), length)

            def exchange_rows(group, step, source, target):
                return pltpu.make_async_remote_copy(
                    src_ref=source,
                    dst_ref=target,
                    send_sem=dense_send.at[group, step],
                    recv_sem=dense_recv.at[group, step],
                    device_id=peer_at(*orders[group][step % bit_count]),
                    device_id_type=pl.DeviceIdType.MESH,
                )

            for step in range(bit_count):
                copies = []
                for group in range(groups):
                    halved, length = plans[group][step]
                    upper = bit_of(orders[group][step])
                    if halved:
                        sent = begins[group] + (1 - upper) * length
                        begins[group] = begins[group] + upper * length
                    else:
                        sent = begins[group]
                    at = sum(size for _, size in plans[group][:step])
                    copy = exchange_rows(
                        group,
                        step,
                        buffers[group].at[window(sent, length, group)],
                        group_landed[group].at[pl.ds(at, length)],
                    )
                    copy.start()
                    copies.append((copy, at, length))
                trail.append(list(begins))
                yield next(times)
                for group, (copy, at, length) in enumerate(copies):
                    copy.wait()
                    add_into(
                        buffers[group].at[window(begins[group], length, group)],
                        group_landed[group].at[pl.ds(at, length)],
                    )
            outputs = [wide_out.at[0], wide_out.at[1], small_out]
            keeps = []
            for group in range(groups):
                part = window(begins[group], plans[group][-1][1], group)
                keep = pltpu.make_async_copy(
                    buffers[group].at[part], outputs[group].at[part], dense_load.at[group]
                )
                keep.start()
                keeps.append(keep)
            for keep in keeps:
                keep.wait()
            for step in range(bit_count - 1, -1, -1):
                copies = []
                for group in range(groups):
                    halved, length = plans[group][step]
                    if halved:
                        part = outputs[group].at[window(trail[step][group], length, group)]
                        copy = exchange_rows(group, bit_count + step, part, part)
                        copy.start()
                        copies.append(copy)
                if copies:
                    yield next(times)
                for copy in copies:
                    copy.wait()

        chains = [dense_chain(DENSE_TIMES)] + [
            expert_chain(kind, piece) for kind in range(kinds) for piece in range(PIECES)
        ]
        due = dict(enumerate(next(chain) for chain in chains))
        planned = list(ORDER) if (shares, ring, exchange_size) == (4, 4, 2) else []
        while due:
            index = planned.pop(0) if planned else min(due, key=lambda one: (due[one], one))
            time = next(chains[index], None)
            if time is None:
                del due[index]
            else:
                due[index] = time

    any_space = pl.BlockSpec(memory_space=pl.ANY)
    extra = len(steps) + spread.bit_length() - 1
    return pl.pallas_call(
        kernel,
        out_shape=[jax.ShapeDtypeStruct((members,) + block, low) for block in blocks]
        + [jax.ShapeDtypeStruct(wide.shape, low), jax.ShapeDtypeStruct(small.shape, full)],
        in_specs=[any_space] * (2 * kinds + 2),
        out_specs=[any_space] * (kinds + 2),
        scratch_shapes=[pltpu.VMEM((shares // 2,) + block, low) for block in blocks]
        + [pltpu.VMEM((extra,) + block, low) for block in blocks]
        + [pltpu.VMEM(wide.shape, low), pltpu.VMEM(small.shape, full)]
        + [
            pltpu.VMEM(
                (sum(length for _, length in plans[group]), (wide, wide, small)[group].shape[-1]),
                (low, low, full)[group],
            )
            for group in range(groups)
        ]
        + [
            pltpu.SemaphoreType.DMA((kinds, shares // 2 + 1)),
            pltpu.SemaphoreType.DMA((kinds * PIECES, extra)),
            pltpu.SemaphoreType.DMA((kinds * PIECES, extra)),
            pltpu.SemaphoreType.DMA((kinds * PIECES,)),
            pltpu.SemaphoreType.DMA((kinds * PIECES, members)),
            pltpu.SemaphoreType.DMA((kinds * PIECES, members)),
            pltpu.SemaphoreType.DMA((groups, 2 * bit_count)),
            pltpu.SemaphoreType.DMA((groups, 2 * bit_count)),
            pltpu.SemaphoreType.DMA((3,)),
        ],
        compiler_params=pltpu.CompilerParams(
            collective_id=3, has_side_effects=True, vmem_limit_bytes=60 * 2**20
        ),
        name="reduce",
    )(*terms, *firsts, wide, small)


def widen_layer(parts, wide, small, experts):
    members = parts[0].shape[0]
    pieces = 1
    steps = members * pieces
    squares = wide.shape[1] // (2 * wide.shape[2])
    width = 2 * wide.shape[2]
    lines = wide.shape[1] // steps
    turns = width // lines
    full = jnp.float32
    kinds = len(parts)

    def kernel(*refs):
        sources, wide_ref, small_ref = refs[:kinds], refs[kinds], refs[kinds + 1]
        targets = refs[kinds + 2 : 2 * kinds + 2]
        square_refs = refs[2 * kinds + 2 : 2 * kinds + 2 + squares]
        head_ref, map_ref, carry_ref, vector_ref, *gain_refs = refs[2 * kinds + 2 + squares :]
        step = pl.program_id(0) * pieces + pl.program_id(1)
        for source, target in zip(sources, targets):
            target[...] = source[...].astype(full)
        for index in range(squares):

            @pl.when(step // turns == index)
            def _():
                square_refs[index][:, 0 : width // 2] = wide_ref[0].astype(full)
                square_refs[index][:, width // 2 :] = wide_ref[1].astype(full)

        @pl.when(step == 0)
        def _():
            head_ref[...] = small_ref[8 : 8 + experts, :]
            for index in range(2):
                begin = 8 + experts + 2 * index
                map_ref[index] = small_ref[begin : begin + 2, :]
            carry_ref[...] = jnp.transpose(small_ref[24:40, 0:128])[0:experts, 0:experts]
            vector_ref[...] = small_ref[2:4, :]
            for index, target in enumerate(gain_refs):
                target[...] = small_ref[index : index + 1, :].reshape(width)

    def chunk(part):
        return pl.BlockSpec(
            (1, part.shape[1] // pieces, part.shape[2]), lambda member, piece: (member, piece, 0)
        )

    def square(index):
        return pl.BlockSpec(
            (lines, width),
            lambda member, piece: (
                jnp.clip(member * pieces + piece - index * turns, 0, turns - 1),
                0,
            ),
        )

    def whole(*shape):
        return pl.BlockSpec(shape, lambda member, piece: (0,) * len(shape))

    smalls = [(experts, width), (2, 2, width), (experts, experts), (2, width), (width,), (width,)]
    return pl.pallas_call(
        kernel,
        out_shape=[jax.ShapeDtypeStruct(part.shape, full) for part in parts]
        + [jax.ShapeDtypeStruct((width, width), full)] * squares
        + [jax.ShapeDtypeStruct(shape, full) for shape in smalls],
        grid=(members, pieces),
        in_specs=[chunk(part) for part in parts]
        + [
            pl.BlockSpec(
                (2, lines, width // 2), lambda member, piece: (0, member * pieces + piece, 0)
            ),
            whole(*small.shape),
        ],
        out_specs=[chunk(part) for part in parts]
        + [square(index) for index in range(squares)]
        + [whole(*shape) for shape in smalls],
        compiler_params=pltpu.CompilerParams(vmem_limit_bytes=60 * 2**20),
        name="widen",
    )(*parts, wide, small)


def local(
    tokens,
    cotangent,
    previous,
    routes,
    boundaries,
    norm_first,
    query_weight,
    key_weight,
    value_weight,
    output_weight,
    norm_second,
    router,
    gate_carry,
    constant_map,
    constant_vector,
    expert_gate,
    expert_linear,
    expert_down,
):
    model_width = tokens.shape[2]
    ring = lax.axis_size("ctx")
    group_size = expert_gate.shape[0]
    exchange_count = lax.axis_size("exp")
    spread = ring // group_size
    ranks = (exchange_count, group_size, spread)
    slot_total = exchange_count * group_size * CAP
    expert_total = router.shape[1]
    params = (
        router.T,
        jnp.transpose(constant_map, (0, 2, 1)),
        norm_first,
        norm_second,
        constant_vector,
    )
    prior = jnp.transpose(previous, (2, 0, 1))
    weights = (query_weight, key_weight, value_weight, output_weight)
    (
        queries,
        keys,
        values,
        attended,
        lse,
        middle,
        probs,
        targets,
        outgoing,
        slot_gates,
        grads_in,
    ) = attend_layer(
        tokens[0],
        cotangent[0],
        prior,
        routes[0].T,
        boundaries,
        weights,
        params,
        gate_carry,
        ranks,
        CAP,
        ring,
    )
    home_grads, produced, dots, gate_terms, linear_terms, down_terms, first = expert_layer(
        outgoing,
        slot_gates,
        grads_in.reshape(slot_total, model_width),
        (expert_gate, expert_linear, expert_down),
        ranks,
        lax.axis_size("dp"),
    )
    terms = (down_terms, gate_terms, linear_terms)
    shares = lax.axis_size("dp")
    result, token_grads, wide, small, *firsts = backward_layer(
        tokens[0],
        cotangent[0],
        prior,
        routes[0].T,
        boundaries,
        (attended, lse, middle, probs, targets, queries, keys, values),
        (home_grads.reshape(slot_total, model_width), produced, dots),
        weights,
        params,
        terms,
        first,
        ranks,
        CAP,
        ring,
        shares,
    )
    *parts, wide, small = reduce_layer(
        terms, firsts, wide, small, spread, shares, ring, exchange_count
    )
    (
        down_grads,
        gate_grads,
        linear_grads,
        query_grads,
        key_grads,
        value_grads,
        output_grads,
        router_grads,
        map_grads,
        carry_grads,
        vector_grads,
        first_grads,
        second_grads,
    ) = widen_layer(parts, wide, small, expert_total)
    return (
        result[None],
        token_grads[None],
        first_grads,
        query_grads,
        key_grads,
        value_grads,
        output_grads,
        second_grads,
        router_grads.T,
        carry_grads,
        jnp.transpose(map_grads, (0, 2, 1)),
        vector_grads,
        gate_grads,
        linear_grads,
        down_grads,
    )


def solution(mesh):
    return jax.shard_map(
        local,
        mesh=mesh,
        in_specs=(
            P(("dp", "exp"), "ctx", None),
            P(("dp", "exp"), "ctx", None),
            P(("dp", "exp"), "ctx", None),
            P(("dp", "exp"), "ctx", None),
            P(("dp", "exp"), None),
            P(),
            P(),
            P(),
            P(),
            P(),
            P(),
            P(),
            P(),
            P(),
            P(),
            P("exp", None, None),
            P("exp", None, None),
            P("exp", None, None),
        ),
        out_specs=(
            P(("dp", "exp"), "ctx", None),
            P(("dp", "exp"), "ctx", None),
            P(),
            P(),
            P(),
            P(),
            P(),
            P(),
            P(),
            P(),
            P(),
            P(),
            P("exp", None, "dp"),
            P("exp", None, "dp"),
            P("exp", "dp", None),
        ),
        check_vma=False,
    )
```

```python
import math

import jax
import jax.numpy as jnp
import numpy as np
from jax import lax
from jax.experimental import pallas as pl
from jax.experimental.pallas import tpu as pltpu
from jax.sharding import PartitionSpec as P

HEAD_DIM = 64
CAP = 96


EPSILON = 1e-06
NEGATIVE = -1e30
HIGH = lax.Precision.HIGHEST


HEAD_ROWS = 16


def mesh_id(exp_index, ctx_index):
    return {"exp": exp_index, "ctx": ctx_index}


def dot(left, right):
    return jnp.dot(left, right, preferred_element_type=jnp.float32)


def dot_nt(left, right):
    return lax.dot_general(
        left, right, (((1,), (1,)), ((), ())), preferred_element_type=jnp.float32
    )


def dot_tn(left, right):
    return lax.dot_general(
        left, right, (((0,), (0,)), ((), ())), preferred_element_type=jnp.float32
    )


def member_of(shift, ranks):
    exchange_size, group_size, spread = ranks
    exp_index, ctx_index = lax.axis_index("exp"), lax.axis_index("ctx")
    far, near = shift // group_size, shift % group_size
    place = jnp.bitwise_xor(ctx_index // spread, near) * spread + lax.rem(ctx_index, spread)
    return mesh_id(jnp.bitwise_xor(exp_index, far), place)


def greet(count, ranks):
    barrier = pltpu.get_barrier_semaphore()
    for shift in range(1, count):
        pl.semaphore_signal(
            barrier, inc=1, device_id=member_of(shift, ranks), device_id_type=pl.DeviceIdType.MESH
        )
    pl.semaphore_wait(barrier, count - 1)


def block_of(shift, count):
    return (shift + count - count // 4) % count


def own_block(count):
    return block_of(0, count)


def send_block(source, target, block, ranks, send_sem, recv_sem):
    count = ranks[0] * ranks[1]
    return pltpu.make_async_remote_copy(
        src_ref=source.at[block],
        dst_ref=target.at[block],
        send_sem=send_sem.at[block],
        recv_sem=recv_sem.at[block],
        device_id=member_of((block + count // 4) % count, ranks),
        device_id_type=pl.DeviceIdType.MESH,
    )


def keep_block(source, target, count, sem):
    block = own_block(count)
    return pltpu.make_async_copy(source.at[block], target.at[block], sem)


def other_blocks(count):
    return [block for block in range(count) if block != own_block(count)]


def expert_layer(outgoing, gates, grads, weights, ranks, shares):
    count, cap, width = outgoing.shape
    hidden_units = weights[0].shape[2]
    rows = count * cap
    share = hidden_units // shares
    spread = ranks[2]

    def kernel(
        outgoing_hbm,
        gates_ref,
        grads_ref,
        gate_hbm,
        linear_hbm,
        down_hbm,
        back_ref,
        output_ref,
        dots_ref,
        gate_terms,
        linear_terms,
        down_terms,
        first_ref,
        received,
        received_gates,
        gate_w,
        linear_w,
        down_w,
        hidden_grad,
        hidden,
        gate_low,
        linear_low,
        rows_t,
        scaled,
        gate_column,
        out_total,
        in_total,
        in_send,
        dots_send,
        terms,
        weight_sem,
        send_sem,
        recv_sem,
        local_sem,
        terms_sem,
        first_send,
        first_recv,
    ):
        own = lax.axis_index("ctx") // spread
        loads = [
            pltpu.make_async_copy(source.at[own], target, weight_sem.at[index])
            for index, (source, target) in enumerate(
                ((down_hbm, down_w), (gate_hbm, gate_w), (linear_hbm, linear_w))
            )
        ]
        for load in loads:
            load.start()
        greet_places([(0,) + place for place in group_places(ranks)] + [(1, 0, 0)])

        def send_some(source, target, index, shifts):
            copies = []
            for shift in shifts:
                if shift == own_block(count):
                    copies.append(keep_block(source, target, count, local_sem.at[index]))
                else:
                    copies.append(
                        send_block(
                            source, target, shift, ranks, send_sem.at[index], recv_sem.at[index]
                        )
                    )
            for copy in copies:
                copy.start()
            return copies

        every = range(count)
        gates_in = send_some(gates_ref, received_gates, 0, every)
        soon = [block for block in every if not count // 2 <= block < count - count // 4]
        incoming = dict(zip(soon, send_some(outgoing_hbm, received, 1, soon)))
        loads[0].wait()

        def backward_in(index, carry):
            part = pl.ds(pl.multiple_of(index * share, share), share)
            hidden_grad[:, part] = dot_nt(grads_ref[...], down_w[part, :])
            return carry

        lax.fori_loop(0, shares, backward_in, 0)
        for copy in gates_in:
            copy.wait()
        for shift in every:
            column = jnp.transpose(received_gates[shift])[:cap, 0:1]
            block = pl.ds(shift * cap, cap)
            gate_column[block, :] = jnp.broadcast_to(column, (cap, 128))
            scaled[block, :] = (column * grads_ref[block, :].astype(jnp.float32)).astype(
                jnp.bfloat16
            )
        for load in loads[1:]:
            load.wait()

        going = []
        batches = 2
        members = count // batches
        lines = rows // batches
        for batch in range(batches):
            chunks = range(batch * members, (batch + 1) * members)
            for shift in chunks:
                incoming[shift].wait()
            if batch == 0:
                late = [block for block in every if block not in soon]
                incoming.update(zip(late, send_some(outgoing_hbm, received, 1, late)))
            block = pl.ds(batch * lines, lines)

            def through(index):
                part = pl.ds(index * share, share)
                tokens = received[batch * members : (batch + 1) * members].reshape(lines, width)
                gate_part = dot(tokens, gate_w[:, part])
                linear_part = dot(tokens, linear_w[:, part])
                sigmoid = 1.0 / (1.0 + jnp.exp(-gate_part))
                silu = gate_part * sigmoid
                low = (silu * linear_part).astype(jnp.bfloat16)
                hidden[block, part] = low
                upper = hidden_grad[block, part] * gate_column[block, 0:1]
                low_gate = (
                    upper * linear_part * sigmoid * (1.0 + gate_part * (1.0 - sigmoid))
                ).astype(jnp.bfloat16)
                gate_low[block, part] = low_gate
                low_linear = (upper * silu).astype(jnp.bfloat16)
                linear_low[block, part] = low_linear
                out = dot(low, down_w[part, :])
                back = dot_nt(low_gate, gate_w[:, part]) + dot_nt(low_linear, linear_w[:, part])

                if index == 0:
                    out_total[block, :] = out
                    in_total[block, :] = back
                else:
                    out_total[block, :] += out
                    in_total[block, :] += back

            for tile in range(shares):
                through(tile)
            in_send[batch * members : (batch + 1) * members] = (
                in_total[block, :].astype(jnp.bfloat16).reshape(members, cap, width)
            )
            going += send_some(in_send, back_ref, 2, chunks)
            low = out_total[block, :].astype(jnp.bfloat16)
            output_ref[batch * members : (batch + 1) * members] = low.reshape(members, cap, width)
            dots = jnp.sum(
                low.astype(jnp.float32) * grads_ref[block, :].astype(jnp.float32),
                axis=1,
                keepdims=True,
            )
            for place, shift in enumerate(chunks):
                column = jnp.broadcast_to(dots[place * cap : (place + 1) * cap], (cap, 128))
                dots_send[shift, :, 0:cap] = jnp.transpose(column)[0:8, :]
                dots_send[shift, :, cap:] = jnp.zeros((8, 128 - cap), jnp.float32)
            going += send_some(dots_send, dots_ref, 3, chunks)
            rows_t[:, batch * lines : (batch + 1) * lines] = jnp.transpose(
                received[batch * members : (batch + 1) * members].reshape(lines, width)
            )

        def term_copy(which, index):
            target = (down_terms, gate_terms, linear_terms)[which]
            return pltpu.make_async_copy(
                terms[which].at[index], target.at[index], terms_sem.at[which, index]
            )

        def weigh(which, turn):
            index = jnp.bitwise_xor(lax.axis_index("dp"), shares - 1 - turn)
            part = pl.ds(pl.multiple_of(index * share, share), share)
            if which == 0:
                value = dot_tn(hidden[:, part], scaled[...])
            else:
                value = dot(rows_t[...], (gate_low if which == 1 else linear_low)[:, part])
            terms[which][index] = value.astype(jnp.bfloat16)
            term_copy(which, index).start()
            return index

        index = weigh(0, 0)
        first = pltpu.make_async_remote_copy(
            src_ref=terms[0].at[index],
            dst_ref=first_ref,
            send_sem=first_send,
            recv_sem=first_recv,
            device_id=peer_at(1, 0, 0),
            device_id_type=pl.DeviceIdType.MESH,
        )
        first.start()

        def weigh_rest(turn, carry):
            weigh(1, turn)
            weigh(2, turn)

            @pl.when(turn > 0)
            def _():
                weigh(0, turn)

            return carry

        lax.fori_loop(0, shares, weigh_rest, 0)
        for which in range(3):
            for index in range(shares):
                term_copy(which, index).wait()
        for copy in going:
            copy.wait()
        first.wait()

    low, full = jnp.bfloat16, jnp.float32
    columns, lines = (shares, width, share), (shares, share, width)
    any_space = pl.BlockSpec(memory_space=pl.ANY)
    in_vmem = pl.BlockSpec(memory_space=pltpu.VMEM)
    return pl.pallas_call(
        kernel,
        out_shape=[
            jax.ShapeDtypeStruct(outgoing.shape, low),
            jax.ShapeDtypeStruct(outgoing.shape, low),
            jax.ShapeDtypeStruct(gates.shape, full),
            jax.ShapeDtypeStruct(columns, low),
            jax.ShapeDtypeStruct(columns, low),
            jax.ShapeDtypeStruct(lines, low),
            jax.ShapeDtypeStruct(lines[1:], low),
        ],
        in_specs=[any_space, in_vmem, in_vmem, any_space, any_space, any_space],
        out_specs=[any_space, in_vmem] + [any_space] * 5,
        scratch_shapes=[
            pltpu.VMEM(outgoing.shape, low),
            pltpu.VMEM(gates.shape, full),
            pltpu.VMEM((width, hidden_units), low),
            pltpu.VMEM((width, hidden_units), low),
            pltpu.VMEM((hidden_units, width), low),
            pltpu.VMEM((rows, hidden_units), full),
            pltpu.VMEM((rows, hidden_units), low),
            pltpu.VMEM((rows, hidden_units), low),
            pltpu.VMEM((rows, hidden_units), low),
            pltpu.VMEM((width, rows), low),
            pltpu.VMEM((rows, width), low),
            pltpu.VMEM((rows, 128), full),
            pltpu.VMEM((rows, width), full),
            pltpu.VMEM((rows, width), full),
            pltpu.VMEM(outgoing.shape, low),
            pltpu.VMEM(gates.shape, full),
            [pltpu.VMEM(lines, low), pltpu.VMEM(columns, low), pltpu.VMEM(columns, low)],
            pltpu.SemaphoreType.DMA((3,)),
            pltpu.SemaphoreType.DMA((4, count)),
            pltpu.SemaphoreType.DMA((4, count)),
            pltpu.SemaphoreType.DMA((4,)),
            pltpu.SemaphoreType.DMA((3, shares)),
            pltpu.SemaphoreType.DMA,
            pltpu.SemaphoreType.DMA,
        ],
        compiler_params=pltpu.CompilerParams(
            collective_id=1, has_side_effects=True, vmem_limit_bytes=60 * 2**20
        ),
        cost_estimate=pl.CostEstimate(
            flops=18 * rows * width * hidden_units,
            bytes_accessed=12 * width * hidden_units + 12 * rows * width,
            transcendentals=rows * hidden_units,
        ),
        name="experts",
    )(outgoing, gates, grads, *weights)


def rope_tables(row_count):
    half = HEAD_DIM // 2
    frequency = np.exp(
        np.arange(half, dtype=np.float32) * np.float32(-2.0 * math.log(10000.0) / HEAD_DIM)
    ).astype(np.float32)
    angles = np.arange(row_count, dtype=np.float32)[:, None] * frequency[None, :]
    cosine, sine = np.cos(angles).astype(np.float32), np.sin(angles).astype(np.float32)
    return (
        np.concatenate([cosine] * 4, axis=1),
        np.concatenate([-sine, sine, -sine, sine], axis=1),
    )


def rotate(values, cosine, sine):
    lane = lax.broadcasted_iota(jnp.int32, cosine.shape, 1)
    leading = jnp.bitwise_and(lane, HEAD_DIM - 1) < HEAD_DIM // 2
    parts = []
    for begin in range(0, values.shape[1], 128):
        part = values[:, begin : begin + 128]
        ahead = pltpu.roll(part, 128 - HEAD_DIM // 2, 1)
        behind = pltpu.roll(part, HEAD_DIM // 2, 1)
        parts.append(part * cosine + jnp.where(leading, ahead, behind) * sine)
    return jnp.concatenate(parts, axis=1)


def inverse_norm(values):
    return lax.rsqrt(jnp.mean(values * values, axis=1, keepdims=True) + EPSILON)


def head_masks(rows):
    first = lax.broadcasted_iota(jnp.int32, (rows, 128), 1) < HEAD_DIM
    return first, jnp.logical_not(first)


def start_of(positions, starts):
    first = jnp.zeros_like(positions)
    for index in range(starts.shape[1]):
        begin = starts[0, index]
        first = jnp.where(begin <= positions, jnp.maximum(first, begin), first)
    return first


def gather_steps(size):
    bits, held, steps = [], [0], []
    bit = size // 2
    while bit >= 1:
        steps.append((bit, list(held)))
        held = held + [place ^ bit for place in held]
        bit //= 2
    return steps


def peer_at(deep, far, near):
    return {
        "dp": jnp.bitwise_xor(lax.axis_index("dp"), deep),
        "exp": jnp.bitwise_xor(lax.axis_index("exp"), far),
        "ctx": jnp.bitwise_xor(lax.axis_index("ctx"), near),
    }


def peer(far, near):
    return peer_at(0, far, near)


def greet_places(places):
    barrier = pltpu.get_barrier_semaphore()
    for place in places:
        pl.semaphore_signal(
            barrier, inc=1, device_id=peer_at(*place), device_id_type=pl.DeviceIdType.MESH
        )
    pl.semaphore_wait(barrier, len(places))


def greet_all(places):
    greet_places([(0,) + place for place in places])


def group_places(ranks):
    return [
        (shift // ranks[1], shift % ranks[1] * ranks[2]) for shift in range(1, ranks[0] * ranks[1])
    ]


def ring_places(size):
    return [(0, bit) for bit, _ in gather_steps(size)]


def places_of(ranks, size):
    places = group_places(ranks)
    return places + [place for place in ring_places(size) if place not in places]


class Gather:
    def __init__(self, buffers, size, send_sem, recv_sem, sources=None):
        self.buffers, self.sources = buffers, sources
        self.send_sem, self.recv_sem = send_sem, recv_sem
        self.steps = gather_steps(size)

    def copy(self, place, bit, index):
        block = jnp.bitwise_xor(lax.axis_index("ctx"), place)
        buffer = self.buffers[index]
        straight = self.sources is not None and place == 0
        return pltpu.make_async_remote_copy(
            src_ref=self.sources[index] if straight else buffer.at[block],
            dst_ref=buffer.at[block],
            send_sem=self.send_sem.at[index, place ^ bit],
            recv_sem=self.recv_sem.at[index, place ^ bit],
            device_id=peer(0, bit),
            device_id_type=pl.DeviceIdType.MESH,
        )

    def forward(self, place):
        for bit, held in self.steps:
            if place in held:
                for index in range(len(self.buffers)):
                    self.copy(place, bit, index).start()

    def arrive(self, place):
        bit = place & -place
        for index in range(len(self.buffers)):
            self.copy(place ^ bit, bit, index).wait_recv()
        self.forward(place)

    def finish(self):
        for bit, held in self.steps:
            for place in held:
                for index in range(len(self.buffers)):
                    self.copy(place, bit, index).wait_send()


def fill_rows(pack, prior, router_ref, map_ref, first_ref, second_ref, vector_ref, previous_ref):
    full = jnp.float32
    experts = router_ref.shape[0]
    width = router_ref.shape[1]
    pack[0:experts, :] = router_ref[...].astype(full)
    for index in range(2):
        pack[experts + 2 * index : experts + 2 * index + 2, :] = map_ref[index].astype(full)
    pack[HEAD_ROWS : HEAD_ROWS + 1, :] = first_ref[...].astype(full).reshape(1, width)
    pack[HEAD_ROWS + 1 : HEAD_ROWS + 2, :] = second_ref[...].astype(full).reshape(1, width)
    pack[HEAD_ROWS + 2 : HEAD_ROWS + 4, :] = vector_ref[...].astype(full)
    for index in range(experts):
        prior[index : index + 1, :] = previous_ref[index]


def slot_targets(routes, ranks, cap):
    exchange_size, group_size, spread = ranks
    rows = routes.shape[1]
    experts = exchange_size * group_size
    expert = lax.broadcasted_iota(jnp.int32, (16, rows), 0)
    hits = [(expert == routes[k : k + 1]).astype(jnp.float32) for k in range(2)]
    before = lax.broadcasted_iota(jnp.int32, (rows, rows), 0) < lax.broadcasted_iota(
        jnp.int32, (rows, rows), 1
    )
    earlier = dot(
        (hits[0] + hits[1]).astype(jnp.bfloat16), before.astype(jnp.float32).astype(jnp.bfloat16)
    )
    targets = []
    for k in range(2):
        route = routes[k : k + 1]
        rank = jnp.sum(hits[k] * earlier, axis=0, keepdims=True)
        far = jnp.bitwise_xor(route // group_size, lax.axis_index("exp"))
        near = jnp.bitwise_xor(route % group_size, lax.axis_index("ctx") // spread)
        count = exchange_size * group_size
        block = jnp.bitwise_and(far * group_size + near + count - count // 4, count - 1)
        place = (block * cap).astype(jnp.float32)
        targets.append(jnp.where(route < experts, place + rank, -1.0))
    return targets


def attend_layer(
    tokens, cotangent, previous, routes, starts, weights, params, carry, ranks, cap, size
):
    rows, width = tokens.shape
    count = ranks[0] * ranks[1]
    slots = count * cap
    pairs = width // 128
    tables = rope_tables(size * rows)
    low, full = jnp.bfloat16, jnp.float32

    def kernel(
        tokens_hbm,
        cotangent_ref,
        previous_ref,
        routes_ref,
        starts_ref,
        query_hbm,
        key_hbm,
        value_hbm,
        output_hbm,
        router_ref,
        map_ref,
        first_ref,
        second_ref,
        vector_ref,
        carry_ref,
        cosine_hbm,
        sine_hbm,
        queries_out,
        keys_out,
        values_out,
        attended_out,
        lse_ref,
        middle_out,
        probs_ref,
        targets_ref,
        outgoing_ref,
        gates_ref,
        grads_ref,
        stream,
        queries,
        keys,
        values,
        query_w,
        key_w,
        value_w,
        output_w,
        cosine,
        sine,
        bias,
        totals,
        highest,
        slot_grads,
        load_sem,
        gather_send,
        gather_recv,
        grad_send,
        grad_recv,
        keep_sem,
        pack,
        prior,
        attended_ref,
        middle_ref,
    ):
        own = lax.axis_index("ctx")
        bring = pltpu.make_async_copy(tokens_hbm, stream.at[own], load_sem.at[6])
        bring.start()
        loads = [
            pltpu.make_async_copy(source, target, load_sem.at[index])
            for index, (source, target) in enumerate(
                (
                    (query_hbm, query_w),
                    (key_hbm, key_w),
                    (value_hbm, value_w),
                    (cosine_hbm, cosine),
                    (sine_hbm, sine),
                    (output_hbm, output_w),
                )
            )
        ]
        for load in loads:
            load.start()
        greet_all(places_of(ranks, size))
        gather = Gather([stream], size, gather_send, gather_recv, [tokens_hbm])
        gather.forward(0)

        fill_rows(
            pack, prior, router_ref, map_ref, first_ref, second_ref, vector_ref, previous_ref
        )
        targets = slot_targets(routes_ref[...], ranks, cap)
        slot = lax.broadcasted_iota(jnp.int32, (slots, rows), 0).astype(full)
        picked = jnp.logical_or(slot == targets[0], slot == targets[1])
        picked = picked.astype(full).astype(low)
        slot_grads[...] = dot(picked, cotangent_ref[...]).astype(low).reshape(count, cap, width)
        grad_copies = [
            send_block(slot_grads, grads_ref, block, ranks, grad_send, grad_recv)
            for block in other_blocks(count)
        ]
        grad_copies.append(keep_block(slot_grads, grads_ref, count, keep_sem.at[0]))

        bring.wait()
        for load in loads[:5]:
            load.wait()
        gain = pack[HEAD_ROWS : HEAD_ROWS + 1, :]

        def project(block, wanted):
            line = pl.ds(pl.multiple_of(block * rows, rows), rows)
            values_in = stream[block].astype(full)
            normed = (values_in * inverse_norm(values_in) * gain).astype(low)
            if "q" in wanted:
                turned = rotate(dot(normed, query_w[...]), cosine[line, :], sine[line, :])
                queries[block] = (turned.astype(low).astype(full) * HEAD_DIM**-0.5).astype(low)
            if "k" in wanted:
                turned = rotate(dot(normed, key_w[...]), cosine[line, :], sine[line, :])
                keys[block] = turned.astype(low)
                values[block] = dot(normed, value_w[...]).astype(low)

        masks = head_masks(rows)
        query_pos = own * rows + lax.broadcasted_iota(jnp.int32, (rows, rows), 1)
        document_start = start_of(query_pos[0:8], starts_ref)[0:1]

        def attend(block):
            key_pos = block * rows + lax.broadcasted_iota(jnp.int32, (rows, rows), 0)
            allowed = jnp.logical_and(key_pos >= document_start, key_pos <= query_pos)
            bias[...] = jnp.where(allowed, 0.0, NEGATIVE)

            def pair(index, carried):
                lanes = pl.ds(pl.multiple_of(index * 128, 128), 128)
                query, key, value = queries[own, :, lanes], keys[block, :, lanes], values[block, :, lanes]
                scores = [dot_nt(jnp.where(mask, key, 0), query) + bias[...] for mask in masks]
                old = [highest[index, head][0:1, :] for head in range(2)]
                new = [
                    jnp.maximum(old[head], jnp.max(scores[head], axis=0, keepdims=True))
                    for head in range(2)
                ]
                weight = [jnp.exp(scores[head] - new[head]).astype(low) for head in range(2)]
                for head in range(2):
                    totals[index, head] = totals[index, head] * jnp.exp(old[head] - new[head]) + dot_tn(
                        jnp.where(masks[head], value, 1), weight[head]
                    )
                    highest[index, head] = jnp.broadcast_to(new[head], (8, rows))
                return carried

            lax.fori_loop(0, pairs, pair, 0)

        totals[...] = jnp.zeros_like(totals)
        highest[...] = jnp.full(highest.shape, NEGATIVE, full)
        project(own, "qk")
        attend(own)
        def others(place, carried):
            for one in range(1, size):

                @pl.when(place == one)
                def _():
                    gather.arrive(one)
                    if one == size // 2:
                        for copy in grad_copies:
                            copy.start()

            block = jnp.bitwise_xor(own, place)

            @pl.when(block < own)
            def _():
                project(block, "k")
                attend(block)

            @pl.when(block > own)
            def _():
                project(block, "q")

            return carried

        lax.fori_loop(1, size, others, 0)
        keep = [
            pltpu.make_async_copy(source, target, keep_sem.at[index + 1])
            for index, (source, target) in enumerate(
                ((queries, queries_out), (keys, keys_out), (values, values_out))
            )
        ]
        for copy in keep:
            copy.start()

        lse_ref[...] = jnp.zeros_like(lse_ref)
        upper = lax.broadcasted_iota(jnp.int32, (128, rows), 0) < HEAD_DIM
        for index in range(pairs):
            halves = []
            for head in range(2):
                total = totals[index, head]
                line = HEAD_DIM if head == 0 else 0
                weight_sum = total[line : line + 1, :]
                halves.append(total / weight_sum)
                lse_ref[2 * index + head : 2 * index + head + 1, :] = highest[index, head][
                    0:1, :
                ] + jnp.log(weight_sum)
            attended_ref[:, index * 128 : index * 128 + 128] = jnp.transpose(
                jnp.where(upper, halves[0], halves[1])
            )
        keep.append(pltpu.make_async_copy(attended_ref, attended_out, keep_sem.at[4]))
        keep[-1].start()
        loads[5].wait()
        middle = stream[own].astype(full) + dot(attended_ref[...].astype(low), output_w[...])
        middle_ref[...] = middle
        keep.append(pltpu.make_async_copy(middle_ref, middle_out, keep_sem.at[5]))
        keep[-1].start()
        second = (
            middle
            * inverse_norm(middle)
            * pack[HEAD_ROWS + 1 : HEAD_ROWS + 2, :]
        )
        second_low = second.astype(low)
        outgoing_ref[...] = dot(picked, second_low).astype(low).reshape(count, cap, width)

        experts = previous_ref.shape[0]
        logits = dot_nt(second_low, pack[0:HEAD_ROWS, :].astype(low))[:, 0:experts] + lax.dot_general(
            prior[0:experts, :],
            carry_ref[...].astype(full),
            (((0,), (0,)), ((), ())),
            precision=HIGH,
        )
        logits = logits - jnp.max(logits, axis=1, keepdims=True)
        powers = jnp.exp(logits)
        probs_ref[...] = jnp.zeros_like(probs_ref)
        probs_ref[:, 0:experts] = powers / jnp.sum(powers, axis=1, keepdims=True)
        turned = jnp.transpose(probs_ref[...])[0:16]
        expert = lax.broadcasted_iota(jnp.int32, (16, rows), 0)
        weighted = jnp.zeros((slots, rows), full)
        for k in range(2):
            route = routes_ref[k : k + 1, :]
            gate = jnp.sum(jnp.where(expert == route, turned, 0.0), axis=0, keepdims=True)
            weighted = jnp.where(slot == targets[k], gate, weighted)
        gate_column = jnp.sum(weighted, axis=1, keepdims=True)
        for shift in range(count):
            column = jnp.broadcast_to(gate_column[shift * cap : (shift + 1) * cap], (cap, 128))
            gates_ref[shift] = jnp.zeros((8, 128), full)
            gates_ref[shift, :, 0:cap] = jnp.transpose(column)[0:8, :]
        pad = jnp.zeros((6, rows), full)
        target_rows = jnp.concatenate([targets[0], targets[1], pad], axis=0)
        target_rows = jnp.concatenate([target_rows] + [jnp.zeros((120, rows), full)], axis=0)
        targets_ref[...] = jnp.transpose(target_rows)

        gather.finish()
        for copy in keep + grad_copies:
            copy.wait()

    stream_shape = (size, rows, width)
    any_space = pl.BlockSpec(memory_space=pl.ANY)
    in_vmem = pl.BlockSpec(memory_space=pltpu.VMEM)
    square = (width, width)
    return pl.pallas_call(
        kernel,
        out_shape=[
            jax.ShapeDtypeStruct(stream_shape, low),
            jax.ShapeDtypeStruct(stream_shape, low),
            jax.ShapeDtypeStruct(stream_shape, low),
            jax.ShapeDtypeStruct((rows, width), full),
            jax.ShapeDtypeStruct((16, rows), full),
            jax.ShapeDtypeStruct((rows, width), full),
            jax.ShapeDtypeStruct((rows, 128), full),
            jax.ShapeDtypeStruct((rows, 128), full),
            jax.ShapeDtypeStruct((count, cap, width), low),
            jax.ShapeDtypeStruct((count, 8, 128), full),
            jax.ShapeDtypeStruct((count, cap, width), low),
        ],
        in_specs=[any_space]
        + [in_vmem] * 3
        + [pl.BlockSpec(memory_space=pltpu.SMEM)]
        + [any_space] * 4
        + [in_vmem] * 6
        + [any_space] * 2,
        out_specs=[any_space] * 4
        + [in_vmem, any_space]
        + [in_vmem] * 4
        + [any_space],
        scratch_shapes=[
            pltpu.VMEM(stream_shape, low),
            pltpu.VMEM(stream_shape, low),
            pltpu.VMEM(stream_shape, low),
            pltpu.VMEM(stream_shape, low),
            pltpu.VMEM(square, low),
            pltpu.VMEM(square, low),
            pltpu.VMEM(square, low),
            pltpu.VMEM(square, low),
            pltpu.VMEM((size * rows, 128), full),
            pltpu.VMEM((size * rows, 128), full),
            pltpu.VMEM((rows, rows), full),
            pltpu.VMEM((pairs, 2, 128, rows), full),
            pltpu.VMEM((pairs, 2, 8, rows), full),
            pltpu.VMEM((count, cap, width), low),
            pltpu.SemaphoreType.DMA((7,)),
            pltpu.SemaphoreType.DMA((1, size)),
            pltpu.SemaphoreType.DMA((1, size)),
            pltpu.SemaphoreType.DMA((count,)),
            pltpu.SemaphoreType.DMA((count,)),
            pltpu.SemaphoreType.DMA((6,)),
            pltpu.VMEM((24, width), full),
            pltpu.VMEM((16, rows), full),
            pltpu.VMEM((rows, width), full),
            pltpu.VMEM((rows, width), full),
        ],
        compiler_params=pltpu.CompilerParams(
            collective_id=0, has_side_effects=True, vmem_limit_bytes=60 * 2**20
        ),
        cost_estimate=pl.CostEstimate(
            flops=2 * size * rows * width * width * 3 + 16 * size * rows * rows * width,
            bytes_accessed=20 * 2**20,
            transcendentals=size * rows * rows * 12,
        ),
        name="attend",
    )(
        tokens,
        cotangent,
        previous,
        routes,
        starts,
        *weights,
        *params,
        carry,
        jnp.asarray(tables[0]),
        jnp.asarray(tables[1]),
    )


def add_into(target, source):
    rows = target.shape[0]
    piece = 96 if rows % 96 == 0 else (64 if rows % 64 == 0 else rows)

    def body(index, carried):
        part = pl.ds(pl.multiple_of(index * piece, piece), piece)
        total = target[part, :].astype(jnp.float32) + source[part, :].astype(jnp.float32)
        target[part, :] = total.astype(target.dtype)
        return carried

    lax.fori_loop(0, rows // piece, body, 0)


def column_of(values, index):
    return values[:, index : index + 1]


def backward_layer(
    tokens,
    cotangent,
    previous,
    routes,
    starts,
    forward,
    returns,
    weights,
    params,
    terms,
    first,
    ranks,
    cap,
    size,
    shares,
):
    rows, width = tokens.shape
    count = ranks[0] * ranks[1]
    slots = count * cap
    pairs = width // 128
    tables = rope_tables(size * rows)
    low, full = jnp.bfloat16, jnp.float32
    experts = previous.shape[0]
    copy_index = count + 1
    stat_rows = 16
    kinds = len(terms)

    def kernel(
        tokens_ref,
        cotangent_hbm,
        previous_ref,
        routes_ref,
        starts_ref,
        attended_hbm,
        lse_ref,
        middle_hbm,
        probs_ref,
        targets_ref,
        queries_hbm,
        keys_hbm,
        values_hbm,
        back_hbm,
        produced_hbm,
        dots_ref,
        query_hbm,
        key_hbm,
        value_hbm,
        output_hbm,
        router_ref,
        map_ref,
        first_gain_ref,
        second_gain_ref,
        vector_ref,
        cosine_hbm,
        sine_hbm,
        *rest,
    ):
        term_refs, first_hbm, rest = rest[:kinds], rest[kinds], rest[kinds + 1 :]
        result_out, token_grads_out, wide_out, small_ref = rest[:4]
        first_refs, rest = rest[4 : 4 + kinds], rest[4 + kinds :]
        (
            queries,
            keys,
            values,
            query_w,
            key_w,
            value_w,
            output_w,
            cosine,
            sine,
            bias,
            out_grads,
            stats,
            outputs,
            middle_grad,
            query_total,
            key_total,
            value_total,
            load_sem,
            gather_send,
            gather_recv,
            first_send,
            first_recv,
            out_send,
            out_recv,
            out_keep,
            sum_part,
            first_part,
            sum_load,
            pack,
            prior,
            cotangent_ref,
            attended_ref,
            middle_ref,
            back_ref,
            result_ref,
            token_grads_ref,
            wide_ref,
            near_sem,
        ) = rest
        own = lax.axis_index("ctx")
        line = pl.ds(pl.multiple_of(own * rows, rows), rows)
        loads = [
            pltpu.make_async_copy(source, target, load_sem.at[index])
            for index, (source, target) in enumerate(
                (
                    (output_hbm, output_w),
                    (queries_hbm, queries),
                    (keys_hbm, keys),
                    (values_hbm, values),
                    (cosine_hbm.at[line], cosine),
                    (sine_hbm.at[line], sine),
                    (query_hbm, query_w),
                    (key_hbm, key_w),
                    (value_hbm, value_w),
                )
            )
        ]
        share = lax.axis_index("dp")
        near_loads = [
            pltpu.make_async_copy(source, target, near_sem.at[index])
            for index, (source, target) in enumerate(
                (
                    (cotangent_hbm, cotangent_ref),
                    (attended_hbm, attended_ref),
                    (middle_hbm, middle_ref),
                    (back_hbm, back_ref),
                )
            )
        ]
        sum_loads = [
            pltpu.make_async_copy(
                term_refs[0].at[jnp.bitwise_xor(share, shares - 2)], sum_part, sum_load.at[0]
            ),
            pltpu.make_async_copy(first_hbm, first_part, sum_load.at[1]),
        ]
        for copy in sum_loads + near_loads:
            copy.start()
        greet_places(
            [(0,) + place for place in places_of(ranks, size)] + [(1, 0, 0), (2, 0, 0)]
        )
        first_copies = [
            pltpu.make_async_remote_copy(
                src_ref=(
                    term_refs[kind].at[jnp.bitwise_xor(share, shares - 1)] if kind else sum_part
                ),
                dst_ref=first_refs[kind],
                send_sem=first_send.at[kind],
                recv_sem=first_recv.at[kind],
                device_id=peer_at(1 if kind else 2, 0, 0),
                device_id_type=pl.DeviceIdType.MESH,
            )
            for kind in range(kinds)
        ]
        for copy in first_copies[1:]:
            copy.start()
        for copy in sum_loads:
            copy.wait()
        add_into(sum_part, first_part)
        first_copies[0].start()
        for load in loads:
            load.start()
        for load in near_loads:
            load.wait()
        output_copies = [
            send_block(produced_hbm, outputs, block, ranks, out_send, out_recv)
            for block in other_blocks(count)
        ]
        output_copies.append(keep_block(produced_hbm, outputs, count, out_keep))

        def keep_wide(index, value):
            half = width // 2
            for part in range(2):
                wide_ref[part, index * width : (index + 1) * width, :] = value[
                    :, part * half : (part + 1) * half
                ].astype(low)

        fill_rows(
            pack,
            prior,
            router_ref,
            map_ref,
            first_gain_ref,
            second_gain_ref,
            vector_ref,
            previous_ref,
        )
        lane = lax.broadcasted_iota(jnp.int32, (rows, 128), 1)
        upstream = cotangent_ref[...].astype(full)
        middle = middle_ref[...]
        inverse_second = inverse_norm(middle)
        unit_second = middle * inverse_second
        gain_second = pack[HEAD_ROWS + 1 : HEAD_ROWS + 2, :]
        second = unit_second * gain_second
        second_low = second.astype(low)
        heads_in = jnp.concatenate(
            [pack[0:HEAD_ROWS, :].astype(low), jnp.zeros((128 - HEAD_ROWS, width), low)], axis=0
        )
        mixed = dot_nt(second_low, heads_in)
        probs = probs_ref[...]
        route_rows = jnp.concatenate(
            [routes_ref[...].astype(full), jnp.zeros((126, rows), full)], axis=0
        )
        route_columns = jnp.transpose(route_rows).astype(jnp.int32)
        route = [column_of(route_columns, k) for k in range(2)]
        chosen = jnp.logical_or(lane == route[0], lane == route[1])
        gates = jnp.where(chosen, probs, 0.0)
        target = [column_of(targets_ref[...], k) for k in range(2)]

        gate_grad = jnp.zeros((rows, 128), full)
        place = lane.astype(full)
        for k in range(2):
            found = jnp.zeros((rows, 128), full)
            for shift in range(count):
                found = found + jnp.where(
                    jnp.logical_and(target[k] - shift * cap == place, lane < cap),
                    dots_ref[shift, 0:1, :],
                    0.0,
                )
            gate_grad = gate_grad + jnp.where(
                lane == route[k], jnp.sum(found, axis=1, keepdims=True), 0.0
            )
        copy_grad = jnp.sum(upstream * second, axis=1, keepdims=True)
        gate_grad = jnp.where(lane == copy_index, copy_grad, gate_grad)
        direct = column_of(gates, copy_index)
        constants = []
        for index in range(2):
            vector = pack[HEAD_ROWS + 2 + index : HEAD_ROWS + 3 + index, :]
            vector_dot = jnp.sum(upstream * vector, axis=1, keepdims=True)
            begin = experts + 2 * index
            spread_of = column_of(mixed, begin + 1) - column_of(mixed, begin)
            mixing = (1.0 / (1.0 + jnp.exp(spread_of)), 1.0 / (1.0 + jnp.exp(-spread_of)))
            gate = column_of(gates, copy_index + 1 + index)
            term = mixing[0] * copy_grad + mixing[1] * vector_dot
            gate_grad = jnp.where(lane == copy_index + 1 + index, term, gate_grad)
            direct = direct + gate * mixing[0]
            constants.append((gate, mixing, vector, vector_dot))
        prob_grad = jnp.where(chosen, gate_grad, 0.0)
        logit_grad = probs * (prob_grad - jnp.sum(probs * prob_grad, axis=1, keepdims=True))
        head_grad = logit_grad
        for index, (gate, mixing, vector, vector_dot) in enumerate(constants):
            mixing_grad = (gate * copy_grad, gate * vector_dot)
            mean = mixing[0] * mixing_grad[0] + mixing[1] * mixing_grad[1]
            for part in range(2):
                head_grad = jnp.where(
                    lane == experts + 2 * index + part,
                    mixing[part] * (mixing_grad[part] - mean),
                    head_grad,
                )
        head_low = head_grad.astype(low)

        slot = lax.broadcasted_iota(jnp.int32, (rows, slots), 1).astype(full)
        picked = [(slot == target[k]).astype(full).astype(low) for k in range(2)]
        second_grad = (
            dot(head_low, heads_in) + direct * upstream + dot(picked[0] + picked[1], back_ref[...])
        )
        normal_grad = second_grad * gain_second
        middle_total = upstream + inverse_second * (
            normal_grad - unit_second * jnp.mean(normal_grad * unit_second, axis=1, keepdims=True)
        )
        middle_grad[...] = middle_total
        middle_low = middle_total.astype(low)
        loads[0].wait()
        out_grad = dot_nt(middle_low, output_w[...]).astype(low)
        out_grads[own] = out_grad
        product = out_grad.astype(full) * attended_ref[...]
        masks = head_masks(rows)
        deltas = jnp.zeros((rows, 128), full)
        for index in range(pairs):
            part = product[:, index * 128 : index * 128 + 128]
            for head in range(2):
                total = jnp.sum(jnp.where(masks[head], part, 0.0), axis=1, keepdims=True)
                deltas = jnp.where(lane == 2 * index + head, total, deltas)
        stats[own, 0:stat_rows] = lse_ref[...]
        stats[own, stat_rows:] = jnp.transpose(deltas)[0:stat_rows]
        gather = Gather([out_grads, stats], size, gather_send, gather_recv)
        gather.forward(0)
        for copy in output_copies:
            copy.start()

        chosen_out = second * direct
        for gate, mixing, vector, vector_dot in constants:
            chosen_out = chosen_out + gate * mixing[1] * vector
        base = middle + chosen_out
        small_ref[...] = jnp.zeros_like(small_ref)
        small_ref[1:2, :] = jnp.sum(second_grad * unit_second, axis=0, keepdims=True)
        for index, (gate, mixing, vector, vector_dot) in enumerate(constants):
            small_ref[2 + index : 3 + index, :] = jnp.sum(
                gate * mixing[1] * upstream, axis=0, keepdims=True
            )
        small_ref[8:24, :] = dot_tn(head_low, second_low)[0:16]
        carry_grad = lax.dot_general(
            jnp.transpose(logit_grad)[0:16],
            prior[0:experts, :],
            (((1,), (1,)), ((), ())),
            precision=HIGH,
        )
        small_ref[24:40, 0:experts] = carry_grad
        keep_wide(3, dot_tn(attended_ref[...].astype(low), middle_low))
        keeps = [
            pltpu.make_async_copy(
                wide_ref.at[:, pl.ds(3 * width, width)],
                wide_out.at[:, pl.ds(3 * width, width)],
                near_sem.at[4],
            )
        ]
        keeps[0].start()

        for load in loads[1:4]:
            load.wait()
        query_total[...] = jnp.zeros_like(query_total)
        key_total[...] = jnp.zeros_like(key_total)
        value_total[...] = jnp.zeros_like(value_total)
        column = lax.broadcasted_iota(jnp.int32, (rows, rows), 0)
        row = lax.broadcasted_iota(jnp.int32, (rows, rows), 1)

        def block_side(block, as_query, as_key):
            key_block, query_block = (own if as_key else block), (own if as_query else block)
            key_pos, query_pos = key_block * rows + column, query_block * rows + row
            first = start_of(query_pos[0:8], starts_ref)[0:1]
            allowed = jnp.logical_and(key_pos >= first, key_pos <= query_pos)
            bias[...] = jnp.where(allowed, 0.0, NEGATIVE)

            def pair(index, carried):
                lanes = pl.ds(pl.multiple_of(index * 128, 128), 128)
                query, grad = queries[query_block, :, lanes], out_grads[query_block, :, lanes]
                key, value = keys[key_block, :, lanes], values[key_block, :, lanes]
                one_key = [jnp.where(mask, key, 0) for mask in masks]
                scores = [dot_nt(one_key[head], query) for head in range(2)]
                weight_grad = [dot_nt(jnp.where(mask, value, 0), grad) for mask in masks]
                weight, score = [], []
                for head in range(2):
                    lse = stats[query_block, pl.ds(2 * index + head, 1), :]
                    mean = stats[query_block, pl.ds(stat_rows + 2 * index + head, 1), :]
                    weight.append(jnp.exp(scores[head] + bias[...] - lse))
                    score.append((weight[head] * (weight_grad[head] - mean)).astype(low))
                if as_key:
                    value_total[:, lanes] += dot(
                        weight[0].astype(low), jnp.where(masks[0], grad, 0)
                    ) + dot(weight[1].astype(low), jnp.where(masks[1], grad, 0))
                    key_total[:, lanes] += dot(score[0], jnp.where(masks[0], query, 0)) + dot(
                        score[1], jnp.where(masks[1], query, 0)
                    )
                if as_query:
                    query_total[lanes, :] += dot_tn(one_key[0], score[0]) + dot_tn(
                        one_key[1], score[1]
                    )
                return carried

            lax.fori_loop(0, pairs, pair, 0)

        block_side(own, True, True)
        def earlier(place, carried):
            block = jnp.bitwise_xor(own, place)

            @pl.when(block < own)
            def _():
                block_side(block, True, False)

            return carried

        def later(place, carried):
            for one in range(1, size):

                @pl.when(place == one)
                def _():
                    gather.arrive(one)

            block = jnp.bitwise_xor(own, place)

            @pl.when(block > own)
            def _():
                block_side(block, False, True)

            return carried

        lax.fori_loop(1, size, earlier, 0)
        lax.fori_loop(1, size, later, 0)
        for load in loads[4:]:
            load.wait()
        inputs = tokens_ref[...].astype(full)
        inverse_first = inverse_norm(inputs)
        unit_first = inputs * inverse_first
        gain_first = pack[HEAD_ROWS : HEAD_ROWS + 1, :]
        normed = (unit_first * gain_first).astype(low)
        turn = -sine[...]
        query_grad = jnp.transpose(query_total[...]) * HEAD_DIM**-0.5
        query_low = rotate(query_grad, cosine[...], turn).astype(low)
        key_low = rotate(key_total[...], cosine[...], turn).astype(low)
        value_low = value_total[...].astype(low)
        first_grad = (
            dot_nt(query_low, query_w[...])
            + dot_nt(key_low, key_w[...])
            + dot_nt(value_low, value_w[...])
        )
        for index, part in enumerate((query_low, key_low, value_low)):
            keep_wide(index, dot_tn(normed, part))
        keeps.append(
            pltpu.make_async_copy(
                wide_ref.at[:, pl.ds(0, 3 * width)],
                wide_out.at[:, pl.ds(0, 3 * width)],
                near_sem.at[5],
            )
        )
        keeps[-1].start()
        small_ref[0:1, :] = jnp.sum(first_grad * unit_first, axis=0, keepdims=True)
        normal_grad = first_grad * gain_first
        token_grads_ref[...] = middle_grad[...] + inverse_first * (
            normal_grad - unit_first * jnp.mean(normal_grad * unit_first, axis=1, keepdims=True)
        )
        keeps.append(pltpu.make_async_copy(token_grads_ref, token_grads_out, near_sem.at[6]))
        keeps[-1].start()
        for copy in output_copies:
            copy.wait()
        for k in range(2):
            weight = jnp.sum(jnp.where(lane == route[k], probs, 0.0), axis=1, keepdims=True)
            base = base + weight * dot(picked[k], outputs[...].reshape(slots, width))
        result_ref[...] = base.astype(low)
        keeps.append(pltpu.make_async_copy(result_ref, result_out, near_sem.at[7]))
        keeps[-1].start()
        gather.finish()
        for copy in first_copies + keeps:
            copy.wait()

    stream_shape = (size, rows, width)
    any_space = pl.BlockSpec(memory_space=pl.ANY)
    in_vmem = pl.BlockSpec(memory_space=pltpu.VMEM)
    square = (width, width)
    return pl.pallas_call(
        kernel,
        out_shape=[
            jax.ShapeDtypeStruct((rows, width), low),
            jax.ShapeDtypeStruct((rows, width), full),
            jax.ShapeDtypeStruct((2, 4 * width, width // 2), low),
            jax.ShapeDtypeStruct((64, width), full),
        ]
        + [jax.ShapeDtypeStruct(term.shape[1:], low) for term in terms],
        in_specs=[in_vmem, any_space, in_vmem, in_vmem]
        + [pl.BlockSpec(memory_space=pltpu.SMEM)]
        + [any_space, in_vmem, any_space, in_vmem, in_vmem]
        + [any_space] * 3
        + [any_space, any_space, in_vmem]
        + [any_space] * 4
        + [in_vmem] * 5
        + [any_space] * (3 + kinds),
        out_specs=[any_space] * 3 + [in_vmem] + [any_space] * kinds,
        scratch_shapes=[
            pltpu.VMEM(stream_shape, low),
            pltpu.VMEM(stream_shape, low),
            pltpu.VMEM(stream_shape, low),
            pltpu.VMEM(square, low),
            pltpu.VMEM(square, low),
            pltpu.VMEM(square, low),
            pltpu.VMEM(square, low),
            pltpu.VMEM((rows, 128), full),
            pltpu.VMEM((rows, 128), full),
            pltpu.VMEM((rows, rows), full),
            pltpu.VMEM(stream_shape, low),
            pltpu.VMEM((size, 2 * stat_rows, rows), full),
            pltpu.VMEM((count, cap, width), low),
            pltpu.VMEM((rows, width), full),
            pltpu.VMEM((width, rows), full),
            pltpu.VMEM((rows, width), full),
            pltpu.VMEM((rows, width), full),
            pltpu.SemaphoreType.DMA((9,)),
            pltpu.SemaphoreType.DMA((2, size)),
            pltpu.SemaphoreType.DMA((2, size)),
            pltpu.SemaphoreType.DMA((kinds,)),
            pltpu.SemaphoreType.DMA((kinds,)),
            pltpu.SemaphoreType.DMA((count,)),
            pltpu.SemaphoreType.DMA((count,)),
            pltpu.SemaphoreType.DMA,
            pltpu.VMEM(terms[0].shape[1:], low),
            pltpu.VMEM(terms[0].shape[1:], low),
            pltpu.SemaphoreType.DMA((2,)),
            pltpu.VMEM((24, width), full),
            pltpu.VMEM((16, rows), full),
            pltpu.VMEM((rows, width), low),
            pltpu.VMEM((rows, width), full),
            pltpu.VMEM((rows, width), full),
            pltpu.VMEM((slots, width), low),
            pltpu.VMEM((rows, width), low),
            pltpu.VMEM((rows, width), full),
            pltpu.VMEM((2, 4 * width, width // 2), low),
            pltpu.SemaphoreType.DMA((8,)),
        ],
        compiler_params=pltpu.CompilerParams(
            collective_id=2, has_side_effects=True, vmem_limit_bytes=60 * 2**20
        ),
        cost_estimate=pl.CostEstimate(
            flops=14 * rows * width * width * 2 + 20 * size * rows * rows * width,
            bytes_accessed=30 * 2**20,
            transcendentals=size * rows * rows * 12,
        ),
        name="backward",
    )(
        tokens,
        cotangent,
        previous,
        routes,
        starts,
        *forward,
        *returns,
        *weights,
        *params,
        jnp.asarray(tables[0]),
        jnp.asarray(tables[1]),
        *terms,
        first,
    )


PIECES = 4
ORDER = (
    6, 0, 3, 10, 0, 5, 0, 1, 0, 5, 6, 6, 5, 3, 5,
    10, 7, 4, 0, 1, 7, 2, 10, 1, 0, 7, 4, 0, 2, 7,
    0, 3, 11, 0, 9, 2, 12, 6, 8, 1, 9, 11, 11, 10, 9,
    0, 5, 9, 4, 11, 10, 12, 7, 4, 3, 3, 10, 6, 1, 12,
    8, 11, 8, 0, 8, 12, 9, 2, 4, 12, 7, 2, 11, 6, 8,
    9, 5, 8, 12,
)
DENSE_TIMES = (7, 24, 34, 48, 62, 77, 91, 101, 118, 125, 132)
EXPERT_TIMES = (19, 14, 19, 4, 11, 2)


def halving_steps(size):
    steps, step = [], 0
    while 1 << step < size:
        bit = 1 << step
        steps += [(step, place) for place in range(size - bit, 0, -2 * bit)]
        step += 1
    return steps


def needed_before(step, place):
    return {(earlier, place | 1 << earlier) for earlier in range(step)}


def reduce_layer(terms, firsts, wide, small, spread, shares, ring, exchange_size):
    low, full = jnp.bfloat16, jnp.float32
    steps = halving_steps(shares)
    done = [[(0, shares - 1), (1, shares - 2)]] + [[(0, shares - 1)]] * (len(terms) - 1)
    kinds = len(terms)
    blocks = [term.shape[1:] for term in terms]
    members = ring // spread
    groups = 3
    near_bits = [1 << step for step in range(ring.bit_length() - 1)]
    far_bits = [1 << step for step in range(exchange_size.bit_length() - 1)]
    deep_bits = [1 << step for step in range(shares.bit_length() - 1)]
    near = [(0, 0, bit) for bit in near_bits]
    far = [(0, bit, 0) for bit in far_bits]
    deep = [(bit, 0, 0) for bit in deep_bits]
    orders = [near + far + deep, near[:1] + far + near[1:] + deep, near + far + deep]
    places = near + far + deep
    bit_count = len(places)
    group_rows = [wide.shape[1], wide.shape[1], small.shape[0]]
    tile = [16, 16, 8]
    plans = []
    for group in range(groups):
        length, plan = group_rows[group], []
        for _ in range(bit_count):
            halved = (length // 2) % tile[group] == 0
            length = length // 2 if halved else length
            plan.append((halved, length))
        plans.append(plan)

    def kernel(*refs):
        refs = list(refs)

        def take(number):
            taken = refs[:number]
            del refs[:number]
            return taken

        term_refs, first_refs = take(kinds), take(kinds)
        (wide_hbm, small_hbm) = take(2)
        gathered = take(kinds)
        (wide_out, small_out) = take(2)
        sums, landed = take(kinds), take(kinds)
        (halves, smalls) = take(2)
        group_landed = take(groups)
        (load_sem, step_send, step_recv, own_sem, ring_send, ring_recv) = take(6)
        (dense_send, dense_recv, dense_load) = take(3)
        share = lax.axis_index("dp")
        mine = lax.axis_index("ctx") // spread

        dense_in = [
            pltpu.make_async_copy(wide_hbm, halves, dense_load.at[0]),
            pltpu.make_async_copy(small_hbm, smalls, dense_load.at[1]),
        ]
        for copy in dense_in:
            copy.start()
        loads = []
        for kind in range(kinds):
            copies = [
                pltpu.make_async_copy(
                    first_refs[kind],
                    landed[kind].at[steps.index(done[kind][-1])],
                    load_sem.at[kind, shares // 2],
                )
            ]
            for place in range(shares - 2, -1, -2):
                copies.append(
                    pltpu.make_async_copy(
                        term_refs[kind].at[jnp.bitwise_xor(share, place)],
                        sums[kind].at[place // 2],
                        load_sem.at[kind, place // 2],
                    )
                )
            for copy in copies:
                copy.start()
            loads.append(copies)
        greet_places(places)

        def expert_chain(kind, piece):
            period, odd_wait, even_wait, near_wait, far_wait, last_wait = EXPERT_TIMES
            begin = time = period * (kind * PIECES + piece)
            slots = {step: index for index, step in enumerate(steps)}
            lines = blocks[kind][0] // PIECES
            window = pl.ds(piece * lines, lines)
            one = kind * PIECES + piece

            def transfer(step, place):
                index = slots[step, place]
                if place % 2 == 1:
                    source = term_refs[kind].at[jnp.bitwise_xor(share, place), window]
                else:
                    source = sums[kind].at[place // 2, window]
                return pltpu.make_async_remote_copy(
                    src_ref=source,
                    dst_ref=landed[kind].at[index, window],
                    send_sem=step_send.at[one, index],
                    recv_sem=step_recv.at[one, index],
                    device_id=peer_at(1 << step, 0, 0),
                    device_id_type=pl.DeviceIdType.MESH,
                )

            yield begin
            arrived, started = set(done[kind]), []
            waiting = [op for op in steps if op not in arrived]
            for op in list(waiting):
                if op[0] == 0:
                    transfer(*op).start()
                    started.append(op)
                    waiting.remove(op)
            while loads[kind]:
                loads[kind].pop().wait()
            step, place = done[kind][-1]
            add_into(
                sums[kind].at[(place ^ 1 << step) // 2, window],
                landed[kind].at[slots[step, place], window],
            )
            while True:
                for op in list(waiting):
                    if needed_before(*op) <= arrived:
                        transfer(*op).start()
                        started.append(op)
                        waiting.remove(op)
                if not started:
                    break
                op = started.pop(0)
                yield time + (even_wait if op[0] else odd_wait)
                transfer(*op).wait()
                arrived.add(op)
                add_into(
                    sums[kind].at[(op[1] ^ 1 << op[0]) // 2, window],
                    landed[kind].at[slots[op], window],
                )
            time += even_wait
            index = len(steps)
            bit = 1
            while bit < spread:
                copy = pltpu.make_async_remote_copy(
                    src_ref=sums[kind].at[0, window],
                    dst_ref=landed[kind].at[index, window],
                    send_sem=step_send.at[one, index],
                    recv_sem=step_recv.at[one, index],
                    device_id=peer_at(0, 0, bit),
                    device_id_type=pl.DeviceIdType.MESH,
                )
                copy.start()
                time += near_wait
                yield time
                copy.wait()
                add_into(sums[kind].at[0, window], landed[kind].at[index, window])
                index += 1
                bit *= 2
            keep = pltpu.make_async_copy(
                sums[kind].at[0, window], gathered[kind].at[mine, window], own_sem.at[one]
            )
            keep.start()
            sent = []

            def pass_on(place, bit):
                block = jnp.bitwise_xor(mine, place)
                target = gathered[kind].at[block, window]
                return pltpu.make_async_remote_copy(
                    src_ref=sums[kind].at[0, window] if place == 0 else target,
                    dst_ref=target,
                    send_sem=ring_send.at[one, place ^ bit],
                    recv_sem=ring_recv.at[one, place ^ bit],
                    device_id=peer_at(0, 0, bit * spread),
                    device_id_type=pl.DeviceIdType.MESH,
                )

            def forward(place):
                for bit, held in gather_steps(members):
                    if place in held:
                        copy = pass_on(place, bit)
                        copy.start()
                        sent.append(copy)

            forward(0)
            for place in range(1, members):
                wait = near_wait if place == 1 else far_wait if place & (place - 1) == 0 else last_wait
                yield time + wait + (far_wait if wait == last_wait else 0)
                bit = place & -place
                pass_on(place ^ bit, bit).wait_recv()
                forward(place)
            yield 1000
            keep.wait()
            for copy in sent:
                copy.wait_send()

        def bit_of(place):
            deep_bit, far_bit, near_bit = place
            axis, bit = ("dp", deep_bit) if deep_bit else ("exp", far_bit) if far_bit else ("ctx", near_bit)
            return lax.rem(lax.axis_index(axis) // bit, 2)

        def dense_chain(times):
            times = iter(times + tuple(range(times[-1] + 8, 900, 8)))
            buffers = [halves.at[0], halves.at[1], smalls]
            yield 0
            for copy in dense_in:
                copy.wait()
            begins = [0] * groups
            trail = []

            def window(begin, length, group):
                if isinstance(begin, int):
                    return pl.ds(begin, length)
                return pl.ds(pl.multiple_of(begin, tile[group]), length)

            def exchange_rows(group, step, source, target):
                return pltpu.make_async_remote_copy(
                    src_ref=source,
                    dst_ref=target,
                    send_sem=dense_send.at[group, step],
                    recv_sem=dense_recv.at[group, step],
                    device_id=peer_at(*orders[group][step % bit_count]),
                    device_id_type=pl.DeviceIdType.MESH,
                )

            for step in range(bit_count):
                copies = []
                for group in range(groups):
                    halved, length = plans[group][step]
                    upper = bit_of(orders[group][step])
                    if halved:
                        sent = begins[group] + (1 - upper) * length
                        begins[group] = begins[group] + upper * length
                    else:
                        sent = begins[group]
                    at = sum(size for _, size in plans[group][:step])
                    copy = exchange_rows(
                        group,
                        step,
                        buffers[group].at[window(sent, length, group)],
                        group_landed[group].at[pl.ds(at, length)],
                    )
                    copy.start()
                    copies.append((copy, at, length))
                trail.append(list(begins))
                yield next(times)
                for group, (copy, at, length) in enumerate(copies):
                    copy.wait()
                    add_into(
                        buffers[group].at[window(begins[group], length, group)],
                        group_landed[group].at[pl.ds(at, length)],
                    )
            outputs = [wide_out.at[0], wide_out.at[1], small_out]
            keeps = []
            for group in range(groups):
                part = window(begins[group], plans[group][-1][1], group)
                keep = pltpu.make_async_copy(
                    buffers[group].at[part], outputs[group].at[part], dense_load.at[group]
                )
                keep.start()
                keeps.append(keep)
            for keep in keeps:
                keep.wait()
            for step in range(bit_count - 1, -1, -1):
                copies = []
                for group in range(groups):
                    halved, length = plans[group][step]
                    if halved:
                        part = outputs[group].at[window(trail[step][group], length, group)]
                        copy = exchange_rows(group, bit_count + step, part, part)
                        copy.start()
                        copies.append(copy)
                if copies:
                    yield next(times)
                for copy in copies:
                    copy.wait()

        chains = [dense_chain(DENSE_TIMES)] + [
            expert_chain(kind, piece) for kind in range(kinds) for piece in range(PIECES)
        ]
        due = dict(enumerate(next(chain) for chain in chains))
        planned = list(ORDER) if (shares, ring, exchange_size) == (4, 4, 2) else []
        while due:
            index = planned.pop(0) if planned else min(due, key=lambda one: (due[one], one))
            time = next(chains[index], None)
            if time is None:
                del due[index]
            else:
                due[index] = time

    any_space = pl.BlockSpec(memory_space=pl.ANY)
    extra = len(steps) + spread.bit_length() - 1
    return pl.pallas_call(
        kernel,
        out_shape=[jax.ShapeDtypeStruct((members,) + block, low) for block in blocks]
        + [jax.ShapeDtypeStruct(wide.shape, low), jax.ShapeDtypeStruct(small.shape, full)],
        in_specs=[any_space] * (2 * kinds + 2),
        out_specs=[any_space] * (kinds + 2),
        scratch_shapes=[pltpu.VMEM((shares // 2,) + block, low) for block in blocks]
        + [pltpu.VMEM((extra,) + block, low) for block in blocks]
        + [pltpu.VMEM(wide.shape, low), pltpu.VMEM(small.shape, full)]
        + [
            pltpu.VMEM(
                (sum(length for _, length in plans[group]), (wide, wide, small)[group].shape[-1]),
                (low, low, full)[group],
            )
            for group in range(groups)
        ]
        + [
            pltpu.SemaphoreType.DMA((kinds, shares // 2 + 1)),
            pltpu.SemaphoreType.DMA((kinds * PIECES, extra)),
            pltpu.SemaphoreType.DMA((kinds * PIECES, extra)),
            pltpu.SemaphoreType.DMA((kinds * PIECES,)),
            pltpu.SemaphoreType.DMA((kinds * PIECES, members)),
            pltpu.SemaphoreType.DMA((kinds * PIECES, members)),
            pltpu.SemaphoreType.DMA((groups, 2 * bit_count)),
            pltpu.SemaphoreType.DMA((groups, 2 * bit_count)),
            pltpu.SemaphoreType.DMA((3,)),
        ],
        compiler_params=pltpu.CompilerParams(
            collective_id=3, has_side_effects=True, vmem_limit_bytes=60 * 2**20
        ),
        name="reduce",
    )(*terms, *firsts, wide, small)


def widen_layer(parts, wide, small, experts):
    members = parts[0].shape[0]
    pieces = 1
    steps = members * pieces
    squares = wide.shape[1] // (2 * wide.shape[2])
    width = 2 * wide.shape[2]
    lines = wide.shape[1] // steps
    turns = width // lines
    full = jnp.float32
    kinds = len(parts)

    def kernel(*refs):
        sources, wide_ref, small_ref = refs[:kinds], refs[kinds], refs[kinds + 1]
        targets = refs[kinds + 2 : 2 * kinds + 2]
        square_refs = refs[2 * kinds + 2 : 2 * kinds + 2 + squares]
        head_ref, map_ref, carry_ref, vector_ref, *gain_refs = refs[2 * kinds + 2 + squares :]
        step = pl.program_id(0) * pieces + pl.program_id(1)
        for source, target in zip(sources, targets):
            target[...] = source[...].astype(full)
        for index in range(squares):

            @pl.when(step // turns == index)
            def _():
                square_refs[index][:, 0 : width // 2] = wide_ref[0].astype(full)
                square_refs[index][:, width // 2 :] = wide_ref[1].astype(full)

        @pl.when(step == 0)
        def _():
            head_ref[...] = small_ref[8 : 8 + experts, :]
            for index in range(2):
                begin = 8 + experts + 2 * index
                map_ref[index] = small_ref[begin : begin + 2, :]
            carry_ref[...] = jnp.transpose(small_ref[24:40, 0:128])[0:experts, 0:experts]
            vector_ref[...] = small_ref[2:4, :]
            for index, target in enumerate(gain_refs):
                target[...] = small_ref[index : index + 1, :].reshape(width)

    def chunk(part):
        return pl.BlockSpec(
            (1, part.shape[1] // pieces, part.shape[2]), lambda member, piece: (member, piece, 0)
        )

    def square(index):
        return pl.BlockSpec(
            (lines, width),
            lambda member, piece: (
                jnp.clip(member * pieces + piece - index * turns, 0, turns - 1),
                0,
            ),
        )

    def whole(*shape):
        return pl.BlockSpec(shape, lambda member, piece: (0,) * len(shape))

    smalls = [(experts, width), (2, 2, width), (experts, experts), (2, width), (width,), (width,)]
    return pl.pallas_call(
        kernel,
        out_shape=[jax.ShapeDtypeStruct(part.shape, full) for part in parts]
        + [jax.ShapeDtypeStruct((width, width), full)] * squares
        + [jax.ShapeDtypeStruct(shape, full) for shape in smalls],
        grid=(members, pieces),
        in_specs=[chunk(part) for part in parts]
        + [
            pl.BlockSpec(
                (2, lines, width // 2), lambda member, piece: (0, member * pieces + piece, 0)
            ),
            whole(*small.shape),
        ],
        out_specs=[chunk(part) for part in parts]
        + [square(index) for index in range(squares)]
        + [whole(*shape) for shape in smalls],
        compiler_params=pltpu.CompilerParams(vmem_limit_bytes=60 * 2**20),
        name="widen",
    )(*parts, wide, small)


def local(
    tokens,
    cotangent,
    previous,
    routes,
    boundaries,
    norm_first,
    query_weight,
    key_weight,
    value_weight,
    output_weight,
    norm_second,
    router,
    gate_carry,
    constant_map,
    constant_vector,
    expert_gate,
    expert_linear,
    expert_down,
):
    model_width = tokens.shape[2]
    ring = lax.axis_size("ctx")
    group_size = expert_gate.shape[0]
    exchange_count = lax.axis_size("exp")
    spread = ring // group_size
    ranks = (exchange_count, group_size, spread)
    slot_total = exchange_count * group_size * CAP
    expert_total = router.shape[1]
    params = (
        router.T,
        jnp.transpose(constant_map, (0, 2, 1)),
        norm_first,
        norm_second,
        constant_vector,
    )
    prior = jnp.transpose(previous, (2, 0, 1))
    weights = (query_weight, key_weight, value_weight, output_weight)
    (
        queries,
        keys,
        values,
        attended,
        lse,
        middle,
        probs,
        targets,
        outgoing,
        slot_gates,
        grads_in,
    ) = attend_layer(
        tokens[0],
        cotangent[0],
        prior,
        routes[0].T,
        boundaries,
        weights,
        params,
        gate_carry,
        ranks,
        CAP,
        ring,
    )
    home_grads, produced, dots, gate_terms, linear_terms, down_terms, first = expert_layer(
        outgoing,
        slot_gates,
        grads_in.reshape(slot_total, model_width),
        (expert_gate, expert_linear, expert_down),
        ranks,
        lax.axis_size("dp"),
    )
    terms = (down_terms, gate_terms, linear_terms)
    shares = lax.axis_size("dp")
    result, token_grads, wide, small, *firsts = backward_layer(
        tokens[0],
        cotangent[0],
        prior,
        routes[0].T,
        boundaries,
        (attended, lse, middle, probs, targets, queries, keys, values),
        (home_grads.reshape(slot_total, model_width), produced, dots),
        weights,
        params,
        terms,
        first,
        ranks,
        CAP,
        ring,
        shares,
    )
    *parts, wide, small = reduce_layer(
        terms, firsts, wide, small, spread, shares, ring, exchange_count
    )
    (
        down_grads,
        gate_grads,
        linear_grads,
        query_grads,
        key_grads,
        value_grads,
        output_grads,
        router_grads,
        map_grads,
        carry_grads,
        vector_grads,
        first_grads,
        second_grads,
    ) = widen_layer(parts, wide, small, expert_total)
    return (
        result[None],
        token_grads[None],
        first_grads,
        query_grads,
        key_grads,
        value_grads,
        output_grads,
        second_grads,
        router_grads.T,
        carry_grads,
        jnp.transpose(map_grads, (0, 2, 1)),
        vector_grads,
        gate_grads,
        linear_grads,
        down_grads,
    )


def solution(mesh):
    return jax.shard_map(
        local,
        mesh=mesh,
        in_specs=(
            P(("dp", "exp"), "ctx", None),
            P(("dp", "exp"), "ctx", None),
            P(("dp", "exp"), "ctx", None),
            P(("dp", "exp"), "ctx", None),
            P(("dp", "exp"), None),
            P(),
            P(),
            P(),
            P(),
            P(),
            P(),
            P(),
            P(),
            P(),
            P(),
            P("exp", None, None),
            P("exp", None, None),
            P("exp", None, None),
        ),
        out_specs=(
            P(("dp", "exp"), "ctx", None),
            P(("dp", "exp"), "ctx", None),
            P(),
            P(),
            P(),
            P(),
            P(),
            P(),
            P(),
            P(),
            P(),
            P(),
            P("exp", None, "dp"),
            P("exp", None, "dp"),
            P("exp", "dp", None),
        ),
        check_vma=False,
    )
```

```python
import math

import jax
import jax.numpy as jnp
import numpy as np
from jax import lax
from jax.experimental import pallas as pl
from jax.experimental.pallas import tpu as pltpu
from jax.sharding import PartitionSpec as P

HEAD_DIM = 64
CAP = 96


EPSILON = 1e-06
NEGATIVE = -1e30
HIGH = lax.Precision.HIGHEST


HEAD_ROWS = 16


def mesh_id(exp_index, ctx_index):
    return {"exp": exp_index, "ctx": ctx_index}


def dot(left, right):
    return jnp.dot(left, right, preferred_element_type=jnp.float32)


def dot_nt(left, right):
    return lax.dot_general(
        left, right, (((1,), (1,)), ((), ())), preferred_element_type=jnp.float32
    )


def dot_tn(left, right):
    return lax.dot_general(
        left, right, (((0,), (0,)), ((), ())), preferred_element_type=jnp.float32
    )


def member_of(shift, ranks):
    exchange_size, group_size, spread = ranks
    exp_index, ctx_index = lax.axis_index("exp"), lax.axis_index("ctx")
    far, near = shift // group_size, shift % group_size
    place = jnp.bitwise_xor(ctx_index // spread, near) * spread + lax.rem(ctx_index, spread)
    return mesh_id(jnp.bitwise_xor(exp_index, far), place)


def greet(count, ranks):
    barrier = pltpu.get_barrier_semaphore()
    for shift in range(1, count):
        pl.semaphore_signal(
            barrier, inc=1, device_id=member_of(shift, ranks), device_id_type=pl.DeviceIdType.MESH
        )
    pl.semaphore_wait(barrier, count - 1)


def block_of(shift, count):
    return (shift + count - count // 4) % count


def own_block(count):
    return block_of(0, count)


def send_block(source, target, block, ranks, send_sem, recv_sem):
    count = ranks[0] * ranks[1]
    return pltpu.make_async_remote_copy(
        src_ref=source.at[block],
        dst_ref=target.at[block],
        send_sem=send_sem.at[block],
        recv_sem=recv_sem.at[block],
        device_id=member_of((block + count // 4) % count, ranks),
        device_id_type=pl.DeviceIdType.MESH,
    )


def keep_block(source, target, count, sem):
    block = own_block(count)
    return pltpu.make_async_copy(source.at[block], target.at[block], sem)


def other_blocks(count):
    return [block for block in range(count) if block != own_block(count)]


def expert_layer(outgoing, gates, grads, weights, ranks, shares):
    count, cap, width = outgoing.shape
    hidden_units = weights[0].shape[2]
    rows = count * cap
    share = hidden_units // shares
    spread = ranks[2]

    def kernel(
        outgoing_hbm,
        gates_ref,
        grads_hbm,
        gate_hbm,
        linear_hbm,
        down_hbm,
        back_ref,
        output_out,
        dots_ref,
        gate_terms,
        linear_terms,
        down_terms,
        first_ref,
        received,
        received_gates,
        gate_w,
        linear_w,
        down_w,
        hidden_grad,
        hidden,
        gate_low,
        linear_low,
        rows_t,
        scaled,
        gate_column,
        out_total,
        in_total,
        in_send,
        dots_send,
        terms,
        weight_sem,
        send_sem,
        recv_sem,
        local_sem,
        terms_sem,
        first_send,
        first_recv,
        grads_ref,
        output_ref,
        extra_sem,
    ):
        own = lax.axis_index("ctx") // spread
        loads = [
            pltpu.make_async_copy(source.at[own], target, weight_sem.at[index])
            for index, (source, target) in enumerate(
                ((down_hbm, down_w), (gate_hbm, gate_w), (linear_hbm, linear_w))
            )
        ]
        bring = pltpu.make_async_copy(grads_hbm, grads_ref, extra_sem.at[0])
        bring.start()
        for load in loads:
            load.start()
        greet_places([(0,) + place for place in group_places(ranks)] + [(1, 0, 0)])

        def send_some(source, target, index, shifts):
            copies = []
            for shift in shifts:
                if shift == own_block(count):
                    copies.append(keep_block(source, target, count, local_sem.at[index]))
                else:
                    copies.append(
                        send_block(
                            source, target, shift, ranks, send_sem.at[index], recv_sem.at[index]
                        )
                    )
            for copy in copies:
                copy.start()
            return copies

        every = range(count)
        gates_in = send_some(gates_ref, received_gates, 0, every)
        soon = [block for block in every if not count // 2 <= block < count - count // 4]
        incoming = dict(zip(soon, send_some(outgoing_hbm, received, 1, soon)))
        bring.wait()
        loads[0].wait()

        def backward_in(index, carry):
            part = pl.ds(pl.multiple_of(index * share, share), share)
            hidden_grad[:, part] = dot_nt(grads_ref[...], down_w[part, :])
            return carry

        lax.fori_loop(0, shares, backward_in, 0)
        for copy in gates_in:
            copy.wait()
        for shift in every:
            column = jnp.transpose(received_gates[shift])[:cap, 0:1]
            block = pl.ds(shift * cap, cap)
            gate_column[block, :] = jnp.broadcast_to(column, (cap, 128))
            scaled[block, :] = (column * grads_ref[block, :].astype(jnp.float32)).astype(
                jnp.bfloat16
            )
        for load in loads[1:]:
            load.wait()

        going = []
        batches = 2
        members = count // batches
        lines = rows // batches
        for batch in range(batches):
            chunks = range(batch * members, (batch + 1) * members)
            for shift in chunks:
                incoming[shift].wait()
            if batch == 0:
                late = [block for block in every if block not in soon]
                incoming.update(zip(late, send_some(outgoing_hbm, received, 1, late)))
            block = pl.ds(batch * lines, lines)

            def through(index):
                part = pl.ds(index * share, share)
                tokens = received[batch * members : (batch + 1) * members].reshape(lines, width)
                gate_part = dot(tokens, gate_w[:, part])
                linear_part = dot(tokens, linear_w[:, part])
                sigmoid = 1.0 / (1.0 + jnp.exp(-gate_part))
                silu = gate_part * sigmoid
                low = (silu * linear_part).astype(jnp.bfloat16)
                hidden[block, part] = low
                upper = hidden_grad[block, part] * gate_column[block, 0:1]
                low_gate = (
                    upper * linear_part * sigmoid * (1.0 + gate_part * (1.0 - sigmoid))
                ).astype(jnp.bfloat16)
                gate_low[block, part] = low_gate
                low_linear = (upper * silu).astype(jnp.bfloat16)
                linear_low[block, part] = low_linear
                out = dot(low, down_w[part, :])
                back = dot_nt(low_gate, gate_w[:, part]) + dot_nt(low_linear, linear_w[:, part])

                if index == 0:
                    out_total[block, :] = out
                    in_total[block, :] = back
                else:
                    out_total[block, :] += out
                    in_total[block, :] += back

            for tile in range(shares):
                through(tile)
            in_send[batch * members : (batch + 1) * members] = (
                in_total[block, :].astype(jnp.bfloat16).reshape(members, cap, width)
            )
            going += send_some(in_send, back_ref, 2, chunks)
            low = out_total[block, :].astype(jnp.bfloat16)
            output_ref[batch * members : (batch + 1) * members] = low.reshape(members, cap, width)
            part = pl.ds(batch * members, members)
            going.append(
                pltpu.make_async_copy(
                    output_ref.at[part], output_out.at[part], extra_sem.at[1 + batch]
                )
            )
            going[-1].start()
            dots = jnp.sum(
                low.astype(jnp.float32) * grads_ref[block, :].astype(jnp.float32),
                axis=1,
                keepdims=True,
            )
            for place, shift in enumerate(chunks):
                column = jnp.broadcast_to(dots[place * cap : (place + 1) * cap], (cap, 128))
                dots_send[shift, :, 0:cap] = jnp.transpose(column)[0:8, :]
                dots_send[shift, :, cap:] = jnp.zeros((8, 128 - cap), jnp.float32)
            going += send_some(dots_send, dots_ref, 3, chunks)
            rows_t[:, batch * lines : (batch + 1) * lines] = jnp.transpose(
                received[batch * members : (batch + 1) * members].reshape(lines, width)
            )

        def term_copy(which, index):
            target = (down_terms, gate_terms, linear_terms)[which]
            return pltpu.make_async_copy(
                terms[which].at[index], target.at[index], terms_sem.at[which, index]
            )

        def weigh(which, turn):
            index = jnp.bitwise_xor(lax.axis_index("dp"), shares - 1 - turn)
            part = pl.ds(pl.multiple_of(index * share, share), share)
            if which == 0:
                value = dot_tn(hidden[:, part], scaled[...])
            else:
                value = dot(rows_t[...], (gate_low if which == 1 else linear_low)[:, part])
            terms[which][index] = value.astype(jnp.bfloat16)
            term_copy(which, index).start()
            return index

        index = weigh(0, 0)
        first = pltpu.make_async_remote_copy(
            src_ref=terms[0].at[index],
            dst_ref=first_ref,
            send_sem=first_send,
            recv_sem=first_recv,
            device_id=peer_at(1, 0, 0),
            device_id_type=pl.DeviceIdType.MESH,
        )
        first.start()

        def weigh_rest(turn, carry):
            weigh(1, turn)
            weigh(2, turn)

            @pl.when(turn > 0)
            def _():
                weigh(0, turn)

            return carry

        lax.fori_loop(0, shares, weigh_rest, 0)
        for which in range(3):
            for index in range(shares):
                term_copy(which, index).wait()
        for copy in going:
            copy.wait()
        first.wait()

    low, full = jnp.bfloat16, jnp.float32
    columns, lines = (shares, width, share), (shares, share, width)
    any_space = pl.BlockSpec(memory_space=pl.ANY)
    in_vmem = pl.BlockSpec(memory_space=pltpu.VMEM)
    return pl.pallas_call(
        kernel,
        out_shape=[
            jax.ShapeDtypeStruct(outgoing.shape, low),
            jax.ShapeDtypeStruct(outgoing.shape, low),
            jax.ShapeDtypeStruct(gates.shape, full),
            jax.ShapeDtypeStruct(columns, low),
            jax.ShapeDtypeStruct(columns, low),
            jax.ShapeDtypeStruct(lines, low),
            jax.ShapeDtypeStruct(lines[1:], low),
        ],
        in_specs=[any_space, in_vmem] + [any_space] * 4,
        out_specs=[any_space] * 7,
        scratch_shapes=[
            pltpu.VMEM(outgoing.shape, low),
            pltpu.VMEM(gates.shape, full),
            pltpu.VMEM((width, hidden_units), low),
            pltpu.VMEM((width, hidden_units), low),
            pltpu.VMEM((hidden_units, width), low),
            pltpu.VMEM((rows, hidden_units), full),
            pltpu.VMEM((rows, hidden_units), low),
            pltpu.VMEM((rows, hidden_units), low),
            pltpu.VMEM((rows, hidden_units), low),
            pltpu.VMEM((width, rows), low),
            pltpu.VMEM((rows, width), low),
            pltpu.VMEM((rows, 128), full),
            pltpu.VMEM((rows, width), full),
            pltpu.VMEM((rows, width), full),
            pltpu.VMEM(outgoing.shape, low),
            pltpu.VMEM(gates.shape, full),
            [pltpu.VMEM(lines, low), pltpu.VMEM(columns, low), pltpu.VMEM(columns, low)],
            pltpu.SemaphoreType.DMA((3,)),
            pltpu.SemaphoreType.DMA((4, count)),
            pltpu.SemaphoreType.DMA((4, count)),
            pltpu.SemaphoreType.DMA((4,)),
            pltpu.SemaphoreType.DMA((3, shares)),
            pltpu.SemaphoreType.DMA,
            pltpu.SemaphoreType.DMA,
            pltpu.VMEM((rows, width), low),
            pltpu.VMEM(outgoing.shape, low),
            pltpu.SemaphoreType.DMA((3,)),
        ],
        compiler_params=pltpu.CompilerParams(
            collective_id=1, has_side_effects=True, vmem_limit_bytes=60 * 2**20
        ),
        cost_estimate=pl.CostEstimate(
            flops=18 * rows * width * hidden_units,
            bytes_accessed=12 * width * hidden_units + 12 * rows * width,
            transcendentals=rows * hidden_units,
        ),
        name="experts",
    )(outgoing, gates, grads, *weights)


def rope_tables(row_count):
    half = HEAD_DIM // 2
    frequency = np.exp(
        np.arange(half, dtype=np.float32) * np.float32(-2.0 * math.log(10000.0) / HEAD_DIM)
    ).astype(np.float32)
    angles = np.arange(row_count, dtype=np.float32)[:, None] * frequency[None, :]
    cosine, sine = np.cos(angles).astype(np.float32), np.sin(angles).astype(np.float32)
    return (
        np.concatenate([cosine] * 4, axis=1),
        np.concatenate([-sine, sine, -sine, sine], axis=1),
    )


def rotate(values, cosine, sine):
    lane = lax.broadcasted_iota(jnp.int32, cosine.shape, 1)
    leading = jnp.bitwise_and(lane, HEAD_DIM - 1) < HEAD_DIM // 2
    parts = []
    for begin in range(0, values.shape[1], 128):
        part = values[:, begin : begin + 128]
        ahead = pltpu.roll(part, 128 - HEAD_DIM // 2, 1)
        behind = pltpu.roll(part, HEAD_DIM // 2, 1)
        parts.append(part * cosine + jnp.where(leading, ahead, behind) * sine)
    return jnp.concatenate(parts, axis=1)


def inverse_norm(values):
    return lax.rsqrt(jnp.mean(values * values, axis=1, keepdims=True) + EPSILON)


def head_masks(rows):
    first = lax.broadcasted_iota(jnp.int32, (rows, 128), 1) < HEAD_DIM
    return first, jnp.logical_not(first)


def start_of(positions, starts):
    first = jnp.zeros_like(positions)
    for index in range(starts.shape[1]):
        begin = starts[0, index]
        first = jnp.where(begin <= positions, jnp.maximum(first, begin), first)
    return first


def gather_steps(size):
    bits, held, steps = [], [0], []
    bit = size // 2
    while bit >= 1:
        steps.append((bit, list(held)))
        held = held + [place ^ bit for place in held]
        bit //= 2
    return steps


def peer_at(deep, far, near):
    return {
        "dp": jnp.bitwise_xor(lax.axis_index("dp"), deep),
        "exp": jnp.bitwise_xor(lax.axis_index("exp"), far),
        "ctx": jnp.bitwise_xor(lax.axis_index("ctx"), near),
    }


def peer(far, near):
    return peer_at(0, far, near)


def greet_places(places):
    barrier = pltpu.get_barrier_semaphore()
    for place in places:
        pl.semaphore_signal(
            barrier, inc=1, device_id=peer_at(*place), device_id_type=pl.DeviceIdType.MESH
        )
    pl.semaphore_wait(barrier, len(places))


def greet_all(places):
    greet_places([(0,) + place for place in places])


def group_places(ranks):
    return [
        (shift // ranks[1], shift % ranks[1] * ranks[2]) for shift in range(1, ranks[0] * ranks[1])
    ]


def ring_places(size):
    return [(0, bit) for bit, _ in gather_steps(size)]


def places_of(ranks, size):
    places = group_places(ranks)
    return places + [place for place in ring_places(size) if place not in places]


class Gather:
    def __init__(self, buffers, size, send_sem, recv_sem, sources=None):
        self.buffers, self.sources = buffers, sources
        self.send_sem, self.recv_sem = send_sem, recv_sem
        self.steps = gather_steps(size)

    def copy(self, place, bit, index):
        block = jnp.bitwise_xor(lax.axis_index("ctx"), place)
        buffer = self.buffers[index]
        straight = self.sources is not None and place == 0
        return pltpu.make_async_remote_copy(
            src_ref=self.sources[index] if straight else buffer.at[block],
            dst_ref=buffer.at[block],
            send_sem=self.send_sem.at[index, place ^ bit],
            recv_sem=self.recv_sem.at[index, place ^ bit],
            device_id=peer(0, bit),
            device_id_type=pl.DeviceIdType.MESH,
        )

    def forward(self, place):
        for bit, held in self.steps:
            if place in held:
                for index in range(len(self.buffers)):
                    self.copy(place, bit, index).start()

    def arrive(self, place):
        bit = place & -place
        for index in range(len(self.buffers)):
            self.copy(place ^ bit, bit, index).wait_recv()
        self.forward(place)

    def finish(self):
        for bit, held in self.steps:
            for place in held:
                for index in range(len(self.buffers)):
                    self.copy(place, bit, index).wait_send()


def fill_rows(pack, prior, router_ref, map_ref, first_ref, second_ref, vector_ref, previous_ref):
    full = jnp.float32
    experts = router_ref.shape[0]
    width = router_ref.shape[1]
    pack[0:experts, :] = router_ref[...].astype(full)
    for index in range(2):
        pack[experts + 2 * index : experts + 2 * index + 2, :] = map_ref[index].astype(full)
    pack[HEAD_ROWS : HEAD_ROWS + 1, :] = first_ref[...].astype(full).reshape(1, width)
    pack[HEAD_ROWS + 1 : HEAD_ROWS + 2, :] = second_ref[...].astype(full).reshape(1, width)
    pack[HEAD_ROWS + 2 : HEAD_ROWS + 4, :] = vector_ref[...].astype(full)
    for index in range(experts):
        prior[index : index + 1, :] = previous_ref[index]


def slot_targets(routes, ranks, cap):
    exchange_size, group_size, spread = ranks
    rows = routes.shape[1]
    experts = exchange_size * group_size
    expert = lax.broadcasted_iota(jnp.int32, (16, rows), 0)
    hits = [(expert == routes[k : k + 1]).astype(jnp.float32) for k in range(2)]
    before = lax.broadcasted_iota(jnp.int32, (rows, rows), 0) < lax.broadcasted_iota(
        jnp.int32, (rows, rows), 1
    )
    earlier = dot(
        (hits[0] + hits[1]).astype(jnp.bfloat16), before.astype(jnp.float32).astype(jnp.bfloat16)
    )
    targets = []
    for k in range(2):
        route = routes[k : k + 1]
        rank = jnp.sum(hits[k] * earlier, axis=0, keepdims=True)
        far = jnp.bitwise_xor(route // group_size, lax.axis_index("exp"))
        near = jnp.bitwise_xor(route % group_size, lax.axis_index("ctx") // spread)
        count = exchange_size * group_size
        block = jnp.bitwise_and(far * group_size + near + count - count // 4, count - 1)
        place = (block * cap).astype(jnp.float32)
        targets.append(jnp.where(route < experts, place + rank, -1.0))
    return targets


def attend_layer(
    tokens, cotangent, previous, routes, starts, weights, params, carry, ranks, cap, size
):
    rows, width = tokens.shape
    count = ranks[0] * ranks[1]
    slots = count * cap
    pairs = width // 128
    tables = rope_tables(size * rows)
    low, full = jnp.bfloat16, jnp.float32

    def kernel(
        tokens_hbm,
        cotangent_ref,
        previous_ref,
        routes_ref,
        starts_ref,
        query_hbm,
        key_hbm,
        value_hbm,
        output_hbm,
        router_ref,
        map_ref,
        first_ref,
        second_ref,
        vector_ref,
        carry_ref,
        cosine_hbm,
        sine_hbm,
        queries_out,
        keys_out,
        values_out,
        attended_out,
        lse_ref,
        middle_out,
        probs_ref,
        targets_ref,
        outgoing_ref,
        gates_ref,
        grads_ref,
        stream,
        queries,
        keys,
        values,
        query_w,
        key_w,
        value_w,
        output_w,
        cosine,
        sine,
        bias,
        totals,
        highest,
        slot_grads,
        load_sem,
        gather_send,
        gather_recv,
        grad_send,
        grad_recv,
        keep_sem,
        pack,
        prior,
        attended_ref,
        middle_ref,
    ):
        own = lax.axis_index("ctx")
        bring = pltpu.make_async_copy(tokens_hbm, stream.at[own], load_sem.at[6])
        bring.start()
        loads = [
            pltpu.make_async_copy(source, target, load_sem.at[index])
            for index, (source, target) in enumerate(
                (
                    (query_hbm, query_w),
                    (key_hbm, key_w),
                    (value_hbm, value_w),
                    (cosine_hbm, cosine),
                    (sine_hbm, sine),
                    (output_hbm, output_w),
                )
            )
        ]
        for load in loads:
            load.start()
        greet_all(places_of(ranks, size))
        gather = Gather([stream], size, gather_send, gather_recv, [tokens_hbm])
        gather.forward(0)

        fill_rows(
            pack, prior, router_ref, map_ref, first_ref, second_ref, vector_ref, previous_ref
        )
        targets = slot_targets(routes_ref[...], ranks, cap)
        slot = lax.broadcasted_iota(jnp.int32, (slots, rows), 0).astype(full)
        picked = jnp.logical_or(slot == targets[0], slot == targets[1])
        picked = picked.astype(full).astype(low)
        slot_grads[...] = dot(picked, cotangent_ref[...]).astype(low).reshape(count, cap, width)
        grad_copies = [
            send_block(slot_grads, grads_ref, block, ranks, grad_send, grad_recv)
            for block in other_blocks(count)
        ]
        grad_copies.append(keep_block(slot_grads, grads_ref, count, keep_sem.at[0]))

        bring.wait()
        for load in loads[:5]:
            load.wait()
        gain = pack[HEAD_ROWS : HEAD_ROWS + 1, :]

        def project(block, wanted):
            line = pl.ds(pl.multiple_of(block * rows, rows), rows)
            values_in = stream[block].astype(full)
            normed = (values_in * inverse_norm(values_in) * gain).astype(low)
            if "q" in wanted:
                turned = rotate(dot(normed, query_w[...]), cosine[line, :], sine[line, :])
                queries[block] = (turned.astype(low).astype(full) * HEAD_DIM**-0.5).astype(low)
            if "k" in wanted:
                turned = rotate(dot(normed, key_w[...]), cosine[line, :], sine[line, :])
                keys[block] = turned.astype(low)
                values[block] = dot(normed, value_w[...]).astype(low)

        masks = head_masks(rows)
        query_pos = own * rows + lax.broadcasted_iota(jnp.int32, (rows, rows), 1)
        document_start = start_of(query_pos[0:8], starts_ref)[0:1]

        def attend(block):
            key_pos = block * rows + lax.broadcasted_iota(jnp.int32, (rows, rows), 0)
            allowed = jnp.logical_and(key_pos >= document_start, key_pos <= query_pos)
            bias[...] = jnp.where(allowed, 0.0, NEGATIVE)

            def pair(index, carried):
                lanes = pl.ds(pl.multiple_of(index * 128, 128), 128)
                query, key, value = queries[own, :, lanes], keys[block, :, lanes], values[block, :, lanes]
                scores = [dot_nt(jnp.where(mask, key, 0), query) + bias[...] for mask in masks]
                old = [highest[index, head][0:1, :] for head in range(2)]
                new = [
                    jnp.maximum(old[head], jnp.max(scores[head], axis=0, keepdims=True))
                    for head in range(2)
                ]
                weight = [jnp.exp(scores[head] - new[head]).astype(low) for head in range(2)]
                for head in range(2):
                    totals[index, head] = totals[index, head] * jnp.exp(old[head] - new[head]) + dot_tn(
                        jnp.where(masks[head], value, 1), weight[head]
                    )
                    highest[index, head] = jnp.broadcast_to(new[head], (8, rows))
                return carried

            lax.fori_loop(0, pairs, pair, 0)

        totals[...] = jnp.zeros_like(totals)
        highest[...] = jnp.full(highest.shape, NEGATIVE, full)
        project(own, "qk")
        attend(own)
        def others(place, carried):
            for one in range(1, size):

                @pl.when(place == one)
                def _():
                    gather.arrive(one)
                    if one == size // 2:
                        for copy in grad_copies:
                            copy.start()

            block = jnp.bitwise_xor(own, place)

            @pl.when(block < own)
            def _():
                project(block, "k")
                attend(block)

            @pl.when(block > own)
            def _():
                project(block, "q")

            return carried

        lax.fori_loop(1, size, others, 0)
        keep = [
            pltpu.make_async_copy(source, target, keep_sem.at[index + 1])
            for index, (source, target) in enumerate(
                ((queries, queries_out), (keys, keys_out), (values, values_out))
            )
        ]
        for copy in keep:
            copy.start()

        lse_ref[...] = jnp.zeros_like(lse_ref)
        upper = lax.broadcasted_iota(jnp.int32, (128, rows), 0) < HEAD_DIM
        for index in range(pairs):
            halves = []
            for head in range(2):
                total = totals[index, head]
                line = HEAD_DIM if head == 0 else 0
                weight_sum = total[line : line + 1, :]
                halves.append(total / weight_sum)
                lse_ref[2 * index + head : 2 * index + head + 1, :] = highest[index, head][
                    0:1, :
                ] + jnp.log(weight_sum)
            attended_ref[:, index * 128 : index * 128 + 128] = jnp.transpose(
                jnp.where(upper, halves[0], halves[1])
            )
        keep.append(pltpu.make_async_copy(attended_ref, attended_out, keep_sem.at[4]))
        keep[-1].start()
        loads[5].wait()
        middle = stream[own].astype(full) + dot(attended_ref[...].astype(low), output_w[...])
        middle_ref[...] = middle
        keep.append(pltpu.make_async_copy(middle_ref, middle_out, keep_sem.at[5]))
        keep[-1].start()
        second = (
            middle
            * inverse_norm(middle)
            * pack[HEAD_ROWS + 1 : HEAD_ROWS + 2, :]
        )
        second_low = second.astype(low)
        outgoing_ref[...] = dot(picked, second_low).astype(low).reshape(count, cap, width)

        experts = previous_ref.shape[0]
        logits = dot_nt(second_low, pack[0:HEAD_ROWS, :].astype(low))[:, 0:experts] + lax.dot_general(
            prior[0:experts, :],
            carry_ref[...].astype(full),
            (((0,), (0,)), ((), ())),
            precision=HIGH,
        )
        logits = logits - jnp.max(logits, axis=1, keepdims=True)
        powers = jnp.exp(logits)
        probs_ref[...] = jnp.zeros_like(probs_ref)
        probs_ref[:, 0:experts] = powers / jnp.sum(powers, axis=1, keepdims=True)
        turned = jnp.transpose(probs_ref[...])[0:16]
        expert = lax.broadcasted_iota(jnp.int32, (16, rows), 0)
        weighted = jnp.zeros((slots, rows), full)
        for k in range(2):
            route = routes_ref[k : k + 1, :]
            gate = jnp.sum(jnp.where(expert == route, turned, 0.0), axis=0, keepdims=True)
            weighted = jnp.where(slot == targets[k], gate, weighted)
        gate_column = jnp.sum(weighted, axis=1, keepdims=True)
        for shift in range(count):
            column = jnp.broadcast_to(gate_column[shift * cap : (shift + 1) * cap], (cap, 128))
            gates_ref[shift] = jnp.zeros((8, 128), full)
            gates_ref[shift, :, 0:cap] = jnp.transpose(column)[0:8, :]
        pad = jnp.zeros((6, rows), full)
        target_rows = jnp.concatenate([targets[0], targets[1], pad], axis=0)
        target_rows = jnp.concatenate([target_rows] + [jnp.zeros((120, rows), full)], axis=0)
        targets_ref[...] = jnp.transpose(target_rows)

        gather.finish()
        for copy in keep + grad_copies:
            copy.wait()

    stream_shape = (size, rows, width)
    any_space = pl.BlockSpec(memory_space=pl.ANY)
    in_vmem = pl.BlockSpec(memory_space=pltpu.VMEM)
    square = (width, width)
    return pl.pallas_call(
        kernel,
        out_shape=[
            jax.ShapeDtypeStruct(stream_shape, low),
            jax.ShapeDtypeStruct(stream_shape, low),
            jax.ShapeDtypeStruct(stream_shape, low),
            jax.ShapeDtypeStruct((rows, width), full),
            jax.ShapeDtypeStruct((16, rows), full),
            jax.ShapeDtypeStruct((rows, width), full),
            jax.ShapeDtypeStruct((rows, 128), full),
            jax.ShapeDtypeStruct((rows, 128), full),
            jax.ShapeDtypeStruct((count, cap, width), low),
            jax.ShapeDtypeStruct((count, 8, 128), full),
            jax.ShapeDtypeStruct((count, cap, width), low),
        ],
        in_specs=[any_space]
        + [in_vmem] * 3
        + [pl.BlockSpec(memory_space=pltpu.SMEM)]
        + [any_space] * 4
        + [in_vmem] * 6
        + [any_space] * 2,
        out_specs=[any_space] * 4
        + [in_vmem, any_space]
        + [in_vmem] * 4
        + [any_space],
        scratch_shapes=[
            pltpu.VMEM(stream_shape, low),
            pltpu.VMEM(stream_shape, low),
            pltpu.VMEM(stream_shape, low),
            pltpu.VMEM(stream_shape, low),
            pltpu.VMEM(square, low),
            pltpu.VMEM(square, low),
            pltpu.VMEM(square, low),
            pltpu.VMEM(square, low),
            pltpu.VMEM((size * rows, 128), full),
            pltpu.VMEM((size * rows, 128), full),
            pltpu.VMEM((rows, rows), full),
            pltpu.VMEM((pairs, 2, 128, rows), full),
            pltpu.VMEM((pairs, 2, 8, rows), full),
            pltpu.VMEM((count, cap, width), low),
            pltpu.SemaphoreType.DMA((7,)),
            pltpu.SemaphoreType.DMA((1, size)),
            pltpu.SemaphoreType.DMA((1, size)),
            pltpu.SemaphoreType.DMA((count,)),
            pltpu.SemaphoreType.DMA((count,)),
            pltpu.SemaphoreType.DMA((6,)),
            pltpu.VMEM((24, width), full),
            pltpu.VMEM((16, rows), full),
            pltpu.VMEM((rows, width), full),
            pltpu.VMEM((rows, width), full),
        ],
        compiler_params=pltpu.CompilerParams(
            collective_id=0, has_side_effects=True, vmem_limit_bytes=60 * 2**20
        ),
        cost_estimate=pl.CostEstimate(
            flops=2 * size * rows * width * width * 3 + 16 * size * rows * rows * width,
            bytes_accessed=20 * 2**20,
            transcendentals=size * rows * rows * 12,
        ),
        name="attend",
    )(
        tokens,
        cotangent,
        previous,
        routes,
        starts,
        *weights,
        *params,
        carry,
        jnp.asarray(tables[0]),
        jnp.asarray(tables[1]),
    )


def add_into(target, source):
    rows = target.shape[0]
    piece = 96 if rows % 96 == 0 else (64 if rows % 64 == 0 else rows)

    def body(index, carried):
        part = pl.ds(pl.multiple_of(index * piece, piece), piece)
        total = target[part, :].astype(jnp.float32) + source[part, :].astype(jnp.float32)
        target[part, :] = total.astype(target.dtype)
        return carried

    lax.fori_loop(0, rows // piece, body, 0)


def column_of(values, index):
    return values[:, index : index + 1]


def backward_layer(
    tokens,
    cotangent,
    previous,
    routes,
    starts,
    forward,
    returns,
    weights,
    params,
    terms,
    first,
    ranks,
    cap,
    size,
    shares,
):
    rows, width = tokens.shape
    count = ranks[0] * ranks[1]
    slots = count * cap
    pairs = width // 128
    tables = rope_tables(size * rows)
    low, full = jnp.bfloat16, jnp.float32
    experts = previous.shape[0]
    copy_index = count + 1
    stat_rows = 16
    kinds = len(terms)

    def kernel(
        tokens_ref,
        cotangent_hbm,
        previous_ref,
        routes_ref,
        starts_ref,
        attended_hbm,
        lse_ref,
        middle_hbm,
        probs_ref,
        targets_ref,
        queries_hbm,
        keys_hbm,
        values_hbm,
        back_hbm,
        produced_hbm,
        dots_ref,
        query_hbm,
        key_hbm,
        value_hbm,
        output_hbm,
        router_ref,
        map_ref,
        first_gain_ref,
        second_gain_ref,
        vector_ref,
        cosine_hbm,
        sine_hbm,
        *rest,
    ):
        term_refs, first_hbm, rest = rest[:kinds], rest[kinds], rest[kinds + 1 :]
        result_out, token_grads_out, wide_out, small_ref = rest[:4]
        first_refs, rest = rest[4 : 4 + kinds], rest[4 + kinds :]
        (
            queries,
            keys,
            values,
            query_w,
            key_w,
            value_w,
            output_w,
            cosine,
            sine,
            bias,
            out_grads,
            stats,
            outputs,
            middle_grad,
            query_total,
            key_total,
            value_total,
            load_sem,
            gather_send,
            gather_recv,
            first_send,
            first_recv,
            out_send,
            out_recv,
            out_keep,
            sum_part,
            first_part,
            sum_load,
            pack,
            prior,
            cotangent_ref,
            attended_ref,
            middle_ref,
            back_ref,
            result_ref,
            token_grads_ref,
            wide_ref,
            near_sem,
        ) = rest
        own = lax.axis_index("ctx")
        line = pl.ds(pl.multiple_of(own * rows, rows), rows)
        loads = [
            pltpu.make_async_copy(source, target, load_sem.at[index])
            for index, (source, target) in enumerate(
                (
                    (output_hbm, output_w),
                    (queries_hbm, queries),
                    (keys_hbm, keys),
                    (values_hbm, values),
                    (cosine_hbm.at[line], cosine),
                    (sine_hbm.at[line], sine),
                    (query_hbm, query_w),
                    (key_hbm, key_w),
                    (value_hbm, value_w),
                )
            )
        ]
        share = lax.axis_index("dp")
        near_loads = [
            pltpu.make_async_copy(source, target, near_sem.at[index])
            for index, (source, target) in enumerate(
                (
                    (cotangent_hbm, cotangent_ref),
                    (attended_hbm, attended_ref),
                    (middle_hbm, middle_ref),
                    (back_hbm, back_ref),
                )
            )
        ]
        sum_loads = [
            pltpu.make_async_copy(
                term_refs[0].at[jnp.bitwise_xor(share, shares - 2)], sum_part, sum_load.at[0]
            ),
            pltpu.make_async_copy(first_hbm, first_part, sum_load.at[1]),
        ]
        for copy in sum_loads + near_loads:
            copy.start()
        greet_places(
            [(0,) + place for place in places_of(ranks, size)] + [(1, 0, 0), (2, 0, 0)]
        )
        first_copies = [
            pltpu.make_async_remote_copy(
                src_ref=(
                    term_refs[kind].at[jnp.bitwise_xor(share, shares - 1)] if kind else sum_part
                ),
                dst_ref=first_refs[kind],
                send_sem=first_send.at[kind],
                recv_sem=first_recv.at[kind],
                device_id=peer_at(1 if kind else 2, 0, 0),
                device_id_type=pl.DeviceIdType.MESH,
            )
            for kind in range(kinds)
        ]
        for copy in first_copies[1:]:
            copy.start()
        for copy in sum_loads:
            copy.wait()
        add_into(sum_part, first_part)
        first_copies[0].start()
        for load in loads:
            load.start()
        for load in near_loads:
            load.wait()
        output_copies = [
            send_block(produced_hbm, outputs, block, ranks, out_send, out_recv)
            for block in other_blocks(count)
        ]
        output_copies.append(keep_block(produced_hbm, outputs, count, out_keep))

        def keep_wide(index, value):
            half = width // 2
            for part in range(2):
                wide_ref[part, index * width : (index + 1) * width, :] = value[
                    :, part * half : (part + 1) * half
                ].astype(low)

        fill_rows(
            pack,
            prior,
            router_ref,
            map_ref,
            first_gain_ref,
            second_gain_ref,
            vector_ref,
            previous_ref,
        )
        lane = lax.broadcasted_iota(jnp.int32, (rows, 128), 1)
        upstream = cotangent_ref[...].astype(full)
        middle = middle_ref[...]
        inverse_second = inverse_norm(middle)
        unit_second = middle * inverse_second
        gain_second = pack[HEAD_ROWS + 1 : HEAD_ROWS + 2, :]
        second = unit_second * gain_second
        second_low = second.astype(low)
        heads_in = jnp.concatenate(
            [pack[0:HEAD_ROWS, :].astype(low), jnp.zeros((128 - HEAD_ROWS, width), low)], axis=0
        )
        mixed = dot_nt(second_low, heads_in)
        probs = probs_ref[...]
        route_rows = jnp.concatenate(
            [routes_ref[...].astype(full), jnp.zeros((126, rows), full)], axis=0
        )
        route_columns = jnp.transpose(route_rows).astype(jnp.int32)
        route = [column_of(route_columns, k) for k in range(2)]
        chosen = jnp.logical_or(lane == route[0], lane == route[1])
        gates = jnp.where(chosen, probs, 0.0)
        target = [column_of(targets_ref[...], k) for k in range(2)]

        gate_grad = jnp.zeros((rows, 128), full)
        place = lane.astype(full)
        for k in range(2):
            found = jnp.zeros((rows, 128), full)
            for shift in range(count):
                found = found + jnp.where(
                    jnp.logical_and(target[k] - shift * cap == place, lane < cap),
                    dots_ref[shift, 0:1, :],
                    0.0,
                )
            gate_grad = gate_grad + jnp.where(
                lane == route[k], jnp.sum(found, axis=1, keepdims=True), 0.0
            )
        copy_grad = jnp.sum(upstream * second, axis=1, keepdims=True)
        gate_grad = jnp.where(lane == copy_index, copy_grad, gate_grad)
        direct = column_of(gates, copy_index)
        constants = []
        for index in range(2):
            vector = pack[HEAD_ROWS + 2 + index : HEAD_ROWS + 3 + index, :]
            vector_dot = jnp.sum(upstream * vector, axis=1, keepdims=True)
            begin = experts + 2 * index
            spread_of = column_of(mixed, begin + 1) - column_of(mixed, begin)
            mixing = (1.0 / (1.0 + jnp.exp(spread_of)), 1.0 / (1.0 + jnp.exp(-spread_of)))
            gate = column_of(gates, copy_index + 1 + index)
            term = mixing[0] * copy_grad + mixing[1] * vector_dot
            gate_grad = jnp.where(lane == copy_index + 1 + index, term, gate_grad)
            direct = direct + gate * mixing[0]
            constants.append((gate, mixing, vector, vector_dot))
        prob_grad = jnp.where(chosen, gate_grad, 0.0)
        logit_grad = probs * (prob_grad - jnp.sum(probs * prob_grad, axis=1, keepdims=True))
        head_grad = logit_grad
        for index, (gate, mixing, vector, vector_dot) in enumerate(constants):
            mixing_grad = (gate * copy_grad, gate * vector_dot)
            mean = mixing[0] * mixing_grad[0] + mixing[1] * mixing_grad[1]
            for part in range(2):
                head_grad = jnp.where(
                    lane == experts + 2 * index + part,
                    mixing[part] * (mixing_grad[part] - mean),
                    head_grad,
                )
        head_low = head_grad.astype(low)

        slot = lax.broadcasted_iota(jnp.int32, (rows, slots), 1).astype(full)
        picked = [(slot == target[k]).astype(full).astype(low) for k in range(2)]
        second_grad = (
            dot(head_low, heads_in) + direct * upstream + dot(picked[0] + picked[1], back_ref[...])
        )
        normal_grad = second_grad * gain_second
        middle_total = upstream + inverse_second * (
            normal_grad - unit_second * jnp.mean(normal_grad * unit_second, axis=1, keepdims=True)
        )
        middle_grad[...] = middle_total
        middle_low = middle_total.astype(low)
        loads[0].wait()
        out_grad = dot_nt(middle_low, output_w[...]).astype(low)
        out_grads[own] = out_grad
        product = out_grad.astype(full) * attended_ref[...]
        masks = head_masks(rows)
        deltas = jnp.zeros((rows, 128), full)
        for index in range(pairs):
            part = product[:, index * 128 : index * 128 + 128]
            for head in range(2):
                total = jnp.sum(jnp.where(masks[head], part, 0.0), axis=1, keepdims=True)
                deltas = jnp.where(lane == 2 * index + head, total, deltas)
        stats[own, 0:stat_rows] = lse_ref[...]
        stats[own, stat_rows:] = jnp.transpose(deltas)[0:stat_rows]
        gather = Gather([out_grads, stats], size, gather_send, gather_recv)
        gather.forward(0)
        for copy in output_copies:
            copy.start()

        chosen_out = second * direct
        for gate, mixing, vector, vector_dot in constants:
            chosen_out = chosen_out + gate * mixing[1] * vector
        base = middle + chosen_out
        small_ref[...] = jnp.zeros_like(small_ref)
        small_ref[1:2, :] = jnp.sum(second_grad * unit_second, axis=0, keepdims=True)
        for index, (gate, mixing, vector, vector_dot) in enumerate(constants):
            small_ref[2 + index : 3 + index, :] = jnp.sum(
                gate * mixing[1] * upstream, axis=0, keepdims=True
            )
        small_ref[8:24, :] = dot_tn(head_low, second_low)[0:16]
        carry_grad = lax.dot_general(
            jnp.transpose(logit_grad)[0:16],
            prior[0:experts, :],
            (((1,), (1,)), ((), ())),
            precision=HIGH,
        )
        small_ref[24:40, 0:experts] = carry_grad
        keep_wide(3, dot_tn(attended_ref[...].astype(low), middle_low))
        keeps = [
            pltpu.make_async_copy(
                wide_ref.at[:, pl.ds(3 * width, width)],
                wide_out.at[:, pl.ds(3 * width, width)],
                near_sem.at[4],
            )
        ]
        keeps[0].start()

        for load in loads[1:4]:
            load.wait()
        query_total[...] = jnp.zeros_like(query_total)
        key_total[...] = jnp.zeros_like(key_total)
        value_total[...] = jnp.zeros_like(value_total)
        column = lax.broadcasted_iota(jnp.int32, (rows, rows), 0)
        row = lax.broadcasted_iota(jnp.int32, (rows, rows), 1)

        def block_side(block, as_query, as_key):
            key_block, query_block = (own if as_key else block), (own if as_query else block)
            key_pos, query_pos = key_block * rows + column, query_block * rows + row
            first = start_of(query_pos[0:8], starts_ref)[0:1]
            allowed = jnp.logical_and(key_pos >= first, key_pos <= query_pos)
            bias[...] = jnp.where(allowed, 0.0, NEGATIVE)

            def pair(index, carried):
                lanes = pl.ds(pl.multiple_of(index * 128, 128), 128)
                query, grad = queries[query_block, :, lanes], out_grads[query_block, :, lanes]
                key, value = keys[key_block, :, lanes], values[key_block, :, lanes]
                one_key = [jnp.where(mask, key, 0) for mask in masks]
                scores = [dot_nt(one_key[head], query) for head in range(2)]
                weight_grad = [dot_nt(jnp.where(mask, value, 0), grad) for mask in masks]
                weight, score = [], []
                for head in range(2):
                    lse = stats[query_block, pl.ds(2 * index + head, 1), :]
                    mean = stats[query_block, pl.ds(stat_rows + 2 * index + head, 1), :]
                    weight.append(jnp.exp(scores[head] + bias[...] - lse))
                    score.append((weight[head] * (weight_grad[head] - mean)).astype(low))
                if as_key:
                    value_total[:, lanes] += dot(
                        weight[0].astype(low), jnp.where(masks[0], grad, 0)
                    ) + dot(weight[1].astype(low), jnp.where(masks[1], grad, 0))
                    key_total[:, lanes] += dot(score[0], jnp.where(masks[0], query, 0)) + dot(
                        score[1], jnp.where(masks[1], query, 0)
                    )
                if as_query:
                    query_total[lanes, :] += dot_tn(one_key[0], score[0]) + dot_tn(
                        one_key[1], score[1]
                    )
                return carried

            lax.fori_loop(0, pairs, pair, 0)

        block_side(own, True, True)
        def earlier(place, carried):
            block = jnp.bitwise_xor(own, place)

            @pl.when(block < own)
            def _():
                block_side(block, True, False)

            return carried

        def later(place, carried):
            for one in range(1, size):

                @pl.when(place == one)
                def _():
                    gather.arrive(one)

            block = jnp.bitwise_xor(own, place)

            @pl.when(block > own)
            def _():
                block_side(block, False, True)

            return carried

        lax.fori_loop(1, size, earlier, 0)
        lax.fori_loop(1, size, later, 0)
        for load in loads[4:]:
            load.wait()
        inputs = tokens_ref[...].astype(full)
        inverse_first = inverse_norm(inputs)
        unit_first = inputs * inverse_first
        gain_first = pack[HEAD_ROWS : HEAD_ROWS + 1, :]
        normed = (unit_first * gain_first).astype(low)
        turn = -sine[...]
        query_grad = jnp.transpose(query_total[...]) * HEAD_DIM**-0.5
        query_low = rotate(query_grad, cosine[...], turn).astype(low)
        key_low = rotate(key_total[...], cosine[...], turn).astype(low)
        value_low = value_total[...].astype(low)
        first_grad = (
            dot_nt(query_low, query_w[...])
            + dot_nt(key_low, key_w[...])
            + dot_nt(value_low, value_w[...])
        )
        for index, part in enumerate((query_low, key_low, value_low)):
            keep_wide(index, dot_tn(normed, part))
        keeps.append(
            pltpu.make_async_copy(
                wide_ref.at[:, pl.ds(0, 3 * width)],
                wide_out.at[:, pl.ds(0, 3 * width)],
                near_sem.at[5],
            )
        )
        keeps[-1].start()
        small_ref[0:1, :] = jnp.sum(first_grad * unit_first, axis=0, keepdims=True)
        normal_grad = first_grad * gain_first
        token_grads_ref[...] = middle_grad[...] + inverse_first * (
            normal_grad - unit_first * jnp.mean(normal_grad * unit_first, axis=1, keepdims=True)
        )
        keeps.append(pltpu.make_async_copy(token_grads_ref, token_grads_out, near_sem.at[6]))
        keeps[-1].start()
        for copy in output_copies:
            copy.wait()
        for k in range(2):
            weight = jnp.sum(jnp.where(lane == route[k], probs, 0.0), axis=1, keepdims=True)
            base = base + weight * dot(picked[k], outputs[...].reshape(slots, width))
        result_ref[...] = base.astype(low)
        keeps.append(pltpu.make_async_copy(result_ref, result_out, near_sem.at[7]))
        keeps[-1].start()
        gather.finish()
        for copy in first_copies + keeps:
            copy.wait()

    stream_shape = (size, rows, width)
    any_space = pl.BlockSpec(memory_space=pl.ANY)
    in_vmem = pl.BlockSpec(memory_space=pltpu.VMEM)
    square = (width, width)
    return pl.pallas_call(
        kernel,
        out_shape=[
            jax.ShapeDtypeStruct((rows, width), low),
            jax.ShapeDtypeStruct((rows, width), full),
            jax.ShapeDtypeStruct((2, 4 * width, width // 2), low),
            jax.ShapeDtypeStruct((64, width), full),
        ]
        + [jax.ShapeDtypeStruct(term.shape[1:], low) for term in terms],
        in_specs=[in_vmem, any_space, in_vmem, in_vmem]
        + [pl.BlockSpec(memory_space=pltpu.SMEM)]
        + [any_space, in_vmem, any_space, in_vmem, in_vmem]
        + [any_space] * 3
        + [any_space, any_space, in_vmem]
        + [any_space] * 4
        + [in_vmem] * 5
        + [any_space] * (3 + kinds),
        out_specs=[any_space] * 3 + [in_vmem] + [any_space] * kinds,
        scratch_shapes=[
            pltpu.VMEM(stream_shape, low),
            pltpu.VMEM(stream_shape, low),
            pltpu.VMEM(stream_shape, low),
            pltpu.VMEM(square, low),
            pltpu.VMEM(square, low),
            pltpu.VMEM(square, low),
            pltpu.VMEM(square, low),
            pltpu.VMEM((rows, 128), full),
            pltpu.VMEM((rows, 128), full),
            pltpu.VMEM((rows, rows), full),
            pltpu.VMEM(stream_shape, low),
            pltpu.VMEM((size, 2 * stat_rows, rows), full),
            pltpu.VMEM((count, cap, width), low),
            pltpu.VMEM((rows, width), full),
            pltpu.VMEM((width, rows), full),
            pltpu.VMEM((rows, width), full),
            pltpu.VMEM((rows, width), full),
            pltpu.SemaphoreType.DMA((9,)),
            pltpu.SemaphoreType.DMA((2, size)),
            pltpu.SemaphoreType.DMA((2, size)),
            pltpu.SemaphoreType.DMA((kinds,)),
            pltpu.SemaphoreType.DMA((kinds,)),
            pltpu.SemaphoreType.DMA((count,)),
            pltpu.SemaphoreType.DMA((count,)),
            pltpu.SemaphoreType.DMA,
            pltpu.VMEM(terms[0].shape[1:], low),
            pltpu.VMEM(terms[0].shape[1:], low),
            pltpu.SemaphoreType.DMA((2,)),
            pltpu.VMEM((24, width), full),
            pltpu.VMEM((16, rows), full),
            pltpu.VMEM((rows, width), low),
            pltpu.VMEM((rows, width), full),
            pltpu.VMEM((rows, width), full),
            pltpu.VMEM((slots, width), low),
            pltpu.VMEM((rows, width), low),
            pltpu.VMEM((rows, width), full),
            pltpu.VMEM((2, 4 * width, width // 2), low),
            pltpu.SemaphoreType.DMA((8,)),
        ],
        compiler_params=pltpu.CompilerParams(
            collective_id=2, has_side_effects=True, vmem_limit_bytes=60 * 2**20
        ),
        cost_estimate=pl.CostEstimate(
            flops=14 * rows * width * width * 2 + 20 * size * rows * rows * width,
            bytes_accessed=30 * 2**20,
            transcendentals=size * rows * rows * 12,
        ),
        name="backward",
    )(
        tokens,
        cotangent,
        previous,
        routes,
        starts,
        *forward,
        *returns,
        *weights,
        *params,
        jnp.asarray(tables[0]),
        jnp.asarray(tables[1]),
        *terms,
        first,
    )


PIECES = 4
ORDER = (
    5, 10, 7, 0, 1, 6, 5, 0, 7, 0, 10, 1, 10, 0, 5,
    4, 2, 6, 0, 5, 7, 4, 0, 4, 3, 6, 10, 2, 0, 6,
    3, 0, 4, 8, 6, 2, 0, 9, 10, 8, 5, 5, 12, 1, 1,
    9, 8, 7, 11, 12, 12, 2, 1, 9, 0, 8, 9, 12, 11, 4,
    7, 11, 8, 11, 12, 9, 8, 0, 6, 3, 3, 12, 11, 7, 2,
    10, 11, 9, 3,
)
DENSE_TIMES = (7, 24, 34, 48, 62, 77, 91, 101, 118, 125, 132)
EXPERT_TIMES = (19, 14, 19, 4, 11, 2)


def halving_steps(size):
    steps, step = [], 0
    while 1 << step < size:
        bit = 1 << step
        steps += [(step, place) for place in range(size - bit, 0, -2 * bit)]
        step += 1
    return steps


def needed_before(step, place):
    return {(earlier, place | 1 << earlier) for earlier in range(step)}


def reduce_layer(terms, firsts, wide, small, spread, shares, ring, exchange_size):
    low, full = jnp.bfloat16, jnp.float32
    steps = halving_steps(shares)
    done = [[(0, shares - 1), (1, shares - 2)]] + [[(0, shares - 1)]] * (len(terms) - 1)
    kinds = len(terms)
    blocks = [term.shape[1:] for term in terms]
    members = ring // spread
    groups = 3
    near_bits = [1 << step for step in range(ring.bit_length() - 1)]
    far_bits = [1 << step for step in range(exchange_size.bit_length() - 1)]
    deep_bits = [1 << step for step in range(shares.bit_length() - 1)]
    near = [(0, 0, bit) for bit in near_bits]
    far = [(0, bit, 0) for bit in far_bits]
    deep = [(bit, 0, 0) for bit in deep_bits]
    orders = [near + far + deep, near[:1] + far + near[1:] + deep, near + far + deep]
    places = near + far + deep
    bit_count = len(places)
    group_rows = [wide.shape[1], wide.shape[1], small.shape[0]]
    tile = [16, 16, 8]
    plans = []
    for group in range(groups):
        length, plan = group_rows[group], []
        for _ in range(bit_count):
            halved = (length // 2) % tile[group] == 0
            length = length // 2 if halved else length
            plan.append((halved, length))
        plans.append(plan)

    def kernel(*refs):
        refs = list(refs)

        def take(number):
            taken = refs[:number]
            del refs[:number]
            return taken

        term_refs, first_refs = take(kinds), take(kinds)
        (wide_hbm, small_hbm) = take(2)
        gathered = take(kinds)
        (wide_out, small_out) = take(2)
        sums, landed = take(kinds), take(kinds)
        (halves, smalls) = take(2)
        group_landed = take(groups)
        (load_sem, step_send, step_recv, own_sem, ring_send, ring_recv) = take(6)
        (dense_send, dense_recv, dense_load) = take(3)
        share = lax.axis_index("dp")
        mine = lax.axis_index("ctx") // spread

        dense_in = [
            pltpu.make_async_copy(wide_hbm, halves, dense_load.at[0]),
            pltpu.make_async_copy(small_hbm, smalls, dense_load.at[1]),
        ]
        for copy in dense_in:
            copy.start()
        loads = []
        for kind in range(kinds):
            copies = [
                pltpu.make_async_copy(
                    first_refs[kind],
                    landed[kind].at[steps.index(done[kind][-1])],
                    load_sem.at[kind, shares // 2],
                )
            ]
            for place in range(shares - 2, -1, -2):
                copies.append(
                    pltpu.make_async_copy(
                        term_refs[kind].at[jnp.bitwise_xor(share, place)],
                        sums[kind].at[place // 2],
                        load_sem.at[kind, place // 2],
                    )
                )
            for copy in copies:
                copy.start()
            loads.append(copies)
        greet_places(places)

        def expert_chain(kind, piece):
            period, odd_wait, even_wait, near_wait, far_wait, last_wait = EXPERT_TIMES
            begin = time = period * (kind * PIECES + piece)
            slots = {step: index for index, step in enumerate(steps)}
            lines = blocks[kind][0] // PIECES
            window = pl.ds(piece * lines, lines)
            one = kind * PIECES + piece

            def transfer(step, place):
                index = slots[step, place]
                if place % 2 == 1:
                    source = term_refs[kind].at[jnp.bitwise_xor(share, place), window]
                else:
                    source = sums[kind].at[place // 2, window]
                return pltpu.make_async_remote_copy(
                    src_ref=source,
                    dst_ref=landed[kind].at[index, window],
                    send_sem=step_send.at[one, index],
                    recv_sem=step_recv.at[one, index],
                    device_id=peer_at(1 << step, 0, 0),
                    device_id_type=pl.DeviceIdType.MESH,
                )

            yield begin
            arrived, started = set(done[kind]), []
            waiting = [op for op in steps if op not in arrived]
            for op in list(waiting):
                if op[0] == 0:
                    transfer(*op).start()
                    started.append(op)
                    waiting.remove(op)
            while loads[kind]:
                loads[kind].pop().wait()
            step, place = done[kind][-1]
            add_into(
                sums[kind].at[(place ^ 1 << step) // 2, window],
                landed[kind].at[slots[step, place], window],
            )
            while True:
                for op in list(waiting):
                    if needed_before(*op) <= arrived:
                        transfer(*op).start()
                        started.append(op)
                        waiting.remove(op)
                if not started:
                    break
                op = started.pop(0)
                yield time + (even_wait if op[0] else odd_wait)
                transfer(*op).wait()
                arrived.add(op)
                add_into(
                    sums[kind].at[(op[1] ^ 1 << op[0]) // 2, window],
                    landed[kind].at[slots[op], window],
                )
            time += even_wait
            index = len(steps)
            bit = 1
            while bit < spread:
                copy = pltpu.make_async_remote_copy(
                    src_ref=sums[kind].at[0, window],
                    dst_ref=landed[kind].at[index, window],
                    send_sem=step_send.at[one, index],
                    recv_sem=step_recv.at[one, index],
                    device_id=peer_at(0, 0, bit),
                    device_id_type=pl.DeviceIdType.MESH,
                )
                copy.start()
                time += near_wait
                yield time
                copy.wait()
                add_into(sums[kind].at[0, window], landed[kind].at[index, window])
                index += 1
                bit *= 2
            keep = pltpu.make_async_copy(
                sums[kind].at[0, window], gathered[kind].at[mine, window], own_sem.at[one]
            )
            keep.start()
            sent = []

            def pass_on(place, bit):
                block = jnp.bitwise_xor(mine, place)
                target = gathered[kind].at[block, window]
                return pltpu.make_async_remote_copy(
                    src_ref=sums[kind].at[0, window] if place == 0 else target,
                    dst_ref=target,
                    send_sem=ring_send.at[one, place ^ bit],
                    recv_sem=ring_recv.at[one, place ^ bit],
                    device_id=peer_at(0, 0, bit * spread),
                    device_id_type=pl.DeviceIdType.MESH,
                )

            def forward(place):
                for bit, held in gather_steps(members):
                    if place in held:
                        copy = pass_on(place, bit)
                        copy.start()
                        sent.append(copy)

            forward(0)
            for place in range(1, members):
                wait = near_wait if place == 1 else far_wait if place & (place - 1) == 0 else last_wait
                yield time + wait + (far_wait if wait == last_wait else 0)
                bit = place & -place
                pass_on(place ^ bit, bit).wait_recv()
                forward(place)
            yield 1000
            keep.wait()
            for copy in sent:
                copy.wait_send()

        def bit_of(place):
            deep_bit, far_bit, near_bit = place
            axis, bit = ("dp", deep_bit) if deep_bit else ("exp", far_bit) if far_bit else ("ctx", near_bit)
            return lax.rem(lax.axis_index(axis) // bit, 2)

        def dense_chain(times):
            times = iter(times + tuple(range(times[-1] + 8, 900, 8)))
            buffers = [halves.at[0], halves.at[1], smalls]
            yield 0
            for copy in dense_in:
                copy.wait()
            begins = [0] * groups
            trail = []

            def window(begin, length, group):
                if isinstance(begin, int):
                    return pl.ds(begin, length)
                return pl.ds(pl.multiple_of(begin, tile[group]), length)

            def exchange_rows(group, step, source, target):
                return pltpu.make_async_remote_copy(
                    src_ref=source,
                    dst_ref=target,
                    send_sem=dense_send.at[group, step],
                    recv_sem=dense_recv.at[group, step],
                    device_id=peer_at(*orders[group][step % bit_count]),
                    device_id_type=pl.DeviceIdType.MESH,
                )

            for step in range(bit_count):
                copies = []
                for group in range(groups):
                    halved, length = plans[group][step]
                    upper = bit_of(orders[group][step])
                    if halved:
                        sent = begins[group] + (1 - upper) * length
                        begins[group] = begins[group] + upper * length
                    else:
                        sent = begins[group]
                    at = sum(size for _, size in plans[group][:step])
                    copy = exchange_rows(
                        group,
                        step,
                        buffers[group].at[window(sent, length, group)],
                        group_landed[group].at[pl.ds(at, length)],
                    )
                    copy.start()
                    copies.append((copy, at, length))
                trail.append(list(begins))
                yield next(times)
                for group, (copy, at, length) in enumerate(copies):
                    copy.wait()
                    add_into(
                        buffers[group].at[window(begins[group], length, group)],
                        group_landed[group].at[pl.ds(at, length)],
                    )
            outputs = [wide_out.at[0], wide_out.at[1], small_out]
            keeps = []
            for group in range(groups):
                part = window(begins[group], plans[group][-1][1], group)
                keep = pltpu.make_async_copy(
                    buffers[group].at[part], outputs[group].at[part], dense_load.at[group]
                )
                keep.start()
                keeps.append(keep)
            for keep in keeps:
                keep.wait()
            for step in range(bit_count - 1, -1, -1):
                copies = []
                for group in range(groups):
                    halved, length = plans[group][step]
                    if halved:
                        part = outputs[group].at[window(trail[step][group], length, group)]
                        copy = exchange_rows(group, bit_count + step, part, part)
                        copy.start()
                        copies.append(copy)
                if copies:
                    yield next(times)
                for copy in copies:
                    copy.wait()

        chains = [dense_chain(DENSE_TIMES)] + [
            expert_chain(kind, piece) for kind in range(kinds) for piece in range(PIECES)
        ]
        due = dict(enumerate(next(chain) for chain in chains))
        planned = list(ORDER) if (shares, ring, exchange_size) == (4, 4, 2) else []
        while due:
            index = planned.pop(0) if planned else min(due, key=lambda one: (due[one], one))
            time = next(chains[index], None)
            if time is None:
                del due[index]
            else:
                due[index] = time

    any_space = pl.BlockSpec(memory_space=pl.ANY)
    extra = len(steps) + spread.bit_length() - 1
    return pl.pallas_call(
        kernel,
        out_shape=[jax.ShapeDtypeStruct((members,) + block, low) for block in blocks]
        + [jax.ShapeDtypeStruct(wide.shape, low), jax.ShapeDtypeStruct(small.shape, full)],
        in_specs=[any_space] * (2 * kinds + 2),
        out_specs=[any_space] * (kinds + 2),
        scratch_shapes=[pltpu.VMEM((shares // 2,) + block, low) for block in blocks]
        + [pltpu.VMEM((extra,) + block, low) for block in blocks]
        + [pltpu.VMEM(wide.shape, low), pltpu.VMEM(small.shape, full)]
        + [
            pltpu.VMEM(
                (sum(length for _, length in plans[group]), (wide, wide, small)[group].shape[-1]),
                (low, low, full)[group],
            )
            for group in range(groups)
        ]
        + [
            pltpu.SemaphoreType.DMA((kinds, shares // 2 + 1)),
            pltpu.SemaphoreType.DMA((kinds * PIECES, extra)),
            pltpu.SemaphoreType.DMA((kinds * PIECES, extra)),
            pltpu.SemaphoreType.DMA((kinds * PIECES,)),
            pltpu.SemaphoreType.DMA((kinds * PIECES, members)),
            pltpu.SemaphoreType.DMA((kinds * PIECES, members)),
            pltpu.SemaphoreType.DMA((groups, 2 * bit_count)),
            pltpu.SemaphoreType.DMA((groups, 2 * bit_count)),
            pltpu.SemaphoreType.DMA((3,)),
        ],
        compiler_params=pltpu.CompilerParams(
            collective_id=3, has_side_effects=True, vmem_limit_bytes=60 * 2**20
        ),
        name="reduce",
    )(*terms, *firsts, wide, small)


def widen_layer(parts, wide, small, experts):
    members = parts[0].shape[0]
    pieces = 1
    steps = members * pieces
    squares = wide.shape[1] // (2 * wide.shape[2])
    width = 2 * wide.shape[2]
    lines = wide.shape[1] // steps
    turns = width // lines
    full = jnp.float32
    kinds = len(parts)

    def kernel(*refs):
        sources, wide_ref, small_ref = refs[:kinds], refs[kinds], refs[kinds + 1]
        targets = refs[kinds + 2 : 2 * kinds + 2]
        square_refs = refs[2 * kinds + 2 : 2 * kinds + 2 + squares]
        head_ref, map_ref, carry_ref, vector_ref, *gain_refs = refs[2 * kinds + 2 + squares :]
        step = pl.program_id(0) * pieces + pl.program_id(1)
        for source, target in zip(sources, targets):
            target[...] = source[...].astype(full)
        for index in range(squares):

            @pl.when(step // turns == index)
            def _():
                square_refs[index][:, 0 : width // 2] = wide_ref[0].astype(full)
                square_refs[index][:, width // 2 :] = wide_ref[1].astype(full)

        @pl.when(step == 0)
        def _():
            head_ref[...] = small_ref[8 : 8 + experts, :]
            for index in range(2):
                begin = 8 + experts + 2 * index
                map_ref[index] = small_ref[begin : begin + 2, :]
            carry_ref[...] = jnp.transpose(small_ref[24:40, 0:128])[0:experts, 0:experts]
            vector_ref[...] = small_ref[2:4, :]
            for index, target in enumerate(gain_refs):
                target[...] = small_ref[index : index + 1, :].reshape(width)

    def chunk(part):
        return pl.BlockSpec(
            (1, part.shape[1] // pieces, part.shape[2]), lambda member, piece: (member, piece, 0)
        )

    def square(index):
        return pl.BlockSpec(
            (lines, width),
            lambda member, piece: (
                jnp.clip(member * pieces + piece - index * turns, 0, turns - 1),
                0,
            ),
        )

    def whole(*shape):
        return pl.BlockSpec(shape, lambda member, piece: (0,) * len(shape))

    smalls = [(experts, width), (2, 2, width), (experts, experts), (2, width), (width,), (width,)]
    return pl.pallas_call(
        kernel,
        out_shape=[jax.ShapeDtypeStruct(part.shape, full) for part in parts]
        + [jax.ShapeDtypeStruct((width, width), full)] * squares
        + [jax.ShapeDtypeStruct(shape, full) for shape in smalls],
        grid=(members, pieces),
        in_specs=[chunk(part) for part in parts]
        + [
            pl.BlockSpec(
                (2, lines, width // 2), lambda member, piece: (0, member * pieces + piece, 0)
            ),
            whole(*small.shape),
        ],
        out_specs=[chunk(part) for part in parts]
        + [square(index) for index in range(squares)]
        + [whole(*shape) for shape in smalls],
        compiler_params=pltpu.CompilerParams(vmem_limit_bytes=60 * 2**20),
        name="widen",
    )(*parts, wide, small)


def local(
    tokens,
    cotangent,
    previous,
    routes,
    boundaries,
    norm_first,
    query_weight,
    key_weight,
    value_weight,
    output_weight,
    norm_second,
    router,
    gate_carry,
    constant_map,
    constant_vector,
    expert_gate,
    expert_linear,
    expert_down,
):
    model_width = tokens.shape[2]
    ring = lax.axis_size("ctx")
    group_size = expert_gate.shape[0]
    exchange_count = lax.axis_size("exp")
    spread = ring // group_size
    ranks = (exchange_count, group_size, spread)
    slot_total = exchange_count * group_size * CAP
    expert_total = router.shape[1]
    params = (
        router.T,
        jnp.transpose(constant_map, (0, 2, 1)),
        norm_first,
        norm_second,
        constant_vector,
    )
    prior = jnp.transpose(previous, (2, 0, 1))
    weights = (query_weight, key_weight, value_weight, output_weight)
    (
        queries,
        keys,
        values,
        attended,
        lse,
        middle,
        probs,
        targets,
        outgoing,
        slot_gates,
        grads_in,
    ) = attend_layer(
        tokens[0],
        cotangent[0],
        prior,
        routes[0].T,
        boundaries,
        weights,
        params,
        gate_carry,
        ranks,
        CAP,
        ring,
    )
    home_grads, produced, dots, gate_terms, linear_terms, down_terms, first = expert_layer(
        outgoing,
        slot_gates,
        grads_in.reshape(slot_total, model_width),
        (expert_gate, expert_linear, expert_down),
        ranks,
        lax.axis_size("dp"),
    )
    terms = (down_terms, gate_terms, linear_terms)
    shares = lax.axis_size("dp")
    result, token_grads, wide, small, *firsts = backward_layer(
        tokens[0],
        cotangent[0],
        prior,
        routes[0].T,
        boundaries,
        (attended, lse, middle, probs, targets, queries, keys, values),
        (home_grads.reshape(slot_total, model_width), produced, dots),
        weights,
        params,
        terms,
        first,
        ranks,
        CAP,
        ring,
        shares,
    )
    *parts, wide, small = reduce_layer(
        terms, firsts, wide, small, spread, shares, ring, exchange_count
    )
    (
        down_grads,
        gate_grads,
        linear_grads,
        query_grads,
        key_grads,
        value_grads,
        output_grads,
        router_grads,
        map_grads,
        carry_grads,
        vector_grads,
        first_grads,
        second_grads,
    ) = widen_layer(parts, wide, small, expert_total)
    return (
        result[None],
        token_grads[None],
        first_grads,
        query_grads,
        key_grads,
        value_grads,
        output_grads,
        second_grads,
        router_grads.T,
        carry_grads,
        jnp.transpose(map_grads, (0, 2, 1)),
        vector_grads,
        gate_grads,
        linear_grads,
        down_grads,
    )


def solution(mesh):
    return jax.shard_map(
        local,
        mesh=mesh,
        in_specs=(
            P(("dp", "exp"), "ctx", None),
            P(("dp", "exp"), "ctx", None),
            P(("dp", "exp"), "ctx", None),
            P(("dp", "exp"), "ctx", None),
            P(("dp", "exp"), None),
            P(),
            P(),
            P(),
            P(),
            P(),
            P(),
            P(),
            P(),
            P(),
            P(),
            P("exp", None, None),
            P("exp", None, None),
            P("exp", None, None),
        ),
        out_specs=(
            P(("dp", "exp"), "ctx", None),
            P(("dp", "exp"), "ctx", None),
            P(),
            P(),
            P(),
            P(),
            P(),
            P(),
            P(),
            P(),
            P(),
            P(),
            P("exp", None, "dp"),
            P("exp", None, "dp"),
            P("exp", "dp", None),
        ),
        check_vma=False,
    )
```

```python
import math

import jax
import jax.numpy as jnp
import numpy as np
from jax import lax
from jax.experimental import pallas as pl
from jax.experimental.pallas import tpu as pltpu
from jax.sharding import PartitionSpec as P

HEAD_DIM = 64
CAP = 96


EPSILON = 1e-06
NEGATIVE = -1e30
HIGH = lax.Precision.HIGHEST


HEAD_ROWS = 16


def mesh_id(exp_index, ctx_index):
    return {"exp": exp_index, "ctx": ctx_index}


def dot(left, right):
    return jnp.dot(left, right, preferred_element_type=jnp.float32)


def dot_nt(left, right):
    return lax.dot_general(
        left, right, (((1,), (1,)), ((), ())), preferred_element_type=jnp.float32
    )


def dot_tn(left, right):
    return lax.dot_general(
        left, right, (((0,), (0,)), ((), ())), preferred_element_type=jnp.float32
    )


def member_of(shift, ranks):
    exchange_size, group_size, spread = ranks
    exp_index, ctx_index = lax.axis_index("exp"), lax.axis_index("ctx")
    far, near = shift // group_size, shift % group_size
    place = jnp.bitwise_xor(ctx_index // spread, near) * spread + lax.rem(ctx_index, spread)
    return mesh_id(jnp.bitwise_xor(exp_index, far), place)


def greet(count, ranks):
    barrier = pltpu.get_barrier_semaphore()
    for shift in range(1, count):
        pl.semaphore_signal(
            barrier, inc=1, device_id=member_of(shift, ranks), device_id_type=pl.DeviceIdType.MESH
        )
    pl.semaphore_wait(barrier, count - 1)


def block_of(shift, count):
    return (shift + count - count // 4) % count


def own_block(count):
    return block_of(0, count)


def send_block(source, target, block, ranks, send_sem, recv_sem):
    count = ranks[0] * ranks[1]
    return pltpu.make_async_remote_copy(
        src_ref=source.at[block],
        dst_ref=target.at[block],
        send_sem=send_sem.at[block],
        recv_sem=recv_sem.at[block],
        device_id=member_of((block + count // 4) % count, ranks),
        device_id_type=pl.DeviceIdType.MESH,
    )


def keep_block(source, target, count, sem):
    block = own_block(count)
    return pltpu.make_async_copy(source.at[block], target.at[block], sem)


def other_blocks(count):
    return [block for block in range(count) if block != own_block(count)]


def expert_layer(outgoing, gates, grads, weights, ranks, shares):
    count, cap, width = outgoing.shape
    hidden_units = weights[0].shape[2]
    rows = count * cap
    share = hidden_units // shares
    spread = ranks[2]

    def kernel(
        outgoing_hbm,
        gates_ref,
        grads_hbm,
        gate_hbm,
        linear_hbm,
        down_hbm,
        back_ref,
        output_out,
        dots_ref,
        gate_terms,
        linear_terms,
        down_terms,
        first_ref,
        received,
        received_gates,
        gate_w,
        linear_w,
        down_w,
        hidden_grad,
        hidden,
        gate_low,
        linear_low,
        rows_t,
        scaled,
        gate_column,
        out_total,
        in_total,
        in_send,
        dots_send,
        terms,
        weight_sem,
        send_sem,
        recv_sem,
        local_sem,
        terms_sem,
        first_send,
        first_recv,
        grads_ref,
        output_ref,
        extra_sem,
    ):
        own = lax.axis_index("ctx") // spread
        loads = [
            pltpu.make_async_copy(source.at[own], target, weight_sem.at[index])
            for index, (source, target) in enumerate(
                ((down_hbm, down_w), (gate_hbm, gate_w), (linear_hbm, linear_w))
            )
        ]
        bring = pltpu.make_async_copy(grads_hbm, grads_ref, extra_sem.at[0])
        bring.start()
        for load in loads:
            load.start()
        greet_places([(0,) + place for place in group_places(ranks)] + [(1, 0, 0)])

        def send_some(source, target, index, shifts):
            copies = []
            for shift in shifts:
                if shift == own_block(count):
                    copies.append(keep_block(source, target, count, local_sem.at[index]))
                else:
                    copies.append(
                        send_block(
                            source, target, shift, ranks, send_sem.at[index], recv_sem.at[index]
                        )
                    )
            for copy in copies:
                copy.start()
            return copies

        every = range(count)
        gates_in = send_some(gates_ref, received_gates, 0, every)
        soon = [block for block in every if not count // 2 <= block < count - count // 4]
        incoming = dict(zip(soon, send_some(outgoing_hbm, received, 1, soon)))
        bring.wait()
        loads[0].wait()

        def backward_in(index, carry):
            part = pl.ds(pl.multiple_of(index * share, share), share)
            hidden_grad[:, part] = dot_nt(grads_ref[...], down_w[part, :])
            return carry

        lax.fori_loop(0, shares, backward_in, 0)
        for copy in gates_in:
            copy.wait()
        for shift in every:
            column = jnp.transpose(received_gates[shift])[:cap, 0:1]
            block = pl.ds(shift * cap, cap)
            gate_column[block, :] = jnp.broadcast_to(column, (cap, 128))
            scaled[block, :] = (column * grads_ref[block, :].astype(jnp.float32)).astype(
                jnp.bfloat16
            )
        for load in loads[1:]:
            load.wait()

        going = []
        batches = 2
        members = count // batches
        lines = rows // batches
        for batch in range(batches):
            chunks = range(batch * members, (batch + 1) * members)
            for shift in chunks:
                incoming[shift].wait()
            if batch == 0:
                late = [block for block in every if block not in soon]
                incoming.update(zip(late, send_some(outgoing_hbm, received, 1, late)))
            block = pl.ds(batch * lines, lines)

            def through(index):
                part = pl.ds(index * share, share)
                tokens = received[batch * members : (batch + 1) * members].reshape(lines, width)
                gate_part = dot(tokens, gate_w[:, part])
                linear_part = dot(tokens, linear_w[:, part])
                sigmoid = 1.0 / (1.0 + jnp.exp(-gate_part))
                silu = gate_part * sigmoid
                low = (silu * linear_part).astype(jnp.bfloat16)
                hidden[block, part] = low
                upper = hidden_grad[block, part] * gate_column[block, 0:1]
                low_gate = (
                    upper * linear_part * sigmoid * (1.0 + gate_part * (1.0 - sigmoid))
                ).astype(jnp.bfloat16)
                gate_low[block, part] = low_gate
                low_linear = (upper * silu).astype(jnp.bfloat16)
                linear_low[block, part] = low_linear
                out = dot(low, down_w[part, :])
                back = dot_nt(low_gate, gate_w[:, part]) + dot_nt(low_linear, linear_w[:, part])

                if index == 0:
                    out_total[block, :] = out
                    in_total[block, :] = back
                else:
                    out_total[block, :] += out
                    in_total[block, :] += back

            for tile in range(shares):
                through(tile)
            in_send[batch * members : (batch + 1) * members] = (
                in_total[block, :].astype(jnp.bfloat16).reshape(members, cap, width)
            )
            going += send_some(in_send, back_ref, 2, chunks)
            low = out_total[block, :].astype(jnp.bfloat16)
            output_ref[batch * members : (batch + 1) * members] = low.reshape(members, cap, width)
            part = pl.ds(batch * members, members)
            going.append(
                pltpu.make_async_copy(
                    output_ref.at[part], output_out.at[part], extra_sem.at[1 + batch]
                )
            )
            going[-1].start()
            dots = jnp.sum(
                low.astype(jnp.float32) * grads_ref[block, :].astype(jnp.float32),
                axis=1,
                keepdims=True,
            )
            for place, shift in enumerate(chunks):
                column = jnp.broadcast_to(dots[place * cap : (place + 1) * cap], (cap, 128))
                dots_send[shift, :, 0:cap] = jnp.transpose(column)[0:8, :]
                dots_send[shift, :, cap:] = jnp.zeros((8, 128 - cap), jnp.float32)
            going += send_some(dots_send, dots_ref, 3, chunks)
            rows_t[:, batch * lines : (batch + 1) * lines] = jnp.transpose(
                received[batch * members : (batch + 1) * members].reshape(lines, width)
            )

        def term_copy(which, index):
            target = (down_terms, gate_terms, linear_terms)[which]
            return pltpu.make_async_copy(
                terms[which].at[index], target.at[index], terms_sem.at[which, index]
            )

        def weigh(which, turn):
            index = jnp.bitwise_xor(lax.axis_index("dp"), shares - 1 - turn)
            part = pl.ds(pl.multiple_of(index * share, share), share)
            if which == 0:
                value = dot_tn(hidden[:, part], scaled[...])
            else:
                value = dot(rows_t[...], (gate_low if which == 1 else linear_low)[:, part])
            terms[which][index] = value.astype(jnp.bfloat16)
            term_copy(which, index).start()
            return index

        index = weigh(0, 0)
        first = pltpu.make_async_remote_copy(
            src_ref=terms[0].at[index],
            dst_ref=first_ref,
            send_sem=first_send,
            recv_sem=first_recv,
            device_id=peer_at(1, 0, 0),
            device_id_type=pl.DeviceIdType.MESH,
        )
        first.start()

        def weigh_rest(turn, carry):
            weigh(1, turn)
            weigh(2, turn)

            @pl.when(turn > 0)
            def _():
                weigh(0, turn)

            return carry

        lax.fori_loop(0, shares, weigh_rest, 0)
        for which in range(3):
            for index in range(shares):
                term_copy(which, index).wait()
        for copy in going:
            copy.wait()
        first.wait()

    low, full = jnp.bfloat16, jnp.float32
    columns, lines = (shares, width, share), (shares, share, width)
    any_space = pl.BlockSpec(memory_space=pl.ANY)
    in_vmem = pl.BlockSpec(memory_space=pltpu.VMEM)
    return pl.pallas_call(
        kernel,
        out_shape=[
            jax.ShapeDtypeStruct(outgoing.shape, low),
            jax.ShapeDtypeStruct(outgoing.shape, low),
            jax.ShapeDtypeStruct(gates.shape, full),
            jax.ShapeDtypeStruct(columns, low),
            jax.ShapeDtypeStruct(columns, low),
            jax.ShapeDtypeStruct(lines, low),
            jax.ShapeDtypeStruct(lines[1:], low),
        ],
        in_specs=[any_space, in_vmem] + [any_space] * 4,
        out_specs=[any_space] * 7,
        scratch_shapes=[
            pltpu.VMEM(outgoing.shape, low),
            pltpu.VMEM(gates.shape, full),
            pltpu.VMEM((width, hidden_units), low),
            pltpu.VMEM((width, hidden_units), low),
            pltpu.VMEM((hidden_units, width), low),
            pltpu.VMEM((rows, hidden_units), full),
            pltpu.VMEM((rows, hidden_units), low),
            pltpu.VMEM((rows, hidden_units), low),
            pltpu.VMEM((rows, hidden_units), low),
            pltpu.VMEM((width, rows), low),
            pltpu.VMEM((rows, width), low),
            pltpu.VMEM((rows, 128), full),
            pltpu.VMEM((rows, width), full),
            pltpu.VMEM((rows, width), full),
            pltpu.VMEM(outgoing.shape, low),
            pltpu.VMEM(gates.shape, full),
            [pltpu.VMEM(lines, low), pltpu.VMEM(columns, low), pltpu.VMEM(columns, low)],
            pltpu.SemaphoreType.DMA((3,)),
            pltpu.SemaphoreType.DMA((4, count)),
            pltpu.SemaphoreType.DMA((4, count)),
            pltpu.SemaphoreType.DMA((4,)),
            pltpu.SemaphoreType.DMA((3, shares)),
            pltpu.SemaphoreType.DMA,
            pltpu.SemaphoreType.DMA,
            pltpu.VMEM((rows, width), low),
            pltpu.VMEM(outgoing.shape, low),
            pltpu.SemaphoreType.DMA((3,)),
        ],
        compiler_params=pltpu.CompilerParams(
            collective_id=1, has_side_effects=True, vmem_limit_bytes=60 * 2**20
        ),
        cost_estimate=pl.CostEstimate(
            flops=18 * rows * width * hidden_units,
            bytes_accessed=12 * width * hidden_units + 12 * rows * width,
            transcendentals=rows * hidden_units,
        ),
        name="experts",
    )(outgoing, gates, grads, *weights)


def rope_tables(row_count):
    half = HEAD_DIM // 2
    frequency = np.exp(
        np.arange(half, dtype=np.float32) * np.float32(-2.0 * math.log(10000.0) / HEAD_DIM)
    ).astype(np.float32)
    angles = np.arange(row_count, dtype=np.float32)[:, None] * frequency[None, :]
    cosine, sine = np.cos(angles).astype(np.float32), np.sin(angles).astype(np.float32)
    return (
        np.concatenate([cosine] * 4, axis=1),
        np.concatenate([-sine, sine, -sine, sine], axis=1),
    )


def rotate(values, cosine, sine):
    lane = lax.broadcasted_iota(jnp.int32, cosine.shape, 1)
    leading = jnp.bitwise_and(lane, HEAD_DIM - 1) < HEAD_DIM // 2
    parts = []
    for begin in range(0, values.shape[1], 128):
        part = values[:, begin : begin + 128]
        ahead = pltpu.roll(part, 128 - HEAD_DIM // 2, 1)
        behind = pltpu.roll(part, HEAD_DIM // 2, 1)
        parts.append(part * cosine + jnp.where(leading, ahead, behind) * sine)
    return jnp.concatenate(parts, axis=1)


def inverse_norm(values):
    return lax.rsqrt(jnp.mean(values * values, axis=1, keepdims=True) + EPSILON)


def head_masks(rows):
    first = lax.broadcasted_iota(jnp.int32, (rows, 128), 1) < HEAD_DIM
    return first, jnp.logical_not(first)


def start_of(positions, starts):
    first = jnp.zeros_like(positions)
    for index in range(starts.shape[1]):
        begin = starts[0, index]
        first = jnp.where(begin <= positions, jnp.maximum(first, begin), first)
    return first


def gather_steps(size):
    bits, held, steps = [], [0], []
    bit = size // 2
    while bit >= 1:
        steps.append((bit, list(held)))
        held = held + [place ^ bit for place in held]
        bit //= 2
    return steps


def peer_at(deep, far, near):
    return {
        "dp": jnp.bitwise_xor(lax.axis_index("dp"), deep),
        "exp": jnp.bitwise_xor(lax.axis_index("exp"), far),
        "ctx": jnp.bitwise_xor(lax.axis_index("ctx"), near),
    }


def peer(far, near):
    return peer_at(0, far, near)


def greet_places(places):
    barrier = pltpu.get_barrier_semaphore()
    for place in places:
        pl.semaphore_signal(
            barrier, inc=1, device_id=peer_at(*place), device_id_type=pl.DeviceIdType.MESH
        )
    pl.semaphore_wait(barrier, len(places))


def greet_all(places):
    greet_places([(0,) + place for place in places])


def group_places(ranks):
    return [
        (shift // ranks[1], shift % ranks[1] * ranks[2]) for shift in range(1, ranks[0] * ranks[1])
    ]


def ring_places(size):
    return [(0, bit) for bit, _ in gather_steps(size)]


def places_of(ranks, size):
    places = group_places(ranks)
    return places + [place for place in ring_places(size) if place not in places]


class Gather:
    def __init__(self, buffers, size, send_sem, recv_sem, sources=None):
        self.buffers, self.sources = buffers, sources
        self.send_sem, self.recv_sem = send_sem, recv_sem
        self.steps = gather_steps(size)

    def copy(self, place, bit, index):
        block = jnp.bitwise_xor(lax.axis_index("ctx"), place)
        buffer = self.buffers[index]
        straight = self.sources is not None and place == 0
        return pltpu.make_async_remote_copy(
            src_ref=self.sources[index] if straight else buffer.at[block],
            dst_ref=buffer.at[block],
            send_sem=self.send_sem.at[index, place ^ bit],
            recv_sem=self.recv_sem.at[index, place ^ bit],
            device_id=peer(0, bit),
            device_id_type=pl.DeviceIdType.MESH,
        )

    def forward(self, place):
        for bit, held in self.steps:
            if place in held:
                for index in range(len(self.buffers)):
                    self.copy(place, bit, index).start()

    def arrive(self, place):
        bit = place & -place
        for index in range(len(self.buffers)):
            self.copy(place ^ bit, bit, index).wait_recv()
        self.forward(place)

    def finish(self):
        for bit, held in self.steps:
            for place in held:
                for index in range(len(self.buffers)):
                    self.copy(place, bit, index).wait_send()


def fill_rows(pack, prior, router_ref, map_ref, first_ref, second_ref, vector_ref, previous_ref):
    full = jnp.float32
    experts = router_ref.shape[0]
    width = router_ref.shape[1]
    pack[0:experts, :] = router_ref[...].astype(full)
    for index in range(2):
        pack[experts + 2 * index : experts + 2 * index + 2, :] = map_ref[index].astype(full)
    pack[HEAD_ROWS : HEAD_ROWS + 1, :] = first_ref[...].astype(full).reshape(1, width)
    pack[HEAD_ROWS + 1 : HEAD_ROWS + 2, :] = second_ref[...].astype(full).reshape(1, width)
    pack[HEAD_ROWS + 2 : HEAD_ROWS + 4, :] = vector_ref[...].astype(full)
    for index in range(experts):
        prior[index : index + 1, :] = previous_ref[index]


def slot_targets(routes, ranks, cap):
    exchange_size, group_size, spread = ranks
    rows = routes.shape[1]
    experts = exchange_size * group_size
    expert = lax.broadcasted_iota(jnp.int32, (16, rows), 0)
    hits = [(expert == routes[k : k + 1]).astype(jnp.float32) for k in range(2)]
    before = lax.broadcasted_iota(jnp.int32, (rows, rows), 0) < lax.broadcasted_iota(
        jnp.int32, (rows, rows), 1
    )
    earlier = dot(
        (hits[0] + hits[1]).astype(jnp.bfloat16), before.astype(jnp.float32).astype(jnp.bfloat16)
    )
    targets = []
    for k in range(2):
        route = routes[k : k + 1]
        rank = jnp.sum(hits[k] * earlier, axis=0, keepdims=True)
        far = jnp.bitwise_xor(route // group_size, lax.axis_index("exp"))
        near = jnp.bitwise_xor(route % group_size, lax.axis_index("ctx") // spread)
        count = exchange_size * group_size
        block = jnp.bitwise_and(far * group_size + near + count - count // 4, count - 1)
        place = (block * cap).astype(jnp.float32)
        targets.append(jnp.where(route < experts, place + rank, -1.0))
    return targets


def attend_layer(
    tokens, cotangent, previous, routes, starts, weights, params, carry, ranks, cap, size
):
    rows, width = tokens.shape
    count = ranks[0] * ranks[1]
    slots = count * cap
    pairs = width // 128
    tables = rope_tables(size * rows)
    low, full = jnp.bfloat16, jnp.float32

    def kernel(
        tokens_hbm,
        cotangent_ref,
        previous_ref,
        routes_ref,
        starts_ref,
        query_hbm,
        key_hbm,
        value_hbm,
        output_hbm,
        router_ref,
        map_ref,
        first_ref,
        second_ref,
        vector_ref,
        carry_ref,
        cosine_hbm,
        sine_hbm,
        queries_out,
        keys_out,
        values_out,
        attended_out,
        lse_ref,
        middle_out,
        probs_ref,
        targets_ref,
        outgoing_ref,
        gates_ref,
        grads_ref,
        stream,
        queries,
        keys,
        values,
        query_w,
        key_w,
        value_w,
        output_w,
        cosine,
        sine,
        bias,
        totals,
        highest,
        slot_grads,
        load_sem,
        gather_send,
        gather_recv,
        grad_send,
        grad_recv,
        keep_sem,
        pack,
        prior,
        attended_ref,
        middle_ref,
    ):
        own = lax.axis_index("ctx")
        bring = pltpu.make_async_copy(tokens_hbm, stream.at[own], load_sem.at[6])
        bring.start()
        loads = [
            pltpu.make_async_copy(source, target, load_sem.at[index])
            for index, (source, target) in enumerate(
                (
                    (query_hbm, query_w),
                    (key_hbm, key_w),
                    (value_hbm, value_w),
                    (cosine_hbm, cosine),
                    (sine_hbm, sine),
                    (output_hbm, output_w),
                )
            )
        ]
        for load in loads:
            load.start()
        greet_all(places_of(ranks, size))
        gather = Gather([stream], size, gather_send, gather_recv, [tokens_hbm])
        gather.forward(0)

        fill_rows(
            pack, prior, router_ref, map_ref, first_ref, second_ref, vector_ref, previous_ref
        )
        targets = slot_targets(routes_ref[...], ranks, cap)
        slot = lax.broadcasted_iota(jnp.int32, (slots, rows), 0).astype(full)
        picked = jnp.logical_or(slot == targets[0], slot == targets[1])
        picked = picked.astype(full).astype(low)
        slot_grads[...] = dot(picked, cotangent_ref[...]).astype(low).reshape(count, cap, width)
        grad_copies = [
            send_block(slot_grads, grads_ref, block, ranks, grad_send, grad_recv)
            for block in other_blocks(count)
        ]
        waiting, leaving = [], [keep_block(slot_grads, grads_ref, count, keep_sem.at[0])]
        for block, copy in zip(other_blocks(count), grad_copies):
            across = block < count // 4 or count // 2 <= block < count - count // 4
            (waiting if across else leaving).append(copy)
        grad_copies.append(leaving[0])
        for copy in leaving:
            copy.start()

        bring.wait()
        for load in loads[:5]:
            load.wait()
        gain = pack[HEAD_ROWS : HEAD_ROWS + 1, :]

        def project(block, wanted):
            line = pl.ds(pl.multiple_of(block * rows, rows), rows)
            values_in = stream[block].astype(full)
            normed = (values_in * inverse_norm(values_in) * gain).astype(low)
            if "q" in wanted:
                turned = rotate(dot(normed, query_w[...]), cosine[line, :], sine[line, :])
                queries[block] = (turned.astype(low).astype(full) * HEAD_DIM**-0.5).astype(low)
            if "k" in wanted:
                turned = rotate(dot(normed, key_w[...]), cosine[line, :], sine[line, :])
                keys[block] = turned.astype(low)
                values[block] = dot(normed, value_w[...]).astype(low)

        masks = head_masks(rows)
        query_pos = own * rows + lax.broadcasted_iota(jnp.int32, (rows, rows), 1)
        document_start = start_of(query_pos[0:8], starts_ref)[0:1]

        def attend(block):
            key_pos = block * rows + lax.broadcasted_iota(jnp.int32, (rows, rows), 0)
            allowed = jnp.logical_and(key_pos >= document_start, key_pos <= query_pos)
            bias[...] = jnp.where(allowed, 0.0, NEGATIVE)

            def pair(index, carried):
                lanes = pl.ds(pl.multiple_of(index * 128, 128), 128)
                query, key, value = queries[own, :, lanes], keys[block, :, lanes], values[block, :, lanes]
                scores = [dot_nt(jnp.where(mask, key, 0), query) + bias[...] for mask in masks]
                old = [highest[index, head][0:1, :] for head in range(2)]
                new = [
                    jnp.maximum(old[head], jnp.max(scores[head], axis=0, keepdims=True))
                    for head in range(2)
                ]
                weight = [jnp.exp(scores[head] - new[head]).astype(low) for head in range(2)]
                for head in range(2):
                    totals[index, head] = totals[index, head] * jnp.exp(old[head] - new[head]) + dot_tn(
                        jnp.where(masks[head], value, 1), weight[head]
                    )
                    highest[index, head] = jnp.broadcast_to(new[head], (8, rows))
                return carried

            lax.fori_loop(0, pairs, pair, 0)

        totals[...] = jnp.zeros_like(totals)
        highest[...] = jnp.full(highest.shape, NEGATIVE, full)
        project(own, "qk")
        attend(own)
        def others(place, carried):
            for one in range(1, size):

                @pl.when(place == one)
                def _():
                    gather.arrive(one)
                    if one == size // 2:
                        for copy in waiting:
                            copy.start()

            block = jnp.bitwise_xor(own, place)

            @pl.when(block < own)
            def _():
                project(block, "k")
                attend(block)

            @pl.when(block > own)
            def _():
                project(block, "q")

            return carried

        lax.fori_loop(1, size, others, 0)
        keep = [
            pltpu.make_async_copy(source, target, keep_sem.at[index + 1])
            for index, (source, target) in enumerate(
                ((queries, queries_out), (keys, keys_out), (values, values_out))
            )
        ]
        for copy in keep:
            copy.start()

        lse_ref[...] = jnp.zeros_like(lse_ref)
        upper = lax.broadcasted_iota(jnp.int32, (128, rows), 0) < HEAD_DIM
        for index in range(pairs):
            halves = []
            for head in range(2):
                total = totals[index, head]
                line = HEAD_DIM if head == 0 else 0
                weight_sum = total[line : line + 1, :]
                halves.append(total / weight_sum)
                lse_ref[2 * index + head : 2 * index + head + 1, :] = highest[index, head][
                    0:1, :
                ] + jnp.log(weight_sum)
            attended_ref[:, index * 128 : index * 128 + 128] = jnp.transpose(
                jnp.where(upper, halves[0], halves[1])
            )
        keep.append(pltpu.make_async_copy(attended_ref, attended_out, keep_sem.at[4]))
        keep[-1].start()
        loads[5].wait()
        middle = stream[own].astype(full) + dot(attended_ref[...].astype(low), output_w[...])
        middle_ref[...] = middle
        keep.append(pltpu.make_async_copy(middle_ref, middle_out, keep_sem.at[5]))
        keep[-1].start()
        second = (
            middle
            * inverse_norm(middle)
            * pack[HEAD_ROWS + 1 : HEAD_ROWS + 2, :]
        )
        second_low = second.astype(low)
        outgoing_ref[...] = dot(picked, second_low).astype(low).reshape(count, cap, width)

        experts = previous_ref.shape[0]
        logits = dot_nt(second_low, pack[0:HEAD_ROWS, :].astype(low))[:, 0:experts] + lax.dot_general(
            prior[0:experts, :],
            carry_ref[...].astype(full),
            (((0,), (0,)), ((), ())),
            precision=HIGH,
        )
        logits = logits - jnp.max(logits, axis=1, keepdims=True)
        powers = jnp.exp(logits)
        probs_ref[...] = jnp.zeros_like(probs_ref)
        probs_ref[:, 0:experts] = powers / jnp.sum(powers, axis=1, keepdims=True)
        turned = jnp.transpose(probs_ref[...])[0:16]
        expert = lax.broadcasted_iota(jnp.int32, (16, rows), 0)
        weighted = jnp.zeros((slots, rows), full)
        for k in range(2):
            route = routes_ref[k : k + 1, :]
            gate = jnp.sum(jnp.where(expert == route, turned, 0.0), axis=0, keepdims=True)
            weighted = jnp.where(slot == targets[k], gate, weighted)
        gate_column = jnp.sum(weighted, axis=1, keepdims=True)
        for shift in range(count):
            column = jnp.broadcast_to(gate_column[shift * cap : (shift + 1) * cap], (cap, 128))
            gates_ref[shift] = jnp.zeros((8, 128), full)
            gates_ref[shift, :, 0:cap] = jnp.transpose(column)[0:8, :]
        pad = jnp.zeros((6, rows), full)
        target_rows = jnp.concatenate([targets[0], targets[1], pad], axis=0)
        target_rows = jnp.concatenate([target_rows] + [jnp.zeros((120, rows), full)], axis=0)
        targets_ref[...] = jnp.transpose(target_rows)

        gather.finish()
        for copy in keep + grad_copies:
            copy.wait()

    stream_shape = (size, rows, width)
    any_space = pl.BlockSpec(memory_space=pl.ANY)
    in_vmem = pl.BlockSpec(memory_space=pltpu.VMEM)
    square = (width, width)
    return pl.pallas_call(
        kernel,
        out_shape=[
            jax.ShapeDtypeStruct(stream_shape, low),
            jax.ShapeDtypeStruct(stream_shape, low),
            jax.ShapeDtypeStruct(stream_shape, low),
            jax.ShapeDtypeStruct((rows, width), full),
            jax.ShapeDtypeStruct((16, rows), full),
            jax.ShapeDtypeStruct((rows, width), full),
            jax.ShapeDtypeStruct((rows, 128), full),
            jax.ShapeDtypeStruct((rows, 128), full),
            jax.ShapeDtypeStruct((count, cap, width), low),
            jax.ShapeDtypeStruct((count, 8, 128), full),
            jax.ShapeDtypeStruct((count, cap, width), low),
        ],
        in_specs=[any_space]
        + [in_vmem] * 3
        + [pl.BlockSpec(memory_space=pltpu.SMEM)]
        + [any_space] * 4
        + [in_vmem] * 6
        + [any_space] * 2,
        out_specs=[any_space] * 4
        + [in_vmem, any_space]
        + [in_vmem] * 4
        + [any_space],
        scratch_shapes=[
            pltpu.VMEM(stream_shape, low),
            pltpu.VMEM(stream_shape, low),
            pltpu.VMEM(stream_shape, low),
            pltpu.VMEM(stream_shape, low),
            pltpu.VMEM(square, low),
            pltpu.VMEM(square, low),
            pltpu.VMEM(square, low),
            pltpu.VMEM(square, low),
            pltpu.VMEM((size * rows, 128), full),
            pltpu.VMEM((size * rows, 128), full),
            pltpu.VMEM((rows, rows), full),
            pltpu.VMEM((pairs, 2, 128, rows), full),
            pltpu.VMEM((pairs, 2, 8, rows), full),
            pltpu.VMEM((count, cap, width), low),
            pltpu.SemaphoreType.DMA((7,)),
            pltpu.SemaphoreType.DMA((1, size)),
            pltpu.SemaphoreType.DMA((1, size)),
            pltpu.SemaphoreType.DMA((count,)),
            pltpu.SemaphoreType.DMA((count,)),
            pltpu.SemaphoreType.DMA((6,)),
            pltpu.VMEM((24, width), full),
            pltpu.VMEM((16, rows), full),
            pltpu.VMEM((rows, width), full),
            pltpu.VMEM((rows, width), full),
        ],
        compiler_params=pltpu.CompilerParams(
            collective_id=0, has_side_effects=True, vmem_limit_bytes=60 * 2**20
        ),
        cost_estimate=pl.CostEstimate(
            flops=2 * size * rows * width * width * 3 + 16 * size * rows * rows * width,
            bytes_accessed=20 * 2**20,
            transcendentals=size * rows * rows * 12,
        ),
        name="attend",
    )(
        tokens,
        cotangent,
        previous,
        routes,
        starts,
        *weights,
        *params,
        carry,
        jnp.asarray(tables[0]),
        jnp.asarray(tables[1]),
    )


def add_into(target, source):
    rows = target.shape[0]
    piece = 96 if rows % 96 == 0 else (64 if rows % 64 == 0 else rows)

    def body(index, carried):
        part = pl.ds(pl.multiple_of(index * piece, piece), piece)
        total = target[part, :].astype(jnp.float32) + source[part, :].astype(jnp.float32)
        target[part, :] = total.astype(target.dtype)
        return carried

    lax.fori_loop(0, rows // piece, body, 0)


def column_of(values, index):
    return values[:, index : index + 1]


def backward_layer(
    tokens,
    cotangent,
    previous,
    routes,
    starts,
    forward,
    returns,
    weights,
    params,
    terms,
    first,
    ranks,
    cap,
    size,
    shares,
):
    rows, width = tokens.shape
    count = ranks[0] * ranks[1]
    slots = count * cap
    pairs = width // 128
    tables = rope_tables(size * rows)
    low, full = jnp.bfloat16, jnp.float32
    experts = previous.shape[0]
    copy_index = count + 1
    stat_rows = 16
    kinds = len(terms)

    def kernel(
        tokens_ref,
        cotangent_hbm,
        previous_ref,
        routes_ref,
        starts_ref,
        attended_hbm,
        lse_ref,
        middle_hbm,
        probs_ref,
        targets_ref,
        queries_hbm,
        keys_hbm,
        values_hbm,
        back_hbm,
        produced_hbm,
        dots_ref,
        query_hbm,
        key_hbm,
        value_hbm,
        output_hbm,
        router_ref,
        map_ref,
        first_gain_ref,
        second_gain_ref,
        vector_ref,
        cosine_hbm,
        sine_hbm,
        *rest,
    ):
        term_refs, first_hbm, rest = rest[:kinds], rest[kinds], rest[kinds + 1 :]
        result_out, token_grads_out, wide_out, small_ref = rest[:4]
        first_refs, rest = rest[4 : 4 + kinds], rest[4 + kinds :]
        (
            queries,
            keys,
            values,
            query_w,
            key_w,
            value_w,
            output_w,
            cosine,
            sine,
            bias,
            out_grads,
            stats,
            outputs,
            middle_grad,
            query_total,
            key_total,
            value_total,
            load_sem,
            gather_send,
            gather_recv,
            first_send,
            first_recv,
            out_send,
            out_recv,
            out_keep,
            sum_part,
            first_part,
            sum_load,
            pack,
            prior,
            cotangent_ref,
            attended_ref,
            middle_ref,
            back_ref,
            result_ref,
            token_grads_ref,
            wide_ref,
            near_sem,
        ) = rest
        own = lax.axis_index("ctx")
        line = pl.ds(pl.multiple_of(own * rows, rows), rows)
        loads = [
            pltpu.make_async_copy(source, target, load_sem.at[index])
            for index, (source, target) in enumerate(
                (
                    (output_hbm, output_w),
                    (queries_hbm, queries),
                    (keys_hbm, keys),
                    (values_hbm, values),
                    (cosine_hbm.at[line], cosine),
                    (sine_hbm.at[line], sine),
                    (query_hbm, query_w),
                    (key_hbm, key_w),
                    (value_hbm, value_w),
                )
            )
        ]
        share = lax.axis_index("dp")
        near_loads = [
            pltpu.make_async_copy(source, target, near_sem.at[index])
            for index, (source, target) in enumerate(
                (
                    (cotangent_hbm, cotangent_ref),
                    (attended_hbm, attended_ref),
                    (middle_hbm, middle_ref),
                    (back_hbm, back_ref),
                )
            )
        ]
        sum_loads = [
            pltpu.make_async_copy(
                term_refs[0].at[jnp.bitwise_xor(share, shares - 2)], sum_part, sum_load.at[0]
            ),
            pltpu.make_async_copy(first_hbm, first_part, sum_load.at[1]),
        ]
        for copy in sum_loads + near_loads:
            copy.start()
        greet_places(
            [(0,) + place for place in places_of(ranks, size)] + [(1, 0, 0), (2, 0, 0)]
        )
        first_copies = [
            pltpu.make_async_remote_copy(
                src_ref=(
                    term_refs[kind].at[jnp.bitwise_xor(share, shares - 1)] if kind else sum_part
                ),
                dst_ref=first_refs[kind],
                send_sem=first_send.at[kind],
                recv_sem=first_recv.at[kind],
                device_id=peer_at(1 if kind else 2, 0, 0),
                device_id_type=pl.DeviceIdType.MESH,
            )
            for kind in range(kinds)
        ]
        for copy in first_copies[1:]:
            copy.start()
        for copy in sum_loads:
            copy.wait()
        add_into(sum_part, first_part)
        first_copies[0].start()
        for load in loads:
            load.start()
        for load in near_loads:
            load.wait()
        output_copies = [
            send_block(produced_hbm, outputs, block, ranks, out_send, out_recv)
            for block in other_blocks(count)
        ]
        output_copies.append(keep_block(produced_hbm, outputs, count, out_keep))

        def keep_wide(index, value):
            half = width // 2
            for part in range(2):
                wide_ref[part, index * width : (index + 1) * width, :] = value[
                    :, part * half : (part + 1) * half
                ].astype(low)

        fill_rows(
            pack,
            prior,
            router_ref,
            map_ref,
            first_gain_ref,
            second_gain_ref,
            vector_ref,
            previous_ref,
        )
        lane = lax.broadcasted_iota(jnp.int32, (rows, 128), 1)
        upstream = cotangent_ref[...].astype(full)
        middle = middle_ref[...]
        inverse_second = inverse_norm(middle)
        unit_second = middle * inverse_second
        gain_second = pack[HEAD_ROWS + 1 : HEAD_ROWS + 2, :]
        second = unit_second * gain_second
        second_low = second.astype(low)
        heads_in = jnp.concatenate(
            [pack[0:HEAD_ROWS, :].astype(low), jnp.zeros((128 - HEAD_ROWS, width), low)], axis=0
        )
        mixed = dot_nt(second_low, heads_in)
        probs = probs_ref[...]
        route_rows = jnp.concatenate(
            [routes_ref[...].astype(full), jnp.zeros((126, rows), full)], axis=0
        )
        route_columns = jnp.transpose(route_rows).astype(jnp.int32)
        route = [column_of(route_columns, k) for k in range(2)]
        chosen = jnp.logical_or(lane == route[0], lane == route[1])
        gates = jnp.where(chosen, probs, 0.0)
        target = [column_of(targets_ref[...], k) for k in range(2)]

        gate_grad = jnp.zeros((rows, 128), full)
        place = lane.astype(full)
        for k in range(2):
            found = jnp.zeros((rows, 128), full)
            for shift in range(count):
                found = found + jnp.where(
                    jnp.logical_and(target[k] - shift * cap == place, lane < cap),
                    dots_ref[shift, 0:1, :],
                    0.0,
                )
            gate_grad = gate_grad + jnp.where(
                lane == route[k], jnp.sum(found, axis=1, keepdims=True), 0.0
            )
        copy_grad = jnp.sum(upstream * second, axis=1, keepdims=True)
        gate_grad = jnp.where(lane == copy_index, copy_grad, gate_grad)
        direct = column_of(gates, copy_index)
        constants = []
        for index in range(2):
            vector = pack[HEAD_ROWS + 2 + index : HEAD_ROWS + 3 + index, :]
            vector_dot = jnp.sum(upstream * vector, axis=1, keepdims=True)
            begin = experts + 2 * index
            spread_of = column_of(mixed, begin + 1) - column_of(mixed, begin)
            mixing = (1.0 / (1.0 + jnp.exp(spread_of)), 1.0 / (1.0 + jnp.exp(-spread_of)))
            gate = column_of(gates, copy_index + 1 + index)
            term = mixing[0] * copy_grad + mixing[1] * vector_dot
            gate_grad = jnp.where(lane == copy_index + 1 + index, term, gate_grad)
            direct = direct + gate * mixing[0]
            constants.append((gate, mixing, vector, vector_dot))
        prob_grad = jnp.where(chosen, gate_grad, 0.0)
        logit_grad = probs * (prob_grad - jnp.sum(probs * prob_grad, axis=1, keepdims=True))
        head_grad = logit_grad
        for index, (gate, mixing, vector, vector_dot) in enumerate(constants):
            mixing_grad = (gate * copy_grad, gate * vector_dot)
            mean = mixing[0] * mixing_grad[0] + mixing[1] * mixing_grad[1]
            for part in range(2):
                head_grad = jnp.where(
                    lane == experts + 2 * index + part,
                    mixing[part] * (mixing_grad[part] - mean),
                    head_grad,
                )
        head_low = head_grad.astype(low)

        slot = lax.broadcasted_iota(jnp.int32, (rows, slots), 1).astype(full)
        picked = [(slot == target[k]).astype(full).astype(low) for k in range(2)]
        second_grad = (
            dot(head_low, heads_in) + direct * upstream + dot(picked[0] + picked[1], back_ref[...])
        )
        normal_grad = second_grad * gain_second
        middle_total = upstream + inverse_second * (
            normal_grad - unit_second * jnp.mean(normal_grad * unit_second, axis=1, keepdims=True)
        )
        middle_grad[...] = middle_total
        middle_low = middle_total.astype(low)
        loads[0].wait()
        out_grad = dot_nt(middle_low, output_w[...]).astype(low)
        out_grads[own] = out_grad
        product = out_grad.astype(full) * attended_ref[...]
        masks = head_masks(rows)
        deltas = jnp.zeros((rows, 128), full)
        for index in range(pairs):
            part = product[:, index * 128 : index * 128 + 128]
            for head in range(2):
                total = jnp.sum(jnp.where(masks[head], part, 0.0), axis=1, keepdims=True)
                deltas = jnp.where(lane == 2 * index + head, total, deltas)
        stats[own, 0:stat_rows] = lse_ref[...]
        stats[own, stat_rows:] = jnp.transpose(deltas)[0:stat_rows]
        gather = Gather([out_grads, stats], size, gather_send, gather_recv)
        gather.forward(0)
        for copy in output_copies:
            copy.start()

        chosen_out = second * direct
        for gate, mixing, vector, vector_dot in constants:
            chosen_out = chosen_out + gate * mixing[1] * vector
        base = middle + chosen_out
        small_ref[...] = jnp.zeros_like(small_ref)
        small_ref[1:2, :] = jnp.sum(second_grad * unit_second, axis=0, keepdims=True)
        for index, (gate, mixing, vector, vector_dot) in enumerate(constants):
            small_ref[2 + index : 3 + index, :] = jnp.sum(
                gate * mixing[1] * upstream, axis=0, keepdims=True
            )
        small_ref[8:24, :] = dot_tn(head_low, second_low)[0:16]
        carry_grad = lax.dot_general(
            jnp.transpose(logit_grad)[0:16],
            prior[0:experts, :],
            (((1,), (1,)), ((), ())),
            precision=HIGH,
        )
        small_ref[24:40, 0:experts] = carry_grad
        keep_wide(3, dot_tn(attended_ref[...].astype(low), middle_low))
        keeps = [
            pltpu.make_async_copy(
                wide_ref.at[:, pl.ds(3 * width, width)],
                wide_out.at[:, pl.ds(3 * width, width)],
                near_sem.at[4],
            )
        ]
        keeps[0].start()

        for load in loads[1:4]:
            load.wait()
        query_total[...] = jnp.zeros_like(query_total)
        key_total[...] = jnp.zeros_like(key_total)
        value_total[...] = jnp.zeros_like(value_total)
        column = lax.broadcasted_iota(jnp.int32, (rows, rows), 0)
        row = lax.broadcasted_iota(jnp.int32, (rows, rows), 1)

        def block_side(block, as_query, as_key):
            key_block, query_block = (own if as_key else block), (own if as_query else block)
            key_pos, query_pos = key_block * rows + column, query_block * rows + row
            first = start_of(query_pos[0:8], starts_ref)[0:1]
            allowed = jnp.logical_and(key_pos >= first, key_pos <= query_pos)
            bias[...] = jnp.where(allowed, 0.0, NEGATIVE)

            def pair(index, carried):
                lanes = pl.ds(pl.multiple_of(index * 128, 128), 128)
                query, grad = queries[query_block, :, lanes], out_grads[query_block, :, lanes]
                key, value = keys[key_block, :, lanes], values[key_block, :, lanes]
                one_key = [jnp.where(mask, key, 0) for mask in masks]
                scores = [dot_nt(one_key[head], query) for head in range(2)]
                weight_grad = [dot_nt(jnp.where(mask, value, 0), grad) for mask in masks]
                weight, score = [], []
                for head in range(2):
                    lse = stats[query_block, pl.ds(2 * index + head, 1), :]
                    mean = stats[query_block, pl.ds(stat_rows + 2 * index + head, 1), :]
                    weight.append(jnp.exp(scores[head] + bias[...] - lse))
                    score.append((weight[head] * (weight_grad[head] - mean)).astype(low))
                if as_key:
                    value_total[:, lanes] += dot(
                        weight[0].astype(low), jnp.where(masks[0], grad, 0)
                    ) + dot(weight[1].astype(low), jnp.where(masks[1], grad, 0))
                    key_total[:, lanes] += dot(score[0], jnp.where(masks[0], query, 0)) + dot(
                        score[1], jnp.where(masks[1], query, 0)
                    )
                if as_query:
                    query_total[lanes, :] += dot_tn(one_key[0], score[0]) + dot_tn(
                        one_key[1], score[1]
                    )
                return carried

            lax.fori_loop(0, pairs, pair, 0)

        block_side(own, True, True)
        def earlier(place, carried):
            block = jnp.bitwise_xor(own, place)

            @pl.when(block < own)
            def _():
                block_side(block, True, False)

            return carried

        def later(place, carried):
            for one in range(1, size):

                @pl.when(place == one)
                def _():
                    gather.arrive(one)

            block = jnp.bitwise_xor(own, place)

            @pl.when(block > own)
            def _():
                block_side(block, False, True)

            return carried

        lax.fori_loop(1, size, earlier, 0)
        lax.fori_loop(1, size, later, 0)
        for load in loads[4:]:
            load.wait()
        inputs = tokens_ref[...].astype(full)
        inverse_first = inverse_norm(inputs)
        unit_first = inputs * inverse_first
        gain_first = pack[HEAD_ROWS : HEAD_ROWS + 1, :]
        normed = (unit_first * gain_first).astype(low)
        turn = -sine[...]
        query_grad = jnp.transpose(query_total[...]) * HEAD_DIM**-0.5
        query_low = rotate(query_grad, cosine[...], turn).astype(low)
        key_low = rotate(key_total[...], cosine[...], turn).astype(low)
        value_low = value_total[...].astype(low)
        first_grad = (
            dot_nt(query_low, query_w[...])
            + dot_nt(key_low, key_w[...])
            + dot_nt(value_low, value_w[...])
        )
        for index, part in enumerate((query_low, key_low, value_low)):
            keep_wide(index, dot_tn(normed, part))
        keeps.append(
            pltpu.make_async_copy(
                wide_ref.at[:, pl.ds(0, 3 * width)],
                wide_out.at[:, pl.ds(0, 3 * width)],
                near_sem.at[5],
            )
        )
        keeps[-1].start()
        small_ref[0:1, :] = jnp.sum(first_grad * unit_first, axis=0, keepdims=True)
        normal_grad = first_grad * gain_first
        token_grads_ref[...] = middle_grad[...] + inverse_first * (
            normal_grad - unit_first * jnp.mean(normal_grad * unit_first, axis=1, keepdims=True)
        )
        keeps.append(pltpu.make_async_copy(token_grads_ref, token_grads_out, near_sem.at[6]))
        keeps[-1].start()
        for copy in output_copies:
            copy.wait()
        for k in range(2):
            weight = jnp.sum(jnp.where(lane == route[k], probs, 0.0), axis=1, keepdims=True)
            base = base + weight * dot(picked[k], outputs[...].reshape(slots, width))
        result_ref[...] = base.astype(low)
        keeps.append(pltpu.make_async_copy(result_ref, result_out, near_sem.at[7]))
        keeps[-1].start()
        gather.finish()
        for copy in first_copies + keeps:
            copy.wait()

    stream_shape = (size, rows, width)
    any_space = pl.BlockSpec(memory_space=pl.ANY)
    in_vmem = pl.BlockSpec(memory_space=pltpu.VMEM)
    square = (width, width)
    return pl.pallas_call(
        kernel,
        out_shape=[
            jax.ShapeDtypeStruct((rows, width), low),
            jax.ShapeDtypeStruct((rows, width), full),
            jax.ShapeDtypeStruct((2, 4 * width, width // 2), low),
            jax.ShapeDtypeStruct((64, width), full),
        ]
        + [jax.ShapeDtypeStruct(term.shape[1:], low) for term in terms],
        in_specs=[in_vmem, any_space, in_vmem, in_vmem]
        + [pl.BlockSpec(memory_space=pltpu.SMEM)]
        + [any_space, in_vmem, any_space, in_vmem, in_vmem]
        + [any_space] * 3
        + [any_space, any_space, in_vmem]
        + [any_space] * 4
        + [in_vmem] * 5
        + [any_space] * (3 + kinds),
        out_specs=[any_space] * 3 + [in_vmem] + [any_space] * kinds,
        scratch_shapes=[
            pltpu.VMEM(stream_shape, low),
            pltpu.VMEM(stream_shape, low),
            pltpu.VMEM(stream_shape, low),
            pltpu.VMEM(square, low),
            pltpu.VMEM(square, low),
            pltpu.VMEM(square, low),
            pltpu.VMEM(square, low),
            pltpu.VMEM((rows, 128), full),
            pltpu.VMEM((rows, 128), full),
            pltpu.VMEM((rows, rows), full),
            pltpu.VMEM(stream_shape, low),
            pltpu.VMEM((size, 2 * stat_rows, rows), full),
            pltpu.VMEM((count, cap, width), low),
            pltpu.VMEM((rows, width), full),
            pltpu.VMEM((width, rows), full),
            pltpu.VMEM((rows, width), full),
            pltpu.VMEM((rows, width), full),
            pltpu.SemaphoreType.DMA((9,)),
            pltpu.SemaphoreType.DMA((2, size)),
            pltpu.SemaphoreType.DMA((2, size)),
            pltpu.SemaphoreType.DMA((kinds,)),
            pltpu.SemaphoreType.DMA((kinds,)),
            pltpu.SemaphoreType.DMA((count,)),
            pltpu.SemaphoreType.DMA((count,)),
            pltpu.SemaphoreType.DMA,
            pltpu.VMEM(terms[0].shape[1:], low),
            pltpu.VMEM(terms[0].shape[1:], low),
            pltpu.SemaphoreType.DMA((2,)),
            pltpu.VMEM((24, width), full),
            pltpu.VMEM((16, rows), full),
            pltpu.VMEM((rows, width), low),
            pltpu.VMEM((rows, width), full),
            pltpu.VMEM((rows, width), full),
            pltpu.VMEM((slots, width), low),
            pltpu.VMEM((rows, width), low),
            pltpu.VMEM((rows, width), full),
            pltpu.VMEM((2, 4 * width, width // 2), low),
            pltpu.SemaphoreType.DMA((8,)),
        ],
        compiler_params=pltpu.CompilerParams(
            collective_id=2, has_side_effects=True, vmem_limit_bytes=60 * 2**20
        ),
        cost_estimate=pl.CostEstimate(
            flops=14 * rows * width * width * 2 + 20 * size * rows * rows * width,
            bytes_accessed=30 * 2**20,
            transcendentals=size * rows * rows * 12,
        ),
        name="backward",
    )(
        tokens,
        cotangent,
        previous,
        routes,
        starts,
        *forward,
        *returns,
        *weights,
        *params,
        jnp.asarray(tables[0]),
        jnp.asarray(tables[1]),
        *terms,
        first,
    )


PIECES = 4
ORDER = (
    5, 10, 7, 0, 1, 6, 5, 0, 7, 0, 10, 1, 10, 0, 5,
    4, 2, 6, 0, 5, 7, 4, 0, 4, 3, 6, 10, 2, 0, 6,
    3, 0, 4, 8, 6, 2, 0, 9, 10, 8, 5, 5, 12, 1, 1,
    9, 8, 7, 11, 12, 12, 2, 1, 9, 0, 8, 9, 12, 11, 4,
    7, 11, 8, 11, 12, 9, 8, 0, 6, 3, 3, 12, 11, 7, 2,
    10, 11, 9, 3,
)
DENSE_TIMES = (7, 24, 34, 48, 62, 77, 91, 101, 118, 125, 132)
EXPERT_TIMES = (19, 14, 19, 4, 11, 2)


def halving_steps(size):
    steps, step = [], 0
    while 1 << step < size:
        bit = 1 << step
        steps += [(step, place) for place in range(size - bit, 0, -2 * bit)]
        step += 1
    return steps


def needed_before(step, place):
    return {(earlier, place | 1 << earlier) for earlier in range(step)}


def reduce_layer(terms, firsts, wide, small, spread, shares, ring, exchange_size):
    low, full = jnp.bfloat16, jnp.float32
    steps = halving_steps(shares)
    done = [[(0, shares - 1), (1, shares - 2)]] + [[(0, shares - 1)]] * (len(terms) - 1)
    kinds = len(terms)
    blocks = [term.shape[1:] for term in terms]
    members = ring // spread
    groups = 3
    near_bits = [1 << step for step in range(ring.bit_length() - 1)]
    far_bits = [1 << step for step in range(exchange_size.bit_length() - 1)]
    deep_bits = [1 << step for step in range(shares.bit_length() - 1)]
    near = [(0, 0, bit) for bit in near_bits]
    far = [(0, bit, 0) for bit in far_bits]
    deep = [(bit, 0, 0) for bit in deep_bits]
    orders = [near + far + deep, near[:1] + far + near[1:] + deep, near + far + deep]
    places = near + far + deep
    bit_count = len(places)
    group_rows = [wide.shape[1], wide.shape[1], small.shape[0]]
    tile = [16, 16, 8]
    plans = []
    for group in range(groups):
        length, plan = group_rows[group], []
        for _ in range(bit_count):
            halved = (length // 2) % tile[group] == 0
            length = length // 2 if halved else length
            plan.append((halved, length))
        plans.append(plan)

    def kernel(*refs):
        refs = list(refs)

        def take(number):
            taken = refs[:number]
            del refs[:number]
            return taken

        term_refs, first_refs = take(kinds), take(kinds)
        (wide_hbm, small_hbm) = take(2)
        gathered = take(kinds)
        (wide_out, small_out) = take(2)
        sums, landed = take(kinds), take(kinds)
        (halves, smalls) = take(2)
        group_landed = take(groups)
        (load_sem, step_send, step_recv, own_sem, ring_send, ring_recv) = take(6)
        (dense_send, dense_recv, dense_load) = take(3)
        share = lax.axis_index("dp")
        mine = lax.axis_index("ctx") // spread

        dense_in = [
            pltpu.make_async_copy(wide_hbm, halves, dense_load.at[0]),
            pltpu.make_async_copy(small_hbm, smalls, dense_load.at[1]),
        ]
        for copy in dense_in:
            copy.start()
        loads = []
        for kind in range(kinds):
            copies = [
                pltpu.make_async_copy(
                    first_refs[kind],
                    landed[kind].at[steps.index(done[kind][-1])],
                    load_sem.at[kind, shares // 2],
                )
            ]
            for place in range(shares - 2, -1, -2):
                copies.append(
                    pltpu.make_async_copy(
                        term_refs[kind].at[jnp.bitwise_xor(share, place)],
                        sums[kind].at[place // 2],
                        load_sem.at[kind, place // 2],
                    )
                )
            for copy in copies:
                copy.start()
            loads.append(copies)
        greet_places(places)

        def expert_chain(kind, piece):
            period, odd_wait, even_wait, near_wait, far_wait, last_wait = EXPERT_TIMES
            begin = time = period * (kind * PIECES + piece)
            slots = {step: index for index, step in enumerate(steps)}
            lines = blocks[kind][0] // PIECES
            window = pl.ds(piece * lines, lines)
            one = kind * PIECES + piece

            def transfer(step, place):
                index = slots[step, place]
                if place % 2 == 1:
                    source = term_refs[kind].at[jnp.bitwise_xor(share, place), window]
                else:
                    source = sums[kind].at[place // 2, window]
                return pltpu.make_async_remote_copy(
                    src_ref=source,
                    dst_ref=landed[kind].at[index, window],
                    send_sem=step_send.at[one, index],
                    recv_sem=step_recv.at[one, index],
                    device_id=peer_at(1 << step, 0, 0),
                    device_id_type=pl.DeviceIdType.MESH,
                )

            yield begin
            arrived, started = set(done[kind]), []
            waiting = [op for op in steps if op not in arrived]
            for op in list(waiting):
                if op[0] == 0:
                    transfer(*op).start()
                    started.append(op)
                    waiting.remove(op)
            while loads[kind]:
                loads[kind].pop().wait()
            step, place = done[kind][-1]
            add_into(
                sums[kind].at[(place ^ 1 << step) // 2, window],
                landed[kind].at[slots[step, place], window],
            )
            while True:
                for op in list(waiting):
                    if needed_before(*op) <= arrived:
                        transfer(*op).start()
                        started.append(op)
                        waiting.remove(op)
                if not started:
                    break
                op = started.pop(0)
                yield time + (even_wait if op[0] else odd_wait)
                transfer(*op).wait()
                arrived.add(op)
                add_into(
                    sums[kind].at[(op[1] ^ 1 << op[0]) // 2, window],
                    landed[kind].at[slots[op], window],
                )
            time += even_wait
            index = len(steps)
            bit = 1
            while bit < spread:
                copy = pltpu.make_async_remote_copy(
                    src_ref=sums[kind].at[0, window],
                    dst_ref=landed[kind].at[index, window],
                    send_sem=step_send.at[one, index],
                    recv_sem=step_recv.at[one, index],
                    device_id=peer_at(0, 0, bit),
                    device_id_type=pl.DeviceIdType.MESH,
                )
                copy.start()
                time += near_wait
                yield time
                copy.wait()
                add_into(sums[kind].at[0, window], landed[kind].at[index, window])
                index += 1
                bit *= 2
            keep = pltpu.make_async_copy(
                sums[kind].at[0, window], gathered[kind].at[mine, window], own_sem.at[one]
            )
            keep.start()
            sent = []

            def pass_on(place, bit):
                block = jnp.bitwise_xor(mine, place)
                target = gathered[kind].at[block, window]
                return pltpu.make_async_remote_copy(
                    src_ref=sums[kind].at[0, window] if place == 0 else target,
                    dst_ref=target,
                    send_sem=ring_send.at[one, place ^ bit],
                    recv_sem=ring_recv.at[one, place ^ bit],
                    device_id=peer_at(0, 0, bit * spread),
                    device_id_type=pl.DeviceIdType.MESH,
                )

            def forward(place):
                for bit, held in gather_steps(members):
                    if place in held:
                        copy = pass_on(place, bit)
                        copy.start()
                        sent.append(copy)

            forward(0)
            for place in range(1, members):
                wait = near_wait if place == 1 else far_wait if place & (place - 1) == 0 else last_wait
                yield time + wait + (far_wait if wait == last_wait else 0)
                bit = place & -place
                pass_on(place ^ bit, bit).wait_recv()
                forward(place)
            yield 1000
            keep.wait()
            for copy in sent:
                copy.wait_send()

        def bit_of(place):
            deep_bit, far_bit, near_bit = place
            axis, bit = ("dp", deep_bit) if deep_bit else ("exp", far_bit) if far_bit else ("ctx", near_bit)
            return lax.rem(lax.axis_index(axis) // bit, 2)

        def dense_chain(times):
            times = iter(times + tuple(range(times[-1] + 8, 900, 8)))
            buffers = [halves.at[0], halves.at[1], smalls]
            yield 0
            for copy in dense_in:
                copy.wait()
            begins = [0] * groups
            trail = []

            def window(begin, length, group):
                if isinstance(begin, int):
                    return pl.ds(begin, length)
                return pl.ds(pl.multiple_of(begin, tile[group]), length)

            def exchange_rows(group, step, source, target):
                return pltpu.make_async_remote_copy(
                    src_ref=source,
                    dst_ref=target,
                    send_sem=dense_send.at[group, step],
                    recv_sem=dense_recv.at[group, step],
                    device_id=peer_at(*orders[group][step % bit_count]),
                    device_id_type=pl.DeviceIdType.MESH,
                )

            for step in range(bit_count):
                copies = []
                for group in range(groups):
                    halved, length = plans[group][step]
                    upper = bit_of(orders[group][step])
                    if halved:
                        sent = begins[group] + (1 - upper) * length
                        begins[group] = begins[group] + upper * length
                    else:
                        sent = begins[group]
                    at = sum(size for _, size in plans[group][:step])
                    copy = exchange_rows(
                        group,
                        step,
                        buffers[group].at[window(sent, length, group)],
                        group_landed[group].at[pl.ds(at, length)],
                    )
                    copy.start()
                    copies.append((copy, at, length))
                trail.append(list(begins))
                yield next(times)
                for group, (copy, at, length) in enumerate(copies):
                    copy.wait()
                    add_into(
                        buffers[group].at[window(begins[group], length, group)],
                        group_landed[group].at[pl.ds(at, length)],
                    )
            outputs = [wide_out.at[0], wide_out.at[1], small_out]
            keeps = []
            for group in range(groups):
                part = window(begins[group], plans[group][-1][1], group)
                keep = pltpu.make_async_copy(
                    buffers[group].at[part], outputs[group].at[part], dense_load.at[group]
                )
                keep.start()
                keeps.append(keep)
            for keep in keeps:
                keep.wait()
            for step in range(bit_count - 1, -1, -1):
                copies = []
                for group in range(groups):
                    halved, length = plans[group][step]
                    if halved:
                        part = outputs[group].at[window(trail[step][group], length, group)]
                        copy = exchange_rows(group, bit_count + step, part, part)
                        copy.start()
                        copies.append(copy)
                if copies:
                    yield next(times)
                for copy in copies:
                    copy.wait()

        chains = [dense_chain(DENSE_TIMES)] + [
            expert_chain(kind, piece) for kind in range(kinds) for piece in range(PIECES)
        ]
        due = dict(enumerate(next(chain) for chain in chains))
        planned = list(ORDER) if (shares, ring, exchange_size) == (4, 4, 2) else []
        while due:
            index = planned.pop(0) if planned else min(due, key=lambda one: (due[one], one))
            time = next(chains[index], None)
            if time is None:
                del due[index]
            else:
                due[index] = time

    any_space = pl.BlockSpec(memory_space=pl.ANY)
    extra = len(steps) + spread.bit_length() - 1
    return pl.pallas_call(
        kernel,
        out_shape=[jax.ShapeDtypeStruct((members,) + block, low) for block in blocks]
        + [jax.ShapeDtypeStruct(wide.shape, low), jax.ShapeDtypeStruct(small.shape, full)],
        in_specs=[any_space] * (2 * kinds + 2),
        out_specs=[any_space] * (kinds + 2),
        scratch_shapes=[pltpu.VMEM((shares // 2,) + block, low) for block in blocks]
        + [pltpu.VMEM((extra,) + block, low) for block in blocks]
        + [pltpu.VMEM(wide.shape, low), pltpu.VMEM(small.shape, full)]
        + [
            pltpu.VMEM(
                (sum(length for _, length in plans[group]), (wide, wide, small)[group].shape[-1]),
                (low, low, full)[group],
            )
            for group in range(groups)
        ]
        + [
            pltpu.SemaphoreType.DMA((kinds, shares // 2 + 1)),
            pltpu.SemaphoreType.DMA((kinds * PIECES, extra)),
            pltpu.SemaphoreType.DMA((kinds * PIECES, extra)),
            pltpu.SemaphoreType.DMA((kinds * PIECES,)),
            pltpu.SemaphoreType.DMA((kinds * PIECES, members)),
            pltpu.SemaphoreType.DMA((kinds * PIECES, members)),
            pltpu.SemaphoreType.DMA((groups, 2 * bit_count)),
            pltpu.SemaphoreType.DMA((groups, 2 * bit_count)),
            pltpu.SemaphoreType.DMA((3,)),
        ],
        compiler_params=pltpu.CompilerParams(
            collective_id=3, has_side_effects=True, vmem_limit_bytes=60 * 2**20
        ),
        name="reduce",
    )(*terms, *firsts, wide, small)


def widen_layer(parts, wide, small, experts):
    members = parts[0].shape[0]
    pieces = 1
    steps = members * pieces
    squares = wide.shape[1] // (2 * wide.shape[2])
    width = 2 * wide.shape[2]
    lines = wide.shape[1] // steps
    turns = width // lines
    full = jnp.float32
    kinds = len(parts)

    def kernel(*refs):
        sources, wide_ref, small_ref = refs[:kinds], refs[kinds], refs[kinds + 1]
        targets = refs[kinds + 2 : 2 * kinds + 2]
        square_refs = refs[2 * kinds + 2 : 2 * kinds + 2 + squares]
        head_ref, map_ref, carry_ref, vector_ref, *gain_refs = refs[2 * kinds + 2 + squares :]
        step = pl.program_id(0) * pieces + pl.program_id(1)
        for source, target in zip(sources, targets):
            target[...] = source[...].astype(full)
        for index in range(squares):

            @pl.when(step // turns == index)
            def _():
                square_refs[index][:, 0 : width // 2] = wide_ref[0].astype(full)
                square_refs[index][:, width // 2 :] = wide_ref[1].astype(full)

        @pl.when(step == 0)
        def _():
            head_ref[...] = small_ref[8 : 8 + experts, :]
            for index in range(2):
                begin = 8 + experts + 2 * index
                map_ref[index] = small_ref[begin : begin + 2, :]
            carry_ref[...] = jnp.transpose(small_ref[24:40, 0:128])[0:experts, 0:experts]
            vector_ref[...] = small_ref[2:4, :]
            for index, target in enumerate(gain_refs):
                target[...] = small_ref[index : index + 1, :].reshape(width)

    def chunk(part):
        return pl.BlockSpec(
            (1, part.shape[1] // pieces, part.shape[2]), lambda member, piece: (member, piece, 0)
        )

    def square(index):
        return pl.BlockSpec(
            (lines, width),
            lambda member, piece: (
                jnp.clip(member * pieces + piece - index * turns, 0, turns - 1),
                0,
            ),
        )

    def whole(*shape):
        return pl.BlockSpec(shape, lambda member, piece: (0,) * len(shape))

    smalls = [(experts, width), (2, 2, width), (experts, experts), (2, width), (width,), (width,)]
    return pl.pallas_call(
        kernel,
        out_shape=[jax.ShapeDtypeStruct(part.shape, full) for part in parts]
        + [jax.ShapeDtypeStruct((width, width), full)] * squares
        + [jax.ShapeDtypeStruct(shape, full) for shape in smalls],
        grid=(members, pieces),
        in_specs=[chunk(part) for part in parts]
        + [
            pl.BlockSpec(
                (2, lines, width // 2), lambda member, piece: (0, member * pieces + piece, 0)
            ),
            whole(*small.shape),
        ],
        out_specs=[chunk(part) for part in parts]
        + [square(index) for index in range(squares)]
        + [whole(*shape) for shape in smalls],
        compiler_params=pltpu.CompilerParams(vmem_limit_bytes=60 * 2**20),
        name="widen",
    )(*parts, wide, small)


def local(
    tokens,
    cotangent,
    previous,
    routes,
    boundaries,
    norm_first,
    query_weight,
    key_weight,
    value_weight,
    output_weight,
    norm_second,
    router,
    gate_carry,
    constant_map,
    constant_vector,
    expert_gate,
    expert_linear,
    expert_down,
):
    model_width = tokens.shape[2]
    ring = lax.axis_size("ctx")
    group_size = expert_gate.shape[0]
    exchange_count = lax.axis_size("exp")
    spread = ring // group_size
    ranks = (exchange_count, group_size, spread)
    slot_total = exchange_count * group_size * CAP
    expert_total = router.shape[1]
    params = (
        router.T,
        jnp.transpose(constant_map, (0, 2, 1)),
        norm_first,
        norm_second,
        constant_vector,
    )
    prior = jnp.transpose(previous, (2, 0, 1))
    weights = (query_weight, key_weight, value_weight, output_weight)
    (
        queries,
        keys,
        values,
        attended,
        lse,
        middle,
        probs,
        targets,
        outgoing,
        slot_gates,
        grads_in,
    ) = attend_layer(
        tokens[0],
        cotangent[0],
        prior,
        routes[0].T,
        boundaries,
        weights,
        params,
        gate_carry,
        ranks,
        CAP,
        ring,
    )
    home_grads, produced, dots, gate_terms, linear_terms, down_terms, first = expert_layer(
        outgoing,
        slot_gates,
        grads_in.reshape(slot_total, model_width),
        (expert_gate, expert_linear, expert_down),
        ranks,
        lax.axis_size("dp"),
    )
    terms = (down_terms, gate_terms, linear_terms)
    shares = lax.axis_size("dp")
    result, token_grads, wide, small, *firsts = backward_layer(
        tokens[0],
        cotangent[0],
        prior,
        routes[0].T,
        boundaries,
        (attended, lse, middle, probs, targets, queries, keys, values),
        (home_grads.reshape(slot_total, model_width), produced, dots),
        weights,
        params,
        terms,
        first,
        ranks,
        CAP,
        ring,
        shares,
    )
    *parts, wide, small = reduce_layer(
        terms, firsts, wide, small, spread, shares, ring, exchange_count
    )
    (
        down_grads,
        gate_grads,
        linear_grads,
        query_grads,
        key_grads,
        value_grads,
        output_grads,
        router_grads,
        map_grads,
        carry_grads,
        vector_grads,
        first_grads,
        second_grads,
    ) = widen_layer(parts, wide, small, expert_total)
    return (
        result[None],
        token_grads[None],
        first_grads,
        query_grads,
        key_grads,
        value_grads,
        output_grads,
        second_grads,
        router_grads.T,
        carry_grads,
        jnp.transpose(map_grads, (0, 2, 1)),
        vector_grads,
        gate_grads,
        linear_grads,
        down_grads,
    )


def solution(mesh):
    return jax.shard_map(
        local,
        mesh=mesh,
        in_specs=(
            P(("dp", "exp"), "ctx", None),
            P(("dp", "exp"), "ctx", None),
            P(("dp", "exp"), "ctx", None),
            P(("dp", "exp"), "ctx", None),
            P(("dp", "exp"), None),
            P(),
            P(),
            P(),
            P(),
            P(),
            P(),
            P(),
            P(),
            P(),
            P(),
            P("exp", None, None),
            P("exp", None, None),
            P("exp", None, None),
        ),
        out_specs=(
            P(("dp", "exp"), "ctx", None),
            P(("dp", "exp"), "ctx", None),
            P(),
            P(),
            P(),
            P(),
            P(),
            P(),
            P(),
            P(),
            P(),
            P(),
            P("exp", None, "dp"),
            P("exp", None, "dp"),
            P("exp", "dp", None),
        ),
        check_vma=False,
    )
```
